32 devices in a mesh: wide: 8 (over z, x), narrow: 4 (over y, core).
Axes of the slice: x: 2, y: 2, z: 4, core: 2. Of those that a mesh axis runs over, the one named last changes fastest.
Arguments:
- hidden_in: bfloat16 [12288, 768], P(('wide', 'narrow')), may hold values from -6 to 6
- seq_lengths: int32 [96], P(('wide', 'narrow')), may hold values from 64 to 128
- mask_positions: int32 [96, 38], P(('wide', 'narrow')), may hold values from 0 to 127, as said below
- mask_vector: bfloat16 [768], P('wide'), may hold values from -5 to 5
- cotangent: bfloat16 [12288, 768], P(('wide', 'narrow')), may hold values from -6 to 6
- norm_gain: bfloat16 [2, 2, 768], P(None, None, 'wide'), may hold values from 0.099609375 to 1.8984375
- norm_bias: bfloat16 [2, 2, 768], P(None, None, 'wide'), may hold values from -1.5 to 1.5
- in_right: bfloat16 [2, 2, 768, 192], P(None, None, 'wide'), may hold values from -0.4375 to 0.4375
- in_left: bfloat16 [2, 2, 768, 192], P(None, None, 'wide'), may hold values from -0.4375 to 0.4375
- conv_taps: bfloat16 [2, 3, 768], P(None, None, 'wide'), may hold values from -3.5 to 3.5
- skip_bias: bfloat16 [2, 768], P(None, 'wide'), may hold values from -4 to 4
- filter_in: bfloat16 [2, 5, 128], P(None, None, 'wide'), may hold values from -6 to 6
- filter_in_bias: bfloat16 [2, 128], P(None, 'wide'), may hold values from -3.140625 to 3.140625
- filter_mid: bfloat16 [2, 128, 128], P(None, 'wide'), may hold values from -0.5 to 0.5
- filter_mid_bias: bfloat16 [2, 128], P(None, 'wide'), may hold values from -3.140625 to 3.140625
- filter_out: bfloat16 [2, 128, 1536], P(None, None, 'wide'), may hold values from -0.5 to 0.5
- decay_rates: bfloat16 [2, 768], P(None, 'wide'), may hold values from 3 to 15
- out_right: bfloat16 [2, 768, 192], P(None, 'wide'), may hold values from -0.4375 to 0.4375
- out_left: bfloat16 [2, 768, 192], P(None, 'wide'), may hold values from -0.4375 to 0.4375
- glu_right: bfloat16 [2, 2, 768, 768], P(None, None, 'wide'), may hold values from -0.4375 to 0.4375
- glu_left: bfloat16 [2, 2, 3072, 768], P(None, None, 'wide'), may hold values from -0.21875 to 0.21875
- down_right: bfloat16 [2, 3072, 192], P(None, 'wide'), may hold values from -0.21875 to 0.21875
- down_left: bfloat16 [2, 768, 192], P(None, 'wide'), may hold values from -0.4375 to 0.4375
Outputs:
- output: bfloat16 [12288, 768], P(('wide', 'narrow'))
- grad_input: float32 [12288, 768], P(('wide', 'narrow'))
- grad_mask_vector: float32 [768], P('wide')
- grad_norm_gain: float32 [2, 2, 768], P(None, None, 'wide')
- grad_norm_bias: float32 [2, 2, 768], P(None, None, 'wide')
- grad_in_right: float32 [2, 2, 768, 192], P(None, None, 'wide')
- grad_in_left: float32 [2, 2, 768, 192], P(None, None, 'wide')
- grad_conv_taps: float32 [2, 3, 768], P(None, None, 'wide')
- grad_skip_bias: float32 [2, 768], P(None, 'wide')
- grad_filter_in: float32 [2, 5, 128], P(None, None, 'wide')
- grad_filter_in_bias: float32 [2, 128], P(None, 'wide')
- grad_filter_mid: float32 [2, 128, 128], P(None, 'wide')
- grad_filter_mid_bias: float32 [2, 128], P(None, 'wide')
- grad_filter_out: float32 [2, 128, 1536], P(None, None, 'wide')
- grad_out_right: float32 [2, 768, 192], P(None, 'wide')
- grad_out_left: float32 [2, 768, 192], P(None, 'wide')
- grad_glu_right: float32 [2, 2, 768, 768], P(None, None, 'wide')
- grad_glu_left: float32 [2, 2, 3072, 768], P(None, None, 'wide')
- grad_down_right: float32 [2, 3072, 192], P(None, 'wide')
- grad_down_left: float32 [2, 768, 192], P(None, 'wide')
The draws below stay inside these ranges and needn't reach their ends.
Inputs may be any that keep to these rules, and one draw needn't show every extreme that they name: `mask_positions`: each row lists 38 different positions of its sequence.
All inputs are finite; a program needn't handle non-finite values.
Results may differ from the reference program's by a relative error of at most 0.024.
Values may be sent and summed in bfloat16 or wider, within the bound.
A program may use at most 320 MiB of HBM per device.

```python
import math
import jax
import jax.numpy as jnp
from jax import lax

D = 768
FF = 3072
BLOCKS = 4
ORDER = 128
EMB = 5
LEN = 128
LAYERS = 2
DB = 192
FB = 768
NMASK = 38
SEQS = 96
TOKENS = 12288


def draw_mask_positions(key, part):
    key = jax.random.fold_in(key, 7)
    scores = jax.random.randint(key, (SEQS, LEN), 0, 1 << 20, dtype=jnp.int32) * LEN
    scores = scores + jnp.arange(LEN, dtype=jnp.int32)[None, :]
    ranking = jnp.argsort(scores, axis=1, stable=True)
    return ranking[:, :NMASK].astype(jnp.int32)


def plant(array, rng, least, high):
    extent = array.shape
    spot = [jax.random.randint(jax.random.fold_in(rng, axis), (), 0, extent[axis]) for axis in range(len(extent))]
    array = array.at[tuple(spot)].set(least)
    longest = extent.index(max(extent))
    spot[longest] = (spot[longest] + 1) % extent[longest]
    return array.at[tuple(spot)].set(high)


def spiked(values, rng, source, target, shards_of, factor):
    owner, partner = [(jnp.arange(values.shape[axis_at]) // (values.shape[axis_at] // shards_of)).reshape([-1 if axis == axis_at else 1 for axis in range(values.ndim)]) for axis_at in (source, target)]
    chosen = jax.random.permutation(rng, shards_of)[partner]
    strong = (owner == chosen) | (owner == (partner + shards_of // 2) % shards_of)
    return jnp.where(strong, factor * values, values)


def steps_of(stream_key, extent, cuts, low, high):
    loudness, own = 1.0, jax.random.fold_in(stream_key, 6)
    for dim, shards_of in cuts:
        heights = jnp.exp(jax.random.uniform(jax.random.fold_in(own, dim), (shards_of,), jnp.float32, low / len(cuts), high / len(cuts)))
        loudness = loudness * jnp.repeat(heights, extent[dim] // shards_of).reshape([-1 if axis == dim else 1 for axis in range(len(extent))])
    return loudness


def noise(rng, dims, scale, reach, shards=(), kind=jnp.bfloat16):
    factor_of = steps_of(rng, dims, shards, -0.22, 0.18) if shards else 1.0
    array = jax.random.normal(rng, dims, jnp.float32) * scale * factor_of
    return jnp.minimum(jnp.maximum(array, -reach), reach).astype(kind)


def heavy_noise(own_key, shape, spread, bound, pieces, heavy, kind=jnp.bfloat16):
    values = spread * jax.random.normal(own_key, shape, jnp.float32)
    if pieces:
        values = values * steps_of(own_key, shape, pieces, -0.22, 0.18)
    return jnp.clip(spiked(values, jax.random.fold_in(own_key, 3), *heavy), -bound, bound).astype(kind)


def setup_inputs(seed: int = 0) -> dict:
    keys = jax.random.split(jax.random.key(seed), 24)
    return {
        "hidden_in": noise(keys[0], (TOKENS, D), 1.0, 6.0, ((0, 32),)),
        "seq_lengths": plant(jax.random.randint(keys[1], (SEQS,), LEN // 2, LEN + 1), jax.random.fold_in(keys[1], 1), LEN // 2, LEN).astype(jnp.int32),
        "mask_positions": draw_mask_positions(jax.random.fold_in(keys[23], 71), 0),
        "mask_vector": noise(keys[3], (D,), 1.0, 5.0, ((0, 8),)),
        "cotangent": heavy_noise(keys[4], (TOKENS, D), 1.0, 6.0, ((0, 32),), (0, 1, 32, 2.75)),
        "norm_gain": jnp.clip(1.0 + 0.18 * jax.random.normal(keys[5], (LAYERS, 2, D), jnp.float32), 0.099609375, 1.8984375).astype(jnp.bfloat16),
        "norm_bias": noise(keys[6], (LAYERS, 2, D), 0.3, 1.5, ((2, 8),)),
        "in_right": noise(keys[7], (LAYERS, 2, D, DB), DB ** -0.5, 0.4375, ((2, 8),)),
        "in_left": noise(keys[8], (LAYERS, 2, D, DB), DB ** -0.5, 0.4375, ((2, 8),)),
        "conv_taps": noise(keys[9], (LAYERS, 3, D), 3 ** -0.5, 3.5, ((2, 8),)),
        "skip_bias": noise(keys[10], (LAYERS, D), 1.0, 4.0, ((1, 8),)),
        "filter_in": noise(keys[11], (LAYERS, EMB, ORDER), 1 ** -0.5, 6.0, ((2, 8),)),
        "filter_in_bias": jnp.clip(jax.random.uniform(keys[12], (LAYERS, ORDER), jnp.float32, -3.140625, 3.140625), -3.140625, 3.140625).astype(jnp.bfloat16),
        "filter_mid": noise(keys[13], (LAYERS, ORDER, ORDER), ORDER ** -0.5, 0.5, ((1, 8),)),
        "filter_mid_bias": jnp.clip(jax.random.uniform(keys[14], (LAYERS, ORDER), jnp.float32, -3.140625, 3.140625), -3.140625, 3.140625).astype(jnp.bfloat16),
        "filter_out": noise(keys[15], (LAYERS, ORDER, 2 * D), ORDER ** -0.5, 0.5, ((2, 8),)),
        "decay_rates": jnp.clip(jnp.exp(math.log(15.0) - 1.609438 * jax.random.uniform(keys[16], (LAYERS, D), jnp.float32) ** steps_of(keys[16], (LAYERS, D), ((1, 8),), -0.2, 0.2)), 3.0, 15.0).astype(jnp.bfloat16),
        "out_right": noise(keys[17], (LAYERS, D, DB), DB ** -0.5, 0.4375, ((1, 8),)),
        "out_left": noise(keys[18], (LAYERS, D, DB), DB ** -0.5, 0.4375, ((1, 8),)),
        "glu_right": noise(keys[19], (LAYERS, 2, D, FB), DB ** -0.5, 0.4375, ((2, 8),)),
        "glu_left": noise(keys[20], (LAYERS, 2, FF, FB), FB ** -0.5, 0.21875, ((2, 8),)),
        "down_right": noise(keys[21], (LAYERS, FF, DB), FB ** -0.5, 0.21875, ((1, 8),)),
        "down_left": noise(keys[22], (LAYERS, D, DB), DB ** -0.5, 0.4375, ((1, 8),)),
    }


@jax.custom_vjp
def low(v):
    return lax.optimization_barrier(v.astype(jnp.bfloat16)).astype(jnp.float32)

@jax.custom_vjp
def low_back(v):
    return v

def low_keep(v):
    return (low(v), None)

def low_pass(kept, grad):
    return (grad,)

def back_keep(v):
    return (v, None)

def back_low(kept, grad):
    return (low(grad),)
low.defvjp(low_keep, low_pass)
low_back.defvjp(back_keep, back_low)
EPSILON = 1e-05
highest_precision = lax.Precision.HIGHEST

def permute(values):
    array_shape = values.shape
    blocks = array_shape[-2]
    split_view = values.reshape(array_shape[:-1] + (blocks, array_shape[-1] // blocks))
    return jnp.swapaxes(split_view, -3, -2).reshape(array_shape)

def monarch(inputs, right_factor, left_factor):
    row_count = inputs.shape[0]
    right_blocks = right_factor.reshape(BLOCKS, -1, right_factor.shape[-1])
    left_blocks = left_factor.reshape(BLOCKS, -1, left_factor.shape[-1])
    middle = jnp.einsum('rbi,bio->rbo', inputs.reshape(row_count, BLOCKS, -1), right_blocks, precision=highest_precision)
    middle = low_back(low(permute(middle)))
    output = jnp.einsum('rbi,bio->rbo', middle, left_blocks, precision=highest_precision)
    return low_back(output.reshape(row_count, -1))

def layer_norm(values, norm_gain, norm_bias):
    average = lax.optimization_barrier(jnp.mean(values, axis=-1, keepdims=True))
    centred = values - average
    variance = lax.optimization_barrier(jnp.mean(centred * centred, axis=-1, keepdims=True))
    return centred * lax.rsqrt(variance + EPSILON) * norm_gain + norm_bias

def position_features(length):
    positions = jnp.arange(length, dtype=jnp.float32)
    fraction = positions / length
    features = [fraction]
    for band_index in range(1, (EMB - 1) // 2 + 1):
        features.append(jnp.cos(2.0 * math.pi * band_index * fraction))
        features.append(jnp.sin(2.0 * math.pi * band_index * fraction))
    return jnp.stack(features, axis=1)

def make_filter(filter_in, filter_in_bias, filter_mid, filter_mid_bias, filter_out, decay_rates):
    length = LEN
    embedding = position_features(length)
    first_hidden = jnp.sin(jnp.dot(embedding, filter_in, precision=highest_precision) + filter_in_bias)
    second = jnp.sin(jnp.dot(first_hidden, filter_mid, precision=highest_precision) + filter_mid_bias)
    kernel = jnp.dot(second, filter_out, precision=highest_precision)
    fraction = jnp.arange(length, dtype=jnp.float32)[:, None] / length
    both_rates = jnp.concatenate([decay_rates, decay_rates])
    return kernel * jnp.exp(-fraction * both_rates[None, :])

def short_convolution(signal_rows, conv_taps):
    padded = jnp.pad(signal_rows, ((0, 0), (2, 0), (0, 0)))
    return conv_taps[0] * padded[:, :-2] + conv_taps[1] * padded[:, 1:-1] + conv_taps[2] * padded[:, 2:]

def circular_kernel(kernel):
    width = kernel.shape[1] // 2
    forward_part = kernel[:, :width]
    reverse_part = kernel[:, width:]
    first_row = forward_part[:1] + reverse_part[:1]
    spacer = jnp.zeros((1, width), jnp.float32)
    return jnp.concatenate([first_row, forward_part[1:], spacer, jnp.flip(reverse_part[1:], axis=0)], axis=0)

def long_convolution(signal_rows, kernel):
    padded_length = 2 * LEN
    circular = circular_kernel(kernel)
    spectrum = jnp.fft.rfft(signal_rows, n=padded_length, axis=1) * jnp.fft.rfft(circular, n=padded_length, axis=0)[None]
    return jnp.fft.irfft(spectrum, n=padded_length, axis=1)[:, :LEN]

def mixer(value_path, gate_path, conv_taps, skip_bias, kernel, live_mask):
    signal_rows = value_path.reshape(live_mask.shape[0], live_mask.shape[1], -1) * live_mask
    signal_rows = short_convolution(signal_rows, conv_taps) * live_mask
    mixed_signal = long_convolution(signal_rows, kernel) + signal_rows * skip_bias
    return mixed_signal.reshape(value_path.shape) * gate_path

def residual_block(hidden, layer_weights, decay_rates, live_mask):
    norm_gain, norm_bias, in_right, in_left, conv_taps, skip_bias, filter_in, filter_in_bias, filter_mid, filter_mid_bias, filter_out, out_right, out_left, glu_right, glu_left, down_right, down_left = layer_weights
    normed = low(layer_norm(hidden, norm_gain[0], norm_bias[0]))
    value_path = monarch(normed, in_right[0], in_left[0])
    gate_path = monarch(normed, in_right[1], in_left[1])
    kernel = make_filter(filter_in, filter_in_bias, filter_mid, filter_mid_bias, filter_out, decay_rates)
    mixed_signal = low(mixer(value_path, gate_path, conv_taps, skip_bias, kernel, live_mask))
    middle_hidden = hidden + monarch(mixed_signal, out_right, out_left)
    normed_two = low(layer_norm(middle_hidden, norm_gain[1], norm_bias[1]))
    upper_branch = monarch(normed_two, glu_right[0], glu_left[0])
    gate_branch = monarch(normed_two, glu_right[1], glu_left[1])
    glu_hidden = low(jax.nn.gelu(gate_branch, approximate=False) * upper_branch)
    return middle_hidden + monarch(glu_hidden, down_right, down_left)

def forward(params, decay_all, mask_value, inputs, live_mask, marked):
    hidden = jnp.where(marked, mask_value[None, :], inputs)
    for layer_index in range(LAYERS):
        layer_weights = tuple((member[layer_index] for member in params))
        hidden = residual_block(hidden, layer_weights, decay_all[layer_index], live_mask)
    return hidden

def reference(hidden_in, seq_lengths, mask_positions, mask_vector, cotangent, norm_gain, norm_bias, in_right, in_left, conv_taps, skip_bias, filter_in, filter_in_bias, filter_mid, filter_mid_bias, filter_out, decay_rates, out_right, out_left, glu_right, glu_left, down_right, down_left):
    weights = tuple((member.astype(jnp.float32) for member in (norm_gain, norm_bias, in_right, in_left, conv_taps, skip_bias, filter_in, filter_in_bias, filter_mid, filter_mid_bias, filter_out, out_right, out_left, glu_right, glu_left, down_right, down_left)))
    decay_all = decay_rates.astype(jnp.float32)
    mask_full = mask_vector.astype(jnp.float32)
    places = jnp.arange(LEN, dtype=jnp.int32)
    live_all = (places[None, :] < seq_lengths[:, None]).astype(jnp.float32)
    marked_all = jnp.any(mask_positions[:, :, None] == places[None, None, :], axis=1)
    group_size = math.gcd(SEQS, max(1, 4096 // LEN))
    group_count = SEQS // group_size
    rows_in = hidden_in.astype(jnp.float32).reshape(group_count, group_size * LEN, D)
    grad_rows_out = cotangent.astype(jnp.float32).reshape(group_count, group_size * LEN, D)
    live_groups = live_all.reshape(group_count, group_size, LEN, 1)
    marked_groups = marked_all.reshape(group_count, group_size * LEN, 1)

    def group_step(carried, group_items):
        row_block, live_part, marked_part, grad_output = group_items

        def forward_group(params, mask_value, inputs):
            return forward(params, decay_all, mask_value, inputs, live_part, marked_part)
        result, pullback = jax.vjp(forward_group, weights, mask_full, row_block)
        grad_params, grad_mask, grad_rows = pullback(grad_output)
        carried = (jax.tree.map(jnp.add, carried[0], grad_params), carried[1] + grad_mask)
        return (carried, (result.astype(jnp.bfloat16), grad_rows))
    initial = (jax.tree.map(jnp.zeros_like, weights), jnp.zeros_like(mask_full))
    (grad_params, grad_mask), (outputs, grad_rows) = lax.scan(group_step, initial, (rows_in, live_groups, marked_groups, grad_rows_out))

    def penalty(params):
        penalty_sum = jnp.zeros((), jnp.float32)
        for layer_index in range(LAYERS):
            kernel = make_filter(params[6][layer_index], params[7][layer_index], params[8][layer_index], params[9][layer_index], params[10][layer_index], decay_all[layer_index])
            penalty_sum = penalty_sum + 0.5 * SEQS * jnp.sum(kernel * kernel)
        return penalty_sum
    grad_params = jax.tree.map(jnp.add, grad_params, jax.grad(penalty)(weights))
    return (outputs.reshape(TOKENS, D), grad_rows.reshape(TOKENS, D), grad_mask, grad_params[0], grad_params[1], grad_params[2], grad_params[3], grad_params[4], grad_params[5], grad_params[6], grad_params[7], grad_params[8], grad_params[9], grad_params[10], grad_params[11], grad_params[12], grad_params[13], grad_params[14], grad_params[15], grad_params[16])
```

```python
from functools import partial
import math

import jax
import jax.numpy as jnp
import numpy as np
from jax import lax
from jax.experimental import pallas as pl
from jax.experimental.pallas import tpu as pltpu
from jax.sharding import PartitionSpec as P

BLOCKS = 4
EMB = 5
LAYERS = 2


EPSILON = 1e-05
highest_precision = lax.Precision.HIGHEST


def permute(values):
    array_shape = values.shape
    blocks = array_shape[-2]
    split_view = values.reshape(array_shape[:-1] + (blocks, array_shape[-1] // blocks))
    return jnp.swapaxes(split_view, -3, -2).reshape(array_shape)


def monarch_forward(inputs, right_factor, left_factor):
    row_count = inputs.shape[0]
    right_blocks = right_factor.reshape(BLOCKS, -1, right_factor.shape[-1])
    left_blocks = left_factor.reshape(BLOCKS, -1, left_factor.shape[-1])
    middle = jnp.einsum(
        "rbi,bio->rbo",
        inputs.reshape(row_count, BLOCKS, -1),
        right_blocks,
        preferred_element_type=jnp.float32,
    )
    middle = permute(middle).astype(jnp.bfloat16)
    output = jnp.einsum("rbi,bio->rbo", middle, left_blocks, preferred_element_type=jnp.float32)
    return (middle, output.reshape(row_count, -1))


def monarch_backward(inputs, middle, right_factor, left_factor, grad_output):
    row_count = inputs.shape[0]
    right_blocks = right_factor.reshape(BLOCKS, -1, right_factor.shape[-1])
    left_blocks = left_factor.reshape(BLOCKS, -1, left_factor.shape[-1])
    grad_low = grad_output.astype(jnp.bfloat16).reshape(row_count, BLOCKS, -1)
    grad_left = jnp.einsum("rbi,rbo->bio", middle, grad_low, preferred_element_type=jnp.float32)
    grad_middle = jnp.einsum(
        "rbo,bio->rbi", grad_low, left_blocks, preferred_element_type=jnp.float32
    )
    grad_middle = permute(grad_middle).astype(jnp.bfloat16)
    input_blocks = inputs.reshape(row_count, BLOCKS, -1)
    grad_right = jnp.einsum(
        "rbi,rbo->bio", input_blocks, grad_middle, preferred_element_type=jnp.float32
    )
    grad_inputs = jnp.einsum(
        "rbo,bio->rbi", grad_middle, right_blocks, preferred_element_type=jnp.float32
    )
    return (
        grad_inputs.reshape(row_count, -1),
        grad_right.reshape(right_factor.shape),
        grad_left.reshape(left_factor.shape),
    )


def layer_norm(values, norm_gain, norm_bias):
    average = jnp.mean(values, axis=-1, keepdims=True)
    centred = values - average
    variance = jnp.mean(centred * centred, axis=-1, keepdims=True)
    return centred * lax.rsqrt(variance + EPSILON) * norm_gain + norm_bias


def position_features(length):
    positions = jnp.arange(length, dtype=jnp.float32)
    fraction = positions / length
    features = [fraction]
    for band_index in range(1, (EMB - 1) // 2 + 1):
        features.append(jnp.cos(2.0 * math.pi * band_index * fraction))
        features.append(jnp.sin(2.0 * math.pi * band_index * fraction))
    return jnp.stack(features, axis=1)


def make_filter(
    filter_in, filter_in_bias, filter_mid, filter_mid_bias, filter_out, decay_rates, length
):
    embedding = position_features(length)
    first_hidden = jnp.sin(
        jnp.dot(embedding, filter_in, precision=highest_precision) + filter_in_bias
    )
    second = jnp.sin(
        jnp.dot(first_hidden, filter_mid, precision=highest_precision) + filter_mid_bias
    )
    kernel = jnp.dot(second, filter_out, precision=highest_precision)
    fraction = jnp.arange(length, dtype=jnp.float32)[:, None] / length
    both_rates = jnp.concatenate([decay_rates, decay_rates])
    return kernel * jnp.exp(-fraction * both_rates[None, :])


def short_convolution(signal_rows, conv_taps):
    padded = jnp.pad(signal_rows, ((0, 0), (2, 0), (0, 0)))
    return (
        conv_taps[0] * padded[:, :-2]
        + conv_taps[1] * padded[:, 1:-1]
        + conv_taps[2] * padded[:, 2:]
    )


def spectral_tables(length, span):
    padded_length = 2 * length
    frequency = jnp.arange(length + 1, dtype=jnp.int32)
    places = jnp.arange(span, dtype=jnp.int32)
    phase_index = frequency[:, None] * places[None, :] % padded_length
    angles = phase_index.astype(jnp.float32) * (2.0 * math.pi / padded_length)
    ends = (frequency == 0) | (frequency == length)
    weights = jnp.where(ends, 1.0, 2.0).astype(jnp.float32) / padded_length
    return (jnp.cos(angles), jnp.sin(angles), weights)


def circular_kernel(kernel):
    width = kernel.shape[1] // 2
    forward_part = kernel[:, :width]
    reverse_part = kernel[:, width:]
    first_row = forward_part[:1] + reverse_part[:1]
    spacer = jnp.zeros((1, width), jnp.float32)
    return jnp.concatenate(
        [first_row, forward_part[1:], spacer, jnp.flip(reverse_part[1:], axis=0)], axis=0
    )


def long_convolution(signal_rows, kernel):
    length = signal_rows.shape[1]
    cosine_lookup, sine_lookup, weights = spectral_tables(length, length)
    kernel_cosine, kernel_sine, unused = spectral_tables(length, 2 * length)
    circular = circular_kernel(kernel)
    real_signal = jnp.einsum("ik,hkm->him", cosine_lookup, signal_rows, precision=highest_precision)
    imaginary_signal = -jnp.einsum(
        "ik,hkm->him", sine_lookup, signal_rows, precision=highest_precision
    )
    kernel_real = jnp.dot(kernel_cosine, circular, precision=highest_precision)
    kernel_imaginary = -jnp.dot(kernel_sine, circular, precision=highest_precision)
    real_product = real_signal * kernel_real - imaginary_signal * kernel_imaginary
    imaginary_product = real_signal * kernel_imaginary + imaginary_signal * kernel_real
    inverse_cosine_table = cosine_lookup * weights[:, None]
    inverse_sine_table = sine_lookup * weights[:, None]
    return jnp.einsum(
        "hp,ihj->ipj", inverse_cosine_table, real_product, precision=highest_precision
    ) - jnp.einsum(
        "hp,ihj->ipj", inverse_sine_table, imaginary_product, precision=highest_precision
    )


def mixer_piece(
    value_path,
    gate_path,
    conv_taps,
    skip_bias,
    filter_in,
    filter_in_bias,
    filter_mid,
    filter_mid_bias,
    filter_out,
    decay_rates,
    live_mask,
    share,
):
    length = live_mask.shape[1]
    kernel = make_filter(
        filter_in, filter_in_bias, filter_mid, filter_mid_bias, filter_out, decay_rates, length
    )
    signal_rows = value_path.reshape(live_mask.shape[0], length, -1) * live_mask
    signal_rows = short_convolution(signal_rows, conv_taps) * live_mask
    mixed_signal = long_convolution(signal_rows, kernel) + signal_rows * skip_bias
    return (mixed_signal.reshape(value_path.shape) * gate_path, share * jnp.sum(kernel * kernel))


def glu_piece(upper_branch, gate_branch):
    return jax.nn.gelu(gate_branch, approximate=False) * upper_branch


def small_weights(layer_weights):
    return tuple(
        (layer_weights[position].astype(jnp.float32) for position in (4, 5, 6, 7, 8, 9, 10))
    )


def forward_layer(hidden, layer_weights, live_mask):
    (
        norm_gain,
        norm_bias,
        in_right,
        in_left,
        conv_taps,
        skip_bias,
        filter_in,
        filter_in_bias,
        filter_mid,
        filter_mid_bias,
        filter_out,
        decay_rates,
        out_right,
        out_left,
        glu_right,
        glu_left,
        down_right,
        down_left,
    ) = layer_weights
    gains = norm_gain.astype(jnp.float32)
    biases = norm_bias.astype(jnp.float32)
    small = small_weights(layer_weights)
    normed = layer_norm(hidden, gains[0], biases[0]).astype(jnp.bfloat16)
    middle_value, value_path = monarch_forward(normed, in_right[0], in_left[0])
    middle_gate, gate_path = monarch_forward(normed, in_right[1], in_left[1])
    mixed_signal, unused = mixer_piece(
        value_path,
        gate_path,
        small[0],
        small[1],
        small[2],
        small[3],
        small[4],
        small[5],
        small[6],
        decay_rates.astype(jnp.float32),
        live_mask,
        0.0,
    )
    mixed_signal = mixed_signal.astype(jnp.bfloat16)
    middle_out, branch = monarch_forward(mixed_signal, out_right, out_left)
    middle_hidden = hidden + branch
    normed_two = layer_norm(middle_hidden, gains[1], biases[1]).astype(jnp.bfloat16)
    middle_up, upper_branch = monarch_forward(normed_two, glu_right[0], glu_left[0])
    middle_glu, gate_branch = monarch_forward(normed_two, glu_right[1], glu_left[1])
    glu_hidden = glu_piece(upper_branch, gate_branch).astype(jnp.bfloat16)
    middle_down, branch_two = monarch_forward(glu_hidden, down_right, down_left)
    saved = (
        hidden,
        normed,
        middle_value,
        value_path,
        middle_gate,
        gate_path,
        mixed_signal,
        middle_out,
        middle_hidden,
        normed_two,
        middle_up,
        upper_branch,
        middle_glu,
        gate_branch,
        glu_hidden,
        middle_down,
    )
    return (middle_hidden + branch_two, saved)


def backward_layer(grad_hidden, layer_weights, saved, live_mask, share):
    (
        norm_gain,
        norm_bias,
        in_right,
        in_left,
        conv_taps,
        skip_bias,
        filter_in,
        filter_in_bias,
        filter_mid,
        filter_mid_bias,
        filter_out,
        decay_rates,
        out_right,
        out_left,
        glu_right,
        glu_left,
        down_right,
        down_left,
    ) = layer_weights
    (
        hidden,
        normed,
        middle_value,
        value_path,
        middle_gate,
        gate_path,
        mixed_signal,
        middle_out,
        middle_hidden,
        normed_two,
        middle_up,
        upper_branch,
        middle_glu,
        gate_branch,
        glu_hidden,
        middle_down,
    ) = saved
    gains = norm_gain.astype(jnp.float32)
    biases = norm_bias.astype(jnp.float32)
    small = small_weights(layer_weights)
    grad_glu, grad_down_right, grad_down_left = monarch_backward(
        glu_hidden, middle_down, down_right, down_left, grad_hidden
    )
    unused, glu_pull = jax.vjp(glu_piece, upper_branch, gate_branch)
    grad_upper, grad_gate = glu_pull(grad_glu)
    grad_normed_up, grad_right_up, grad_left_up = monarch_backward(
        normed_two, middle_up, glu_right[0], glu_left[0], grad_upper
    )
    grad_normed_gate, grad_right_gate, grad_left_gate = monarch_backward(
        normed_two, middle_glu, glu_right[1], glu_left[1], grad_gate
    )
    unused, norm_pull = jax.vjp(layer_norm, middle_hidden, gains[1], biases[1])
    grad_middle, grad_gain_two, grad_bias_two = norm_pull(grad_normed_up + grad_normed_gate)
    grad_middle = grad_middle + grad_hidden
    grad_mixed, grad_out_right, grad_out_left = monarch_backward(
        mixed_signal, middle_out, out_right, out_left, grad_middle
    )
    mixer_local = partial(
        mixer_piece, decay_rates=decay_rates.astype(jnp.float32), live_mask=live_mask, share=share
    )
    unused, mixer_pull = jax.vjp(
        mixer_local,
        value_path,
        gate_path,
        small[0],
        small[1],
        small[2],
        small[3],
        small[4],
        small[5],
        small[6],
    )
    mixer_grads = mixer_pull((grad_mixed, jnp.ones((), jnp.float32)))
    grad_normed_value, grad_right_value, grad_left_value = monarch_backward(
        normed, middle_value, in_right[0], in_left[0], mixer_grads[0]
    )
    grad_normed_path, grad_right_path, grad_left_path = monarch_backward(
        normed, middle_gate, in_right[1], in_left[1], mixer_grads[1]
    )
    unused, norm_pull_one = jax.vjp(layer_norm, hidden, gains[0], biases[0])
    grad_before, grad_gain_one, grad_bias_one = norm_pull_one(grad_normed_value + grad_normed_path)
    grads = (
        jnp.stack([grad_gain_one, grad_gain_two]),
        jnp.stack([grad_bias_one, grad_bias_two]),
        jnp.stack([grad_right_value, grad_right_path]),
        jnp.stack([grad_left_value, grad_left_path]),
        mixer_grads[2],
        mixer_grads[3],
        mixer_grads[4],
        mixer_grads[5],
        mixer_grads[6],
        mixer_grads[7],
        mixer_grads[8],
        grad_out_right,
        grad_out_left,
        jnp.stack([grad_right_up, grad_right_gate]),
        jnp.stack([grad_left_up, grad_left_gate]),
        grad_down_right,
        grad_down_left,
    )
    return (grad_before + grad_middle, grads)


F32 = jnp.float32
BF16 = jnp.bfloat16
VMEM_BYTES = 60 * 1024 * 1024


def dot(left, right):
    return jnp.dot(left, right, preferred_element_type=F32)


def dot_rows(left, right):
    return lax.dot_general(left, right, (((0,), (0,)), ((), ())), preferred_element_type=F32)


def dot_columns(left, right):
    return lax.dot_general(left, right, (((1,), (1,)), ((), ())), preferred_element_type=F32)


def exact(left, right, dims=(1, 0)):
    return lax.dot_general(
        left,
        right,
        (((dims[0],), (dims[1],)), ((), ())),
        precision=highest_precision,
        preferred_element_type=F32,
    )


def columns(values, index, width):
    return values[:, index * width : (index + 1) * width]


def shuffled(parts):
    chunk = parts[0].shape[1] // BLOCKS
    return [
        jnp.concatenate([columns(part, index, chunk) for part in parts], axis=1)
        for index in range(BLOCKS)
    ]


def normalised(values):
    average = jnp.mean(values, axis=-1, keepdims=True)
    centred = values - average
    variance = jnp.mean(centred * centred, axis=-1, keepdims=True)
    scale = lax.rsqrt(variance + EPSILON)
    return centred * scale, scale


def norm_backward(grad, hidden, gain):
    unit, scale = normalised(hidden)
    grad_gain = jnp.sum(grad * unit, axis=0, keepdims=True)
    grad_bias = jnp.sum(grad, axis=0, keepdims=True)
    scaled = grad * gain
    mean_one = jnp.mean(scaled, axis=-1, keepdims=True)
    mean_two = jnp.mean(scaled * unit, axis=-1, keepdims=True)
    return scale * (scaled - mean_one - unit * mean_two), grad_gain, grad_bias


def flip(bit, by):
    return 1 - bit if by else bit


def place():
    w = lax.axis_index("wide")
    n = lax.axis_index("narrow")
    return w // 2, w % 2, n // 2, n % 2


KINDS = ((0, 0, 0, 4), (1, 0, 0, 4), (0, 1, 0, 4), (1, 1, 0, 2), (1, 1, 2, 2))


def relative(z, distance):
    high, low = z // 2, z % 2
    return 2 * flip(high, distance // 2) + flip(low, distance % 2)


def piece_copies(pieces, sems, targets_of):
    z, x, y, c = place()
    copies = []
    for core in range(2):
        for kind, (dx, dy, first, count) in enumerate(KINDS):
            source = pieces[core * len(KINDS) + kind]
            for slot in range(count):
                owner = (relative(z, first + slot), flip(x, dx), flip(y, dy), flip(c, core))
                for row, target in targets_of(*owner):
                    view = source.at[slot, pl.ds(row, target.shape[0])]
                    copies.append(pltpu.make_async_copy(view, target, sems.at[len(copies)]))
    return copies


def grad_copies(result, sems, sources_of):
    z, x, y, c = place()
    copies = []
    for core in range(2):
        for dx in range(2):
            for dy in range(2):
                for dz in range(4):
                    owner = (relative(z, dz), flip(x, dx), flip(y, dy), flip(c, core))
                    for row, source in sources_of(*owner):
                        view = result.at[core, dx, dy, dz, pl.ds(row, source.shape[0])]
                        copies.append(pltpu.make_async_copy(source, view, sems.at[len(copies)]))
    return copies


def start_all(copies):
    for copy in copies:
        copy.start()


def wait_all(copies):
    for copy in copies:
        copy.wait()


def glu_spots(left, right):
    def spots(z, x, y, c):
        tall, short = left.shape[2] // 4, right.shape[1] // 16
        return (
            (0, left.at[y, z, pl.ds(pl.multiple_of((2 * x + c) * tall, 16), tall)]),
            (tall, right.at[y, pl.ds(pl.multiple_of((4 * z + 2 * x + c) * short, 16), short)]),
        )

    return spots


def mix_spots(mix):
    def spots(z, x, y, c):
        rows = mix.shape[1] // 4
        return ((0, mix.at[2 * z + x, pl.ds(pl.multiple_of((2 * y + c) * rows, 16), rows)]),)

    return spots


def factor(mix, rows, kind, block):
    width = mix.shape[2] // 4
    low = kind * width
    top = mix[2 * block, rows : rows + width // 2, low : low + width]
    bottom = mix[2 * block + 1, rows : rows + width // 2, low : low + width]
    return jnp.concatenate([top, bottom], axis=0)


def down_factor(mix, first, block):
    width = mix.shape[2] // 4
    half = width // 2
    parts = []
    for shard in (2 * block, 2 * block + 1):
        for index in range(4):
            parts.append(mix[shard, first : first + half, index * width : (index + 1) * width])
    return jnp.concatenate(parts, axis=0)


def monarch_small(inputs, right, left):
    width = inputs.shape[1] // BLOCKS
    parts = [dot(columns(inputs, b, width), right(b)) for b in range(BLOCKS)]
    middle = [part.astype(BF16) for part in shuffled(parts)]
    return middle, [dot(middle[b], left(b)) for b in range(BLOCKS)]


def monarch_small_backward(inputs, middle, grads, right, left):
    width = inputs.shape[1] // BLOCKS
    grad_left = [dot_rows(middle[b], grads[b]) for b in range(BLOCKS)]
    back = shuffled([dot_columns(grads[b], left(b)) for b in range(BLOCKS)])
    back = [part.astype(BF16) for part in back]
    grad_right = [dot_rows(columns(inputs, b, width), back[b]) for b in range(BLOCKS)]
    return [dot_columns(back[b], right(b)) for b in range(BLOCKS)], grad_right, grad_left


def store_factor(mix, rows, kind, block, value):
    width = mix.shape[2] // 4
    half = width // 2
    low = kind * width
    mix[2 * block, rows : rows + half, low : low + width] = value[:half].astype(BF16)
    mix[2 * block + 1, rows : rows + half, low : low + width] = value[half:].astype(BF16)


def cell(values):
    rise = 0.5 * (1.0 + lax.erf(values * (0.5**0.5)))
    return rise, jnp.exp(-0.5 * values * values) * ((2.0 * math.pi) ** -0.5)


def glu_forward_kernel(hidden, table, mix, *refs):
    pieces = refs[:10]
    result, normed_out, middle_out, branch_out, glu_out, down_out = refs[10:16]
    left, right, parts, sems = refs[16:]
    copies = piece_copies(pieces, sems, glu_spots(left, right))
    start_all(copies)
    rows, width = hidden.shape
    block = width // BLOCKS
    unit, unused = normalised(hidden[...])
    normed = (unit * table[1:2] + table[3:4]).astype(BF16)
    normed_out[...] = normed
    wait_all(copies)
    for u in range(2):
        for b in range(BLOCKS):
            part = dot(columns(normed, b, block), right[u, b * block : (b + 1) * block]).astype(BF16)
            for q in range(BLOCKS):
                middle_out[u, q, :, b * block : (b + 1) * block] = columns(part, q, block)
    for q in range(BLOCKS):
        upper = dot(middle_out[0, q], left[0, q])
        gate = dot(middle_out[1, q], left[1, q])
        branch_out[0, q] = upper.astype(BF16)
        branch_out[1, q] = gate.astype(BF16)
        glu = (gate * cell(gate)[0] * upper).astype(BF16)
        glu_out[q] = glu
        parts[q] = dot(glu, down_factor(mix, 7 * block // 6, q))
    down = [part.astype(BF16) for part in shuffled([parts[q] for q in range(BLOCKS)])]
    for b in range(BLOCKS):
        down_out[b] = down[b]
        span = slice(b * block, (b + 1) * block)
        result[:, span] = hidden[:, span] + dot(down[b], factor(mix, block // 2, 2, b))


def glu_backward_kernel(grad, hidden, table, mix, normed, middle, branch, glu, down, *refs):
    pieces = refs[:10]
    result, norm_out, mix_grad, glu_grad = refs[10:14]
    left, right, low, back, sems, out_sems = refs[14:]
    copies = piece_copies(pieces, sems, glu_spots(left, right))
    start_all(copies)
    rows, width = hidden.shape
    block = width // BLOCKS
    incoming = grad[...]
    half = incoming.astype(BF16)
    backs = []
    for b in range(BLOCKS):
        part = columns(half, b, block)
        mix_grad[1, b] = dot_rows(down[b], part).astype(BF16)
        backs.append(dot_columns(part, factor(mix, block // 2, 2, b)))
    backs = shuffled(backs)
    for q in range(BLOCKS):
        low[q] = backs[q].astype(BF16)
    wait_all(copies)
    for q in range(BLOCKS):
        step = low[q]
        product = dot_rows(glu[q], step).astype(BF16)
        for index in range(BLOCKS):
            mix_grad[2 + index, q] = product[index * block : (index + 1) * block]
        grad_glu = dot_columns(step, down_factor(mix, 7 * block // 6, q))
        upper = branch[0, q].astype(F32)
        gate = branch[1, q].astype(F32)
        rise, density = cell(gate)
        terms = (grad_glu * gate * rise, grad_glu * upper * (rise + gate * density))
        for u in range(2):
            term = terms[u].astype(BF16)
            wide = dot_columns(term, left[u, q]).astype(BF16)
            left[u, q] = dot_rows(middle[u, q], term).astype(BF16)
            for b in range(BLOCKS):
                back[u, b, :, q * block : (q + 1) * block] = columns(wide, b, block)
    outgoing = []
    for b in range(BLOCKS):
        span = slice(b * block, (b + 1) * block)
        total = None
        for u in range(2):
            term = dot_columns(back[u, b], right[u, span])
            right[u, span] = dot_rows(normed[:, span], back[u, b]).astype(BF16)
            total = term if total is None else total + term
        outgoing.append(total)
    writes = grad_copies(glu_grad, out_sems, glu_spots(left, right))
    start_all(writes)
    through, gain, bias = norm_backward(
        jnp.concatenate(outgoing, axis=1), hidden[...], table[1:2]
    )
    result[...] = incoming + through
    norm_out[0:1] = gain
    norm_out[1:2] = bias
    wait_all(writes)


def shifted(values, by):
    length = values.shape[0]
    rolled = pltpu.roll(values, by % length, 0)
    row = lax.broadcasted_iota(jnp.int32, values.shape, 0)
    keep = row >= by if by > 0 else row < length + by
    return jnp.where(keep, rolled, 0.0)


def two_parts(values):
    high = values.astype(BF16)
    return high, (values - high.astype(F32)).astype(BF16)


def to_spectrum(waves, values):
    high, low = two_parts(values)
    return dot(waves[0], high) + (dot(waves[1], high) + dot(waves[0], low))


def from_spectrum(waves, values):
    high, low = two_parts(values)
    return dot_rows(waves[0], high) + (dot_rows(waves[1], high) + dot_rows(waves[0], low))


def multiplied(spectrum, kernel, back):
    length = kernel.shape[1]
    real, imaginary = spectrum[:length], spectrum[length:]
    sign = -1.0 if back else 1.0
    return jnp.concatenate(
        [
            real * kernel[0] - sign * imaginary * kernel[1],
            sign * real * kernel[1] + imaginary * kernel[2],
        ],
        axis=0,
    )


def mixer_forward_kernel(first_layer, *refs):
    hidden_in, marked, live, waves, features = refs[:5]
    pieces = refs[5:15]
    outs = refs[15:27]
    (
        result,
        hidden_out,
        mix,
        table,
        spectrum_out,
        kernel_out,
        filter_out,
        normed_out,
        middle_out,
        saved_out,
        mixed_out,
        middle_two_out,
    ) = outs
    sems = refs[27]
    copies = piece_copies(pieces, sems, mix_spots(mix))
    start_all(copies)
    wait_all(copies)
    rows, width = hidden_in.shape
    block = width // BLOCKS
    half = block // 2
    length = waves.shape[2]
    wide = mix.shape[0]
    third = 2 * half
    fourth = third + length - half
    span = half
    for w in range(wide):
        table[:, w * span : (w + 1) * span] = mix[w, third : third + 16, block : block + span].astype(F32)
    order = length
    step = order // wide
    smalls = jnp.concatenate(
        [mix[w, third + 16 : third + 32, 2 * block : 2 * block + step] for w in range(wide)], axis=1
    ).astype(F32)
    middle_filter = jnp.concatenate(
        [mix[w, third : third + 16, 2 * block : 2 * block + order] for w in range(wide)], axis=0
    ).astype(F32)
    last = jnp.concatenate(
        [
            mix[w, half:fourth, 3 * block :]
            for w in range(wide)
        ],
        axis=1,
    ).astype(F32)
    lead = exact(features[...], smalls[:8]) + smalls[8:9]
    one = jnp.sin(lead)
    lead_two = exact(one, middle_filter) + smalls[9:10]
    two = jnp.sin(lead_two)
    filter_out[0] = one
    filter_out[1] = two
    filter_out[2] = jnp.cos(lead)
    filter_out[3] = jnp.cos(lead_two)
    fraction = features[:, 0:1]
    window = jnp.exp(-fraction * table[8:9])
    ahead = exact(two, last[:, :width]) * window
    behind = exact(two, last[:, width:]) * window
    kernel_out[:, :width] = ahead
    kernel_out[:, width:] = behind
    wave = waves[0].astype(F32) + waves[1].astype(F32)
    row = lax.broadcasted_iota(jnp.int32, (length, 1), 0)
    weight = jnp.where(row == 0, 0.5 / length, 1.0 / length)
    sums = exact(wave, ahead + behind)
    differences = exact(wave[length:], ahead - behind)
    real = sums[:length]
    spectrum_out[0] = real * weight
    spectrum_out[1] = jnp.where(row == 0, 0.0, differences) * weight
    spectrum_out[2] = jnp.where(row == 0, sums[length : length + 1], real) * weight

    if first_layer:
        hidden = jnp.where(marked[...] > 0.5, table[9:10], hidden_in[...].astype(F32))
    else:
        hidden = hidden_in[...]
    hidden_out[...] = hidden
    unit, unused = normalised(hidden)
    normed = (unit * table[0:1] + table[2:3]).astype(BF16)
    normed_out[...] = normed
    for u in range(2):
        middle, blocks = monarch_small(
            normed, lambda b: factor(mix, 0, u, b), lambda b: factor(mix, 0, 2 + u, b)
        )
        for b in range(BLOCKS):
            middle_out[u, b] = middle[b]
        path = jnp.concatenate(blocks, axis=1)
        saved_out[u] = (path * live[...] if u == 0 else path).astype(BF16)
        if u == 0:
            value = path * live[...]
    gate = path
    for s in range(rows // length):
        inside = slice(s * length, (s + 1) * length)
        alive = live[inside]
        signal = value[inside]
        signal = alive * (
            table[4:5] * shifted(signal, 2) + table[5:6] * shifted(signal, 1) + table[6:7] * signal
        )
        product = multiplied(to_spectrum(waves, signal), spectrum_out, False)
        mixed = from_spectrum(waves, product) + table[7:8] * signal
        saved_out[2, inside] = mixed.astype(BF16)
        mixed_out[inside] = (mixed * gate[inside]).astype(BF16)
    middle, blocks = monarch_small(
        mixed_out[...], lambda b: factor(mix, half, 0, b), lambda b: factor(mix, half, 1, b)
    )
    for b in range(BLOCKS):
        middle_two_out[b] = middle[b]
    result[...] = hidden + jnp.concatenate(blocks, axis=1)


def mixer_backward_kernel(first_layer, *refs):
    (
        grad,
        hidden_in,
        marked,
        live,
        waves,
        features,
        mix,
        table,
        spectrum,
        kernel_in,
        filters,
        normed,
        middle,
        saved,
        mixed,
        middle_two,
        norm_two,
        down_grads,
    ) = refs[:18]
    result, grad_out = refs[18:20]
    mix_grad, sum_scratch, value_scratch, table_grad, sems = refs[20:]
    rows, width = hidden_in.shape
    block = width // BLOCKS
    half = block // 2
    length = waves.shape[2]
    wide = mix.shape[0]
    third = 2 * half
    fourth = third + length - half
    mix_grad[:, third:fourth] = jnp.zeros((wide, fourth - third, width), BF16)
    incoming = grad[...]
    low = incoming.astype(BF16)
    blocks = [columns(low, b, block) for b in range(BLOCKS)]
    outs, right_grads, left_grads = monarch_small_backward(
        mixed[...],
        [middle_two[b] for b in range(BLOCKS)],
        blocks,
        lambda b: factor(mix, half, 0, b),
        lambda b: factor(mix, half, 1, b),
    )
    for b in range(BLOCKS):
        store_factor(mix_grad, half, 0, b, right_grads[b])
        store_factor(mix_grad, half, 1, b, left_grads[b])
        store_factor(mix_grad, half, 2, b, down_grads[1, b])
        for index in range(4):
            w = 2 * b + index // 2
            for part in range(2):
                position = (index % 2) * 2 + part
                mix_grad[w, fourth : fourth + half, position * block : (position + 1) * block] = (
                    down_grads[2 + index, b, part * half : (part + 1) * half]
                )
    grad_mixed = jnp.concatenate(outs, axis=1)
    gate = saved[1].astype(F32)
    value_scratch[1] = grad_mixed * saved[2].astype(F32)
    grad_mixed = grad_mixed * gate
    table_grad[...] = jnp.zeros_like(table_grad)
    sum_scratch[...] = jnp.zeros_like(sum_scratch)
    for s in range(rows // length):
        inside = slice(s * length, (s + 1) * length)
        alive = live[inside]
        value = saved[0, inside].astype(F32)
        behind_two, behind_one = shifted(value, 2), shifted(value, 1)
        signal = alive * (
            table[4:5] * behind_two + table[5:6] * behind_one + table[6:7] * value
        )
        inner = grad_mixed[inside]
        table_grad[7:8] += jnp.sum(inner * signal, axis=0, keepdims=True)
        wave_signal = to_spectrum(waves, signal)
        wave_grad = to_spectrum(waves, inner)
        real, imaginary = wave_signal[:length], wave_signal[length:]
        grad_real, grad_imaginary = wave_grad[:length], wave_grad[length:]
        sum_scratch[0] += grad_real * real
        sum_scratch[1] += grad_imaginary * real - grad_real * imaginary
        sum_scratch[2] += grad_imaginary * imaginary
        grad_signal = from_spectrum(waves, multiplied(wave_grad, spectrum, True))
        grad_signal = alive * (grad_signal + table[7:8] * inner)
        table_grad[4:5] += jnp.sum(grad_signal * behind_two, axis=0, keepdims=True)
        table_grad[5:6] += jnp.sum(grad_signal * behind_one, axis=0, keepdims=True)
        table_grad[6:7] += jnp.sum(grad_signal * value, axis=0, keepdims=True)
        value_scratch[0, inside] = alive * (
            table[6:7] * grad_signal
            + table[5:6] * shifted(grad_signal, -1)
            + table[4:5] * shifted(grad_signal, -2)
        )
    row = lax.broadcasted_iota(jnp.int32, (length, 1), 0)
    weight = jnp.where(row == 0, 0.5 / length, 1.0 / length)
    wave = waves[0].astype(F32) + waves[1].astype(F32)
    real = sum_scratch[0] * weight
    other = sum_scratch[2] * weight
    turning = jnp.where(row == 0, 0.0, sum_scratch[1] * weight)
    total = jnp.where(row == 0, real, real + other)
    last_row = jnp.where(row == 0, other, 0.0)
    sums = exact(wave[:length], total, (0, 0)) + exact(wave[length:], last_row, (0, 0))
    differences = exact(wave[length:], turning, (0, 0))
    fraction = features[:, 0:1]
    window = jnp.exp(-fraction * table[8:9])
    count = float(rows // length)
    grad_ahead = (sums + differences + count * kernel_in[:, :width]) * window
    grad_behind = (sums - differences + count * kernel_in[:, width:]) * window
    one, two = filters[0], filters[1]
    middle_filter = jnp.concatenate(
        [mix[w, third : third + 16, 2 * block : 2 * block + length] for w in range(wide)], axis=0
    ).astype(F32)
    grad_two = None
    for w in range(wide):
        source = grad_ahead if w < wide // 2 else grad_behind
        piece = columns(source, w % (wide // 2), block)
        factor_out = mix[w, half:fourth, 3 * block :].astype(F32)
        term = exact(piece, factor_out, (1, 1))
        grad_two = term if grad_two is None else grad_two + term
        mix_grad[w, half:fourth, 3 * block :] = exact(two, piece, (0, 0)).astype(BF16)
    grad_two = grad_two * filters[3]
    grad_one = exact(grad_two, middle_filter, (1, 1)) * filters[2]
    filter_grad = exact(one, grad_two, (0, 0)).astype(BF16)
    smalls = jnp.concatenate(
        [
            exact(features[...], grad_one, (0, 0)),
            jnp.sum(grad_one, axis=0, keepdims=True),
            jnp.sum(grad_two, axis=0, keepdims=True),
            jnp.zeros((6, length), F32),
        ],
        axis=0,
    )
    step = length // wide
    for w in range(wide):
        mix_grad[w, third : third + 16, 2 * block : 2 * block + length] = filter_grad[
            w * step : (w + 1) * step
        ]
        mix_grad[w, third + 16 : third + 32, 2 * block : 2 * block + step] = columns(
            smalls, w, step
        ).astype(BF16)
    total_in = None
    for u in range(2):
        low = value_scratch[u].astype(BF16)
        outs, right_grads, left_grads = monarch_small_backward(
            normed[...],
            [middle[u, b] for b in range(BLOCKS)],
            [columns(low, b, block) for b in range(BLOCKS)],
            lambda b: factor(mix, 0, u, b),
            lambda b: factor(mix, 0, 2 + u, b),
        )
        for b in range(BLOCKS):
            store_factor(mix_grad, 0, u, b, right_grads[b])
            store_factor(mix_grad, 0, 2 + u, b, left_grads[b])
        joint = jnp.concatenate(outs, axis=1)
        total_in = joint if total_in is None else total_in + joint
    through, gain, bias = norm_backward(total_in, hidden_in[...], table[0:1])
    outgoing = incoming + through
    table_grad[0:1] = gain
    table_grad[1:2] = norm_two[0:1]
    table_grad[2:3] = bias
    table_grad[3:4] = norm_two[1:2]
    if first_layer:
        chosen = marked[...] > 0.5
        table_grad[9:10] = jnp.sum(jnp.where(chosen, outgoing, 0.0), axis=0, keepdims=True)
        outgoing = jnp.where(chosen, 0.0, outgoing)
    result[...] = outgoing
    for w in range(wide):
        mix_grad[w, third : third + 16, block : block + half] = columns(
            table_grad[...], w, half
        ).astype(BF16)
    writes = grad_copies(grad_out, sems, mix_spots(mix_grad))
    start_all(writes)
    wait_all(writes)


def call(kernel, name, outs, operands, anywhere, any_outs, scratch):
    vmem = pl.BlockSpec(memory_space=pltpu.VMEM)
    any_space = pl.BlockSpec(memory_space=pl.ANY)
    return pl.pallas_call(
        kernel,
        out_shape=[jax.ShapeDtypeStruct(shape, dtype) for shape, dtype in outs],
        in_specs=[any_space if index in anywhere else vmem for index in range(len(operands))],
        out_specs=[any_space if index in any_outs else vmem for index in range(len(outs))],
        scratch_shapes=scratch,
        compiler_params=pltpu.CompilerParams(vmem_limit_bytes=VMEM_BYTES),
        name=name,
    )(*operands)


def mixer_forward(first_layer, hidden, marked, live, waves, features, pieces):
    rows, width = hidden.shape
    length = waves.shape[2]
    block = width // BLOCKS
    quarter = pieces[0].shape[1]
    outs = [
        ((rows, width), F32),
        ((rows, width), F32),
        ((8, 4 * quarter, width), BF16),
        ((16, width), F32),
        ((3, length, width), F32),
        ((length, 2 * width), F32),
        ((4, length, length), F32),
        ((rows, width), BF16),
        ((2, BLOCKS, rows, block), BF16),
        ((3, rows, width), BF16),
        ((rows, width), BF16),
        ((BLOCKS, rows, block), BF16),
    ]
    operands = (hidden, marked, live, waves, features) + tuple(pieces)
    return call(
        partial(mixer_forward_kernel, first_layer),
        "mixer_forward",
        outs,
        operands,
        range(5, 15),
        (),
        [pltpu.SemaphoreType.DMA((32,))],
    )


def glu_forward(hidden, table, mix, pieces):
    rows, width = hidden.shape
    block = width // BLOCKS
    outs = [
        ((rows, width), F32),
        ((rows, width), BF16),
        ((2, BLOCKS, rows, width), BF16),
        ((2, BLOCKS, rows, width), BF16),
        ((BLOCKS, rows, width), BF16),
        ((BLOCKS, rows, block), BF16),
    ]
    return call(
        glu_forward_kernel,
        "glu_forward",
        outs,
        (hidden, table, mix) + tuple(pieces),
        range(3, 13),
        (),
        [
            pltpu.VMEM((2, BLOCKS, width, width), BF16),
            pltpu.VMEM((2, width, width), BF16),
            pltpu.VMEM((BLOCKS, rows, block), F32),
            pltpu.SemaphoreType.DMA((64,)),
        ],
    )


def glu_backward(grad, hidden, table, mix, saved, pieces):
    rows, width = hidden.shape
    block = width // BLOCKS
    quarter = pieces[0].shape[1]
    outs = [
        ((rows, width), F32),
        ((8, width), F32),
        ((6, BLOCKS, block, block), BF16),
        ((2, 2, 2, 4, quarter, width), BF16),
    ]
    return call(
        glu_backward_kernel,
        "glu_backward",
        outs,
        (grad, hidden, table, mix) + tuple(saved) + tuple(pieces),
        range(9, 19),
        (3,),
        [
            pltpu.VMEM((2, BLOCKS, width, width), BF16),
            pltpu.VMEM((2, width, width), BF16),
            pltpu.VMEM((BLOCKS, rows, block), BF16),
            pltpu.VMEM((2, BLOCKS, rows, width), BF16),
            pltpu.SemaphoreType.DMA((64,)),
            pltpu.SemaphoreType.DMA((64,)),
        ],
    )


def mixer_backward(first_layer, grad, marked, live, waves, features, saved, norm_two, down_grads):
    hidden, mix, table, spectrum, kernel, filters = saved[:6]
    rows, width = hidden.shape
    length = waves.shape[2]
    outs = [((rows, width), F32), ((2, 2, 2, 4, mix.shape[1] // 4, width), BF16)]
    operands = (
        (grad, hidden, marked, live, waves, features)
        + tuple(saved[1:])
        + (norm_two, down_grads)
    )
    return call(
        partial(mixer_backward_kernel, first_layer),
        "mixer_backward",
        outs,
        operands,
        (),
        (1,),
        [
            pltpu.VMEM(mix.shape, BF16),
            pltpu.VMEM((3, length, width), F32),
            pltpu.VMEM((2, rows, width), F32),
            pltpu.VMEM((16, width), F32),
            pltpu.SemaphoreType.DMA((32,)),
        ],
    )
def neighbour(values, mesh_shape, flip_wide, flip_narrow):
    wide, narrow = mesh_shape
    pairs = [
        (w * narrow + n, (w ^ flip_wide) * narrow + (n ^ flip_narrow))
        for w in range(wide)
        for n in range(narrow)
    ]
    return lax.ppermute(values, ("wide", "narrow"), pairs)


def gather_pieces(part, mesh_shape):
    own = part[None]
    own = jnp.concatenate([own, neighbour(own, mesh_shape, 2, 0)], axis=0)
    own = jnp.concatenate([own, neighbour(own, mesh_shape, 4, 0)], axis=0)
    along_x = neighbour(own, mesh_shape, 1, 0)
    along_y = neighbour(own, mesh_shape, 0, 2)
    low = neighbour(along_y[:2], mesh_shape, 1, 0)
    high = neighbour(along_x[2:], mesh_shape, 0, 2)
    near = (own, along_x, along_y, low, high)
    return near + tuple(neighbour(piece, mesh_shape, 0, 1) for piece in near)


def scatter_sum(parts, mesh_shape):
    def total(own, other):
        return (own.astype(F32) + other.astype(F32)).astype(BF16)

    both = total(parts[0], neighbour(parts[1], mesh_shape, 0, 1))
    low, high = both[:, :, :2], both[:, :, 2:]
    low = total(low[0], neighbour(low[1], mesh_shape, 1, 0))
    high = total(high[:, 0], neighbour(high[:, 1], mesh_shape, 0, 2))
    low = total(low[0], neighbour(low[1], mesh_shape, 0, 2))
    high = total(high[0], neighbour(high[1], mesh_shape, 1, 0))
    line = total(low, neighbour(high, mesh_shape, 4, 0))
    return total(line[0], neighbour(line[1], mesh_shape, 2, 0))


def ordered(bit, own, other):
    return jnp.where(bit == 0, jnp.stack([own, other]), jnp.stack([other, own]))


def spread(quarter, mesh_shape):
    unused, unused, y, c = place()
    pair = ordered(c, quarter, neighbour(quarter, mesh_shape, 0, 1))
    return ordered(y, pair, neighbour(pair, mesh_shape, 0, 2)).astype(F32)


def mix_pack(local, mask_vector):
    (
        norm_gain,
        norm_bias,
        in_right,
        in_left,
        conv_taps,
        skip_bias,
        filter_in,
        filter_in_bias,
        filter_mid,
        filter_mid_bias,
        filter_out,
        decay_rates,
        out_right,
        out_left,
        unused_right,
        unused_left,
        down_right,
        down_left,
    ) = local
    rows, block = in_right.shape[1:]
    step, order = filter_mid.shape
    features = filter_in.shape[0]
    zeros = lambda height, width: jnp.zeros((height, width), BF16)
    last = [] if mask_vector is None else [mask_vector[None]]
    table = jnp.concatenate(
        [norm_gain, norm_bias, conv_taps, skip_bias[None], decay_rates[None]] + last, axis=0
    )
    table = jnp.pad(table, ((0, 16 - table.shape[0]), (0, 0)))
    smalls = jnp.concatenate(
        [filter_in, zeros(8 - features, step), filter_in_bias[None], filter_mid_bias[None], zeros(6, step)],
        axis=0,
    )
    tail = filter_out[rows:]
    down = down_right.reshape(4, rows, block)
    return jnp.concatenate(
        [
            jnp.concatenate([in_right[0], in_right[1], in_left[0], in_left[1]], axis=1),
            jnp.concatenate([out_right, out_left, down_left, filter_out[:rows]], axis=1),
            jnp.concatenate(
                [
                    zeros(16, block),
                    table,
                    zeros(16, block - rows),
                    filter_mid,
                    zeros(16, block - order),
                    tail[:16],
                ],
                axis=1,
            ),
            jnp.concatenate(
                [zeros(16, 2 * block), smalls, zeros(16, block - step), tail[16:]], axis=1
            ),
            jnp.concatenate([down[0], down[1], down[2], down[3]], axis=1),
        ],
        axis=0,
    )


def mix_unpack(pack, shards):
    rows, block = shards[2].shape[2:]
    order = shards[10].shape[1]
    step = shards[9].shape[1]
    features = shards[6].shape[1]
    third, fourth = 2 * rows, rows + order
    cut = lambda low, high, k: pack[low:high, k * block : (k + 1) * block]
    table = pack[third : third + 16, block : block + rows]
    smalls = pack[third + 16 : third + 32, 2 * block : 2 * block + step]
    result = {
        0: table[0:2],
        1: table[2:4],
        2: jnp.stack([cut(0, rows, 0), cut(0, rows, 1)]),
        3: jnp.stack([cut(0, rows, 2), cut(0, rows, 3)]),
        4: table[4:7],
        5: table[7],
        6: smalls[:features],
        7: smalls[8],
        8: pack[third : third + step, 2 * block : 2 * block + order],
        9: smalls[9],
        10: cut(rows, fourth, 3),
        12: cut(rows, third, 0),
        13: cut(rows, third, 1),
        16: jnp.concatenate([cut(fourth, fourth + rows, k) for k in range(4)], axis=0),
        17: cut(rows, third, 2),
    }
    return result, table[9]


def layer_quarters(local, mask_vector):
    unused, unused, y, c = place()
    mix = mix_pack(local, mask_vector)
    rows = mix.shape[0] // 4
    glu = []
    for array in (local[15], local[14]):
        size = array.shape[1] // 2
        picked = lax.dynamic_index_in_dim(array, y, 0, keepdims=False)
        glu.append(lax.dynamic_slice_in_dim(picked, c * size, size, 0))
    return (
        lax.dynamic_slice_in_dim(mix, (2 * y + c) * rows, rows, 0),
        jnp.concatenate(glu, axis=0),
    )


GRADS = (0, 1, 2, 3, 4, 5, 6, 7, 8, 9, 10, 12, 13, 14, 15, 16, 17)
SHARD_AXIS = (1, 1, 1, 1, 1, 0, 1, 0, 0, 0, 1, 0, 0, 0, 1, 1, 0, 0)


def gather_plain(shards, layer_index):
    return tuple(
        lax.all_gather(shards[index][layer_index], "wide", axis=SHARD_AXIS[index], tiled=True)
        for index in range(18)
    )


def scatter_plain(grads, mask_term):
    terms = list(grads) + ([] if mask_term is None else [mask_term])
    axes = [SHARD_AXIS[index] for index in GRADS] + [0]
    return narrow_total(
        [
            lax.psum_scatter(term, "wide", scatter_dimension=axis, tiled=True)
            for term, axis in zip(terms, axes)
        ]
    )


def wave_table(length):
    frequency = np.arange(length)[:, None]
    places = np.arange(length)[None, :]
    angles = (frequency * places % (2 * length)) * (math.pi / length)
    turned = -np.sin(angles)
    turned[0] = np.where(np.arange(length) % 2 == 0, 1.0, -1.0)
    table = jnp.asarray(np.concatenate([np.cos(angles), turned]), F32)
    high = table.astype(BF16)
    return jnp.stack([high, (table - high.astype(F32)).astype(BF16)])


def staged_body(shards, mask_vector, hidden_in, cotangent, live, marked, mesh_shape):
    rows = hidden_in.shape[0]
    length = live.shape[1]
    live = live.reshape(rows, 1)
    marked = marked.astype(F32)
    waves = wave_table(length)
    features = jnp.pad(position_features(length), ((0, 0), (0, 8 - EMB)))
    pieces = []
    for layer_index in range(LAYERS):
        local = tuple(member[layer_index] for member in shards)
        quarters = layer_quarters(local, mask_vector if layer_index == 0 else None)
        pieces.append([gather_pieces(quarter, mesh_shape) for quarter in quarters])
    hidden = hidden_in
    kept = []
    for layer_index in range(LAYERS):
        mixed = mixer_forward(
            layer_index == 0, hidden, marked, live, waves, features, pieces[layer_index][0]
        )
        second = glu_forward(mixed[0], mixed[3], mixed[2], pieces[layer_index][1])
        kept.append((mixed, second))
        hidden = second[0]
    output = hidden.astype(BF16)
    grad = cotangent.astype(F32)
    layer_grads = [None] * LAYERS
    mask_grad = None
    for layer_index in reversed(range(LAYERS)):
        mixed, second = kept[layer_index]
        grad, norm_two, down_grads, glu_grads = glu_backward(
            grad, mixed[0], mixed[3], mixed[2], second[1:], pieces[layer_index][1]
        )
        glu = spread(scatter_sum(glu_grads, mesh_shape), mesh_shape)
        grad, mix_grads = mixer_backward(
            layer_index == 0,
            grad,
            marked,
            live,
            waves,
            features,
            mixed[1:],
            norm_two,
            down_grads,
        )
        mix = spread(scatter_sum(mix_grads, mesh_shape), mesh_shape)
        found, mask_grad = mix_unpack(mix.reshape(-1, mix.shape[-1]), shards)
        tall = shards[15].shape[2] // 2
        found[15] = glu[:, :, :tall].reshape(2, 2 * tall, -1)
        found[14] = glu[:, :, tall:].reshape(2, shards[14].shape[2], -1)
        layer_grads[layer_index] = [found[index] for index in GRADS]
    return output, grad, mask_grad, layer_grads


def is_staged(shards, mesh_shape):
    short, block = shards[2].shape[2:]
    order, outs = shards[10].shape[1:]
    return (
        tuple(mesh_shape) == (8, 4)
        and short == 96
        and block == 192
        and order == 128
        and outs == block
        and shards[14].shape[2:] == (short, 8 * short)
        and shards[15].shape[2:] == (4 * short, 8 * short)
    )


def narrow_total(parts):
    flattened = jnp.concatenate([member.reshape(-1) for member in parts])
    summed = lax.psum(flattened.astype(jnp.bfloat16), "narrow").astype(jnp.float32)
    result = []
    offset = 0
    for member in parts:
        result.append(summed[offset : offset + member.size].reshape(member.shape))
        offset = offset + member.size
    return result


def plain_body(shards, mask_vector, hidden_in, cotangent, live_mask, marked):
    seq_count = live_mask.shape[0]
    mask_full = lax.all_gather(mask_vector, "wide", axis=0, tiled=True)
    weights = [gather_plain(shards, layer_index) for layer_index in range(LAYERS)]
    hidden = jnp.where(
        marked, mask_full.astype(jnp.float32)[None, :], hidden_in.astype(jnp.float32)
    )
    saved_layers = []
    for layer_index in range(LAYERS):
        hidden, saved = forward_layer(hidden, weights[layer_index], live_mask)
        saved_layers.append(saved)
    output = hidden.astype(jnp.bfloat16)
    share = 0.5 * seq_count
    grad_hidden = cotangent.astype(jnp.float32)
    layer_grads = [None] * LAYERS
    mask_grad = None
    for layer_index in reversed(range(LAYERS)):
        grad_hidden, grads = backward_layer(
            grad_hidden, weights[layer_index], saved_layers[layer_index], live_mask, share
        )
        if layer_index > 0:
            layer_grads[layer_index] = scatter_plain(grads, None)
        else:
            mask_term = jnp.sum(jnp.where(marked, grad_hidden, 0.0), axis=0)
            reduced = scatter_plain(grads, mask_term)
            layer_grads[0] = reduced[:-1]
            mask_grad = reduced[-1]
    grad_input = jnp.where(marked, 0.0, grad_hidden)
    return output, grad_input, mask_grad, layer_grads


def body(
    mesh_shape,
    hidden_in,
    seq_lengths,
    mask_positions,
    mask_vector,
    cotangent,
    norm_gain,
    norm_bias,
    in_right,
    in_left,
    conv_taps,
    skip_bias,
    filter_in,
    filter_in_bias,
    filter_mid,
    filter_mid_bias,
    filter_out,
    decay_rates,
    out_right,
    out_left,
    glu_right,
    glu_left,
    down_right,
    down_left,
):
    row_count = hidden_in.shape[0]
    seq_count = seq_lengths.shape[0]
    length = row_count // seq_count
    places = jnp.arange(length, dtype=jnp.int32)
    live_mask = (places[None, :] < seq_lengths[:, None]).astype(jnp.float32)[:, :, None]
    marked = jnp.any(mask_positions[:, :, None] == places[None, None, :], axis=1).reshape(
        row_count, 1
    )
    shards = (
        norm_gain,
        norm_bias,
        in_right,
        in_left,
        conv_taps,
        skip_bias,
        filter_in,
        filter_in_bias,
        filter_mid,
        filter_mid_bias,
        filter_out,
        decay_rates,
        out_right,
        out_left,
        glu_right,
        glu_left,
        down_right,
        down_left,
    )
    if is_staged(shards, mesh_shape):
        output, grad_input, mask_grad, layer_grads = staged_body(
            shards, mask_vector, hidden_in, cotangent, live_mask, marked, mesh_shape
        )
    else:
        output, grad_input, mask_grad, layer_grads = plain_body(
            shards, mask_vector, hidden_in, cotangent, live_mask, marked
        )
    final_grads = [
        jnp.stack([layer_grads[position][member_index] for position in range(LAYERS)])
        for member_index in range(17)
    ]
    return (output, grad_input, mask_grad) + tuple(final_grads)


def solution(mesh):
    placed = (
        P(("wide", "narrow"), None),
        P(("wide", "narrow")),
        P(("wide", "narrow"), None),
        P("wide"),
        P(("wide", "narrow"), None),
        P(None, None, "wide"),
        P(None, None, "wide"),
        P(None, None, "wide", None),
        P(None, None, "wide", None),
        P(None, None, "wide"),
        P(None, "wide"),
        P(None, None, "wide"),
        P(None, "wide"),
        P(None, "wide", None),
        P(None, "wide"),
        P(None, None, "wide"),
        P(None, "wide"),
        P(None, "wide", None),
        P(None, "wide", None),
        P(None, None, "wide", None),
        P(None, None, "wide", None),
        P(None, "wide", None),
        P(None, "wide", None),
    )
    return jax.shard_map(
        partial(body, (mesh.shape["wide"], mesh.shape["narrow"])),
        mesh=mesh,
        in_specs=placed,
        out_specs=(
            P(("wide", "narrow"), None),
            P(("wide", "narrow"), None),
            P("wide"),
            P(None, None, "wide"),
            P(None, None, "wide"),
            P(None, None, "wide", None),
            P(None, None, "wide", None),
            P(None, None, "wide"),
            P(None, "wide"),
            P(None, None, "wide"),
            P(None, "wide"),
            P(None, "wide", None),
            P(None, "wide"),
            P(None, None, "wide"),
            P(None, "wide", None),
            P(None, "wide", None),
            P(None, None, "wide", None),
            P(None, None, "wide", None),
            P(None, "wide", None),
            P(None, "wide", None),
        ),
        check_vma=False,
    )
```

```python
from functools import partial
import math

import jax
import jax.numpy as jnp
import numpy as np
from jax import lax
from jax.experimental import pallas as pl
from jax.experimental.pallas import tpu as pltpu
from jax.sharding import PartitionSpec as P

BLOCKS = 4
EMB = 5
LAYERS = 2


EPSILON = 1e-05
highest_precision = lax.Precision.HIGHEST


def permute(values):
    array_shape = values.shape
    blocks = array_shape[-2]
    split_view = values.reshape(array_shape[:-1] + (blocks, array_shape[-1] // blocks))
    return jnp.swapaxes(split_view, -3, -2).reshape(array_shape)


def monarch_forward(inputs, right_factor, left_factor):
    row_count = inputs.shape[0]
    right_blocks = right_factor.reshape(BLOCKS, -1, right_factor.shape[-1])
    left_blocks = left_factor.reshape(BLOCKS, -1, left_factor.shape[-1])
    middle = jnp.einsum(
        "rbi,bio->rbo",
        inputs.reshape(row_count, BLOCKS, -1),
        right_blocks,
        preferred_element_type=jnp.float32,
    )
    middle = permute(middle).astype(jnp.bfloat16)
    output = jnp.einsum("rbi,bio->rbo", middle, left_blocks, preferred_element_type=jnp.float32)
    return (middle, output.reshape(row_count, -1))


def monarch_backward(inputs, middle, right_factor, left_factor, grad_output):
    row_count = inputs.shape[0]
    right_blocks = right_factor.reshape(BLOCKS, -1, right_factor.shape[-1])
    left_blocks = left_factor.reshape(BLOCKS, -1, left_factor.shape[-1])
    grad_low = grad_output.astype(jnp.bfloat16).reshape(row_count, BLOCKS, -1)
    grad_left = jnp.einsum("rbi,rbo->bio", middle, grad_low, preferred_element_type=jnp.float32)
    grad_middle = jnp.einsum(
        "rbo,bio->rbi", grad_low, left_blocks, preferred_element_type=jnp.float32
    )
    grad_middle = permute(grad_middle).astype(jnp.bfloat16)
    input_blocks = inputs.reshape(row_count, BLOCKS, -1)
    grad_right = jnp.einsum(
        "rbi,rbo->bio", input_blocks, grad_middle, preferred_element_type=jnp.float32
    )
    grad_inputs = jnp.einsum(
        "rbo,bio->rbi", grad_middle, right_blocks, preferred_element_type=jnp.float32
    )
    return (
        grad_inputs.reshape(row_count, -1),
        grad_right.reshape(right_factor.shape),
        grad_left.reshape(left_factor.shape),
    )


def layer_norm(values, norm_gain, norm_bias):
    average = jnp.mean(values, axis=-1, keepdims=True)
    centred = values - average
    variance = jnp.mean(centred * centred, axis=-1, keepdims=True)
    return centred * lax.rsqrt(variance + EPSILON) * norm_gain + norm_bias


def position_features(length):
    positions = jnp.arange(length, dtype=jnp.float32)
    fraction = positions / length
    features = [fraction]
    for band_index in range(1, (EMB - 1) // 2 + 1):
        features.append(jnp.cos(2.0 * math.pi * band_index * fraction))
        features.append(jnp.sin(2.0 * math.pi * band_index * fraction))
    return jnp.stack(features, axis=1)


def make_filter(
    filter_in, filter_in_bias, filter_mid, filter_mid_bias, filter_out, decay_rates, length
):
    embedding = position_features(length)
    first_hidden = jnp.sin(
        jnp.dot(embedding, filter_in, precision=highest_precision) + filter_in_bias
    )
    second = jnp.sin(
        jnp.dot(first_hidden, filter_mid, precision=highest_precision) + filter_mid_bias
    )
    kernel = jnp.dot(second, filter_out, precision=highest_precision)
    fraction = jnp.arange(length, dtype=jnp.float32)[:, None] / length
    both_rates = jnp.concatenate([decay_rates, decay_rates])
    return kernel * jnp.exp(-fraction * both_rates[None, :])


def short_convolution(signal_rows, conv_taps):
    padded = jnp.pad(signal_rows, ((0, 0), (2, 0), (0, 0)))
    return (
        conv_taps[0] * padded[:, :-2]
        + conv_taps[1] * padded[:, 1:-1]
        + conv_taps[2] * padded[:, 2:]
    )


def spectral_tables(length, span):
    padded_length = 2 * length
    frequency = jnp.arange(length + 1, dtype=jnp.int32)
    places = jnp.arange(span, dtype=jnp.int32)
    phase_index = frequency[:, None] * places[None, :] % padded_length
    angles = phase_index.astype(jnp.float32) * (2.0 * math.pi / padded_length)
    ends = (frequency == 0) | (frequency == length)
    weights = jnp.where(ends, 1.0, 2.0).astype(jnp.float32) / padded_length
    return (jnp.cos(angles), jnp.sin(angles), weights)


def circular_kernel(kernel):
    width = kernel.shape[1] // 2
    forward_part = kernel[:, :width]
    reverse_part = kernel[:, width:]
    first_row = forward_part[:1] + reverse_part[:1]
    spacer = jnp.zeros((1, width), jnp.float32)
    return jnp.concatenate(
        [first_row, forward_part[1:], spacer, jnp.flip(reverse_part[1:], axis=0)], axis=0
    )


def long_convolution(signal_rows, kernel):
    length = signal_rows.shape[1]
    cosine_lookup, sine_lookup, weights = spectral_tables(length, length)
    kernel_cosine, kernel_sine, unused = spectral_tables(length, 2 * length)
    circular = circular_kernel(kernel)
    real_signal = jnp.einsum("ik,hkm->him", cosine_lookup, signal_rows, precision=highest_precision)
    imaginary_signal = -jnp.einsum(
        "ik,hkm->him", sine_lookup, signal_rows, precision=highest_precision
    )
    kernel_real = jnp.dot(kernel_cosine, circular, precision=highest_precision)
    kernel_imaginary = -jnp.dot(kernel_sine, circular, precision=highest_precision)
    real_product = real_signal * kernel_real - imaginary_signal * kernel_imaginary
    imaginary_product = real_signal * kernel_imaginary + imaginary_signal * kernel_real
    inverse_cosine_table = cosine_lookup * weights[:, None]
    inverse_sine_table = sine_lookup * weights[:, None]
    return jnp.einsum(
        "hp,ihj->ipj", inverse_cosine_table, real_product, precision=highest_precision
    ) - jnp.einsum(
        "hp,ihj->ipj", inverse_sine_table, imaginary_product, precision=highest_precision
    )


def mixer_piece(
    value_path,
    gate_path,
    conv_taps,
    skip_bias,
    filter_in,
    filter_in_bias,
    filter_mid,
    filter_mid_bias,
    filter_out,
    decay_rates,
    live_mask,
    share,
):
    length = live_mask.shape[1]
    kernel = make_filter(
        filter_in, filter_in_bias, filter_mid, filter_mid_bias, filter_out, decay_rates, length
    )
    signal_rows = value_path.reshape(live_mask.shape[0], length, -1) * live_mask
    signal_rows = short_convolution(signal_rows, conv_taps) * live_mask
    mixed_signal = long_convolution(signal_rows, kernel) + signal_rows * skip_bias
    return (mixed_signal.reshape(value_path.shape) * gate_path, share * jnp.sum(kernel * kernel))


def glu_piece(upper_branch, gate_branch):
    return jax.nn.gelu(gate_branch, approximate=False) * upper_branch


def small_weights(layer_weights):
    return tuple(
        (layer_weights[position].astype(jnp.float32) for position in (4, 5, 6, 7, 8, 9, 10))
    )


def forward_layer(hidden, layer_weights, live_mask):
    (
        norm_gain,
        norm_bias,
        in_right,
        in_left,
        conv_taps,
        skip_bias,
        filter_in,
        filter_in_bias,
        filter_mid,
        filter_mid_bias,
        filter_out,
        decay_rates,
        out_right,
        out_left,
        glu_right,
        glu_left,
        down_right,
        down_left,
    ) = layer_weights
    gains = norm_gain.astype(jnp.float32)
    biases = norm_bias.astype(jnp.float32)
    small = small_weights(layer_weights)
    normed = layer_norm(hidden, gains[0], biases[0]).astype(jnp.bfloat16)
    middle_value, value_path = monarch_forward(normed, in_right[0], in_left[0])
    middle_gate, gate_path = monarch_forward(normed, in_right[1], in_left[1])
    mixed_signal, unused = mixer_piece(
        value_path,
        gate_path,
        small[0],
        small[1],
        small[2],
        small[3],
        small[4],
        small[5],
        small[6],
        decay_rates.astype(jnp.float32),
        live_mask,
        0.0,
    )
    mixed_signal = mixed_signal.astype(jnp.bfloat16)
    middle_out, branch = monarch_forward(mixed_signal, out_right, out_left)
    middle_hidden = hidden + branch
    normed_two = layer_norm(middle_hidden, gains[1], biases[1]).astype(jnp.bfloat16)
    middle_up, upper_branch = monarch_forward(normed_two, glu_right[0], glu_left[0])
    middle_glu, gate_branch = monarch_forward(normed_two, glu_right[1], glu_left[1])
    glu_hidden = glu_piece(upper_branch, gate_branch).astype(jnp.bfloat16)
    middle_down, branch_two = monarch_forward(glu_hidden, down_right, down_left)
    saved = (
        hidden,
        normed,
        middle_value,
        value_path,
        middle_gate,
        gate_path,
        mixed_signal,
        middle_out,
        middle_hidden,
        normed_two,
        middle_up,
        upper_branch,
        middle_glu,
        gate_branch,
        glu_hidden,
        middle_down,
    )
    return (middle_hidden + branch_two, saved)


def backward_layer(grad_hidden, layer_weights, saved, live_mask, share):
    (
        norm_gain,
        norm_bias,
        in_right,
        in_left,
        conv_taps,
        skip_bias,
        filter_in,
        filter_in_bias,
        filter_mid,
        filter_mid_bias,
        filter_out,
        decay_rates,
        out_right,
        out_left,
        glu_right,
        glu_left,
        down_right,
        down_left,
    ) = layer_weights
    (
        hidden,
        normed,
        middle_value,
        value_path,
        middle_gate,
        gate_path,
        mixed_signal,
        middle_out,
        middle_hidden,
        normed_two,
        middle_up,
        upper_branch,
        middle_glu,
        gate_branch,
        glu_hidden,
        middle_down,
    ) = saved
    gains = norm_gain.astype(jnp.float32)
    biases = norm_bias.astype(jnp.float32)
    small = small_weights(layer_weights)
    grad_glu, grad_down_right, grad_down_left = monarch_backward(
        glu_hidden, middle_down, down_right, down_left, grad_hidden
    )
    unused, glu_pull = jax.vjp(glu_piece, upper_branch, gate_branch)
    grad_upper, grad_gate = glu_pull(grad_glu)
    grad_normed_up, grad_right_up, grad_left_up = monarch_backward(
        normed_two, middle_up, glu_right[0], glu_left[0], grad_upper
    )
    grad_normed_gate, grad_right_gate, grad_left_gate = monarch_backward(
        normed_two, middle_glu, glu_right[1], glu_left[1], grad_gate
    )
    unused, norm_pull = jax.vjp(layer_norm, middle_hidden, gains[1], biases[1])
    grad_middle, grad_gain_two, grad_bias_two = norm_pull(grad_normed_up + grad_normed_gate)
    grad_middle = grad_middle + grad_hidden
    grad_mixed, grad_out_right, grad_out_left = monarch_backward(
        mixed_signal, middle_out, out_right, out_left, grad_middle
    )
    mixer_local = partial(
        mixer_piece, decay_rates=decay_rates.astype(jnp.float32), live_mask=live_mask, share=share
    )
    unused, mixer_pull = jax.vjp(
        mixer_local,
        value_path,
        gate_path,
        small[0],
        small[1],
        small[2],
        small[3],
        small[4],
        small[5],
        small[6],
    )
    mixer_grads = mixer_pull((grad_mixed, jnp.ones((), jnp.float32)))
    grad_normed_value, grad_right_value, grad_left_value = monarch_backward(
        normed, middle_value, in_right[0], in_left[0], mixer_grads[0]
    )
    grad_normed_path, grad_right_path, grad_left_path = monarch_backward(
        normed, middle_gate, in_right[1], in_left[1], mixer_grads[1]
    )
    unused, norm_pull_one = jax.vjp(layer_norm, hidden, gains[0], biases[0])
    grad_before, grad_gain_one, grad_bias_one = norm_pull_one(grad_normed_value + grad_normed_path)
    grads = (
        jnp.stack([grad_gain_one, grad_gain_two]),
        jnp.stack([grad_bias_one, grad_bias_two]),
        jnp.stack([grad_right_value, grad_right_path]),
        jnp.stack([grad_left_value, grad_left_path]),
        mixer_grads[2],
        mixer_grads[3],
        mixer_grads[4],
        mixer_grads[5],
        mixer_grads[6],
        mixer_grads[7],
        mixer_grads[8],
        grad_out_right,
        grad_out_left,
        jnp.stack([grad_right_up, grad_right_gate]),
        jnp.stack([grad_left_up, grad_left_gate]),
        grad_down_right,
        grad_down_left,
    )
    return (grad_before + grad_middle, grads)


F32 = jnp.float32
BF16 = jnp.bfloat16
VMEM_BYTES = 60 * 1024 * 1024


def dot(left, right):
    return jnp.dot(left, right, preferred_element_type=F32)


def dot_rows(left, right):
    return lax.dot_general(left, right, (((0,), (0,)), ((), ())), preferred_element_type=F32)


def dot_columns(left, right):
    return lax.dot_general(left, right, (((1,), (1,)), ((), ())), preferred_element_type=F32)


def exact(left, right, dims=(1, 0)):
    return lax.dot_general(
        left,
        right,
        (((dims[0],), (dims[1],)), ((), ())),
        precision=highest_precision,
        preferred_element_type=F32,
    )


def columns(values, index, width):
    return values[:, index * width : (index + 1) * width]


def shuffled(parts):
    chunk = parts[0].shape[1] // BLOCKS
    return [
        jnp.concatenate([columns(part, index, chunk) for part in parts], axis=1)
        for index in range(BLOCKS)
    ]


def normalised(values):
    average = jnp.mean(values, axis=-1, keepdims=True)
    centred = values - average
    variance = jnp.mean(centred * centred, axis=-1, keepdims=True)
    scale = lax.rsqrt(variance + EPSILON)
    return centred * scale, scale


def norm_backward(grad, hidden, gain):
    unit, scale = normalised(hidden)
    grad_gain = jnp.sum(grad * unit, axis=0, keepdims=True)
    grad_bias = jnp.sum(grad, axis=0, keepdims=True)
    scaled = grad * gain
    mean_one = jnp.mean(scaled, axis=-1, keepdims=True)
    mean_two = jnp.mean(scaled * unit, axis=-1, keepdims=True)
    return scale * (scaled - mean_one - unit * mean_two), grad_gain, grad_bias


def flip(bit, by):
    return 1 - bit if by else bit


def place():
    w = lax.axis_index("wide")
    n = lax.axis_index("narrow")
    return w // 2, w % 2, n // 2, n % 2


def relative(z, distance):
    high, low = z // 2, z % 2
    return 2 * flip(high, distance // 2) + flip(low, distance % 2)


def piece_copies(pieces, sems, targets_of):
    z, x, y, c = place()
    copies = []
    for core in range(2):
        for dx in range(2):
            for dy in range(2):
                for dz in range(4):
                    owner = (relative(z, dz), flip(x, dx), flip(y, dy), flip(c, core))
                    for row, target in targets_of(*owner):
                        view = pieces.at[core, dx, dy, dz, pl.ds(row, target.shape[0])]
                        copies.append(pltpu.make_async_copy(view, target, sems.at[len(copies)]))
    return copies


def grad_copies(result, sems, sources_of):
    z, x, y, c = place()
    copies = []
    for core in range(2):
        for dx in range(2):
            for dy in range(2):
                for dz in range(4):
                    owner = (relative(z, dz), flip(x, dx), flip(y, dy), flip(c, core))
                    for row, source in sources_of(*owner):
                        view = result.at[core, dx, dy, dz, pl.ds(row, source.shape[0])]
                        copies.append(pltpu.make_async_copy(source, view, sems.at[len(copies)]))
    return copies


def start_all(copies):
    for copy in copies:
        copy.start()


def wait_all(copies):
    for copy in copies:
        copy.wait()


def glu_spots(left, right):
    def spots(z, x, y, c):
        tall, short = left.shape[2] // 4, right.shape[1] // 16
        return (
            (0, left.at[y, z, pl.ds(pl.multiple_of((2 * x + c) * tall, 16), tall)]),
            (tall, right.at[y, pl.ds(pl.multiple_of((4 * z + 2 * x + c) * short, 16), short)]),
        )

    return spots


def mix_spots(mix):
    def spots(z, x, y, c):
        rows = mix.shape[1] // 4
        return ((0, mix.at[2 * z + x, pl.ds(pl.multiple_of((2 * y + c) * rows, 16), rows)]),)

    return spots


def factor(mix, rows, kind, block):
    width = mix.shape[2] // 4
    low = kind * width
    top = mix[2 * block, rows : rows + width // 2, low : low + width]
    bottom = mix[2 * block + 1, rows : rows + width // 2, low : low + width]
    return jnp.concatenate([top, bottom], axis=0)


def down_factor(mix, first, block):
    width = mix.shape[2] // 4
    half = width // 2
    parts = []
    for shard in (2 * block, 2 * block + 1):
        for index in range(4):
            parts.append(mix[shard, first : first + half, index * width : (index + 1) * width])
    return jnp.concatenate(parts, axis=0)


def monarch_small(inputs, right, left):
    width = inputs.shape[1] // BLOCKS
    parts = [dot(columns(inputs, b, width), right(b)) for b in range(BLOCKS)]
    middle = [part.astype(BF16) for part in shuffled(parts)]
    return middle, [dot(middle[b], left(b)) for b in range(BLOCKS)]


def monarch_small_backward(inputs, middle, grads, right, left):
    width = inputs.shape[1] // BLOCKS
    grad_left = [dot_rows(middle[b], grads[b]) for b in range(BLOCKS)]
    back = shuffled([dot_columns(grads[b], left(b)) for b in range(BLOCKS)])
    back = [part.astype(BF16) for part in back]
    grad_right = [dot_rows(columns(inputs, b, width), back[b]) for b in range(BLOCKS)]
    return [dot_columns(back[b], right(b)) for b in range(BLOCKS)], grad_right, grad_left


def store_factor(mix, rows, kind, block, value):
    width = mix.shape[2] // 4
    half = width // 2
    low = kind * width
    mix[2 * block, rows : rows + half, low : low + width] = value[:half].astype(BF16)
    mix[2 * block + 1, rows : rows + half, low : low + width] = value[half:].astype(BF16)


def cell(values):
    rise = 0.5 * (1.0 + lax.erf(values * (0.5**0.5)))
    return rise, jnp.exp(-0.5 * values * values) * ((2.0 * math.pi) ** -0.5)


def glu_forward_kernel(hidden, table, mix, *refs):
    pieces, result, normed_out, middle_out, branch_out, glu_out, down_out = refs[:7]
    left, right, parts, sems = refs[7:]
    copies = piece_copies(pieces, sems, glu_spots(left, right))
    start_all(copies)
    rows, width = hidden.shape
    block = width // BLOCKS
    unit, unused = normalised(hidden[...])
    normed = (unit * table[1:2] + table[3:4]).astype(BF16)
    normed_out[...] = normed
    wait_all(copies)
    for u in range(2):
        for b in range(BLOCKS):
            part = dot(columns(normed, b, block), right[u, b * block : (b + 1) * block]).astype(BF16)
            for q in range(BLOCKS):
                middle_out[u, q, :, b * block : (b + 1) * block] = columns(part, q, block)
    for q in range(BLOCKS):
        upper = dot(middle_out[0, q], left[0, q])
        gate = dot(middle_out[1, q], left[1, q])
        branch_out[0, q] = upper.astype(BF16)
        branch_out[1, q] = gate.astype(BF16)
        glu = (gate * cell(gate)[0] * upper).astype(BF16)
        glu_out[q] = glu
        parts[q] = dot(glu, down_factor(mix, 7 * block // 6, q))
    down = [part.astype(BF16) for part in shuffled([parts[q] for q in range(BLOCKS)])]
    for b in range(BLOCKS):
        down_out[b] = down[b]
        span = slice(b * block, (b + 1) * block)
        result[:, span] = hidden[:, span] + dot(down[b], factor(mix, block // 2, 2, b))


def glu_backward_kernel(grad, hidden, table, mix, normed, middle, branch, glu, down, *refs):
    pieces, result, norm_out, mix_grad, glu_grad = refs[:5]
    left, right, low, back, sems, out_sems = refs[5:]
    copies = piece_copies(pieces, sems, glu_spots(left, right))
    start_all(copies)
    rows, width = hidden.shape
    block = width // BLOCKS
    incoming = grad[...]
    half = incoming.astype(BF16)
    backs = []
    for b in range(BLOCKS):
        part = columns(half, b, block)
        mix_grad[1, b] = dot_rows(down[b], part).astype(BF16)
        backs.append(dot_columns(part, factor(mix, block // 2, 2, b)))
    backs = shuffled(backs)
    for q in range(BLOCKS):
        low[q] = backs[q].astype(BF16)
    wait_all(copies)
    for q in range(BLOCKS):
        step = low[q]
        product = dot_rows(glu[q], step).astype(BF16)
        for index in range(BLOCKS):
            mix_grad[2 + index, q] = product[index * block : (index + 1) * block]
        grad_glu = dot_columns(step, down_factor(mix, 7 * block // 6, q))
        upper = branch[0, q].astype(F32)
        gate = branch[1, q].astype(F32)
        rise, density = cell(gate)
        terms = (grad_glu * gate * rise, grad_glu * upper * (rise + gate * density))
        for u in range(2):
            term = terms[u].astype(BF16)
            wide = dot_columns(term, left[u, q]).astype(BF16)
            left[u, q] = dot_rows(middle[u, q], term).astype(BF16)
            for b in range(BLOCKS):
                back[u, b, :, q * block : (q + 1) * block] = columns(wide, b, block)
    outgoing = []
    for b in range(BLOCKS):
        span = slice(b * block, (b + 1) * block)
        total = None
        for u in range(2):
            term = dot_columns(back[u, b], right[u, span])
            right[u, span] = dot_rows(normed[:, span], back[u, b]).astype(BF16)
            total = term if total is None else total + term
        outgoing.append(total)
    writes = grad_copies(glu_grad, out_sems, glu_spots(left, right))
    start_all(writes)
    through, gain, bias = norm_backward(
        jnp.concatenate(outgoing, axis=1), hidden[...], table[1:2]
    )
    result[...] = incoming + through
    norm_out[0:1] = gain
    norm_out[1:2] = bias
    wait_all(writes)


def shifted(values, by):
    length = values.shape[0]
    rolled = pltpu.roll(values, by % length, 0)
    row = lax.broadcasted_iota(jnp.int32, values.shape, 0)
    keep = row >= by if by > 0 else row < length + by
    return jnp.where(keep, rolled, 0.0)


def two_parts(values):
    high = values.astype(BF16)
    return high, (values - high.astype(F32)).astype(BF16)


def to_spectrum(waves, values):
    high, low = two_parts(values)
    return dot(waves[0], high) + (dot(waves[1], high) + dot(waves[0], low))


def from_spectrum(waves, values):
    high, low = two_parts(values)
    return dot_rows(waves[0], high) + (dot_rows(waves[1], high) + dot_rows(waves[0], low))


def multiplied(spectrum, kernel, back):
    length = kernel.shape[1]
    real, imaginary = spectrum[:length], spectrum[length:]
    sign = -1.0 if back else 1.0
    return jnp.concatenate(
        [
            real * kernel[0] - sign * imaginary * kernel[1],
            sign * real * kernel[1] + imaginary * kernel[2],
        ],
        axis=0,
    )


def mixer_forward_kernel(first_layer, *refs):
    hidden_in, marked, live, waves, features = refs[:5]
    pieces = refs[5]
    outs = refs[6:18]
    (
        result,
        hidden_out,
        mix,
        table,
        spectrum_out,
        kernel_out,
        filter_out,
        normed_out,
        middle_out,
        saved_out,
        mixed_out,
        middle_two_out,
    ) = outs
    sems = refs[18]
    copies = piece_copies(pieces, sems, mix_spots(mix))
    start_all(copies)
    wait_all(copies)
    rows, width = hidden_in.shape
    block = width // BLOCKS
    half = block // 2
    length = waves.shape[2]
    wide = mix.shape[0]
    third = 2 * half
    fourth = third + length - half
    span = half
    for w in range(wide):
        table[:, w * span : (w + 1) * span] = mix[w, third : third + 16, block : block + span].astype(F32)
    order = length
    step = order // wide
    smalls = jnp.concatenate(
        [mix[w, third + 16 : third + 32, 2 * block : 2 * block + step] for w in range(wide)], axis=1
    ).astype(F32)
    middle_filter = jnp.concatenate(
        [mix[w, third : third + 16, 2 * block : 2 * block + order] for w in range(wide)], axis=0
    ).astype(F32)
    last = jnp.concatenate(
        [
            mix[w, half:fourth, 3 * block :]
            for w in range(wide)
        ],
        axis=1,
    ).astype(F32)
    lead = exact(features[...], smalls[:8]) + smalls[8:9]
    one = jnp.sin(lead)
    lead_two = exact(one, middle_filter) + smalls[9:10]
    two = jnp.sin(lead_two)
    filter_out[0] = one
    filter_out[1] = two
    filter_out[2] = jnp.cos(lead)
    filter_out[3] = jnp.cos(lead_two)
    fraction = features[:, 0:1]
    window = jnp.exp(-fraction * table[8:9])
    ahead = exact(two, last[:, :width]) * window
    behind = exact(two, last[:, width:]) * window
    kernel_out[:, :width] = ahead
    kernel_out[:, width:] = behind
    wave = waves[0].astype(F32) + waves[1].astype(F32)
    row = lax.broadcasted_iota(jnp.int32, (length, 1), 0)
    weight = jnp.where(row == 0, 0.5 / length, 1.0 / length)
    sums = exact(wave, ahead + behind)
    differences = exact(wave[length:], ahead - behind)
    real = sums[:length]
    spectrum_out[0] = real * weight
    spectrum_out[1] = jnp.where(row == 0, 0.0, differences) * weight
    spectrum_out[2] = jnp.where(row == 0, sums[length : length + 1], real) * weight

    if first_layer:
        hidden = jnp.where(marked[...] > 0.5, table[9:10], hidden_in[...].astype(F32))
    else:
        hidden = hidden_in[...]
    hidden_out[...] = hidden
    unit, unused = normalised(hidden)
    normed = (unit * table[0:1] + table[2:3]).astype(BF16)
    normed_out[...] = normed
    for u in range(2):
        middle, blocks = monarch_small(
            normed, lambda b: factor(mix, 0, u, b), lambda b: factor(mix, 0, 2 + u, b)
        )
        for b in range(BLOCKS):
            middle_out[u, b] = middle[b]
        path = jnp.concatenate(blocks, axis=1)
        saved_out[u] = (path * live[...] if u == 0 else path).astype(BF16)
        if u == 0:
            value = path * live[...]
    gate = path
    for s in range(rows // length):
        inside = slice(s * length, (s + 1) * length)
        alive = live[inside]
        signal = value[inside]
        signal = alive * (
            table[4:5] * shifted(signal, 2) + table[5:6] * shifted(signal, 1) + table[6:7] * signal
        )
        product = multiplied(to_spectrum(waves, signal), spectrum_out, False)
        mixed = from_spectrum(waves, product) + table[7:8] * signal
        saved_out[2, inside] = mixed.astype(BF16)
        mixed_out[inside] = (mixed * gate[inside]).astype(BF16)
    middle, blocks = monarch_small(
        mixed_out[...], lambda b: factor(mix, half, 0, b), lambda b: factor(mix, half, 1, b)
    )
    for b in range(BLOCKS):
        middle_two_out[b] = middle[b]
    result[...] = hidden + jnp.concatenate(blocks, axis=1)


def mixer_backward_kernel(first_layer, *refs):
    (
        grad,
        hidden_in,
        marked,
        live,
        waves,
        features,
        mix,
        table,
        spectrum,
        kernel_in,
        filters,
        normed,
        middle,
        saved,
        mixed,
        middle_two,
        norm_two,
        down_grads,
    ) = refs[:18]
    result, grad_out = refs[18:20]
    mix_grad, sum_scratch, value_scratch, table_grad, sems = refs[20:]
    rows, width = hidden_in.shape
    block = width // BLOCKS
    half = block // 2
    length = waves.shape[2]
    wide = mix.shape[0]
    third = 2 * half
    fourth = third + length - half
    mix_grad[:, third:fourth] = jnp.zeros((wide, fourth - third, width), BF16)
    incoming = grad[...]
    low = incoming.astype(BF16)
    blocks = [columns(low, b, block) for b in range(BLOCKS)]
    outs, right_grads, left_grads = monarch_small_backward(
        mixed[...],
        [middle_two[b] for b in range(BLOCKS)],
        blocks,
        lambda b: factor(mix, half, 0, b),
        lambda b: factor(mix, half, 1, b),
    )
    for b in range(BLOCKS):
        store_factor(mix_grad, half, 0, b, right_grads[b])
        store_factor(mix_grad, half, 1, b, left_grads[b])
        store_factor(mix_grad, half, 2, b, down_grads[1, b])
        for index in range(4):
            w = 2 * b + index // 2
            for part in range(2):
                position = (index % 2) * 2 + part
                mix_grad[w, fourth : fourth + half, position * block : (position + 1) * block] = (
                    down_grads[2 + index, b, part * half : (part + 1) * half]
                )
    grad_mixed = jnp.concatenate(outs, axis=1)
    gate = saved[1].astype(F32)
    value_scratch[1] = grad_mixed * saved[2].astype(F32)
    grad_mixed = grad_mixed * gate
    table_grad[...] = jnp.zeros_like(table_grad)
    sum_scratch[...] = jnp.zeros_like(sum_scratch)
    for s in range(rows // length):
        inside = slice(s * length, (s + 1) * length)
        alive = live[inside]
        value = saved[0, inside].astype(F32)
        behind_two, behind_one = shifted(value, 2), shifted(value, 1)
        signal = alive * (
            table[4:5] * behind_two + table[5:6] * behind_one + table[6:7] * value
        )
        inner = grad_mixed[inside]
        table_grad[7:8] += jnp.sum(inner * signal, axis=0, keepdims=True)
        wave_signal = to_spectrum(waves, signal)
        wave_grad = to_spectrum(waves, inner)
        real, imaginary = wave_signal[:length], wave_signal[length:]
        grad_real, grad_imaginary = wave_grad[:length], wave_grad[length:]
        sum_scratch[0] += grad_real * real
        sum_scratch[1] += grad_imaginary * real - grad_real * imaginary
        sum_scratch[2] += grad_imaginary * imaginary
        grad_signal = from_spectrum(waves, multiplied(wave_grad, spectrum, True))
        grad_signal = alive * (grad_signal + table[7:8] * inner)
        table_grad[4:5] += jnp.sum(grad_signal * behind_two, axis=0, keepdims=True)
        table_grad[5:6] += jnp.sum(grad_signal * behind_one, axis=0, keepdims=True)
        table_grad[6:7] += jnp.sum(grad_signal * value, axis=0, keepdims=True)
        value_scratch[0, inside] = alive * (
            table[6:7] * grad_signal
            + table[5:6] * shifted(grad_signal, -1)
            + table[4:5] * shifted(grad_signal, -2)
        )
    row = lax.broadcasted_iota(jnp.int32, (length, 1), 0)
    weight = jnp.where(row == 0, 0.5 / length, 1.0 / length)
    wave = waves[0].astype(F32) + waves[1].astype(F32)
    real = sum_scratch[0] * weight
    other = sum_scratch[2] * weight
    turning = jnp.where(row == 0, 0.0, sum_scratch[1] * weight)
    total = jnp.where(row == 0, real, real + other)
    last_row = jnp.where(row == 0, other, 0.0)
    sums = exact(wave[:length], total, (0, 0)) + exact(wave[length:], last_row, (0, 0))
    differences = exact(wave[length:], turning, (0, 0))
    fraction = features[:, 0:1]
    window = jnp.exp(-fraction * table[8:9])
    count = float(rows // length)
    grad_ahead = (sums + differences + count * kernel_in[:, :width]) * window
    grad_behind = (sums - differences + count * kernel_in[:, width:]) * window
    one, two = filters[0], filters[1]
    middle_filter = jnp.concatenate(
        [mix[w, third : third + 16, 2 * block : 2 * block + length] for w in range(wide)], axis=0
    ).astype(F32)
    grad_two = None
    for w in range(wide):
        source = grad_ahead if w < wide // 2 else grad_behind
        piece = columns(source, w % (wide // 2), block)
        factor_out = mix[w, half:fourth, 3 * block :].astype(F32)
        term = exact(piece, factor_out, (1, 1))
        grad_two = term if grad_two is None else grad_two + term
        mix_grad[w, half:fourth, 3 * block :] = exact(two, piece, (0, 0)).astype(BF16)
    grad_two = grad_two * filters[3]
    grad_one = exact(grad_two, middle_filter, (1, 1)) * filters[2]
    filter_grad = exact(one, grad_two, (0, 0)).astype(BF16)
    smalls = jnp.concatenate(
        [
            exact(features[...], grad_one, (0, 0)),
            jnp.sum(grad_one, axis=0, keepdims=True),
            jnp.sum(grad_two, axis=0, keepdims=True),
            jnp.zeros((6, length), F32),
        ],
        axis=0,
    )
    step = length // wide
    for w in range(wide):
        mix_grad[w, third : third + 16, 2 * block : 2 * block + length] = filter_grad[
            w * step : (w + 1) * step
        ]
        mix_grad[w, third + 16 : third + 32, 2 * block : 2 * block + step] = columns(
            smalls, w, step
        ).astype(BF16)
    total_in = None
    for u in range(2):
        low = value_scratch[u].astype(BF16)
        outs, right_grads, left_grads = monarch_small_backward(
            normed[...],
            [middle[u, b] for b in range(BLOCKS)],
            [columns(low, b, block) for b in range(BLOCKS)],
            lambda b: factor(mix, 0, u, b),
            lambda b: factor(mix, 0, 2 + u, b),
        )
        for b in range(BLOCKS):
            store_factor(mix_grad, 0, u, b, right_grads[b])
            store_factor(mix_grad, 0, 2 + u, b, left_grads[b])
        joint = jnp.concatenate(outs, axis=1)
        total_in = joint if total_in is None else total_in + joint
    through, gain, bias = norm_backward(total_in, hidden_in[...], table[0:1])
    outgoing = incoming + through
    table_grad[0:1] = gain
    table_grad[1:2] = norm_two[0:1]
    table_grad[2:3] = bias
    table_grad[3:4] = norm_two[1:2]
    if first_layer:
        chosen = marked[...] > 0.5
        table_grad[9:10] = jnp.sum(jnp.where(chosen, outgoing, 0.0), axis=0, keepdims=True)
        outgoing = jnp.where(chosen, 0.0, outgoing)
    result[...] = outgoing
    for w in range(wide):
        mix_grad[w, third : third + 16, block : block + half] = columns(
            table_grad[...], w, half
        ).astype(BF16)
    writes = grad_copies(grad_out, sems, mix_spots(mix_grad))
    start_all(writes)
    wait_all(writes)


COSTS = {"mixer_forward": 17, "glu_forward": 20, "glu_backward": 38, "mixer_backward": 24}


def call(kernel, name, outs, operands, anywhere, any_outs, scratch):
    vmem = pl.BlockSpec(memory_space=pltpu.VMEM)
    any_space = pl.BlockSpec(memory_space=pl.ANY)
    return pl.pallas_call(
        kernel,
        out_shape=[jax.ShapeDtypeStruct(shape, dtype) for shape, dtype in outs],
        in_specs=[any_space if index in anywhere else vmem for index in range(len(operands))],
        out_specs=[any_space if index in any_outs else vmem for index in range(len(outs))],
        scratch_shapes=scratch,
        compiler_params=pltpu.CompilerParams(vmem_limit_bytes=VMEM_BYTES),
        cost_estimate=pl.CostEstimate(
            flops=COSTS[name] * 10**9, bytes_accessed=COSTS[name] * 10**6, transcendentals=0
        ),
        name=name,
    )(*operands)


def mixer_forward(first_layer, hidden, marked, live, waves, features, pieces):
    rows, width = hidden.shape
    length = waves.shape[2]
    block = width // BLOCKS
    quarter = pieces.shape[4]
    outs = [
        ((rows, width), F32),
        ((rows, width), F32),
        ((8, 4 * quarter, width), BF16),
        ((16, width), F32),
        ((3, length, width), F32),
        ((length, 2 * width), F32),
        ((4, length, length), F32),
        ((rows, width), BF16),
        ((2, BLOCKS, rows, block), BF16),
        ((3, rows, width), BF16),
        ((rows, width), BF16),
        ((BLOCKS, rows, block), BF16),
    ]
    operands = (hidden, marked, live, waves, features, pieces)
    return call(
        partial(mixer_forward_kernel, first_layer),
        "mixer_forward",
        outs,
        operands,
        (5,),
        (),
        [pltpu.SemaphoreType.DMA((32,))],
    )


def glu_forward(hidden, table, mix, pieces):
    rows, width = hidden.shape
    block = width // BLOCKS
    outs = [
        ((rows, width), F32),
        ((rows, width), BF16),
        ((2, BLOCKS, rows, width), BF16),
        ((2, BLOCKS, rows, width), BF16),
        ((BLOCKS, rows, width), BF16),
        ((BLOCKS, rows, block), BF16),
    ]
    return call(
        glu_forward_kernel,
        "glu_forward",
        outs,
        (hidden, table, mix, pieces),
        (3,),
        (),
        [
            pltpu.VMEM((2, BLOCKS, width, width), BF16),
            pltpu.VMEM((2, width, width), BF16),
            pltpu.VMEM((BLOCKS, rows, block), F32),
            pltpu.SemaphoreType.DMA((64,)),
        ],
    )


def glu_backward(grad, hidden, table, mix, saved, pieces):
    rows, width = hidden.shape
    block = width // BLOCKS
    quarter = pieces.shape[4]
    outs = [
        ((rows, width), F32),
        ((8, width), F32),
        ((6, BLOCKS, block, block), BF16),
        ((2, 2, 2, 4, quarter, width), BF16),
    ]
    return call(
        glu_backward_kernel,
        "glu_backward",
        outs,
        (grad, hidden, table, mix) + tuple(saved) + (pieces,),
        (9,),
        (3,),
        [
            pltpu.VMEM((2, BLOCKS, width, width), BF16),
            pltpu.VMEM((2, width, width), BF16),
            pltpu.VMEM((BLOCKS, rows, block), BF16),
            pltpu.VMEM((2, BLOCKS, rows, width), BF16),
            pltpu.SemaphoreType.DMA((64,)),
            pltpu.SemaphoreType.DMA((64,)),
        ],
    )


def mixer_backward(first_layer, grad, marked, live, waves, features, saved, norm_two, down_grads):
    hidden, mix, table, spectrum, kernel, filters = saved[:6]
    rows, width = hidden.shape
    length = waves.shape[2]
    outs = [((rows, width), F32), ((2, 2, 2, 4, mix.shape[1] // 4, width), BF16)]
    operands = (
        (grad, hidden, marked, live, waves, features)
        + tuple(saved[1:])
        + (norm_two, down_grads)
    )
    return call(
        partial(mixer_backward_kernel, first_layer),
        "mixer_backward",
        outs,
        operands,
        (),
        (1,),
        [
            pltpu.VMEM(mix.shape, BF16),
            pltpu.VMEM((3, length, width), F32),
            pltpu.VMEM((2, rows, width), F32),
            pltpu.VMEM((16, width), F32),
            pltpu.SemaphoreType.DMA((32,)),
        ],
    )
PEERS = ((1, 0, 0, 0), (2, 0, 0, 0), (3, 0, 0, 0), (0, 1, 0, 0), (0, 0, 1, 0), (0, 0, 0, 1))
ALONG_X, ALONG_Y, ACROSS = PEERS[3], PEERS[4], PEERS[5]


def peer(distance, dx, dy, dc):
    z, x, y, c = place()
    return (2 * relative(z, distance) + flip(x, dx), 2 * flip(y, dy) + flip(c, dc))


def greet():
    barrier = pltpu.get_barrier_semaphore()
    for target in PEERS:
        pl.semaphore_signal(
            barrier, inc=1, device_id=peer(*target), device_id_type=pl.DeviceIdType.MESH
        )
    pl.semaphore_wait(barrier, len(PEERS))


class Mail:
    def __init__(self, sent, received):
        self.sent, self.received, self.copies = sent, received, []

    def send(self, source, target, to):
        index = len(self.copies)
        copy = pltpu.make_async_remote_copy(
            src_ref=source,
            dst_ref=target,
            send_sem=self.sent.at[index],
            recv_sem=self.received.at[index],
            device_id=peer(*to),
            device_id_type=pl.DeviceIdType.MESH,
        )
        copy.start()
        self.copies.append(copy)
        return copy

    def finish(self):
        for copy in self.copies:
            copy.wait_send()


GATHER_COPIES = 12


def gather_steps(mail, own, pieces, rows):
    view = lambda core, dx, dy, first, count: pieces.at[core, dx, dy, pl.ds(first, count), rows]
    along_z = [
        mail.send(own, pieces.at[0, 0, 0, distance, rows], PEERS[distance - 1])
        for distance in (1, 2, 3)
    ]
    yield
    for copy in along_z:
        copy.wait_recv()
    along_x = mail.send(view(0, 0, 0, 0, 4), view(0, 1, 0, 0, 4), ALONG_X)
    along_y = mail.send(view(0, 0, 0, 0, 4), view(0, 0, 1, 0, 4), ALONG_Y)
    across = [mail.send(view(0, 0, 0, 0, 4), view(1, 0, 0, 0, 4), ACROSS)]
    yield
    along_y.wait_recv()
    low = mail.send(view(0, 0, 1, 0, 2), view(0, 1, 1, 0, 2), ALONG_X)
    across.append(mail.send(view(0, 0, 1, 0, 4), view(1, 0, 1, 0, 4), ACROSS))
    along_x.wait_recv()
    high = mail.send(view(0, 1, 0, 2, 2), view(0, 1, 1, 2, 2), ALONG_Y)
    across.append(mail.send(view(0, 1, 0, 0, 4), view(1, 1, 0, 0, 4), ACROSS))
    yield
    low.wait_recv()
    across.append(mail.send(view(0, 1, 1, 0, 2), view(1, 1, 1, 0, 2), ACROSS))
    high.wait_recv()
    across.append(mail.send(view(0, 1, 1, 2, 2), view(1, 1, 1, 2, 2), ACROSS))
    yield
    for copy in across:
        copy.wait_recv()
    yield


def pipeline(starts, ahead):
    running = []
    waiting = list(starts)
    while waiting or running:
        if waiting:
            running.append(waiting.pop(0)())
        for chunk in list(running):
            try:
                next(chunk)
            except StopIteration:
                running.remove(chunk)


def gather_kernel(counts, *refs):
    groups = len(counts)
    owns, pieces = refs[:groups], refs[groups : 2 * groups]
    sent, received, local = refs[2 * groups :]
    mail = Mail(sent, received)
    greet()
    copies = []
    for index in range(groups):
        copy = pltpu.make_async_copy(owns[index], pieces[index].at[0, 0, 0, 0], local.at[index])
        copy.start()
        copies.append(copy)
    starts = []
    for index, count in enumerate(counts):
        size = owns[index].shape[0] // count
        for part in range(count):
            rows = pl.ds(part * size, size)
            starts.append(
                partial(gather_steps, mail, owns[index].at[rows], pieces[index], rows)
            )
    wait_all(copies)
    pipeline(starts, 1)
    mail.finish()


def gather_all(quarters, counts, number):
    anywhere = pl.BlockSpec(memory_space=pl.ANY)
    total = GATHER_COPIES * sum(counts)
    return pl.pallas_call(
        partial(gather_kernel, counts),
        out_shape=[
            jax.ShapeDtypeStruct((2, 2, 2, 4) + quarter.shape, quarter.dtype)
            for quarter in quarters
        ],
        in_specs=[anywhere] * len(quarters),
        out_specs=[anywhere] * len(quarters),
        scratch_shapes=[
            pltpu.SemaphoreType.DMA((total,)),
            pltpu.SemaphoreType.DMA((total,)),
            pltpu.SemaphoreType.DMA((len(quarters),)),
        ],
        compiler_params=pltpu.CompilerParams(collective_id=number, has_side_effects=True),
        name="gather",
    )(*quarters)


SCATTER_COPIES = 11


def scatter_steps(mail, local, grads, rows, result, spots, buffers):
    first, one, two_x, two_y, three, four, own, last = buffers
    x_core = mail.send(grads.at[1, :, :, :, rows], one, ACROSS)
    load = pltpu.make_async_copy(grads.at[0, :, :, :, rows], first, local.at[0])
    load.start()
    yield
    load.wait()
    x_core.wait_recv()
    for dx in range(2):
        for dy in range(2):
            first[dx, dy] += one[dx, dy]
    low = mail.send(first.at[1, :, pl.ds(0, 2)], two_x, ALONG_X)
    high = mail.send(first.at[:, 1, pl.ds(2, 2)], two_y, ALONG_Y)
    yield
    low.wait_recv()
    for dy in (1, 0):
        two_x[dy] += first[0, dy, 0:2]
        if dy == 1:
            low = mail.send(two_x.at[1], three.at[pl.ds(0, 2)], ALONG_Y)
    high.wait_recv()
    for dx in (1, 0):
        two_y[dx] += first[dx, 0, 2:4]
        if dx == 1:
            high = mail.send(two_y.at[1], three.at[pl.ds(2, 2)], ALONG_X)
    yield
    low.wait_recv()
    three[0:2] += two_x[0]
    along_z = [mail.send(three.at[1], four.at[0], PEERS[0])]
    high.wait_recv()
    three[2:4] += two_y[0]
    along_z += [mail.send(three.at[d], four.at[d - 1], PEERS[d - 1]) for d in (2, 3)]
    yield
    total = three[0].astype(F32)
    for index, copy in enumerate(along_z):
        copy.wait_recv()
        total = total + four[index].astype(F32)
    own[...] = total.astype(BF16)
    mine, theirs = spots
    across = [mail.send(own, result.at[mine, rows], ACROSS)]
    along_y = mail.send(own, last, ALONG_Y)
    keep = pltpu.make_async_copy(own, result.at[mine, rows], local.at[1])
    keep.start()
    yield
    along_y.wait_recv()
    across.append(mail.send(last, result.at[theirs, rows], ACROSS))
    keep_too = pltpu.make_async_copy(last, result.at[theirs, rows], local.at[2])
    keep_too.start()
    yield
    for copy in across:
        copy.wait_recv()
    keep.wait()
    keep_too.wait()
    yield


def scatter_buffers(size, width):
    return [
        pltpu.VMEM((2, 2, 4, size, width), BF16),
        pltpu.VMEM((2, 2, 4, size, width), BF16),
        pltpu.VMEM((2, 2, size, width), BF16),
        pltpu.VMEM((2, 2, size, width), BF16),
        pltpu.VMEM((4, size, width), BF16),
        pltpu.VMEM((3, size, width), BF16),
        pltpu.VMEM((size, width), BF16),
        pltpu.VMEM((size, width), BF16),
    ]


def scatter_kernel(counts, *refs):
    groups = len(counts)
    chunks = sum(counts)
    grads, results = refs[:groups], refs[groups : 2 * groups]
    sent, received, local = refs[2 * groups : 2 * groups + 3]
    buffers = refs[2 * groups + 3 :]
    mail = Mail(sent, received)
    unused, unused, y, c = place()
    spots = (2 * y + c, 2 * (1 - y) + c)
    greet()
    starts = []
    for index, count in enumerate(counts):
        size = results[index].shape[1] // count
        for part in range(count):
            number = len(starts)
            starts.append(
                partial(
                    scatter_steps,
                    mail,
                    local.at[number],
                    grads[index],
                    pl.ds(part * size, size),
                    results[index],
                    spots,
                    buffers[8 * number : 8 * number + 8],
                )
            )
    pipeline(starts, 1)
    mail.finish()


def scatter_all(grads, counts, number):
    anywhere = pl.BlockSpec(memory_space=pl.ANY)
    chunks = sum(counts)
    size, width = grads[0].shape[4] // counts[0], grads[0].shape[5]
    buffers = []
    for index, count in enumerate(counts):
        for part in range(count):
            buffers += scatter_buffers(grads[index].shape[4] // count, width)
    total = SCATTER_COPIES * chunks
    return pl.pallas_call(
        partial(scatter_kernel, counts),
        out_shape=[jax.ShapeDtypeStruct((4,) + array.shape[4:], BF16) for array in grads],
        in_specs=[anywhere] * len(grads),
        out_specs=[anywhere] * len(grads),
        scratch_shapes=[
            pltpu.SemaphoreType.DMA((total,)),
            pltpu.SemaphoreType.DMA((total,)),
            pltpu.SemaphoreType.DMA((chunks, 3)),
        ]
        + buffers,
        compiler_params=pltpu.CompilerParams(
            collective_id=number, has_side_effects=True, vmem_limit_bytes=VMEM_BYTES
        ),
        name="scatter",
    )(*grads)


def mix_pack(local, mask_vector):
    (
        norm_gain,
        norm_bias,
        in_right,
        in_left,
        conv_taps,
        skip_bias,
        filter_in,
        filter_in_bias,
        filter_mid,
        filter_mid_bias,
        filter_out,
        decay_rates,
        out_right,
        out_left,
        unused_right,
        unused_left,
        down_right,
        down_left,
    ) = local
    rows, block = in_right.shape[1:]
    step, order = filter_mid.shape
    features = filter_in.shape[0]
    zeros = lambda height, width: jnp.zeros((height, width), BF16)
    last = [] if mask_vector is None else [mask_vector[None]]
    table = jnp.concatenate(
        [norm_gain, norm_bias, conv_taps, skip_bias[None], decay_rates[None]] + last, axis=0
    )
    table = jnp.pad(table, ((0, 16 - table.shape[0]), (0, 0)))
    smalls = jnp.concatenate(
        [filter_in, zeros(8 - features, step), filter_in_bias[None], filter_mid_bias[None], zeros(6, step)],
        axis=0,
    )
    tail = filter_out[rows:]
    down = down_right.reshape(4, rows, block)
    return jnp.concatenate(
        [
            jnp.concatenate([in_right[0], in_right[1], in_left[0], in_left[1]], axis=1),
            jnp.concatenate([out_right, out_left, down_left, filter_out[:rows]], axis=1),
            jnp.concatenate(
                [
                    zeros(16, block),
                    table,
                    zeros(16, block - rows),
                    filter_mid,
                    zeros(16, block - order),
                    tail[:16],
                ],
                axis=1,
            ),
            jnp.concatenate(
                [zeros(16, 2 * block), smalls, zeros(16, block - step), tail[16:]], axis=1
            ),
            jnp.concatenate([down[0], down[1], down[2], down[3]], axis=1),
        ],
        axis=0,
    )


def mix_unpack(pack, shards):
    rows, block = shards[2].shape[2:]
    order = shards[10].shape[1]
    step = shards[9].shape[1]
    features = shards[6].shape[1]
    third, fourth = 2 * rows, rows + order
    cut = lambda low, high, k: pack[low:high, k * block : (k + 1) * block]
    table = pack[third : third + 16, block : block + rows]
    smalls = pack[third + 16 : third + 32, 2 * block : 2 * block + step]
    result = {
        0: table[0:2],
        1: table[2:4],
        2: jnp.stack([cut(0, rows, 0), cut(0, rows, 1)]),
        3: jnp.stack([cut(0, rows, 2), cut(0, rows, 3)]),
        4: table[4:7],
        5: table[7],
        6: smalls[:features],
        7: smalls[8],
        8: pack[third : third + step, 2 * block : 2 * block + order],
        9: smalls[9],
        10: cut(rows, fourth, 3),
        12: cut(rows, third, 0),
        13: cut(rows, third, 1),
        16: jnp.concatenate([cut(fourth, fourth + rows, k) for k in range(4)], axis=0),
        17: cut(rows, third, 2),
    }
    return result, table[9]


def layer_quarters(local, mask_vector):
    unused, unused, y, c = place()
    mix = mix_pack(local, mask_vector)
    rows = mix.shape[0] // 4
    glu = []
    for array in (local[15], local[14]):
        size = array.shape[1] // 2
        picked = lax.dynamic_index_in_dim(array, y, 0, keepdims=False)
        glu.append(lax.dynamic_slice_in_dim(picked, c * size, size, 0))
    return (
        lax.dynamic_slice_in_dim(mix, (2 * y + c) * rows, rows, 0),
        jnp.concatenate(glu, axis=0),
    )


GRADS = (0, 1, 2, 3, 4, 5, 6, 7, 8, 9, 10, 12, 13, 14, 15, 16, 17)
SHARD_AXIS = (1, 1, 1, 1, 1, 0, 1, 0, 0, 0, 1, 0, 0, 0, 1, 1, 0, 0)


def gather_plain(shards, layer_index):
    return tuple(
        lax.all_gather(shards[index][layer_index], "wide", axis=SHARD_AXIS[index], tiled=True)
        for index in range(18)
    )


def scatter_plain(grads, mask_term):
    terms = list(grads) + ([] if mask_term is None else [mask_term])
    axes = [SHARD_AXIS[index] for index in GRADS] + [0]
    return narrow_total(
        [
            lax.psum_scatter(term, "wide", scatter_dimension=axis, tiled=True)
            for term, axis in zip(terms, axes)
        ]
    )


def wave_table(length):
    frequency = np.arange(length)[:, None]
    places = np.arange(length)[None, :]
    angles = (frequency * places % (2 * length)) * (math.pi / length)
    turned = -np.sin(angles)
    turned[0] = np.where(np.arange(length) % 2 == 0, 1.0, -1.0)
    table = jnp.asarray(np.concatenate([np.cos(angles), turned]), F32)
    high = table.astype(BF16)
    return jnp.stack([high, (table - high.astype(F32)).astype(BF16)])


def staged_body(shards, mask_vector, hidden_in, cotangent, live, marked, mesh_shape):
    rows = hidden_in.shape[0]
    length = live.shape[1]
    live = live.reshape(rows, 1)
    marked = marked.astype(F32)
    waves = wave_table(length)
    features = jnp.pad(position_features(length), ((0, 0), (0, 8 - EMB)))
    quarters = []
    for layer_index in range(LAYERS):
        local = tuple(member[layer_index] for member in shards)
        quarters += layer_quarters(local, mask_vector if layer_index == 0 else None)
    pieces = gather_all(quarters, (1, 3) * LAYERS, 1)
    hidden = hidden_in
    kept = []
    for layer_index in range(LAYERS):
        mixed = mixer_forward(
            layer_index == 0, hidden, marked, live, waves, features, pieces[2 * layer_index]
        )
        second = glu_forward(mixed[0], mixed[3], mixed[2], pieces[2 * layer_index + 1])
        kept.append((mixed, second))
        hidden = second[0]
    output = hidden.astype(BF16)
    grad = cotangent.astype(F32)
    layer_grads = [None] * LAYERS
    totals = [None] * LAYERS
    for layer_index in reversed(range(LAYERS)):
        mixed, second = kept[layer_index]
        grad, norm_two, down_grads, glu_grads = glu_backward(
            grad, mixed[0], mixed[3], mixed[2], second[1:], pieces[2 * layer_index + 1]
        )
        grad, mix_grads = mixer_backward(
            layer_index == 0,
            grad,
            marked,
            live,
            waves,
            features,
            mixed[1:],
            norm_two,
            down_grads,
        )
        totals[layer_index] = (mix_grads, glu_grads)
    sums = scatter_all(totals[0] + totals[1], (1, 3) * LAYERS, 2)
    for layer_index in reversed(range(LAYERS)):
        mix, glu = (array.astype(F32) for array in sums[2 * layer_index : 2 * layer_index + 2])
        found, mask_grad = mix_unpack(mix.reshape(-1, mix.shape[-1]), shards)
        tall = shards[15].shape[2] // 2
        found[15] = glu[:, :tall].reshape(2, 2 * tall, -1)
        found[14] = glu[:, tall:].reshape(2, shards[14].shape[2], -1)
        layer_grads[layer_index] = [found[index] for index in GRADS]
    return output, grad, mask_grad, layer_grads


def is_staged(shards, mesh_shape):
    short, block = shards[2].shape[2:]
    order, outs = shards[10].shape[1:]
    return (
        tuple(mesh_shape) == (8, 4)
        and short == 96
        and block == 192
        and order == 128
        and outs == block
        and shards[14].shape[2:] == (short, 8 * short)
        and shards[15].shape[2:] == (4 * short, 8 * short)
    )


def narrow_total(parts):
    flattened = jnp.concatenate([member.reshape(-1) for member in parts])
    summed = lax.psum(flattened.astype(jnp.bfloat16), "narrow").astype(jnp.float32)
    result = []
    offset = 0
    for member in parts:
        result.append(summed[offset : offset + member.size].reshape(member.shape))
        offset = offset + member.size
    return result


def plain_body(shards, mask_vector, hidden_in, cotangent, live_mask, marked):
    seq_count = live_mask.shape[0]
    mask_full = lax.all_gather(mask_vector, "wide", axis=0, tiled=True)
    weights = [gather_plain(shards, layer_index) for layer_index in range(LAYERS)]
    hidden = jnp.where(
        marked, mask_full.astype(jnp.float32)[None, :], hidden_in.astype(jnp.float32)
    )
    saved_layers = []
    for layer_index in range(LAYERS):
        hidden, saved = forward_layer(hidden, weights[layer_index], live_mask)
        saved_layers.append(saved)
    output = hidden.astype(jnp.bfloat16)
    share = 0.5 * seq_count
    grad_hidden = cotangent.astype(jnp.float32)
    layer_grads = [None] * LAYERS
    mask_grad = None
    for layer_index in reversed(range(LAYERS)):
        grad_hidden, grads = backward_layer(
            grad_hidden, weights[layer_index], saved_layers[layer_index], live_mask, share
        )
        if layer_index > 0:
            layer_grads[layer_index] = scatter_plain(grads, None)
        else:
            mask_term = jnp.sum(jnp.where(marked, grad_hidden, 0.0), axis=0)
            reduced = scatter_plain(grads, mask_term)
            layer_grads[0] = reduced[:-1]
            mask_grad = reduced[-1]
    grad_input = jnp.where(marked, 0.0, grad_hidden)
    return output, grad_input, mask_grad, layer_grads


def body(
    mesh_shape,
    hidden_in,
    seq_lengths,
    mask_positions,
    mask_vector,
    cotangent,
    norm_gain,
    norm_bias,
    in_right,
    in_left,
    conv_taps,
    skip_bias,
    filter_in,
    filter_in_bias,
    filter_mid,
    filter_mid_bias,
    filter_out,
    decay_rates,
    out_right,
    out_left,
    glu_right,
    glu_left,
    down_right,
    down_left,
):
    row_count = hidden_in.shape[0]
    seq_count = seq_lengths.shape[0]
    length = row_count // seq_count
    places = jnp.arange(length, dtype=jnp.int32)
    live_mask = (places[None, :] < seq_lengths[:, None]).astype(jnp.float32)[:, :, None]
    marked = jnp.any(mask_positions[:, :, None] == places[None, None, :], axis=1).reshape(
        row_count, 1
    )
    shards = (
        norm_gain,
        norm_bias,
        in_right,
        in_left,
        conv_taps,
        skip_bias,
        filter_in,
        filter_in_bias,
        filter_mid,
        filter_mid_bias,
        filter_out,
        decay_rates,
        out_right,
        out_left,
        glu_right,
        glu_left,
        down_right,
        down_left,
    )
    if is_staged(shards, mesh_shape):
        output, grad_input, mask_grad, layer_grads = staged_body(
            shards, mask_vector, hidden_in, cotangent, live_mask, marked, mesh_shape
        )
    else:
        output, grad_input, mask_grad, layer_grads = plain_body(
            shards, mask_vector, hidden_in, cotangent, live_mask, marked
        )
    final_grads = [
        jnp.stack([layer_grads[position][member_index] for position in range(LAYERS)])
        for member_index in range(17)
    ]
    return (output, grad_input, mask_grad) + tuple(final_grads)


def solution(mesh):
    placed = (
        P(("wide", "narrow"), None),
        P(("wide", "narrow")),
        P(("wide", "narrow"), None),
        P("wide"),
        P(("wide", "narrow"), None),
        P(None, None, "wide"),
        P(None, None, "wide"),
        P(None, None, "wide", None),
        P(None, None, "wide", None),
        P(None, None, "wide"),
        P(None, "wide"),
        P(None, None, "wide"),
        P(None, "wide"),
        P(None, "wide", None),
        P(None, "wide"),
        P(None, None, "wide"),
        P(None, "wide"),
        P(None, "wide", None),
        P(None, "wide", None),
        P(None, None, "wide", None),
        P(None, None, "wide", None),
        P(None, "wide", None),
        P(None, "wide", None),
    )
    return jax.shard_map(
        partial(body, (mesh.shape["wide"], mesh.shape["narrow"])),
        mesh=mesh,
        in_specs=placed,
        out_specs=(
            P(("wide", "narrow"), None),
            P(("wide", "narrow"), None),
            P("wide"),
            P(None, None, "wide"),
            P(None, None, "wide"),
            P(None, None, "wide", None),
            P(None, None, "wide", None),
            P(None, None, "wide"),
            P(None, "wide"),
            P(None, None, "wide"),
            P(None, "wide"),
            P(None, "wide", None),
            P(None, "wide"),
            P(None, None, "wide"),
            P(None, "wide", None),
            P(None, "wide", None),
            P(None, None, "wide", None),
            P(None, None, "wide", None),
            P(None, "wide", None),
            P(None, "wide", None),
        ),
        check_vma=False,
    )
```

```python
from functools import partial
import math

import jax
import jax.numpy as jnp
import numpy as np
from jax import lax
from jax.experimental import pallas as pl
from jax.experimental.pallas import tpu as pltpu
from jax.sharding import PartitionSpec as P

BLOCKS = 4
EMB = 5
LAYERS = 2


EPSILON = 1e-05
highest_precision = lax.Precision.HIGHEST


def permute(values):
    array_shape = values.shape
    blocks = array_shape[-2]
    split_view = values.reshape(array_shape[:-1] + (blocks, array_shape[-1] // blocks))
    return jnp.swapaxes(split_view, -3, -2).reshape(array_shape)


def monarch_forward(inputs, right_factor, left_factor):
    row_count = inputs.shape[0]
    right_blocks = right_factor.reshape(BLOCKS, -1, right_factor.shape[-1])
    left_blocks = left_factor.reshape(BLOCKS, -1, left_factor.shape[-1])
    middle = jnp.einsum(
        "rbi,bio->rbo",
        inputs.reshape(row_count, BLOCKS, -1),
        right_blocks,
        preferred_element_type=jnp.float32,
    )
    middle = permute(middle).astype(jnp.bfloat16)
    output = jnp.einsum("rbi,bio->rbo", middle, left_blocks, preferred_element_type=jnp.float32)
    return (middle, output.reshape(row_count, -1))


def monarch_backward(inputs, middle, right_factor, left_factor, grad_output):
    row_count = inputs.shape[0]
    right_blocks = right_factor.reshape(BLOCKS, -1, right_factor.shape[-1])
    left_blocks = left_factor.reshape(BLOCKS, -1, left_factor.shape[-1])
    grad_low = grad_output.astype(jnp.bfloat16).reshape(row_count, BLOCKS, -1)
    grad_left = jnp.einsum("rbi,rbo->bio", middle, grad_low, preferred_element_type=jnp.float32)
    grad_middle = jnp.einsum(
        "rbo,bio->rbi", grad_low, left_blocks, preferred_element_type=jnp.float32
    )
    grad_middle = permute(grad_middle).astype(jnp.bfloat16)
    input_blocks = inputs.reshape(row_count, BLOCKS, -1)
    grad_right = jnp.einsum(
        "rbi,rbo->bio", input_blocks, grad_middle, preferred_element_type=jnp.float32
    )
    grad_inputs = jnp.einsum(
        "rbo,bio->rbi", grad_middle, right_blocks, preferred_element_type=jnp.float32
    )
    return (
        grad_inputs.reshape(row_count, -1),
        grad_right.reshape(right_factor.shape),
        grad_left.reshape(left_factor.shape),
    )


def layer_norm(values, norm_gain, norm_bias):
    average = jnp.mean(values, axis=-1, keepdims=True)
    centred = values - average
    variance = jnp.mean(centred * centred, axis=-1, keepdims=True)
    return centred * lax.rsqrt(variance + EPSILON) * norm_gain + norm_bias


def position_features(length):
    positions = jnp.arange(length, dtype=jnp.float32)
    fraction = positions / length
    features = [fraction]
    for band_index in range(1, (EMB - 1) // 2 + 1):
        features.append(jnp.cos(2.0 * math.pi * band_index * fraction))
        features.append(jnp.sin(2.0 * math.pi * band_index * fraction))
    return jnp.stack(features, axis=1)


def make_filter(
    filter_in, filter_in_bias, filter_mid, filter_mid_bias, filter_out, decay_rates, length
):
    embedding = position_features(length)
    first_hidden = jnp.sin(
        jnp.dot(embedding, filter_in, precision=highest_precision) + filter_in_bias
    )
    second = jnp.sin(
        jnp.dot(first_hidden, filter_mid, precision=highest_precision) + filter_mid_bias
    )
    kernel = jnp.dot(second, filter_out, precision=highest_precision)
    fraction = jnp.arange(length, dtype=jnp.float32)[:, None] / length
    both_rates = jnp.concatenate([decay_rates, decay_rates])
    return kernel * jnp.exp(-fraction * both_rates[None, :])


def short_convolution(signal_rows, conv_taps):
    padded = jnp.pad(signal_rows, ((0, 0), (2, 0), (0, 0)))
    return (
        conv_taps[0] * padded[:, :-2]
        + conv_taps[1] * padded[:, 1:-1]
        + conv_taps[2] * padded[:, 2:]
    )


def spectral_tables(length, span):
    padded_length = 2 * length
    frequency = jnp.arange(length + 1, dtype=jnp.int32)
    places = jnp.arange(span, dtype=jnp.int32)
    phase_index = frequency[:, None] * places[None, :] % padded_length
    angles = phase_index.astype(jnp.float32) * (2.0 * math.pi / padded_length)
    ends = (frequency == 0) | (frequency == length)
    weights = jnp.where(ends, 1.0, 2.0).astype(jnp.float32) / padded_length
    return (jnp.cos(angles), jnp.sin(angles), weights)


def circular_kernel(kernel):
    width = kernel.shape[1] // 2
    forward_part = kernel[:, :width]
    reverse_part = kernel[:, width:]
    first_row = forward_part[:1] + reverse_part[:1]
    spacer = jnp.zeros((1, width), jnp.float32)
    return jnp.concatenate(
        [first_row, forward_part[1:], spacer, jnp.flip(reverse_part[1:], axis=0)], axis=0
    )


def long_convolution(signal_rows, kernel):
    length = signal_rows.shape[1]
    cosine_lookup, sine_lookup, weights = spectral_tables(length, length)
    kernel_cosine, kernel_sine, unused = spectral_tables(length, 2 * length)
    circular = circular_kernel(kernel)
    real_signal = jnp.einsum("ik,hkm->him", cosine_lookup, signal_rows, precision=highest_precision)
    imaginary_signal = -jnp.einsum(
        "ik,hkm->him", sine_lookup, signal_rows, precision=highest_precision
    )
    kernel_real = jnp.dot(kernel_cosine, circular, precision=highest_precision)
    kernel_imaginary = -jnp.dot(kernel_sine, circular, precision=highest_precision)
    real_product = real_signal * kernel_real - imaginary_signal * kernel_imaginary
    imaginary_product = real_signal * kernel_imaginary + imaginary_signal * kernel_real
    inverse_cosine_table = cosine_lookup * weights[:, None]
    inverse_sine_table = sine_lookup * weights[:, None]
    return jnp.einsum(
        "hp,ihj->ipj", inverse_cosine_table, real_product, precision=highest_precision
    ) - jnp.einsum(
        "hp,ihj->ipj", inverse_sine_table, imaginary_product, precision=highest_precision
    )


def mixer_piece(
    value_path,
    gate_path,
    conv_taps,
    skip_bias,
    filter_in,
    filter_in_bias,
    filter_mid,
    filter_mid_bias,
    filter_out,
    decay_rates,
    live_mask,
    share,
):
    length = live_mask.shape[1]
    kernel = make_filter(
        filter_in, filter_in_bias, filter_mid, filter_mid_bias, filter_out, decay_rates, length
    )
    signal_rows = value_path.reshape(live_mask.shape[0], length, -1) * live_mask
    signal_rows = short_convolution(signal_rows, conv_taps) * live_mask
    mixed_signal = long_convolution(signal_rows, kernel) + signal_rows * skip_bias
    return (mixed_signal.reshape(value_path.shape) * gate_path, share * jnp.sum(kernel * kernel))


def glu_piece(upper_branch, gate_branch):
    return jax.nn.gelu(gate_branch, approximate=False) * upper_branch


def small_weights(layer_weights):
    return tuple(
        (layer_weights[position].astype(jnp.float32) for position in (4, 5, 6, 7, 8, 9, 10))
    )


def forward_layer(hidden, layer_weights, live_mask):
    (
        norm_gain,
        norm_bias,
        in_right,
        in_left,
        conv_taps,
        skip_bias,
        filter_in,
        filter_in_bias,
        filter_mid,
        filter_mid_bias,
        filter_out,
        decay_rates,
        out_right,
        out_left,
        glu_right,
        glu_left,
        down_right,
        down_left,
    ) = layer_weights
    gains = norm_gain.astype(jnp.float32)
    biases = norm_bias.astype(jnp.float32)
    small = small_weights(layer_weights)
    normed = layer_norm(hidden, gains[0], biases[0]).astype(jnp.bfloat16)
    middle_value, value_path = monarch_forward(normed, in_right[0], in_left[0])
    middle_gate, gate_path = monarch_forward(normed, in_right[1], in_left[1])
    mixed_signal, unused = mixer_piece(
        value_path,
        gate_path,
        small[0],
        small[1],
        small[2],
        small[3],
        small[4],
        small[5],
        small[6],
        decay_rates.astype(jnp.float32),
        live_mask,
        0.0,
    )
    mixed_signal = mixed_signal.astype(jnp.bfloat16)
    middle_out, branch = monarch_forward(mixed_signal, out_right, out_left)
    middle_hidden = hidden + branch
    normed_two = layer_norm(middle_hidden, gains[1], biases[1]).astype(jnp.bfloat16)
    middle_up, upper_branch = monarch_forward(normed_two, glu_right[0], glu_left[0])
    middle_glu, gate_branch = monarch_forward(normed_two, glu_right[1], glu_left[1])
    glu_hidden = glu_piece(upper_branch, gate_branch).astype(jnp.bfloat16)
    middle_down, branch_two = monarch_forward(glu_hidden, down_right, down_left)
    saved = (
        hidden,
        normed,
        middle_value,
        value_path,
        middle_gate,
        gate_path,
        mixed_signal,
        middle_out,
        middle_hidden,
        normed_two,
        middle_up,
        upper_branch,
        middle_glu,
        gate_branch,
        glu_hidden,
        middle_down,
    )
    return (middle_hidden + branch_two, saved)


def backward_layer(grad_hidden, layer_weights, saved, live_mask, share):
    (
        norm_gain,
        norm_bias,
        in_right,
        in_left,
        conv_taps,
        skip_bias,
        filter_in,
        filter_in_bias,
        filter_mid,
        filter_mid_bias,
        filter_out,
        decay_rates,
        out_right,
        out_left,
        glu_right,
        glu_left,
        down_right,
        down_left,
    ) = layer_weights
    (
        hidden,
        normed,
        middle_value,
        value_path,
        middle_gate,
        gate_path,
        mixed_signal,
        middle_out,
        middle_hidden,
        normed_two,
        middle_up,
        upper_branch,
        middle_glu,
        gate_branch,
        glu_hidden,
        middle_down,
    ) = saved
    gains = norm_gain.astype(jnp.float32)
    biases = norm_bias.astype(jnp.float32)
    small = small_weights(layer_weights)
    grad_glu, grad_down_right, grad_down_left = monarch_backward(
        glu_hidden, middle_down, down_right, down_left, grad_hidden
    )
    unused, glu_pull = jax.vjp(glu_piece, upper_branch, gate_branch)
    grad_upper, grad_gate = glu_pull(grad_glu)
    grad_normed_up, grad_right_up, grad_left_up = monarch_backward(
        normed_two, middle_up, glu_right[0], glu_left[0], grad_upper
    )
    grad_normed_gate, grad_right_gate, grad_left_gate = monarch_backward(
        normed_two, middle_glu, glu_right[1], glu_left[1], grad_gate
    )
    unused, norm_pull = jax.vjp(layer_norm, middle_hidden, gains[1], biases[1])
    grad_middle, grad_gain_two, grad_bias_two = norm_pull(grad_normed_up + grad_normed_gate)
    grad_middle = grad_middle + grad_hidden
    grad_mixed, grad_out_right, grad_out_left = monarch_backward(
        mixed_signal, middle_out, out_right, out_left, grad_middle
    )
    mixer_local = partial(
        mixer_piece, decay_rates=decay_rates.astype(jnp.float32), live_mask=live_mask, share=share
    )
    unused, mixer_pull = jax.vjp(
        mixer_local,
        value_path,
        gate_path,
        small[0],
        small[1],
        small[2],
        small[3],
        small[4],
        small[5],
        small[6],
    )
    mixer_grads = mixer_pull((grad_mixed, jnp.ones((), jnp.float32)))
    grad_normed_value, grad_right_value, grad_left_value = monarch_backward(
        normed, middle_value, in_right[0], in_left[0], mixer_grads[0]
    )
    grad_normed_path, grad_right_path, grad_left_path = monarch_backward(
        normed, middle_gate, in_right[1], in_left[1], mixer_grads[1]
    )
    unused, norm_pull_one = jax.vjp(layer_norm, hidden, gains[0], biases[0])
    grad_before, grad_gain_one, grad_bias_one = norm_pull_one(grad_normed_value + grad_normed_path)
    grads = (
        jnp.stack([grad_gain_one, grad_gain_two]),
        jnp.stack([grad_bias_one, grad_bias_two]),
        jnp.stack([grad_right_value, grad_right_path]),
        jnp.stack([grad_left_value, grad_left_path]),
        mixer_grads[2],
        mixer_grads[3],
        mixer_grads[4],
        mixer_grads[5],
        mixer_grads[6],
        mixer_grads[7],
        mixer_grads[8],
        grad_out_right,
        grad_out_left,
        jnp.stack([grad_right_up, grad_right_gate]),
        jnp.stack([grad_left_up, grad_left_gate]),
        grad_down_right,
        grad_down_left,
    )
    return (grad_before + grad_middle, grads)


F32 = jnp.float32
BF16 = jnp.bfloat16
VMEM_BYTES = 60 * 1024 * 1024


def dot(left, right):
    return jnp.dot(left, right, preferred_element_type=F32)


def dot_rows(left, right):
    return lax.dot_general(left, right, (((0,), (0,)), ((), ())), preferred_element_type=F32)


def dot_columns(left, right):
    return lax.dot_general(left, right, (((1,), (1,)), ((), ())), preferred_element_type=F32)


def exact(left, right, dims=(1, 0)):
    return lax.dot_general(
        left,
        right,
        (((dims[0],), (dims[1],)), ((), ())),
        precision=highest_precision,
        preferred_element_type=F32,
    )


def columns(values, index, width):
    return values[:, index * width : (index + 1) * width]


def shuffled(parts):
    chunk = parts[0].shape[1] // BLOCKS
    return [
        jnp.concatenate([columns(part, index, chunk) for part in parts], axis=1)
        for index in range(BLOCKS)
    ]


def normalised(values):
    average = jnp.mean(values, axis=-1, keepdims=True)
    centred = values - average
    variance = jnp.mean(centred * centred, axis=-1, keepdims=True)
    scale = lax.rsqrt(variance + EPSILON)
    return centred * scale, scale


def norm_backward(grad, hidden, gain):
    unit, scale = normalised(hidden)
    grad_gain = jnp.sum(grad * unit, axis=0, keepdims=True)
    grad_bias = jnp.sum(grad, axis=0, keepdims=True)
    scaled = grad * gain
    mean_one = jnp.mean(scaled, axis=-1, keepdims=True)
    mean_two = jnp.mean(scaled * unit, axis=-1, keepdims=True)
    return scale * (scaled - mean_one - unit * mean_two), grad_gain, grad_bias


def flip(bit, by):
    return 1 - bit if by else bit


def place():
    w = lax.axis_index("wide")
    n = lax.axis_index("narrow")
    return w // 2, w % 2, n // 2, n % 2


def relative(z, distance):
    high, low = z // 2, z % 2
    return 2 * flip(high, distance // 2) + flip(low, distance % 2)


def piece_copies(pieces, sems, targets_of):
    z, x, y, c = place()
    copies = []
    for core in range(2):
        for dx in range(2):
            for dy in range(2):
                for dz in range(4):
                    owner = (relative(z, dz), flip(x, dx), flip(y, dy), flip(c, core))
                    for row, target in targets_of(*owner):
                        view = pieces.at[core, dx, dy, dz, pl.ds(row, target.shape[0])]
                        copies.append(pltpu.make_async_copy(view, target, sems.at[len(copies)]))
    return copies


def grad_copies(result, sems, sources_of):
    z, x, y, c = place()
    copies = []
    for core in range(2):
        for dx in range(2):
            for dy in range(2):
                for dz in range(4):
                    owner = (relative(z, dz), flip(x, dx), flip(y, dy), flip(c, core))
                    for row, source in sources_of(*owner):
                        view = result.at[core, dx, dy, dz, pl.ds(row, source.shape[0])]
                        copies.append(pltpu.make_async_copy(source, view, sems.at[len(copies)]))
    return copies


def start_all(copies):
    for copy in copies:
        copy.start()


def wait_all(copies):
    for copy in copies:
        copy.wait()


def glu_spots(left, right):
    def spots(z, x, y, c):
        tall, short = left.shape[2] // 4, right.shape[1] // 16
        return (
            (0, left.at[y, z, pl.ds(pl.multiple_of((2 * x + c) * tall, 16), tall)]),
            (tall, right.at[y, pl.ds(pl.multiple_of((4 * z + 2 * x + c) * short, 16), short)]),
        )

    return spots


def mix_spots(mix):
    def spots(z, x, y, c):
        rows = mix.shape[1] // 4
        return ((0, mix.at[2 * z + x, pl.ds(pl.multiple_of((2 * y + c) * rows, 16), rows)]),)

    return spots


def factor(mix, rows, kind, block):
    width = mix.shape[2] // 4
    low = kind * width
    top = mix[2 * block, rows : rows + width // 2, low : low + width]
    bottom = mix[2 * block + 1, rows : rows + width // 2, low : low + width]
    return jnp.concatenate([top, bottom], axis=0)


def down_factor(mix, first, block):
    width = mix.shape[2] // 4
    half = width // 2
    parts = []
    for shard in (2 * block, 2 * block + 1):
        for index in range(4):
            parts.append(mix[shard, first : first + half, index * width : (index + 1) * width])
    return jnp.concatenate(parts, axis=0)


def monarch_small(inputs, right, left):
    width = inputs.shape[1] // BLOCKS
    parts = [dot(columns(inputs, b, width), right(b)) for b in range(BLOCKS)]
    middle = [part.astype(BF16) for part in shuffled(parts)]
    return middle, [dot(middle[b], left(b)) for b in range(BLOCKS)]


def monarch_small_backward(inputs, middle, grads, right, left):
    width = inputs.shape[1] // BLOCKS
    grad_left = [dot_rows(middle[b], grads[b]) for b in range(BLOCKS)]
    back = shuffled([dot_columns(grads[b], left(b)) for b in range(BLOCKS)])
    back = [part.astype(BF16) for part in back]
    grad_right = [dot_rows(columns(inputs, b, width), back[b]) for b in range(BLOCKS)]
    return [dot_columns(back[b], right(b)) for b in range(BLOCKS)], grad_right, grad_left


def store_factor(mix, rows, kind, block, value):
    width = mix.shape[2] // 4
    half = width // 2
    low = kind * width
    mix[2 * block, rows : rows + half, low : low + width] = value[:half].astype(BF16)
    mix[2 * block + 1, rows : rows + half, low : low + width] = value[half:].astype(BF16)


def cell(values):
    rise = 0.5 * (1.0 + lax.erf(values * (0.5**0.5)))
    return rise, jnp.exp(-0.5 * values * values) * ((2.0 * math.pi) ** -0.5)


def glu_forward_kernel(hidden, table, mix, *refs):
    pieces, result, normed_out, middle_out, branch_out, glu_out, down_out = refs[:7]
    left, right, parts, sems = refs[7:]
    copies = piece_copies(pieces, sems, glu_spots(left, right))
    start_all(copies)
    rows, width = hidden.shape
    block = width // BLOCKS
    unit, unused = normalised(hidden[...])
    normed = (unit * table[1:2] + table[3:4]).astype(BF16)
    normed_out[...] = normed
    wait_all(copies)
    for u in range(2):
        for b in range(BLOCKS):
            part = dot(columns(normed, b, block), right[u, b * block : (b + 1) * block]).astype(BF16)
            for q in range(BLOCKS):
                middle_out[u, q, :, b * block : (b + 1) * block] = columns(part, q, block)
    for q in range(BLOCKS):
        upper = dot(middle_out[0, q], left[0, q])
        gate = dot(middle_out[1, q], left[1, q])
        branch_out[0, q] = upper.astype(BF16)
        branch_out[1, q] = gate.astype(BF16)
        glu = (gate * cell(gate)[0] * upper).astype(BF16)
        glu_out[q] = glu
        parts[q] = dot(glu, down_factor(mix, 7 * block // 6, q))
    down = [part.astype(BF16) for part in shuffled([parts[q] for q in range(BLOCKS)])]
    for b in range(BLOCKS):
        down_out[b] = down[b]
        span = slice(b * block, (b + 1) * block)
        result[:, span] = hidden[:, span] + dot(down[b], factor(mix, block // 2, 2, b))


def glu_backward_kernel(grad, hidden, table, mix, normed, middle, branch, glu, down, *refs):
    pieces, result, norm_out, mix_grad, glu_grad = refs[:5]
    left, right, low, back, sems, out_sems = refs[5:]
    copies = piece_copies(pieces, sems, glu_spots(left, right))
    start_all(copies)
    rows, width = hidden.shape
    block = width // BLOCKS
    incoming = grad[...]
    half = incoming.astype(BF16)
    backs = []
    for b in range(BLOCKS):
        part = columns(half, b, block)
        mix_grad[1, b] = dot_rows(down[b], part).astype(BF16)
        backs.append(dot_columns(part, factor(mix, block // 2, 2, b)))
    backs = shuffled(backs)
    for q in range(BLOCKS):
        low[q] = backs[q].astype(BF16)
    wait_all(copies)
    for q in range(BLOCKS):
        step = low[q]
        product = dot_rows(glu[q], step).astype(BF16)
        for index in range(BLOCKS):
            mix_grad[2 + index, q] = product[index * block : (index + 1) * block]
        grad_glu = dot_columns(step, down_factor(mix, 7 * block // 6, q))
        upper = branch[0, q].astype(F32)
        gate = branch[1, q].astype(F32)
        rise, density = cell(gate)
        terms = (grad_glu * gate * rise, grad_glu * upper * (rise + gate * density))
        for u in range(2):
            term = terms[u].astype(BF16)
            wide = dot_columns(term, left[u, q]).astype(BF16)
            left[u, q] = dot_rows(middle[u, q], term).astype(BF16)
            for b in range(BLOCKS):
                back[u, b, :, q * block : (q + 1) * block] = columns(wide, b, block)
    outgoing = []
    for b in range(BLOCKS):
        span = slice(b * block, (b + 1) * block)
        total = None
        for u in range(2):
            term = dot_columns(back[u, b], right[u, span])
            right[u, span] = dot_rows(normed[:, span], back[u, b]).astype(BF16)
            total = term if total is None else total + term
        outgoing.append(total)
    writes = grad_copies(glu_grad, out_sems, glu_spots(left, right))
    start_all(writes)
    through, gain, bias = norm_backward(
        jnp.concatenate(outgoing, axis=1), hidden[...], table[1:2]
    )
    result[...] = incoming + through
    norm_out[0:1] = gain
    norm_out[1:2] = bias
    wait_all(writes)


def shifted(values, by):
    length = values.shape[0]
    rolled = pltpu.roll(values, by % length, 0)
    row = lax.broadcasted_iota(jnp.int32, values.shape, 0)
    keep = row >= by if by > 0 else row < length + by
    return jnp.where(keep, rolled, 0.0)


def two_parts(values):
    high = values.astype(BF16)
    return high, (values - high.astype(F32)).astype(BF16)


def to_spectrum(waves, values):
    high, low = two_parts(values)
    return dot(waves[0], high) + (dot(waves[1], high) + dot(waves[0], low))


def from_spectrum(waves, values):
    high, low = two_parts(values)
    return dot_rows(waves[0], high) + (dot_rows(waves[1], high) + dot_rows(waves[0], low))


def multiplied(spectrum, kernel, back):
    length = kernel.shape[1]
    real, imaginary = spectrum[:length], spectrum[length:]
    sign = -1.0 if back else 1.0
    return jnp.concatenate(
        [
            real * kernel[0] - sign * imaginary * kernel[1],
            sign * real * kernel[1] + imaginary * kernel[2],
        ],
        axis=0,
    )


def mixer_forward_kernel(first_layer, *refs):
    hidden_in, marked, live, waves, features = refs[:5]
    pieces = refs[5]
    outs = refs[6:18]
    (
        result,
        hidden_out,
        mix,
        table,
        spectrum_out,
        kernel_out,
        filter_out,
        normed_out,
        middle_out,
        saved_out,
        mixed_out,
        middle_two_out,
    ) = outs
    sems = refs[18]
    copies = piece_copies(pieces, sems, mix_spots(mix))
    start_all(copies)
    wait_all(copies)
    rows, width = hidden_in.shape
    block = width // BLOCKS
    half = block // 2
    length = waves.shape[2]
    wide = mix.shape[0]
    third = 2 * half
    fourth = third + length - half
    span = half
    for w in range(wide):
        table[:, w * span : (w + 1) * span] = mix[w, third : third + 16, block : block + span].astype(F32)
    order = length
    step = order // wide
    smalls = jnp.concatenate(
        [mix[w, third + 16 : third + 32, 2 * block : 2 * block + step] for w in range(wide)], axis=1
    ).astype(F32)
    middle_filter = jnp.concatenate(
        [mix[w, third : third + 16, 2 * block : 2 * block + order] for w in range(wide)], axis=0
    ).astype(F32)
    last = jnp.concatenate(
        [
            mix[w, half:fourth, 3 * block :]
            for w in range(wide)
        ],
        axis=1,
    ).astype(F32)
    lead = exact(features[...], smalls[:8]) + smalls[8:9]
    one = jnp.sin(lead)
    lead_two = exact(one, middle_filter) + smalls[9:10]
    two = jnp.sin(lead_two)
    filter_out[0] = one
    filter_out[1] = two
    filter_out[2] = jnp.cos(lead)
    filter_out[3] = jnp.cos(lead_two)
    fraction = features[:, 0:1]
    window = jnp.exp(-fraction * table[8:9])
    ahead = exact(two, last[:, :width]) * window
    behind = exact(two, last[:, width:]) * window
    kernel_out[:, :width] = ahead
    kernel_out[:, width:] = behind
    wave = waves[0].astype(F32) + waves[1].astype(F32)
    row = lax.broadcasted_iota(jnp.int32, (length, 1), 0)
    weight = jnp.where(row == 0, 0.5 / length, 1.0 / length)
    sums = exact(wave, ahead + behind)
    differences = exact(wave[length:], ahead - behind)
    real = sums[:length]
    spectrum_out[0] = real * weight
    spectrum_out[1] = jnp.where(row == 0, 0.0, differences) * weight
    spectrum_out[2] = jnp.where(row == 0, sums[length : length + 1], real) * weight

    if first_layer:
        hidden = jnp.where(marked[...] > 0.5, table[9:10], hidden_in[...].astype(F32))
    else:
        hidden = hidden_in[...]
    hidden_out[...] = hidden
    unit, unused = normalised(hidden)
    normed = (unit * table[0:1] + table[2:3]).astype(BF16)
    normed_out[...] = normed
    for u in range(2):
        middle, blocks = monarch_small(
            normed, lambda b: factor(mix, 0, u, b), lambda b: factor(mix, 0, 2 + u, b)
        )
        for b in range(BLOCKS):
            middle_out[u, b] = middle[b]
        path = jnp.concatenate(blocks, axis=1)
        saved_out[u] = (path * live[...] if u == 0 else path).astype(BF16)
        if u == 0:
            value = path * live[...]
    gate = path
    for s in range(rows // length):
        inside = slice(s * length, (s + 1) * length)
        alive = live[inside]
        signal = value[inside]
        signal = alive * (
            table[4:5] * shifted(signal, 2) + table[5:6] * shifted(signal, 1) + table[6:7] * signal
        )
        product = multiplied(to_spectrum(waves, signal), spectrum_out, False)
        mixed = from_spectrum(waves, product) + table[7:8] * signal
        saved_out[2, inside] = mixed.astype(BF16)
        mixed_out[inside] = (mixed * gate[inside]).astype(BF16)
    middle, blocks = monarch_small(
        mixed_out[...], lambda b: factor(mix, half, 0, b), lambda b: factor(mix, half, 1, b)
    )
    for b in range(BLOCKS):
        middle_two_out[b] = middle[b]
    result[...] = hidden + jnp.concatenate(blocks, axis=1)


def mixer_backward_kernel(first_layer, *refs):
    (
        grad,
        hidden_in,
        marked,
        live,
        waves,
        features,
        mix,
        table,
        spectrum,
        kernel_in,
        filters,
        normed,
        middle,
        saved,
        mixed,
        middle_two,
        norm_two,
        down_grads,
    ) = refs[:18]
    result, grad_out = refs[18:20]
    mix_grad, sum_scratch, value_scratch, table_grad, sems = refs[20:]
    rows, width = hidden_in.shape
    block = width // BLOCKS
    half = block // 2
    length = waves.shape[2]
    wide = mix.shape[0]
    third = 2 * half
    fourth = third + length - half
    mix_grad[:, third:fourth] = jnp.zeros((wide, fourth - third, width), BF16)
    incoming = grad[...]
    low = incoming.astype(BF16)
    blocks = [columns(low, b, block) for b in range(BLOCKS)]
    outs, right_grads, left_grads = monarch_small_backward(
        mixed[...],
        [middle_two[b] for b in range(BLOCKS)],
        blocks,
        lambda b: factor(mix, half, 0, b),
        lambda b: factor(mix, half, 1, b),
    )
    for b in range(BLOCKS):
        store_factor(mix_grad, half, 0, b, right_grads[b])
        store_factor(mix_grad, half, 1, b, left_grads[b])
        store_factor(mix_grad, half, 2, b, down_grads[1, b])
        for index in range(4):
            w = 2 * b + index // 2
            for part in range(2):
                position = (index % 2) * 2 + part
                mix_grad[w, fourth : fourth + half, position * block : (position + 1) * block] = (
                    down_grads[2 + index, b, part * half : (part + 1) * half]
                )
    grad_mixed = jnp.concatenate(outs, axis=1)
    gate = saved[1].astype(F32)
    value_scratch[1] = grad_mixed * saved[2].astype(F32)
    grad_mixed = grad_mixed * gate
    table_grad[...] = jnp.zeros_like(table_grad)
    sum_scratch[...] = jnp.zeros_like(sum_scratch)
    for s in range(rows // length):
        inside = slice(s * length, (s + 1) * length)
        alive = live[inside]
        value = saved[0, inside].astype(F32)
        behind_two, behind_one = shifted(value, 2), shifted(value, 1)
        signal = alive * (
            table[4:5] * behind_two + table[5:6] * behind_one + table[6:7] * value
        )
        inner = grad_mixed[inside]
        table_grad[7:8] += jnp.sum(inner * signal, axis=0, keepdims=True)
        wave_signal = to_spectrum(waves, signal)
        wave_grad = to_spectrum(waves, inner)
        real, imaginary = wave_signal[:length], wave_signal[length:]
        grad_real, grad_imaginary = wave_grad[:length], wave_grad[length:]
        sum_scratch[0] += grad_real * real
        sum_scratch[1] += grad_imaginary * real - grad_real * imaginary
        sum_scratch[2] += grad_imaginary * imaginary
        grad_signal = from_spectrum(waves, multiplied(wave_grad, spectrum, True))
        grad_signal = alive * (grad_signal + table[7:8] * inner)
        table_grad[4:5] += jnp.sum(grad_signal * behind_two, axis=0, keepdims=True)
        table_grad[5:6] += jnp.sum(grad_signal * behind_one, axis=0, keepdims=True)
        table_grad[6:7] += jnp.sum(grad_signal * value, axis=0, keepdims=True)
        value_scratch[0, inside] = alive * (
            table[6:7] * grad_signal
            + table[5:6] * shifted(grad_signal, -1)
            + table[4:5] * shifted(grad_signal, -2)
        )
    row = lax.broadcasted_iota(jnp.int32, (length, 1), 0)
    weight = jnp.where(row == 0, 0.5 / length, 1.0 / length)
    wave = waves[0].astype(F32) + waves[1].astype(F32)
    real = sum_scratch[0] * weight
    other = sum_scratch[2] * weight
    turning = jnp.where(row == 0, 0.0, sum_scratch[1] * weight)
    total = jnp.where(row == 0, real, real + other)
    last_row = jnp.where(row == 0, other, 0.0)
    sums = exact(wave[:length], total, (0, 0)) + exact(wave[length:], last_row, (0, 0))
    differences = exact(wave[length:], turning, (0, 0))
    fraction = features[:, 0:1]
    window = jnp.exp(-fraction * table[8:9])
    count = float(rows // length)
    grad_ahead = (sums + differences + count * kernel_in[:, :width]) * window
    grad_behind = (sums - differences + count * kernel_in[:, width:]) * window
    one, two = filters[0], filters[1]
    middle_filter = jnp.concatenate(
        [mix[w, third : third + 16, 2 * block : 2 * block + length] for w in range(wide)], axis=0
    ).astype(F32)
    grad_two = None
    for w in range(wide):
        source = grad_ahead if w < wide // 2 else grad_behind
        piece = columns(source, w % (wide // 2), block)
        factor_out = mix[w, half:fourth, 3 * block :].astype(F32)
        term = exact(piece, factor_out, (1, 1))
        grad_two = term if grad_two is None else grad_two + term
        mix_grad[w, half:fourth, 3 * block :] = exact(two, piece, (0, 0)).astype(BF16)
    grad_two = grad_two * filters[3]
    grad_one = exact(grad_two, middle_filter, (1, 1)) * filters[2]
    filter_grad = exact(one, grad_two, (0, 0)).astype(BF16)
    smalls = jnp.concatenate(
        [
            exact(features[...], grad_one, (0, 0)),
            jnp.sum(grad_one, axis=0, keepdims=True),
            jnp.sum(grad_two, axis=0, keepdims=True),
            jnp.zeros((6, length), F32),
        ],
        axis=0,
    )
    step = length // wide
    for w in range(wide):
        mix_grad[w, third : third + 16, 2 * block : 2 * block + length] = filter_grad[
            w * step : (w + 1) * step
        ]
        mix_grad[w, third + 16 : third + 32, 2 * block : 2 * block + step] = columns(
            smalls, w, step
        ).astype(BF16)
    total_in = None
    for u in range(2):
        low = value_scratch[u].astype(BF16)
        outs, right_grads, left_grads = monarch_small_backward(
            normed[...],
            [middle[u, b] for b in range(BLOCKS)],
            [columns(low, b, block) for b in range(BLOCKS)],
            lambda b: factor(mix, 0, u, b),
            lambda b: factor(mix, 0, 2 + u, b),
        )
        for b in range(BLOCKS):
            store_factor(mix_grad, 0, u, b, right_grads[b])
            store_factor(mix_grad, 0, 2 + u, b, left_grads[b])
        joint = jnp.concatenate(outs, axis=1)
        total_in = joint if total_in is None else total_in + joint
    through, gain, bias = norm_backward(total_in, hidden_in[...], table[0:1])
    outgoing = incoming + through
    table_grad[0:1] = gain
    table_grad[1:2] = norm_two[0:1]
    table_grad[2:3] = bias
    table_grad[3:4] = norm_two[1:2]
    if first_layer:
        chosen = marked[...] > 0.5
        table_grad[9:10] = jnp.sum(jnp.where(chosen, outgoing, 0.0), axis=0, keepdims=True)
        outgoing = jnp.where(chosen, 0.0, outgoing)
    result[...] = outgoing
    for w in range(wide):
        mix_grad[w, third : third + 16, block : block + half] = columns(
            table_grad[...], w, half
        ).astype(BF16)
    writes = grad_copies(grad_out, sems, mix_spots(mix_grad))
    start_all(writes)
    wait_all(writes)


COSTS = {"mixer_forward": 17, "glu_forward": 20, "glu_backward": 38, "mixer_backward": 24}


def call(kernel, name, outs, operands, anywhere, any_outs, scratch):
    vmem = pl.BlockSpec(memory_space=pltpu.VMEM)
    any_space = pl.BlockSpec(memory_space=pl.ANY)
    return pl.pallas_call(
        kernel,
        out_shape=[jax.ShapeDtypeStruct(shape, dtype) for shape, dtype in outs],
        in_specs=[any_space if index in anywhere else vmem for index in range(len(operands))],
        out_specs=[any_space if index in any_outs else vmem for index in range(len(outs))],
        scratch_shapes=scratch,
        compiler_params=pltpu.CompilerParams(vmem_limit_bytes=VMEM_BYTES),
        cost_estimate=pl.CostEstimate(
            flops=COSTS[name] * 10**9, bytes_accessed=COSTS[name] * 10**6, transcendentals=0
        ),
        name=name,
    )(*operands)


def mixer_outs(rows, width, length, quarter):
    block = width // BLOCKS
    return [
        ((rows, width), F32),
        ((rows, width), F32),
        ((8, 4 * quarter, width), BF16),
        ((16, width), F32),
        ((3, length, width), F32),
        ((length, 2 * width), F32),
        ((4, length, length), F32),
        ((rows, width), BF16),
        ((2, BLOCKS, rows, block), BF16),
        ((3, rows, width), BF16),
        ((rows, width), BF16),
        ((BLOCKS, rows, block), BF16),
    ]


def glu_outs(rows, width):
    return [
        ((rows, width), F32),
        ((rows, width), BF16),
        ((2, BLOCKS, rows, width), BF16),
        ((2, BLOCKS, rows, width), BF16),
        ((BLOCKS, rows, width), BF16),
        ((BLOCKS, rows, width // BLOCKS), BF16),
    ]


def glu_forward(hidden, table, mix, pieces):
    rows, width = hidden.shape
    block = width // BLOCKS
    outs = glu_outs(rows, width)
    return call(
        glu_forward_kernel,
        "glu_forward",
        outs,
        (hidden, table, mix, pieces),
        (3,),
        (),
        [
            pltpu.VMEM((2, BLOCKS, width, width), BF16),
            pltpu.VMEM((2, width, width), BF16),
            pltpu.VMEM((BLOCKS, rows, block), F32),
            pltpu.SemaphoreType.DMA((64,)),
        ],
    )


def glu_backward(grad, hidden, table, mix, saved, pieces):
    rows, width = hidden.shape
    block = width // BLOCKS
    quarter = pieces.shape[4]
    outs = [
        ((rows, width), F32),
        ((8, width), F32),
        ((6, BLOCKS, block, block), BF16),
        ((2, 2, 2, 4, quarter, width), BF16),
    ]
    return call(
        glu_backward_kernel,
        "glu_backward",
        outs,
        (grad, hidden, table, mix) + tuple(saved) + (pieces,),
        (9,),
        (3,),
        [
            pltpu.VMEM((2, BLOCKS, width, width), BF16),
            pltpu.VMEM((2, width, width), BF16),
            pltpu.VMEM((BLOCKS, rows, block), BF16),
            pltpu.VMEM((2, BLOCKS, rows, width), BF16),
            pltpu.SemaphoreType.DMA((64,)),
            pltpu.SemaphoreType.DMA((64,)),
        ],
    )


def mixer_backward(first_layer, grad, marked, live, waves, features, saved, norm_two, down_grads):
    hidden, mix, table, spectrum, kernel, filters = saved[:6]
    rows, width = hidden.shape
    length = waves.shape[2]
    outs = [((rows, width), F32), ((2, 2, 2, 4, mix.shape[1] // 4, width), BF16)]
    operands = (
        (grad, hidden, marked, live, waves, features)
        + tuple(saved[1:])
        + (norm_two, down_grads)
    )
    return call(
        partial(mixer_backward_kernel, first_layer),
        "mixer_backward",
        outs,
        operands,
        (),
        (1,),
        [
            pltpu.VMEM(mix.shape, BF16),
            pltpu.VMEM((3, length, width), F32),
            pltpu.VMEM((2, rows, width), F32),
            pltpu.VMEM((16, width), F32),
            pltpu.SemaphoreType.DMA((32,)),
        ],
    )
PEERS = ((1, 0, 0, 0), (2, 0, 0, 0), (3, 0, 0, 0), (0, 1, 0, 0), (0, 0, 1, 0), (0, 0, 0, 1))
ALONG_X, ALONG_Y, ACROSS = PEERS[3], PEERS[4], PEERS[5]


def peer(distance, dx, dy, dc):
    z, x, y, c = place()
    return (2 * relative(z, distance) + flip(x, dx), 2 * flip(y, dy) + flip(c, dc))


def greet():
    barrier = pltpu.get_barrier_semaphore()
    for target in PEERS:
        pl.semaphore_signal(
            barrier, inc=1, device_id=peer(*target), device_id_type=pl.DeviceIdType.MESH
        )
    pl.semaphore_wait(barrier, len(PEERS))


class Mail:
    def __init__(self, sent, received):
        self.sent, self.received, self.copies = sent, received, []

    def send(self, source, target, to):
        index = len(self.copies)
        copy = pltpu.make_async_remote_copy(
            src_ref=source,
            dst_ref=target,
            send_sem=self.sent.at[index],
            recv_sem=self.received.at[index],
            device_id=peer(*to),
            device_id_type=pl.DeviceIdType.MESH,
        )
        copy.start()
        self.copies.append(copy)
        return copy

    def finish(self):
        for copy in self.copies:
            copy.wait_send()


GATHER_COPIES = 12


def gather_steps(mail, own, pieces, rows):
    view = lambda core, dx, dy, first, count: pieces.at[core, dx, dy, pl.ds(first, count), rows]
    along_z = [
        mail.send(own, pieces.at[0, 0, 0, distance, rows], PEERS[distance - 1])
        for distance in (1, 2, 3)
    ]
    yield
    for copy in along_z:
        copy.wait_recv()
    along_x = mail.send(view(0, 0, 0, 0, 4), view(0, 1, 0, 0, 4), ALONG_X)
    along_y = mail.send(view(0, 0, 0, 0, 4), view(0, 0, 1, 0, 4), ALONG_Y)
    across = [mail.send(view(0, 0, 0, 0, 4), view(1, 0, 0, 0, 4), ACROSS)]
    yield
    along_y.wait_recv()
    low = mail.send(view(0, 0, 1, 0, 2), view(0, 1, 1, 0, 2), ALONG_X)
    across.append(mail.send(view(0, 0, 1, 0, 4), view(1, 0, 1, 0, 4), ACROSS))
    along_x.wait_recv()
    high = mail.send(view(0, 1, 0, 2, 2), view(0, 1, 1, 2, 2), ALONG_Y)
    across.append(mail.send(view(0, 1, 0, 0, 4), view(1, 1, 0, 0, 4), ACROSS))
    yield
    low.wait_recv()
    across.append(mail.send(view(0, 1, 1, 0, 2), view(1, 1, 1, 0, 2), ACROSS))
    high.wait_recv()
    across.append(mail.send(view(0, 1, 1, 2, 2), view(1, 1, 1, 2, 2), ACROSS))
    yield
    for copy in across:
        copy.wait_recv()
    yield


def pipeline(starts, between):
    running = []
    waiting = list(starts)
    number = 0
    while waiting or running:
        if waiting:
            running.append(waiting.pop(0)())
        for chunk in reversed(list(running)):
            try:
                next(chunk)
            except StopIteration:
                running.remove(chunk)
        if number in between:
            between[number]()
        number += 1


def save_all(sources, targets, sems, first):
    copies = [
        pltpu.make_async_copy(source, target, sems.at[first + index])
        for index, (source, target) in enumerate(zip(sources, targets))
    ]
    start_all(copies)
    return copies


MIXER_OUTS, GLU_OUTS = 12, 6


def forward_kernel(counts, *refs):
    groups = len(counts)
    owns, refs = refs[:groups], refs[groups:]
    hidden_in, marked, live, waves, features = refs[:5]
    pieces, refs = refs[5 : 5 + groups], refs[5 + groups :]
    first_outs, refs = refs[:MIXER_OUTS], refs[MIXER_OUTS:]
    glu_outs, refs = refs[:GLU_OUTS], refs[GLU_OUTS:]
    second_outs, refs = refs[:MIXER_OUTS], refs[MIXER_OUTS:]
    mixer, refs = refs[:MIXER_OUTS], refs[MIXER_OUTS:]
    glu, refs = refs[:GLU_OUTS], refs[GLU_OUTS:]
    staged, refs = refs[:groups], refs[groups:]
    left, right, parts, sent, received, local, loads = refs
    mail = Mail(sent, received)
    copies = [
        pltpu.make_async_copy(own, stage, local.at[index])
        for index, (own, stage) in enumerate(zip(owns, staged))
    ]
    start_all(copies)
    greet()
    starts = []
    for index, count in enumerate(counts):
        size = owns[index].shape[0] // count
        for part in range(count):
            rows = pl.ds(part * size, size)
            starts.append(
                partial(gather_steps, mail, owns[index].at[rows], pieces[index], rows)
            )
    wait_all(copies)
    own_copies = save_all(
        staged, [array.at[0, 0, 0, 0] for array in pieces], local, groups
    )
    saves = []

    def store_own():
        wait_all(own_copies)

    def first_mixer():
        mixer_forward_kernel(
            True, hidden_in, marked, live, waves, features, pieces[0], *mixer, loads
        )
        saves.extend(save_all(mixer, first_outs, local, 2 * groups))

    def first_glu():
        glu_forward_kernel(
            mixer[0], mixer[3], mixer[2], pieces[1], *glu, left, right, parts, loads
        )
        saves.extend(save_all(glu, glu_outs, local, 2 * groups + MIXER_OUTS))

    def second_mixer():
        wait_all(saves[:MIXER_OUTS])
        mixer_forward_kernel(
            False, glu[0], marked, live, waves, features, pieces[2], *mixer, loads
        )
        saves.extend(save_all(mixer, second_outs, local, 2 * groups + MIXER_OUTS + GLU_OUTS))

    ready = [sum(counts[: index + 1]) + 3 for index in range(3)]
    pipeline(
        starts, {0: store_own, ready[0]: first_mixer, ready[1]: first_glu, ready[2]: second_mixer}
    )
    wait_all(saves[MIXER_OUTS:])
    mail.finish()


def forward(quarters, counts, hidden, marked, live, waves, features, number):
    rows, width = hidden.shape
    groups = len(counts)
    anywhere = pl.BlockSpec(memory_space=pl.ANY)
    vmem = pl.BlockSpec(memory_space=pltpu.VMEM)
    total = GATHER_COPIES * sum(counts)
    mixer = mixer_outs(rows, width, waves.shape[2], quarters[0].shape[0])
    glu = glu_outs(rows, width)
    outs = [((2, 2, 2, 4) + quarter.shape, BF16) for quarter in quarters] + mixer + glu + mixer
    block = width // BLOCKS
    result = pl.pallas_call(
        partial(forward_kernel, counts),
        out_shape=[jax.ShapeDtypeStruct(shape, dtype) for shape, dtype in outs],
        in_specs=[anywhere] * groups + [vmem] * 5,
        out_specs=[anywhere] * len(outs),
        scratch_shapes=[pltpu.VMEM(shape, dtype) for shape, dtype in mixer + glu]
        + [pltpu.VMEM(quarter.shape, BF16) for quarter in quarters]
        + [
            pltpu.VMEM((2, BLOCKS, width, width), BF16),
            pltpu.VMEM((2, width, width), BF16),
            pltpu.VMEM((BLOCKS, rows, block), F32),
            pltpu.SemaphoreType.DMA((total,)),
            pltpu.SemaphoreType.DMA((total,)),
            pltpu.SemaphoreType.DMA((2 * groups + 2 * MIXER_OUTS + GLU_OUTS,)),
            pltpu.SemaphoreType.DMA((64,)),
        ],
        compiler_params=pltpu.CompilerParams(
            collective_id=number, has_side_effects=True, vmem_limit_bytes=VMEM_BYTES
        ),
        name="forward",
    )(*quarters, hidden, marked, live, waves, features)
    pieces, result = result[:groups], result[groups:]
    return (
        pieces,
        result[:MIXER_OUTS],
        result[MIXER_OUTS : MIXER_OUTS + GLU_OUTS],
        result[MIXER_OUTS + GLU_OUTS :],
    )


SCATTER_COPIES = 11


def scatter_steps(mail, local, grads, rows, result, spots, buffers):
    first, one, two_x, two_y, three, four, own, last = buffers
    x_core = mail.send(grads.at[1, :, :, :, rows], one, ACROSS)
    load = pltpu.make_async_copy(grads.at[0, :, :, :, rows], first, local.at[0])
    load.start()
    yield
    load.wait()
    x_core.wait_recv()
    for dx in range(2):
        for dy in range(2):
            first[dx, dy] += one[dx, dy]
    low = mail.send(first.at[1, :, pl.ds(0, 2)], two_x, ALONG_X)
    high = mail.send(first.at[:, 1, pl.ds(2, 2)], two_y, ALONG_Y)
    yield
    low.wait_recv()
    for dy in (1, 0):
        two_x[dy] += first[0, dy, 0:2]
        if dy == 1:
            low = mail.send(two_x.at[1], three.at[pl.ds(0, 2)], ALONG_Y)
    high.wait_recv()
    for dx in (1, 0):
        two_y[dx] += first[dx, 0, 2:4]
        if dx == 1:
            high = mail.send(two_y.at[1], three.at[pl.ds(2, 2)], ALONG_X)
    yield
    low.wait_recv()
    three[0:2] += two_x[0]
    along_z = [mail.send(three.at[1], four.at[0], PEERS[0])]
    high.wait_recv()
    three[2:4] += two_y[0]
    along_z += [mail.send(three.at[d], four.at[d - 1], PEERS[d - 1]) for d in (2, 3)]
    yield
    total = three[0].astype(F32)
    for index, copy in enumerate(along_z):
        copy.wait_recv()
        total = total + four[index].astype(F32)
    own[...] = total.astype(BF16)
    mine, theirs = spots
    across = [mail.send(own, result.at[mine, rows], ACROSS)]
    along_y = mail.send(own, last, ALONG_Y)
    keep = pltpu.make_async_copy(own, result.at[mine, rows], local.at[1])
    keep.start()
    yield
    along_y.wait_recv()
    across.append(mail.send(last, result.at[theirs, rows], ACROSS))
    keep_too = pltpu.make_async_copy(last, result.at[theirs, rows], local.at[2])
    keep_too.start()
    yield
    for copy in across:
        copy.wait_recv()
    keep.wait()
    keep_too.wait()
    yield


def scatter_buffers(size, width):
    return [
        pltpu.VMEM((2, 2, 4, size, width), BF16),
        pltpu.VMEM((2, 2, 4, size, width), BF16),
        pltpu.VMEM((2, 2, size, width), BF16),
        pltpu.VMEM((2, 2, size, width), BF16),
        pltpu.VMEM((4, size, width), BF16),
        pltpu.VMEM((3, size, width), BF16),
        pltpu.VMEM((size, width), BF16),
        pltpu.VMEM((size, width), BF16),
    ]


def scatter_kernel(counts, *refs):
    groups = len(counts)
    chunks = sum(counts)
    grads, results = refs[:groups], refs[groups : 2 * groups]
    sent, received, local = refs[2 * groups : 2 * groups + 3]
    buffers = refs[2 * groups + 3 :]
    mail = Mail(sent, received)
    unused, unused, y, c = place()
    spots = (2 * y + c, 2 * (1 - y) + c)
    greet()
    starts = []
    for index, count in enumerate(counts):
        size = results[index].shape[1] // count
        for part in range(count):
            number = len(starts)
            starts.append(
                partial(
                    scatter_steps,
                    mail,
                    local.at[number],
                    grads[index],
                    pl.ds(part * size, size),
                    results[index],
                    spots,
                    buffers[8 * number : 8 * number + 8],
                )
            )
    pipeline(starts, {})
    mail.finish()


def scatter_all(grads, counts, number):
    anywhere = pl.BlockSpec(memory_space=pl.ANY)
    chunks = sum(counts)
    size, width = grads[0].shape[4] // counts[0], grads[0].shape[5]
    buffers = []
    for index, count in enumerate(counts):
        for part in range(count):
            buffers += scatter_buffers(grads[index].shape[4] // count, width)
    total = SCATTER_COPIES * chunks
    return pl.pallas_call(
        partial(scatter_kernel, counts),
        out_shape=[jax.ShapeDtypeStruct((4,) + array.shape[4:], BF16) for array in grads],
        in_specs=[anywhere] * len(grads),
        out_specs=[anywhere] * len(grads),
        scratch_shapes=[
            pltpu.SemaphoreType.DMA((total,)),
            pltpu.SemaphoreType.DMA((total,)),
            pltpu.SemaphoreType.DMA((chunks, 3)),
        ]
        + buffers,
        compiler_params=pltpu.CompilerParams(
            collective_id=number, has_side_effects=True, vmem_limit_bytes=VMEM_BYTES
        ),
        name="scatter",
    )(*grads)


def mix_pack(local, mask_vector):
    (
        norm_gain,
        norm_bias,
        in_right,
        in_left,
        conv_taps,
        skip_bias,
        filter_in,
        filter_in_bias,
        filter_mid,
        filter_mid_bias,
        filter_out,
        decay_rates,
        out_right,
        out_left,
        unused_right,
        unused_left,
        down_right,
        down_left,
    ) = local
    rows, block = in_right.shape[1:]
    step, order = filter_mid.shape
    features = filter_in.shape[0]
    zeros = lambda height, width: jnp.zeros((height, width), BF16)
    last = [] if mask_vector is None else [mask_vector[None]]
    table = jnp.concatenate(
        [norm_gain, norm_bias, conv_taps, skip_bias[None], decay_rates[None]] + last, axis=0
    )
    table = jnp.pad(table, ((0, 16 - table.shape[0]), (0, 0)))
    smalls = jnp.concatenate(
        [filter_in, zeros(8 - features, step), filter_in_bias[None], filter_mid_bias[None], zeros(6, step)],
        axis=0,
    )
    tail = filter_out[rows:]
    down = down_right.reshape(4, rows, block)
    return jnp.concatenate(
        [
            jnp.concatenate([in_right[0], in_right[1], in_left[0], in_left[1]], axis=1),
            jnp.concatenate([out_right, out_left, down_left, filter_out[:rows]], axis=1),
            jnp.concatenate(
                [
                    zeros(16, block),
                    table,
                    zeros(16, block - rows),
                    filter_mid,
                    zeros(16, block - order),
                    tail[:16],
                ],
                axis=1,
            ),
            jnp.concatenate(
                [zeros(16, 2 * block), smalls, zeros(16, block - step), tail[16:]], axis=1
            ),
            jnp.concatenate([down[0], down[1], down[2], down[3]], axis=1),
        ],
        axis=0,
    )


def mix_unpack(pack, shards):
    rows, block = shards[2].shape[2:]
    order = shards[10].shape[1]
    step = shards[9].shape[1]
    features = shards[6].shape[1]
    third, fourth = 2 * rows, rows + order
    cut = lambda low, high, k: pack[low:high, k * block : (k + 1) * block]
    table = pack[third : third + 16, block : block + rows]
    smalls = pack[third + 16 : third + 32, 2 * block : 2 * block + step]
    result = {
        0: table[0:2],
        1: table[2:4],
        2: jnp.stack([cut(0, rows, 0), cut(0, rows, 1)]),
        3: jnp.stack([cut(0, rows, 2), cut(0, rows, 3)]),
        4: table[4:7],
        5: table[7],
        6: smalls[:features],
        7: smalls[8],
        8: pack[third : third + step, 2 * block : 2 * block + order],
        9: smalls[9],
        10: cut(rows, fourth, 3),
        12: cut(rows, third, 0),
        13: cut(rows, third, 1),
        16: jnp.concatenate([cut(fourth, fourth + rows, k) for k in range(4)], axis=0),
        17: cut(rows, third, 2),
    }
    return result, table[9]


def layer_quarters(local, mask_vector):
    unused, unused, y, c = place()
    mix = mix_pack(local, mask_vector)
    rows = mix.shape[0] // 4
    glu = []
    for array in (local[15], local[14]):
        size = array.shape[1] // 2
        picked = lax.dynamic_index_in_dim(array, y, 0, keepdims=False)
        glu.append(lax.dynamic_slice_in_dim(picked, c * size, size, 0))
    return (
        lax.dynamic_slice_in_dim(mix, (2 * y + c) * rows, rows, 0),
        jnp.concatenate(glu, axis=0),
    )


GRADS = (0, 1, 2, 3, 4, 5, 6, 7, 8, 9, 10, 12, 13, 14, 15, 16, 17)
SHARD_AXIS = (1, 1, 1, 1, 1, 0, 1, 0, 0, 0, 1, 0, 0, 0, 1, 1, 0, 0)


def gather_plain(shards, layer_index):
    return tuple(
        lax.all_gather(shards[index][layer_index], "wide", axis=SHARD_AXIS[index], tiled=True)
        for index in range(18)
    )


def scatter_plain(grads, mask_term):
    terms = list(grads) + ([] if mask_term is None else [mask_term])
    axes = [SHARD_AXIS[index] for index in GRADS] + [0]
    return narrow_total(
        [
            lax.psum_scatter(term, "wide", scatter_dimension=axis, tiled=True)
            for term, axis in zip(terms, axes)
        ]
    )


def wave_table(length):
    frequency = np.arange(length)[:, None]
    places = np.arange(length)[None, :]
    angles = (frequency * places % (2 * length)) * (math.pi / length)
    turned = -np.sin(angles)
    turned[0] = np.where(np.arange(length) % 2 == 0, 1.0, -1.0)
    table = jnp.asarray(np.concatenate([np.cos(angles), turned]), F32)
    high = table.astype(BF16)
    return jnp.stack([high, (table - high.astype(F32)).astype(BF16)])


def staged_body(shards, mask_vector, hidden_in, cotangent, live, marked, mesh_shape):
    rows = hidden_in.shape[0]
    length = live.shape[1]
    live = live.reshape(rows, 1)
    marked = marked.astype(F32)
    waves = wave_table(length)
    features = jnp.pad(position_features(length), ((0, 0), (0, 8 - EMB)))
    quarters = []
    for layer_index in range(LAYERS):
        local = tuple(member[layer_index] for member in shards)
        quarters += layer_quarters(local, mask_vector if layer_index == 0 else None)
    pieces, mixed, second, mixed_two = forward(
        quarters, (1, 3) * LAYERS, hidden_in, marked, live, waves, features, 1
    )
    kept = [
        (mixed, second),
        (mixed_two, glu_forward(mixed_two[0], mixed_two[3], mixed_two[2], pieces[3])),
    ]
    hidden = kept[1][1][0]
    output = hidden.astype(BF16)
    grad = cotangent.astype(F32)
    layer_grads = [None] * LAYERS
    totals = [None] * LAYERS
    for layer_index in reversed(range(LAYERS)):
        mixed, second = kept[layer_index]
        grad, norm_two, down_grads, glu_grads = glu_backward(
            grad, mixed[0], mixed[3], mixed[2], second[1:], pieces[2 * layer_index + 1]
        )
        grad, mix_grads = mixer_backward(
            layer_index == 0,
            grad,
            marked,
            live,
            waves,
            features,
            mixed[1:],
            norm_two,
            down_grads,
        )
        totals[layer_index] = (mix_grads, glu_grads)
    sums = scatter_all(totals[0] + totals[1], (1, 3) * LAYERS, 2)
    for layer_index in reversed(range(LAYERS)):
        mix, glu = (array.astype(F32) for array in sums[2 * layer_index : 2 * layer_index + 2])
        found, mask_grad = mix_unpack(mix.reshape(-1, mix.shape[-1]), shards)
        tall = shards[15].shape[2] // 2
        found[15] = glu[:, :tall].reshape(2, 2 * tall, -1)
        found[14] = glu[:, tall:].reshape(2, shards[14].shape[2], -1)
        layer_grads[layer_index] = [found[index] for index in GRADS]
    return output, grad, mask_grad, layer_grads


def is_staged(shards, mesh_shape):
    short, block = shards[2].shape[2:]
    order, outs = shards[10].shape[1:]
    return (
        tuple(mesh_shape) == (8, 4)
        and short == 96
        and block == 192
        and order == 128
        and outs == block
        and shards[14].shape[2:] == (short, 8 * short)
        and shards[15].shape[2:] == (4 * short, 8 * short)
    )


def narrow_total(parts):
    flattened = jnp.concatenate([member.reshape(-1) for member in parts])
    summed = lax.psum(flattened.astype(jnp.bfloat16), "narrow").astype(jnp.float32)
    result = []
    offset = 0
    for member in parts:
        result.append(summed[offset : offset + member.size].reshape(member.shape))
        offset = offset + member.size
    return result


def plain_body(shards, mask_vector, hidden_in, cotangent, live_mask, marked):
    seq_count = live_mask.shape[0]
    mask_full = lax.all_gather(mask_vector, "wide", axis=0, tiled=True)
    weights = [gather_plain(shards, layer_index) for layer_index in range(LAYERS)]
    hidden = jnp.where(
        marked, mask_full.astype(jnp.float32)[None, :], hidden_in.astype(jnp.float32)
    )
    saved_layers = []
    for layer_index in range(LAYERS):
        hidden, saved = forward_layer(hidden, weights[layer_index], live_mask)
        saved_layers.append(saved)
    output = hidden.astype(jnp.bfloat16)
    share = 0.5 * seq_count
    grad_hidden = cotangent.astype(jnp.float32)
    layer_grads = [None] * LAYERS
    mask_grad = None
    for layer_index in reversed(range(LAYERS)):
        grad_hidden, grads = backward_layer(
            grad_hidden, weights[layer_index], saved_layers[layer_index], live_mask, share
        )
        if layer_index > 0:
            layer_grads[layer_index] = scatter_plain(grads, None)
        else:
            mask_term = jnp.sum(jnp.where(marked, grad_hidden, 0.0), axis=0)
            reduced = scatter_plain(grads, mask_term)
            layer_grads[0] = reduced[:-1]
            mask_grad = reduced[-1]
    grad_input = jnp.where(marked, 0.0, grad_hidden)
    return output, grad_input, mask_grad, layer_grads


def body(
    mesh_shape,
    hidden_in,
    seq_lengths,
    mask_positions,
    mask_vector,
    cotangent,
    norm_gain,
    norm_bias,
    in_right,
    in_left,
    conv_taps,
    skip_bias,
    filter_in,
    filter_in_bias,
    filter_mid,
    filter_mid_bias,
    filter_out,
    decay_rates,
    out_right,
    out_left,
    glu_right,
    glu_left,
    down_right,
    down_left,
):
    row_count = hidden_in.shape[0]
    seq_count = seq_lengths.shape[0]
    length = row_count // seq_count
    places = jnp.arange(length, dtype=jnp.int32)
    live_mask = (places[None, :] < seq_lengths[:, None]).astype(jnp.float32)[:, :, None]
    marked = jnp.any(mask_positions[:, :, None] == places[None, None, :], axis=1).reshape(
        row_count, 1
    )
    shards = (
        norm_gain,
        norm_bias,
        in_right,
        in_left,
        conv_taps,
        skip_bias,
        filter_in,
        filter_in_bias,
        filter_mid,
        filter_mid_bias,
        filter_out,
        decay_rates,
        out_right,
        out_left,
        glu_right,
        glu_left,
        down_right,
        down_left,
    )
    if is_staged(shards, mesh_shape):
        output, grad_input, mask_grad, layer_grads = staged_body(
            shards, mask_vector, hidden_in, cotangent, live_mask, marked, mesh_shape
        )
    else:
        output, grad_input, mask_grad, layer_grads = plain_body(
            shards, mask_vector, hidden_in, cotangent, live_mask, marked
        )
    final_grads = [
        jnp.stack([layer_grads[position][member_index] for position in range(LAYERS)])
        for member_index in range(17)
    ]
    return (output, grad_input, mask_grad) + tuple(final_grads)


def solution(mesh):
    placed = (
        P(("wide", "narrow"), None),
        P(("wide", "narrow")),
        P(("wide", "narrow"), None),
        P("wide"),
        P(("wide", "narrow"), None),
        P(None, None, "wide"),
        P(None, None, "wide"),
        P(None, None, "wide", None),
        P(None, None, "wide", None),
        P(None, None, "wide"),
        P(None, "wide"),
        P(None, None, "wide"),
        P(None, "wide"),
        P(None, "wide", None),
        P(None, "wide"),
        P(None, None, "wide"),
        P(None, "wide"),
        P(None, "wide", None),
        P(None, "wide", None),
        P(None, None, "wide", None),
        P(None, None, "wide", None),
        P(None, "wide", None),
        P(None, "wide", None),
    )
    return jax.shard_map(
        partial(body, (mesh.shape["wide"], mesh.shape["narrow"])),
        mesh=mesh,
        in_specs=placed,
        out_specs=(
            P(("wide", "narrow"), None),
            P(("wide", "narrow"), None),
            P("wide"),
            P(None, None, "wide"),
            P(None, None, "wide"),
            P(None, None, "wide", None),
            P(None, None, "wide", None),
            P(None, None, "wide"),
            P(None, "wide"),
            P(None, None, "wide"),
            P(None, "wide"),
            P(None, "wide", None),
            P(None, "wide"),
            P(None, None, "wide"),
            P(None, "wide", None),
            P(None, "wide", None),
            P(None, None, "wide", None),
            P(None, None, "wide", None),
            P(None, "wide", None),
            P(None, "wide", None),
        ),
        check_vma=False,
    )
```

```python
from functools import partial
import math

import jax
import jax.numpy as jnp
import numpy as np
from jax import lax
from jax.experimental import pallas as pl
from jax.experimental.pallas import tpu as pltpu
from jax.sharding import PartitionSpec as P

BLOCKS = 4
EMB = 5
LAYERS = 2


EPSILON = 1e-05
highest_precision = lax.Precision.HIGHEST


def permute(values):
    array_shape = values.shape
    blocks = array_shape[-2]
    split_view = values.reshape(array_shape[:-1] + (blocks, array_shape[-1] // blocks))
    return jnp.swapaxes(split_view, -3, -2).reshape(array_shape)


def monarch_forward(inputs, right_factor, left_factor):
    row_count = inputs.shape[0]
    right_blocks = right_factor.reshape(BLOCKS, -1, right_factor.shape[-1])
    left_blocks = left_factor.reshape(BLOCKS, -1, left_factor.shape[-1])
    middle = jnp.einsum(
        "rbi,bio->rbo",
        inputs.reshape(row_count, BLOCKS, -1),
        right_blocks,
        preferred_element_type=jnp.float32,
    )
    middle = permute(middle).astype(jnp.bfloat16)
    output = jnp.einsum("rbi,bio->rbo", middle, left_blocks, preferred_element_type=jnp.float32)
    return (middle, output.reshape(row_count, -1))


def monarch_backward(inputs, middle, right_factor, left_factor, grad_output):
    row_count = inputs.shape[0]
    right_blocks = right_factor.reshape(BLOCKS, -1, right_factor.shape[-1])
    left_blocks = left_factor.reshape(BLOCKS, -1, left_factor.shape[-1])
    grad_low = grad_output.astype(jnp.bfloat16).reshape(row_count, BLOCKS, -1)
    grad_left = jnp.einsum("rbi,rbo->bio", middle, grad_low, preferred_element_type=jnp.float32)
    grad_middle = jnp.einsum(
        "rbo,bio->rbi", grad_low, left_blocks, preferred_element_type=jnp.float32
    )
    grad_middle = permute(grad_middle).astype(jnp.bfloat16)
    input_blocks = inputs.reshape(row_count, BLOCKS, -1)
    grad_right = jnp.einsum(
        "rbi,rbo->bio", input_blocks, grad_middle, preferred_element_type=jnp.float32
    )
    grad_inputs = jnp.einsum(
        "rbo,bio->rbi", grad_middle, right_blocks, preferred_element_type=jnp.float32
    )
    return (
        grad_inputs.reshape(row_count, -1),
        grad_right.reshape(right_factor.shape),
        grad_left.reshape(left_factor.shape),
    )


def layer_norm(values, norm_gain, norm_bias):
    average = jnp.mean(values, axis=-1, keepdims=True)
    centred = values - average
    variance = jnp.mean(centred * centred, axis=-1, keepdims=True)
    return centred * lax.rsqrt(variance + EPSILON) * norm_gain + norm_bias


def position_features(length):
    positions = jnp.arange(length, dtype=jnp.float32)
    fraction = positions / length
    features = [fraction]
    for band_index in range(1, (EMB - 1) // 2 + 1):
        features.append(jnp.cos(2.0 * math.pi * band_index * fraction))
        features.append(jnp.sin(2.0 * math.pi * band_index * fraction))
    return jnp.stack(features, axis=1)


def make_filter(
    filter_in, filter_in_bias, filter_mid, filter_mid_bias, filter_out, decay_rates, length
):
    embedding = position_features(length)
    first_hidden = jnp.sin(
        jnp.dot(embedding, filter_in, precision=highest_precision) + filter_in_bias
    )
    second = jnp.sin(
        jnp.dot(first_hidden, filter_mid, precision=highest_precision) + filter_mid_bias
    )
    kernel = jnp.dot(second, filter_out, precision=highest_precision)
    fraction = jnp.arange(length, dtype=jnp.float32)[:, None] / length
    both_rates = jnp.concatenate([decay_rates, decay_rates])
    return kernel * jnp.exp(-fraction * both_rates[None, :])


def short_convolution(signal_rows, conv_taps):
    padded = jnp.pad(signal_rows, ((0, 0), (2, 0), (0, 0)))
    return (
        conv_taps[0] * padded[:, :-2]
        + conv_taps[1] * padded[:, 1:-1]
        + conv_taps[2] * padded[:, 2:]
    )


def spectral_tables(length, span):
    padded_length = 2 * length
    frequency = jnp.arange(length + 1, dtype=jnp.int32)
    places = jnp.arange(span, dtype=jnp.int32)
    phase_index = frequency[:, None] * places[None, :] % padded_length
    angles = phase_index.astype(jnp.float32) * (2.0 * math.pi / padded_length)
    ends = (frequency == 0) | (frequency == length)
    weights = jnp.where(ends, 1.0, 2.0).astype(jnp.float32) / padded_length
    return (jnp.cos(angles), jnp.sin(angles), weights)


def circular_kernel(kernel):
    width = kernel.shape[1] // 2
    forward_part = kernel[:, :width]
    reverse_part = kernel[:, width:]
    first_row = forward_part[:1] + reverse_part[:1]
    spacer = jnp.zeros((1, width), jnp.float32)
    return jnp.concatenate(
        [first_row, forward_part[1:], spacer, jnp.flip(reverse_part[1:], axis=0)], axis=0
    )


def long_convolution(signal_rows, kernel):
    length = signal_rows.shape[1]
    cosine_lookup, sine_lookup, weights = spectral_tables(length, length)
    kernel_cosine, kernel_sine, unused = spectral_tables(length, 2 * length)
    circular = circular_kernel(kernel)
    real_signal = jnp.einsum("ik,hkm->him", cosine_lookup, signal_rows, precision=highest_precision)
    imaginary_signal = -jnp.einsum(
        "ik,hkm->him", sine_lookup, signal_rows, precision=highest_precision
    )
    kernel_real = jnp.dot(kernel_cosine, circular, precision=highest_precision)
    kernel_imaginary = -jnp.dot(kernel_sine, circular, precision=highest_precision)
    real_product = real_signal * kernel_real - imaginary_signal * kernel_imaginary
    imaginary_product = real_signal * kernel_imaginary + imaginary_signal * kernel_real
    inverse_cosine_table = cosine_lookup * weights[:, None]
    inverse_sine_table = sine_lookup * weights[:, None]
    return jnp.einsum(
        "hp,ihj->ipj", inverse_cosine_table, real_product, precision=highest_precision
    ) - jnp.einsum(
        "hp,ihj->ipj", inverse_sine_table, imaginary_product, precision=highest_precision
    )


def mixer_piece(
    value_path,
    gate_path,
    conv_taps,
    skip_bias,
    filter_in,
    filter_in_bias,
    filter_mid,
    filter_mid_bias,
    filter_out,
    decay_rates,
    live_mask,
    share,
):
    length = live_mask.shape[1]
    kernel = make_filter(
        filter_in, filter_in_bias, filter_mid, filter_mid_bias, filter_out, decay_rates, length
    )
    signal_rows = value_path.reshape(live_mask.shape[0], length, -1) * live_mask
    signal_rows = short_convolution(signal_rows, conv_taps) * live_mask
    mixed_signal = long_convolution(signal_rows, kernel) + signal_rows * skip_bias
    return (mixed_signal.reshape(value_path.shape) * gate_path, share * jnp.sum(kernel * kernel))


def glu_piece(upper_branch, gate_branch):
    return jax.nn.gelu(gate_branch, approximate=False) * upper_branch


def small_weights(layer_weights):
    return tuple(
        (layer_weights[position].astype(jnp.float32) for position in (4, 5, 6, 7, 8, 9, 10))
    )


def forward_layer(hidden, layer_weights, live_mask):
    (
        norm_gain,
        norm_bias,
        in_right,
        in_left,
        conv_taps,
        skip_bias,
        filter_in,
        filter_in_bias,
        filter_mid,
        filter_mid_bias,
        filter_out,
        decay_rates,
        out_right,
        out_left,
        glu_right,
        glu_left,
        down_right,
        down_left,
    ) = layer_weights
    gains = norm_gain.astype(jnp.float32)
    biases = norm_bias.astype(jnp.float32)
    small = small_weights(layer_weights)
    normed = layer_norm(hidden, gains[0], biases[0]).astype(jnp.bfloat16)
    middle_value, value_path = monarch_forward(normed, in_right[0], in_left[0])
    middle_gate, gate_path = monarch_forward(normed, in_right[1], in_left[1])
    mixed_signal, unused = mixer_piece(
        value_path,
        gate_path,
        small[0],
        small[1],
        small[2],
        small[3],
        small[4],
        small[5],
        small[6],
        decay_rates.astype(jnp.float32),
        live_mask,
        0.0,
    )
    mixed_signal = mixed_signal.astype(jnp.bfloat16)
    middle_out, branch = monarch_forward(mixed_signal, out_right, out_left)
    middle_hidden = hidden + branch
    normed_two = layer_norm(middle_hidden, gains[1], biases[1]).astype(jnp.bfloat16)
    middle_up, upper_branch = monarch_forward(normed_two, glu_right[0], glu_left[0])
    middle_glu, gate_branch = monarch_forward(normed_two, glu_right[1], glu_left[1])
    glu_hidden = glu_piece(upper_branch, gate_branch).astype(jnp.bfloat16)
    middle_down, branch_two = monarch_forward(glu_hidden, down_right, down_left)
    saved = (
        hidden,
        normed,
        middle_value,
        value_path,
        middle_gate,
        gate_path,
        mixed_signal,
        middle_out,
        middle_hidden,
        normed_two,
        middle_up,
        upper_branch,
        middle_glu,
        gate_branch,
        glu_hidden,
        middle_down,
    )
    return (middle_hidden + branch_two, saved)


def backward_layer(grad_hidden, layer_weights, saved, live_mask, share):
    (
        norm_gain,
        norm_bias,
        in_right,
        in_left,
        conv_taps,
        skip_bias,
        filter_in,
        filter_in_bias,
        filter_mid,
        filter_mid_bias,
        filter_out,
        decay_rates,
        out_right,
        out_left,
        glu_right,
        glu_left,
        down_right,
        down_left,
    ) = layer_weights
    (
        hidden,
        normed,
        middle_value,
        value_path,
        middle_gate,
        gate_path,
        mixed_signal,
        middle_out,
        middle_hidden,
        normed_two,
        middle_up,
        upper_branch,
        middle_glu,
        gate_branch,
        glu_hidden,
        middle_down,
    ) = saved
    gains = norm_gain.astype(jnp.float32)
    biases = norm_bias.astype(jnp.float32)
    small = small_weights(layer_weights)
    grad_glu, grad_down_right, grad_down_left = monarch_backward(
        glu_hidden, middle_down, down_right, down_left, grad_hidden
    )
    unused, glu_pull = jax.vjp(glu_piece, upper_branch, gate_branch)
    grad_upper, grad_gate = glu_pull(grad_glu)
    grad_normed_up, grad_right_up, grad_left_up = monarch_backward(
        normed_two, middle_up, glu_right[0], glu_left[0], grad_upper
    )
    grad_normed_gate, grad_right_gate, grad_left_gate = monarch_backward(
        normed_two, middle_glu, glu_right[1], glu_left[1], grad_gate
    )
    unused, norm_pull = jax.vjp(layer_norm, middle_hidden, gains[1], biases[1])
    grad_middle, grad_gain_two, grad_bias_two = norm_pull(grad_normed_up + grad_normed_gate)
    grad_middle = grad_middle + grad_hidden
    grad_mixed, grad_out_right, grad_out_left = monarch_backward(
        mixed_signal, middle_out, out_right, out_left, grad_middle
    )
    mixer_local = partial(
        mixer_piece, decay_rates=decay_rates.astype(jnp.float32), live_mask=live_mask, share=share
    )
    unused, mixer_pull = jax.vjp(
        mixer_local,
        value_path,
        gate_path,
        small[0],
        small[1],
        small[2],
        small[3],
        small[4],
        small[5],
        small[6],
    )
    mixer_grads = mixer_pull((grad_mixed, jnp.ones((), jnp.float32)))
    grad_normed_value, grad_right_value, grad_left_value = monarch_backward(
        normed, middle_value, in_right[0], in_left[0], mixer_grads[0]
    )
    grad_normed_path, grad_right_path, grad_left_path = monarch_backward(
        normed, middle_gate, in_right[1], in_left[1], mixer_grads[1]
    )
    unused, norm_pull_one = jax.vjp(layer_norm, hidden, gains[0], biases[0])
    grad_before, grad_gain_one, grad_bias_one = norm_pull_one(grad_normed_value + grad_normed_path)
    grads = (
        jnp.stack([grad_gain_one, grad_gain_two]),
        jnp.stack([grad_bias_one, grad_bias_two]),
        jnp.stack([grad_right_value, grad_right_path]),
        jnp.stack([grad_left_value, grad_left_path]),
        mixer_grads[2],
        mixer_grads[3],
        mixer_grads[4],
        mixer_grads[5],
        mixer_grads[6],
        mixer_grads[7],
        mixer_grads[8],
        grad_out_right,
        grad_out_left,
        jnp.stack([grad_right_up, grad_right_gate]),
        jnp.stack([grad_left_up, grad_left_gate]),
        grad_down_right,
        grad_down_left,
    )
    return (grad_before + grad_middle, grads)


F32 = jnp.float32
BF16 = jnp.bfloat16
VMEM_BYTES = 60 * 1024 * 1024


def dot(left, right):
    return jnp.dot(left, right, preferred_element_type=F32)


def dot_rows(left, right):
    return lax.dot_general(left, right, (((0,), (0,)), ((), ())), preferred_element_type=F32)


def dot_columns(left, right):
    return lax.dot_general(left, right, (((1,), (1,)), ((), ())), preferred_element_type=F32)


def exact(left, right, dims=(1, 0)):
    return lax.dot_general(
        left,
        right,
        (((dims[0],), (dims[1],)), ((), ())),
        precision=highest_precision,
        preferred_element_type=F32,
    )


def columns(values, index, width):
    return values[:, index * width : (index + 1) * width]


def shuffled(parts):
    chunk = parts[0].shape[1] // BLOCKS
    return [
        jnp.concatenate([columns(part, index, chunk) for part in parts], axis=1)
        for index in range(BLOCKS)
    ]


def normalised(values):
    average = jnp.mean(values, axis=-1, keepdims=True)
    centred = values - average
    variance = jnp.mean(centred * centred, axis=-1, keepdims=True)
    scale = lax.rsqrt(variance + EPSILON)
    return centred * scale, scale


def norm_backward(grad, hidden, gain):
    unit, scale = normalised(hidden)
    grad_gain = jnp.sum(grad * unit, axis=0, keepdims=True)
    grad_bias = jnp.sum(grad, axis=0, keepdims=True)
    scaled = grad * gain
    mean_one = jnp.mean(scaled, axis=-1, keepdims=True)
    mean_two = jnp.mean(scaled * unit, axis=-1, keepdims=True)
    return scale * (scaled - mean_one - unit * mean_two), grad_gain, grad_bias


def flip(bit, by):
    return 1 - bit if by else bit


def place():
    w = lax.axis_index("wide")
    n = lax.axis_index("narrow")
    return w // 2, w % 2, n // 2, n % 2


def relative(z, distance):
    high, low = z // 2, z % 2
    return 2 * flip(high, distance // 2) + flip(low, distance % 2)


def piece_copies(pieces, sems, targets_of):
    z, x, y, c = place()
    copies = []
    for core in range(2):
        for dx in range(2):
            for dy in range(2):
                for dz in range(4):
                    owner = (relative(z, dz), flip(x, dx), flip(y, dy), flip(c, core))
                    for row, target in targets_of(*owner):
                        view = pieces.at[core, dx, dy, dz, pl.ds(row, target.shape[0])]
                        copies.append(pltpu.make_async_copy(view, target, sems.at[len(copies)]))
    return copies


def grad_copies(result, sems, sources_of):
    z, x, y, c = place()
    copies = []
    for core in range(2):
        for dx in range(2):
            for dy in range(2):
                for dz in range(4):
                    owner = (relative(z, dz), flip(x, dx), flip(y, dy), flip(c, core))
                    for row, source in sources_of(*owner):
                        view = result.at[core, dx, dy, dz, pl.ds(row, source.shape[0])]
                        copies.append(pltpu.make_async_copy(source, view, sems.at[len(copies)]))
    return copies


def start_all(copies):
    for copy in copies:
        copy.start()


def wait_all(copies):
    for copy in copies:
        copy.wait()


def glu_spots(left, right):
    def spots(z, x, y, c):
        tall, short = left.shape[2] // 4, right.shape[1] // 16
        return (
            (0, left.at[y, z, pl.ds(pl.multiple_of((2 * x + c) * tall, 16), tall)]),
            (tall, right.at[y, pl.ds(pl.multiple_of((4 * z + 2 * x + c) * short, 16), short)]),
        )

    return spots


def mix_spots(mix):
    def spots(z, x, y, c):
        rows = mix.shape[1] // 4
        return ((0, mix.at[2 * z + x, pl.ds(pl.multiple_of((2 * y + c) * rows, 16), rows)]),)

    return spots


def factor(mix, rows, kind, block):
    width = mix.shape[2] // 4
    low = kind * width
    top = mix[2 * block, rows : rows + width // 2, low : low + width]
    bottom = mix[2 * block + 1, rows : rows + width // 2, low : low + width]
    return jnp.concatenate([top, bottom], axis=0)


def down_factor(mix, first, block):
    width = mix.shape[2] // 4
    half = width // 2
    parts = []
    for shard in (2 * block, 2 * block + 1):
        for index in range(4):
            parts.append(mix[shard, first : first + half, index * width : (index + 1) * width])
    return jnp.concatenate(parts, axis=0)


def monarch_small(inputs, right, left):
    width = inputs.shape[1] // BLOCKS
    parts = [dot(columns(inputs, b, width), right(b)) for b in range(BLOCKS)]
    middle = [part.astype(BF16) for part in shuffled(parts)]
    return middle, [dot(middle[b], left(b)) for b in range(BLOCKS)]


def monarch_small_backward(inputs, middle, grads, right, left):
    width = inputs.shape[1] // BLOCKS
    grad_left = [dot_rows(middle[b], grads[b]) for b in range(BLOCKS)]
    back = shuffled([dot_columns(grads[b], left(b)) for b in range(BLOCKS)])
    back = [part.astype(BF16) for part in back]
    grad_right = [dot_rows(columns(inputs, b, width), back[b]) for b in range(BLOCKS)]
    return [dot_columns(back[b], right(b)) for b in range(BLOCKS)], grad_right, grad_left


def store_factor(mix, rows, kind, block, value):
    width = mix.shape[2] // 4
    half = width // 2
    low = kind * width
    mix[2 * block, rows : rows + half, low : low + width] = value[:half].astype(BF16)
    mix[2 * block + 1, rows : rows + half, low : low + width] = value[half:].astype(BF16)


MIXER_OUTS, GLU_OUTS = 12, 6


def cell(values):
    rise = 0.5 * (1.0 + lax.erf(values * (0.5**0.5)))
    return rise, jnp.exp(-0.5 * values * values) * ((2.0 * math.pi) ** -0.5)


def glu_forward_kernel(hidden, table, mix, *refs):
    pieces, result, normed_out, middle_out, branch_out, glu_out, down_out = refs[:7]
    left, right, parts, sems = refs[7:]
    copies = piece_copies(pieces, sems, glu_spots(left, right))
    start_all(copies)
    rows, width = hidden.shape
    block = width // BLOCKS
    unit, unused = normalised(hidden[...])
    normed = (unit * table[1:2] + table[3:4]).astype(BF16)
    normed_out[...] = normed
    wait_all(copies)
    for u in range(2):
        for b in range(BLOCKS):
            part = dot(columns(normed, b, block), right[u, b * block : (b + 1) * block]).astype(BF16)
            for q in range(BLOCKS):
                middle_out[u, q, :, b * block : (b + 1) * block] = columns(part, q, block)
    for q in range(BLOCKS):
        upper = dot(middle_out[0, q], left[0, q])
        gate = dot(middle_out[1, q], left[1, q])
        branch_out[0, q] = upper.astype(BF16)
        branch_out[1, q] = gate.astype(BF16)
        glu = (gate * cell(gate)[0] * upper).astype(BF16)
        glu_out[q] = glu
        parts[q] = dot(glu, down_factor(mix, 7 * block // 6, q))
    down = [part.astype(BF16) for part in shuffled([parts[q] for q in range(BLOCKS)])]
    for b in range(BLOCKS):
        down_out[b] = down[b]
        span = slice(b * block, (b + 1) * block)
        result[:, span] = hidden[:, span] + dot(down[b], factor(mix, block // 2, 2, b))


def glu_backward_kernel(load, grad, hidden, table, mix, normed, middle, branch, glu, down, *refs):
    pieces, result, norm_out, mix_grad, glu_grad = refs[:5]
    left, right, low, back, sems, out_sems = refs[5:]
    copies = piece_copies(pieces, sems, glu_spots(left, right)) if load else []
    start_all(copies)
    rows, width = hidden.shape
    block = width // BLOCKS
    incoming = grad[...].astype(F32)
    half = incoming.astype(BF16)
    backs = []
    for b in range(BLOCKS):
        part = columns(half, b, block)
        mix_grad[1, b] = dot_rows(down[b], part).astype(BF16)
        backs.append(dot_columns(part, factor(mix, block // 2, 2, b)))
    backs = shuffled(backs)
    for q in range(BLOCKS):
        low[q] = backs[q].astype(BF16)
    wait_all(copies)
    for q in range(BLOCKS):
        step = low[q]
        product = dot_rows(glu[q], step).astype(BF16)
        for index in range(BLOCKS):
            mix_grad[2 + index, q] = product[index * block : (index + 1) * block]
        grad_glu = dot_columns(step, down_factor(mix, 7 * block // 6, q))
        upper = branch[0, q].astype(F32)
        gate = branch[1, q].astype(F32)
        rise, density = cell(gate)
        terms = (grad_glu * gate * rise, grad_glu * upper * (rise + gate * density))
        for u in range(2):
            term = terms[u].astype(BF16)
            wide = dot_columns(term, left[u, q]).astype(BF16)
            left[u, q] = dot_rows(middle[u, q], term).astype(BF16)
            for b in range(BLOCKS):
                back[u, b, :, q * block : (q + 1) * block] = columns(wide, b, block)
    outgoing = []
    for b in range(BLOCKS):
        span = slice(b * block, (b + 1) * block)
        total = None
        for u in range(2):
            term = dot_columns(back[u, b], right[u, span])
            right[u, span] = dot_rows(normed[:, span], back[u, b]).astype(BF16)
            total = term if total is None else total + term
        outgoing.append(total)
    writes = grad_copies(glu_grad, out_sems, glu_spots(left, right))
    start_all(writes)
    through, gain, bias = norm_backward(
        jnp.concatenate(outgoing, axis=1), hidden[...], table[1:2]
    )
    result[...] = incoming + through
    norm_out[0:1] = gain
    norm_out[1:2] = bias
    wait_all(writes)


def shifted(values, by):
    length = values.shape[0]
    rolled = pltpu.roll(values, by % length, 0)
    row = lax.broadcasted_iota(jnp.int32, values.shape, 0)
    keep = row >= by if by > 0 else row < length + by
    return jnp.where(keep, rolled, 0.0)


def two_parts(values):
    high = values.astype(BF16)
    return high, (values - high.astype(F32)).astype(BF16)


def to_spectrum(waves, values):
    high, low = two_parts(values)
    return dot(waves[0], high) + (dot(waves[1], high) + dot(waves[0], low))


def from_spectrum(waves, values):
    high, low = two_parts(values)
    return dot_rows(waves[0], high) + (dot_rows(waves[1], high) + dot_rows(waves[0], low))


def multiplied(spectrum, kernel, back):
    length = kernel.shape[1]
    real, imaginary = spectrum[:length], spectrum[length:]
    sign = -1.0 if back else 1.0
    return jnp.concatenate(
        [
            real * kernel[0] - sign * imaginary * kernel[1],
            sign * real * kernel[1] + imaginary * kernel[2],
        ],
        axis=0,
    )


def mixer_forward_kernel(first_layer, *refs):
    hidden_in, marked, live, waves, features = refs[:5]
    pieces = refs[5]
    outs = refs[6:18]
    (
        result,
        hidden_out,
        mix,
        table,
        spectrum_out,
        kernel_out,
        filter_out,
        normed_out,
        middle_out,
        saved_out,
        mixed_out,
        middle_two_out,
    ) = outs
    sems = refs[18]
    copies = piece_copies(pieces, sems, mix_spots(mix))
    start_all(copies)
    wait_all(copies)
    rows, width = hidden_in.shape
    block = width // BLOCKS
    half = block // 2
    length = waves.shape[2]
    wide = mix.shape[0]
    third = 2 * half
    fourth = third + length - half
    span = half
    for w in range(wide):
        table[:, w * span : (w + 1) * span] = mix[w, third : third + 16, block : block + span].astype(F32)
    order = length
    step = order // wide
    smalls = jnp.concatenate(
        [mix[w, third + 16 : third + 32, 2 * block : 2 * block + step] for w in range(wide)], axis=1
    ).astype(F32)
    middle_filter = jnp.concatenate(
        [mix[w, third : third + 16, 2 * block : 2 * block + order] for w in range(wide)], axis=0
    ).astype(F32)
    last = jnp.concatenate(
        [
            mix[w, half:fourth, 3 * block :]
            for w in range(wide)
        ],
        axis=1,
    ).astype(F32)
    lead = exact(features[...], smalls[:8]) + smalls[8:9]
    one = jnp.sin(lead)
    lead_two = exact(one, middle_filter) + smalls[9:10]
    two = jnp.sin(lead_two)
    filter_out[0] = one
    filter_out[1] = two
    filter_out[2] = jnp.cos(lead)
    filter_out[3] = jnp.cos(lead_two)
    fraction = features[:, 0:1]
    window = jnp.exp(-fraction * table[8:9])
    ahead = exact(two, last[:, :width]) * window
    behind = exact(two, last[:, width:]) * window
    kernel_out[:, :width] = ahead
    kernel_out[:, width:] = behind
    wave = waves[0].astype(F32) + waves[1].astype(F32)
    row = lax.broadcasted_iota(jnp.int32, (length, 1), 0)
    weight = jnp.where(row == 0, 0.5 / length, 1.0 / length)
    sums = exact(wave, ahead + behind)
    differences = exact(wave[length:], ahead - behind)
    real = sums[:length]
    spectrum_out[0] = real * weight
    spectrum_out[1] = jnp.where(row == 0, 0.0, differences) * weight
    spectrum_out[2] = jnp.where(row == 0, sums[length : length + 1], real) * weight

    if first_layer:
        hidden = jnp.where(marked[...] > 0.5, table[9:10], hidden_in[...].astype(F32))
    else:
        hidden = hidden_in[...]
    hidden_out[...] = hidden
    unit, unused = normalised(hidden)
    normed = (unit * table[0:1] + table[2:3]).astype(BF16)
    normed_out[...] = normed
    for u in range(2):
        middle, blocks = monarch_small(
            normed, lambda b: factor(mix, 0, u, b), lambda b: factor(mix, 0, 2 + u, b)
        )
        for b in range(BLOCKS):
            middle_out[u, b] = middle[b]
        path = jnp.concatenate(blocks, axis=1)
        saved_out[u] = (path * live[...] if u == 0 else path).astype(BF16)
        if u == 0:
            value = path * live[...]
    gate = path
    for s in range(rows // length):
        inside = slice(s * length, (s + 1) * length)
        alive = live[inside]
        signal = value[inside]
        signal = alive * (
            table[4:5] * shifted(signal, 2) + table[5:6] * shifted(signal, 1) + table[6:7] * signal
        )
        product = multiplied(to_spectrum(waves, signal), spectrum_out, False)
        mixed = from_spectrum(waves, product) + table[7:8] * signal
        saved_out[2, inside] = mixed.astype(BF16)
        mixed_out[inside] = (mixed * gate[inside]).astype(BF16)
    middle, blocks = monarch_small(
        mixed_out[...], lambda b: factor(mix, half, 0, b), lambda b: factor(mix, half, 1, b)
    )
    for b in range(BLOCKS):
        middle_two_out[b] = middle[b]
    result[...] = hidden + jnp.concatenate(blocks, axis=1)


def mixer_backward_kernel(first_layer, *refs):
    (
        grad,
        hidden_in,
        marked,
        live,
        waves,
        features,
        mix,
        table,
        spectrum,
        kernel_in,
        filters,
        normed,
        middle,
        saved,
        mixed,
        middle_two,
        norm_two,
        down_grads,
    ) = refs[:18]
    result, grad_out = refs[18:20]
    mix_grad, sum_scratch, value_scratch, table_grad, sems = refs[20:]
    rows, width = hidden_in.shape
    block = width // BLOCKS
    half = block // 2
    length = waves.shape[2]
    wide = mix.shape[0]
    third = 2 * half
    fourth = third + length - half
    mix_grad[:, third:fourth] = jnp.zeros((wide, fourth - third, width), BF16)
    incoming = grad[...]
    low = incoming.astype(BF16)
    blocks = [columns(low, b, block) for b in range(BLOCKS)]
    outs, right_grads, left_grads = monarch_small_backward(
        mixed[...],
        [middle_two[b] for b in range(BLOCKS)],
        blocks,
        lambda b: factor(mix, half, 0, b),
        lambda b: factor(mix, half, 1, b),
    )
    for b in range(BLOCKS):
        store_factor(mix_grad, half, 0, b, right_grads[b])
        store_factor(mix_grad, half, 1, b, left_grads[b])
        store_factor(mix_grad, half, 2, b, down_grads[1, b])
        for index in range(4):
            w = 2 * b + index // 2
            for part in range(2):
                position = (index % 2) * 2 + part
                mix_grad[w, fourth : fourth + half, position * block : (position + 1) * block] = (
                    down_grads[2 + index, b, part * half : (part + 1) * half]
                )
    grad_mixed = jnp.concatenate(outs, axis=1)
    gate = saved[1].astype(F32)
    value_scratch[1] = grad_mixed * saved[2].astype(F32)
    grad_mixed = grad_mixed * gate
    table_grad[...] = jnp.zeros_like(table_grad)
    sum_scratch[...] = jnp.zeros_like(sum_scratch)
    for s in range(rows // length):
        inside = slice(s * length, (s + 1) * length)
        alive = live[inside]
        value = saved[0, inside].astype(F32)
        behind_two, behind_one = shifted(value, 2), shifted(value, 1)
        signal = alive * (
            table[4:5] * behind_two + table[5:6] * behind_one + table[6:7] * value
        )
        inner = grad_mixed[inside]
        table_grad[7:8] += jnp.sum(inner * signal, axis=0, keepdims=True)
        wave_signal = to_spectrum(waves, signal)
        wave_grad = to_spectrum(waves, inner)
        real, imaginary = wave_signal[:length], wave_signal[length:]
        grad_real, grad_imaginary = wave_grad[:length], wave_grad[length:]
        sum_scratch[0] += grad_real * real
        sum_scratch[1] += grad_imaginary * real - grad_real * imaginary
        sum_scratch[2] += grad_imaginary * imaginary
        grad_signal = from_spectrum(waves, multiplied(wave_grad, spectrum, True))
        grad_signal = alive * (grad_signal + table[7:8] * inner)
        table_grad[4:5] += jnp.sum(grad_signal * behind_two, axis=0, keepdims=True)
        table_grad[5:6] += jnp.sum(grad_signal * behind_one, axis=0, keepdims=True)
        table_grad[6:7] += jnp.sum(grad_signal * value, axis=0, keepdims=True)
        value_scratch[0, inside] = alive * (
            table[6:7] * grad_signal
            + table[5:6] * shifted(grad_signal, -1)
            + table[4:5] * shifted(grad_signal, -2)
        )
    row = lax.broadcasted_iota(jnp.int32, (length, 1), 0)
    weight = jnp.where(row == 0, 0.5 / length, 1.0 / length)
    wave = waves[0].astype(F32) + waves[1].astype(F32)
    real = sum_scratch[0] * weight
    other = sum_scratch[2] * weight
    turning = jnp.where(row == 0, 0.0, sum_scratch[1] * weight)
    total = jnp.where(row == 0, real, real + other)
    last_row = jnp.where(row == 0, other, 0.0)
    sums = exact(wave[:length], total, (0, 0)) + exact(wave[length:], last_row, (0, 0))
    differences = exact(wave[length:], turning, (0, 0))
    fraction = features[:, 0:1]
    window = jnp.exp(-fraction * table[8:9])
    count = float(rows // length)
    grad_ahead = (sums + differences + count * kernel_in[:, :width]) * window
    grad_behind = (sums - differences + count * kernel_in[:, width:]) * window
    one, two = filters[0], filters[1]
    middle_filter = jnp.concatenate(
        [mix[w, third : third + 16, 2 * block : 2 * block + length] for w in range(wide)], axis=0
    ).astype(F32)
    grad_two = None
    for w in range(wide):
        source = grad_ahead if w < wide // 2 else grad_behind
        piece = columns(source, w % (wide // 2), block)
        factor_out = mix[w, half:fourth, 3 * block :].astype(F32)
        term = exact(piece, factor_out, (1, 1))
        grad_two = term if grad_two is None else grad_two + term
        mix_grad[w, half:fourth, 3 * block :] = exact(two, piece, (0, 0)).astype(BF16)
    grad_two = grad_two * filters[3]
    grad_one = exact(grad_two, middle_filter, (1, 1)) * filters[2]
    filter_grad = exact(one, grad_two, (0, 0)).astype(BF16)
    smalls = jnp.concatenate(
        [
            exact(features[...], grad_one, (0, 0)),
            jnp.sum(grad_one, axis=0, keepdims=True),
            jnp.sum(grad_two, axis=0, keepdims=True),
            jnp.zeros((6, length), F32),
        ],
        axis=0,
    )
    step = length // wide
    for w in range(wide):
        mix_grad[w, third : third + 16, 2 * block : 2 * block + length] = filter_grad[
            w * step : (w + 1) * step
        ]
        mix_grad[w, third + 16 : third + 32, 2 * block : 2 * block + step] = columns(
            smalls, w, step
        ).astype(BF16)
    total_in = None
    for u in range(2):
        low = value_scratch[u].astype(BF16)
        outs, right_grads, left_grads = monarch_small_backward(
            normed[...],
            [middle[u, b] for b in range(BLOCKS)],
            [columns(low, b, block) for b in range(BLOCKS)],
            lambda b: factor(mix, 0, u, b),
            lambda b: factor(mix, 0, 2 + u, b),
        )
        for b in range(BLOCKS):
            store_factor(mix_grad, 0, u, b, right_grads[b])
            store_factor(mix_grad, 0, 2 + u, b, left_grads[b])
        joint = jnp.concatenate(outs, axis=1)
        total_in = joint if total_in is None else total_in + joint
    through, gain, bias = norm_backward(total_in, hidden_in[...], table[0:1])
    outgoing = incoming + through
    table_grad[0:1] = gain
    table_grad[1:2] = norm_two[0:1]
    table_grad[2:3] = bias
    table_grad[3:4] = norm_two[1:2]
    if first_layer:
        chosen = marked[...] > 0.5
        table_grad[9:10] = jnp.sum(jnp.where(chosen, outgoing, 0.0), axis=0, keepdims=True)
        outgoing = jnp.where(chosen, 0.0, outgoing)
    result[...] = outgoing
    for w in range(wide):
        mix_grad[w, third : third + 16, block : block + half] = columns(
            table_grad[...], w, half
        ).astype(BF16)
    writes = grad_copies(grad_out, sems, mix_spots(mix_grad))
    start_all(writes)
    wait_all(writes)


COSTS = {"finish": 10, "glu_middle": 50, "glu_backward": 38, "mixer_backward": 24}


def call(kernel, name, outs, operands, anywhere, any_outs, scratch):
    vmem = pl.BlockSpec(memory_space=pltpu.VMEM)
    any_space = pl.BlockSpec(memory_space=pl.ANY)
    return pl.pallas_call(
        kernel,
        out_shape=[jax.ShapeDtypeStruct(shape, dtype) for shape, dtype in outs],
        in_specs=[any_space if index in anywhere else vmem for index in range(len(operands))],
        out_specs=[any_space if index in any_outs else vmem for index in range(len(outs))],
        scratch_shapes=scratch,
        compiler_params=pltpu.CompilerParams(vmem_limit_bytes=VMEM_BYTES),
        cost_estimate=pl.CostEstimate(
            flops=COSTS[name] * 10**9, bytes_accessed=COSTS[name] * 10**6, transcendentals=0
        ),
        name=name,
    )(*operands)


def mixer_outs(rows, width, length, quarter):
    block = width // BLOCKS
    return [
        ((rows, width), F32),
        ((rows, width), F32),
        ((8, 4 * quarter, width), BF16),
        ((16, width), F32),
        ((3, length, width), F32),
        ((length, 2 * width), F32),
        ((4, length, length), F32),
        ((rows, width), BF16),
        ((2, BLOCKS, rows, block), BF16),
        ((3, rows, width), BF16),
        ((rows, width), BF16),
        ((BLOCKS, rows, block), BF16),
    ]


def glu_outs(rows, width):
    return [
        ((rows, width), F32),
        ((rows, width), BF16),
        ((2, BLOCKS, rows, width), BF16),
        ((2, BLOCKS, rows, width), BF16),
        ((BLOCKS, rows, width), BF16),
        ((BLOCKS, rows, width // BLOCKS), BF16),
    ]


def glu_middle_kernel(hidden, table, mix, cotangent, pieces, *refs):
    output, result, norm_out, mix_grad, glu_grad = refs[:5]
    saved, refs = refs[5 : 5 + GLU_OUTS], refs[5 + GLU_OUTS :]
    left, right, parts, low, back, sems, out_sems = refs
    glu_forward_kernel(hidden, table, mix, pieces, *saved, left, right, parts, sems)
    output[...] = saved[0][...].astype(BF16)
    outs = (result, norm_out, mix_grad, glu_grad)
    scratch = (left, right, low, back, sems, out_sems)
    glu_backward_kernel(
        False, cotangent, hidden, table, mix, *saved[1:], pieces, *outs, *scratch
    )


def glu_middle(hidden, table, mix, cotangent, pieces):
    rows, width = hidden.shape
    block = width // BLOCKS
    outs = [
        ((rows, width), BF16),
        ((rows, width), F32),
        ((8, width), F32),
        ((6, BLOCKS, block, block), BF16),
        (pieces.shape, BF16),
    ]
    return call(
        glu_middle_kernel,
        "glu_middle",
        outs,
        (hidden, table, mix, cotangent, pieces),
        (4,),
        (4,),
        [pltpu.VMEM(shape, dtype) for shape, dtype in glu_outs(rows, width)]
        + [
            pltpu.VMEM((2, BLOCKS, width, width), BF16),
            pltpu.VMEM((2, width, width), BF16),
            pltpu.VMEM((BLOCKS, rows, block), F32),
            pltpu.VMEM((BLOCKS, rows, block), BF16),
            pltpu.VMEM((2, BLOCKS, rows, width), BF16),
            pltpu.SemaphoreType.DMA((64,)),
            pltpu.SemaphoreType.DMA((64,)),
        ],
    )


def glu_backward(grad, hidden, table, mix, saved, pieces):
    rows, width = hidden.shape
    block = width // BLOCKS
    quarter = pieces.shape[4]
    outs = [
        ((rows, width), F32),
        ((8, width), F32),
        ((6, BLOCKS, block, block), BF16),
        ((2, 2, 2, 4, quarter, width), BF16),
    ]
    return call(
        partial(glu_backward_kernel, True),
        "glu_backward",
        outs,
        (grad, hidden, table, mix) + tuple(saved) + (pieces,),
        (9,),
        (3,),
        [
            pltpu.VMEM((2, BLOCKS, width, width), BF16),
            pltpu.VMEM((2, width, width), BF16),
            pltpu.VMEM((BLOCKS, rows, block), BF16),
            pltpu.VMEM((2, BLOCKS, rows, width), BF16),
            pltpu.SemaphoreType.DMA((64,)),
            pltpu.SemaphoreType.DMA((64,)),
        ],
    )


def mixer_backward(first_layer, grad, marked, live, waves, features, saved, norm_two, down_grads):
    hidden, mix, table, spectrum, kernel, filters = saved[:6]
    rows, width = hidden.shape
    length = waves.shape[2]
    outs = [((rows, width), F32), ((2, 2, 2, 4, mix.shape[1] // 4, width), BF16)]
    operands = (
        (grad, hidden, marked, live, waves, features)
        + tuple(saved[1:])
        + (norm_two, down_grads)
    )
    return call(
        partial(mixer_backward_kernel, first_layer),
        "mixer_backward",
        outs,
        operands,
        (),
        (1,),
        [
            pltpu.VMEM(mix.shape, BF16),
            pltpu.VMEM((3, length, width), F32),
            pltpu.VMEM((2, rows, width), F32),
            pltpu.VMEM((16, width), F32),
            pltpu.SemaphoreType.DMA((32,)),
        ],
    )
PEERS = ((1, 0, 0, 0), (2, 0, 0, 0), (3, 0, 0, 0), (0, 1, 0, 0), (0, 0, 1, 0), (0, 0, 0, 1))
ALONG_X, ALONG_Y, ACROSS = PEERS[3], PEERS[4], PEERS[5]


def peer(distance, dx, dy, dc):
    z, x, y, c = place()
    return (2 * relative(z, distance) + flip(x, dx), 2 * flip(y, dy) + flip(c, dc))


def greet():
    barrier = pltpu.get_barrier_semaphore()
    for target in PEERS:
        pl.semaphore_signal(
            barrier, inc=1, device_id=peer(*target), device_id_type=pl.DeviceIdType.MESH
        )
    pl.semaphore_wait(barrier, len(PEERS))


class Mail:
    def __init__(self, sent, received):
        self.sent, self.received, self.copies, self.settled = sent, received, [], []

    def send(self, source, target, to):
        index = len(self.copies)
        copy = pltpu.make_async_remote_copy(
            src_ref=source,
            dst_ref=target,
            send_sem=self.sent.at[index],
            recv_sem=self.received.at[index],
            device_id=peer(*to),
            device_id_type=pl.DeviceIdType.MESH,
        )
        copy.start()
        self.copies.append(copy)
        return copy

    def settle(self, copy):
        copy.wait_send()
        self.settled.append(copy)

    def finish(self):
        for copy in self.copies:
            if not any(copy is other for other in self.settled):
                copy.wait_send()


MIXER_BACK = 18
GATHER_COPIES = 12


def gather_steps(mail, own, pieces, rows):
    view = lambda core, dx, dy, first, count: pieces.at[core, dx, dy, pl.ds(first, count), rows]
    along_z = [
        mail.send(own, pieces.at[0, 0, 0, distance, rows], PEERS[distance - 1])
        for distance in (1, 2, 3)
    ]
    yield
    for copy in along_z:
        copy.wait_recv()
    along_x = mail.send(view(0, 0, 0, 0, 4), view(0, 1, 0, 0, 4), ALONG_X)
    along_y = mail.send(view(0, 0, 0, 0, 4), view(0, 0, 1, 0, 4), ALONG_Y)
    across = [mail.send(view(0, 0, 0, 0, 4), view(1, 0, 0, 0, 4), ACROSS)]
    yield
    along_y.wait_recv()
    low = mail.send(view(0, 0, 1, 0, 2), view(0, 1, 1, 0, 2), ALONG_X)
    across.append(mail.send(view(0, 0, 1, 0, 4), view(1, 0, 1, 0, 4), ACROSS))
    along_x.wait_recv()
    high = mail.send(view(0, 1, 0, 2, 2), view(0, 1, 1, 2, 2), ALONG_Y)
    across.append(mail.send(view(0, 1, 0, 0, 4), view(1, 1, 0, 0, 4), ACROSS))
    yield
    low.wait_recv()
    across.append(mail.send(view(0, 1, 1, 0, 2), view(1, 1, 1, 0, 2), ACROSS))
    high.wait_recv()
    across.append(mail.send(view(0, 1, 1, 2, 2), view(1, 1, 1, 2, 2), ACROSS))
    yield
    for copy in across:
        copy.wait_recv()
    yield


def pipeline(starts, between):
    running = []
    waiting = list(starts)
    number = 0
    while waiting or running:
        if waiting:
            running.append(waiting.pop(0)())
        for chunk in reversed(list(running)):
            try:
                next(chunk)
            except StopIteration:
                running.remove(chunk)
        if number in between:
            between[number]()
        number += 1


def save_all(sources, targets, sems, first):
    copies = [
        pltpu.make_async_copy(source, target, sems.at[first + index])
        for index, (source, target) in enumerate(zip(sources, targets))
    ]
    start_all(copies)
    return copies


def forward_kernel(counts, *refs):
    groups = len(counts)
    owns, refs = refs[:groups], refs[groups:]
    hidden_in, marked, live, waves, features = refs[:5]
    pieces, refs = refs[5 : 5 + groups], refs[5 + groups :]
    first_outs, refs = refs[:MIXER_OUTS], refs[MIXER_OUTS:]
    glu_outs, refs = refs[:GLU_OUTS], refs[GLU_OUTS:]
    second_outs, refs = refs[:MIXER_OUTS], refs[MIXER_OUTS:]
    mixer, refs = refs[:MIXER_OUTS], refs[MIXER_OUTS:]
    glu, refs = refs[:GLU_OUTS], refs[GLU_OUTS:]
    staged, refs = refs[:groups], refs[groups:]
    left, right, parts, sent, received, local, loads = refs
    mail = Mail(sent, received)
    copies = [
        pltpu.make_async_copy(own, stage, local.at[index])
        for index, (own, stage) in enumerate(zip(owns, staged))
    ]
    start_all(copies)
    greet()
    starts = []
    for index, count in enumerate(counts):
        size = owns[index].shape[0] // count
        for part in range(count):
            rows = pl.ds(part * size, size)
            starts.append(
                partial(gather_steps, mail, owns[index].at[rows], pieces[index], rows)
            )
    wait_all(copies)
    own_copies = save_all(
        staged, [array.at[0, 0, 0, 0] for array in pieces], local, groups
    )
    saves = []

    def store_own():
        wait_all(own_copies)

    def first_mixer():
        mixer_forward_kernel(
            True, hidden_in, marked, live, waves, features, pieces[0], *mixer, loads
        )
        saves.extend(save_all(mixer, first_outs, local, 2 * groups))

    def first_glu():
        glu_forward_kernel(
            mixer[0], mixer[3], mixer[2], pieces[1], *glu, left, right, parts, loads
        )
        saves.extend(save_all(glu, glu_outs, local, 2 * groups + MIXER_OUTS))

    def second_mixer():
        wait_all(saves[:MIXER_OUTS])
        mixer_forward_kernel(
            False, glu[0], marked, live, waves, features, pieces[2], *mixer, loads
        )
        saves.extend(save_all(mixer, second_outs, local, 2 * groups + MIXER_OUTS + GLU_OUTS))

    ready = [sum(counts[: index + 1]) + 3 for index in range(3)]
    pipeline(
        starts, {0: store_own, ready[0]: first_mixer, ready[1]: first_glu, ready[2]: second_mixer}
    )
    wait_all(saves[MIXER_OUTS:])
    mail.finish()


def forward(quarters, counts, hidden, marked, live, waves, features, number):
    rows, width = hidden.shape
    groups = len(counts)
    anywhere = pl.BlockSpec(memory_space=pl.ANY)
    vmem = pl.BlockSpec(memory_space=pltpu.VMEM)
    total = GATHER_COPIES * sum(counts)
    mixer = mixer_outs(rows, width, waves.shape[2], quarters[0].shape[0])
    glu = glu_outs(rows, width)
    outs = [((2, 2, 2, 4) + quarter.shape, BF16) for quarter in quarters] + mixer + glu + mixer
    block = width // BLOCKS
    result = pl.pallas_call(
        partial(forward_kernel, counts),
        out_shape=[jax.ShapeDtypeStruct(shape, dtype) for shape, dtype in outs],
        in_specs=[anywhere] * groups + [vmem] * 5,
        out_specs=[anywhere] * len(outs),
        scratch_shapes=[pltpu.VMEM(shape, dtype) for shape, dtype in mixer + glu]
        + [pltpu.VMEM(quarter.shape, BF16) for quarter in quarters]
        + [
            pltpu.VMEM((2, BLOCKS, width, width), BF16),
            pltpu.VMEM((2, width, width), BF16),
            pltpu.VMEM((BLOCKS, rows, block), F32),
            pltpu.SemaphoreType.DMA((total,)),
            pltpu.SemaphoreType.DMA((total,)),
            pltpu.SemaphoreType.DMA((2 * groups + 2 * MIXER_OUTS + GLU_OUTS,)),
            pltpu.SemaphoreType.DMA((64,)),
        ],
        compiler_params=pltpu.CompilerParams(
            collective_id=number, has_side_effects=True, vmem_limit_bytes=VMEM_BYTES
        ),
        name="forward",
    )(*quarters, hidden, marked, live, waves, features)
    pieces, result = result[:groups], result[groups:]
    return (
        pieces,
        result[:MIXER_OUTS],
        result[MIXER_OUTS : MIXER_OUTS + GLU_OUTS],
        result[MIXER_OUTS + GLU_OUTS :],
    )


SCATTER_COPIES = 11
SLOTS = 3


def scatter_steps(mail, local, number, grads, landing, rows, result, spots, users, buffers):
    slots, other, two_x, two_y, three, four, own, last = buffers
    size = own.shape[0]
    slot = number % SLOTS
    first = slots.at[slot, :, :, :, pl.ds(0, size)]
    other = other.at[:, :, :, pl.ds(0, size)]
    split = 2 + number % 2
    landed = landing.at[:, :, :, rows]
    x_core = mail.send(grads.at[1, :, :, :, rows], landed, ACROSS)
    for copy in users.pop(slot, ()):
        mail.settle(copy)
    load = pltpu.make_async_copy(grads.at[0, :, :, :, rows], first, local.at[0])
    load.start()
    yield
    x_core.wait_recv()
    fetch = pltpu.make_async_copy(landed, other, local.at[3])
    fetch.start()
    load.wait()
    fetch.wait()
    for dx in range(2):
        for dy in range(2):
            first[dx, dy] += other[dx, dy]
    low = mail.send(first.at[1, :, pl.ds(0, split)], two_x, ALONG_X)
    high = mail.send(first.at[:, 1, pl.ds(split, 4 - split)], two_y, ALONG_Y)
    users[slot] = (low, high)
    yield
    low.wait_recv()
    for dy in (1, 0):
        two_x[dy] += first[0, dy, 0:split]
        if dy == 1:
            low = mail.send(two_x.at[1], three.at[pl.ds(0, split)], ALONG_Y)
    high.wait_recv()
    for dx in (1, 0):
        two_y[dx] += first[dx, 0, split:4]
        if dx == 1:
            high = mail.send(two_y.at[1], three.at[pl.ds(split, 4 - split)], ALONG_X)
    yield
    low.wait_recv()
    three[0:split] += two_x[0]
    along_z = [mail.send(three.at[d], four.at[d - 1], PEERS[d - 1]) for d in range(1, split)]
    high.wait_recv()
    three[split:4] += two_y[0]
    along_z += [mail.send(three.at[d], four.at[d - 1], PEERS[d - 1]) for d in range(split, 4)]
    yield
    total = three[0].astype(F32)
    for index, copy in enumerate(along_z):
        copy.wait_recv()
        total = total + four[index].astype(F32)
    own[...] = total.astype(BF16)
    mine, theirs = spots
    across = [mail.send(own, result.at[mine, rows], ACROSS)]
    along_y = mail.send(own, last, ALONG_Y)
    keep = pltpu.make_async_copy(own, result.at[mine, rows], local.at[1])
    keep.start()
    yield
    along_y.wait_recv()
    across.append(mail.send(last, result.at[theirs, rows], ACROSS))
    keep_too = pltpu.make_async_copy(last, result.at[theirs, rows], local.at[2])
    keep_too.start()
    yield
    for copy in across:
        copy.wait_recv()
    keep.wait()
    keep_too.wait()
    yield


def scatter_buffers(number, size, width):
    split = 2 + number % 2
    return [
        pltpu.VMEM((2, split, size, width), BF16),
        pltpu.VMEM((2, 4 - split, size, width), BF16),
        pltpu.VMEM((4, size, width), BF16),
        pltpu.VMEM((3, size, width), BF16),
        pltpu.VMEM((size, width), BF16),
        pltpu.VMEM((size, width), BF16),
    ]


def backward_kernel(parts, *refs):
    groups = len(parts)
    chunks = sum(len(part) for part in parts)
    grads, refs = list(refs[: groups - 1]), refs[groups - 1 :]
    operands, refs = refs[:MIXER_BACK], refs[MIXER_BACK:]
    result, mix_grads = refs[:2]
    results, landings = refs[2 : 2 + groups], refs[2 + groups : 2 + 2 * groups]
    refs = refs[2 + 2 * groups :]
    inner, refs = refs[:MIXER_BACK], refs[MIXER_BACK:]
    outgoing, scratch, refs = refs[0], refs[1:5], refs[5:]
    sent, received, local, loads, slots, other = refs[:6]
    buffers = refs[6:]
    grads.append(mix_grads)
    fetched = save_all(operands, inner, loads, 32)
    mail = Mail(sent, received)
    unused, unused, y, c = place()
    spots = (2 * y + c, 2 * (1 - y) + c)
    greet()
    users = {}
    starts = []
    for index, sizes in enumerate(parts):
        row = 0
        for size in sizes:
            number = len(starts)
            starts.append(
                partial(
                    scatter_steps,
                    mail,
                    local.at[number],
                    number,
                    grads[index],
                    landings[index],
                    pl.ds(row, size),
                    results[index],
                    spots,
                    users,
                    (slots, other) + tuple(buffers[6 * number : 6 * number + 6]),
                )
            )
            row += size
    saves = []

    def mixer():
        wait_all(fetched)
        mixer_backward_kernel(True, *inner, outgoing, mix_grads, *scratch, loads)
        saves.extend(save_all([outgoing], [result], loads, 32))

    pipeline(starts, {2: mixer})
    wait_all(saves)
    mail.finish()


def backward(grads, parts, operands, number):
    anywhere = pl.BlockSpec(memory_space=pl.ANY)
    chunks = sum(len(part) for part in parts)
    rows, width = operands[0].shape
    mix = operands[6]
    length = operands[4].shape[2]
    shapes = [array.shape for array in grads] + [(2, 2, 2, 4, mix.shape[1] // 4, width)]
    largest = max(max(part) for part in parts)
    buffers = []
    number_of = 0
    for part in parts:
        for size in part:
            buffers += scatter_buffers(number_of, size, width)
            number_of += 1
    total = SCATTER_COPIES * chunks
    outs = (
        [((rows, width), F32), (shapes[-1], BF16)]
        + [((4,) + shape[4:], BF16) for shape in shapes]
        + [(shape[1:], BF16) for shape in shapes]
    )
    results = pl.pallas_call(
        partial(backward_kernel, parts),
        out_shape=[jax.ShapeDtypeStruct(shape, dtype) for shape, dtype in outs],
        in_specs=[anywhere] * (len(grads) + len(operands)),
        out_specs=[anywhere] * len(outs),
        scratch_shapes=[pltpu.VMEM(array.shape, array.dtype) for array in operands]
        + [
            pltpu.VMEM((rows, width), F32),
            pltpu.VMEM(mix.shape, BF16),
            pltpu.VMEM((3, length, width), F32),
            pltpu.VMEM((2, rows, width), F32),
            pltpu.VMEM((16, width), F32),
            pltpu.SemaphoreType.DMA((total,)),
            pltpu.SemaphoreType.DMA((total,)),
            pltpu.SemaphoreType.DMA((chunks, 4)),
            pltpu.SemaphoreType.DMA((32 + MIXER_BACK,)),
            pltpu.VMEM((SLOTS, 2, 2, 4, largest, width), BF16),
            pltpu.VMEM((2, 2, 4, largest, width), BF16),
        ]
        + buffers,
        compiler_params=pltpu.CompilerParams(
            collective_id=number, has_side_effects=True, vmem_limit_bytes=VMEM_BYTES
        ),
        name="backward",
    )(*grads, *operands)
    return results[0], results[2 : 2 + len(parts)]


def prepare_kernel(lengths, positions, mask_vector, *refs):
    members, refs = refs[:18], refs[18:]
    quarters, (live, marked, pack) = refs[: 2 * LAYERS], refs[2 * LAYERS :]
    unused, unused, y, c = place()
    rows, block = members[2].shape[2:]
    order = members[10].shape[2]
    step = members[9].shape[1]
    features = members[6].shape[1]
    third, fourth = 2 * rows, rows + order
    size = pack.shape[0] // 4
    length = live.shape[0] // positions.shape[0]
    place_of = lax.broadcasted_iota(jnp.int32, (length, positions.shape[1]), 0)
    for s in range(positions.shape[0]):
        inside = slice(s * length, (s + 1) * length)
        found = jnp.where(place_of == positions[s : s + 1], 1.0, 0.0)
        marked[inside] = jnp.max(found, axis=1, keepdims=True)
        live[inside] = jnp.where(place_of[:, :1] < lengths[s], 1.0, 0.0)
    flat = {index: members[index][...].astype(F32) for index in (5, 7, 9, 11)}
    for layer in range(LAYERS):
        for u in range(2):
            pack[:rows, u * block : (u + 1) * block] = members[2][layer, u]
            pack[:rows, (2 + u) * block : (3 + u) * block] = members[3][layer, u]
        pack[rows:third, :block] = members[12][layer]
        pack[rows:third, block : 2 * block] = members[13][layer]
        pack[rows:third, 2 * block : 3 * block] = members[17][layer]
        pack[third:fourth] = jnp.zeros((fourth - third, pack.shape[1]), BF16)
        pack[rows:fourth, 3 * block :] = members[10][layer].astype(F32).T.astype(BF16)
        top = [members[index][layer].astype(F32) for index in (0, 1, 4)]
        top += [flat[5][layer : layer + 1], flat[11][layer : layer + 1]]
        top += [mask_vector[...].astype(F32), jnp.zeros((6, rows), F32)]
        pack[third : third + 16, block : block + rows] = jnp.concatenate(top, axis=0).astype(BF16)
        pack[third : third + step, 2 * block : 2 * block + order] = members[8][layer]
        low = [members[6][layer].astype(F32), jnp.zeros((8 - features, step), F32)]
        low += [flat[7][layer : layer + 1], flat[9][layer : layer + 1], jnp.zeros((6, step), F32)]
        pack[third + 16 : third + 32, 2 * block : 2 * block + step] = jnp.concatenate(
            low, axis=0
        ).astype(BF16)
        down = members[16][layer].astype(F32).T.astype(BF16)
        for index in range(4):
            pack[fourth:, index * block : (index + 1) * block] = down[
                index * rows : (index + 1) * rows
            ]
        first = pl.multiple_of((2 * y + c) * size, 16)
        quarters[2 * layer][...] = pack[pl.ds(first, size)]
        start = 0
        for index in (15, 14):
            count = members[index].shape[2] // 2
            first = pl.multiple_of(c * count, 16)
            quarters[2 * layer + 1][start : start + count] = members[index][
                layer, y, pl.ds(first, count)
            ]
            start += count


def prepare(lengths, positions, mask_vector, shards, rows):
    members = list(shards)
    for index in (10, 16):
        members[index] = jnp.swapaxes(members[index], 1, 2)
    width = shards[15].shape[3]
    tall, short = shards[15].shape[2] // 2, shards[14].shape[2] // 2
    height = 2 * shards[2].shape[2] + shards[10].shape[1]
    outs = [((height // 4, width), BF16), ((tall + short, width), BF16)] * LAYERS
    outs += [((rows, 1), F32)] * 2
    vmem = pl.BlockSpec(memory_space=pltpu.VMEM)
    result = pl.pallas_call(
        prepare_kernel,
        out_shape=[jax.ShapeDtypeStruct(shape, dtype) for shape, dtype in outs],
        in_specs=[pl.BlockSpec(memory_space=pltpu.SMEM)] + [vmem] * (2 + len(members)),
        out_specs=[vmem] * len(outs),
        scratch_shapes=[pltpu.VMEM((height, width), BF16)],
        compiler_params=pltpu.CompilerParams(vmem_limit_bytes=VMEM_BYTES),
        name="prepare",
    )(lengths, positions, mask_vector[None], *members)
    return result[: 2 * LAYERS], result[2 * LAYERS], result[2 * LAYERS + 1]


GRADS = (0, 1, 2, 3, 4, 5, 6, 7, 8, 9, 10, 12, 13, 14, 15, 16, 17)
SHARD_AXIS = (1, 1, 1, 1, 1, 0, 1, 0, 0, 0, 1, 0, 0, 0, 1, 1, 0, 0)


def gather_plain(shards, layer_index):
    return tuple(
        lax.all_gather(shards[index][layer_index], "wide", axis=SHARD_AXIS[index], tiled=True)
        for index in range(18)
    )


def scatter_plain(grads, mask_term):
    terms = list(grads) + ([] if mask_term is None else [mask_term])
    axes = [SHARD_AXIS[index] for index in GRADS] + [0]
    return narrow_total(
        [
            lax.psum_scatter(term, "wide", scatter_dimension=axis, tiled=True)
            for term, axis in zip(terms, axes)
        ]
    )


def wave_table(length):
    frequency = np.arange(length)[:, None]
    places = np.arange(length)[None, :]
    angles = (frequency * places % (2 * length)) * (math.pi / length)
    turned = -np.sin(angles)
    turned[0] = np.where(np.arange(length) % 2 == 0, 1.0, -1.0)
    table = jnp.asarray(np.concatenate([np.cos(angles), turned]), F32)
    high = table.astype(BF16)
    return jnp.stack([high, (table - high.astype(F32)).astype(BF16)])


def staged_body(shards, mask_vector, hidden_in, cotangent, seq_lengths, mask_positions):
    rows = hidden_in.shape[0]
    length = rows // seq_lengths.shape[0]
    waves = wave_table(length)
    features = jnp.pad(position_features(length), ((0, 0), (0, 8 - EMB)))
    quarters, live, marked = prepare(seq_lengths, mask_positions, mask_vector, shards, rows)
    pieces, mixed_one, second, mixed_two = forward(
        quarters, (1, 3) * LAYERS, hidden_in, marked, live, waves, features, 1
    )
    output, grad, norm_two, down_grads, glu_grads_two = glu_middle(
        mixed_two[0], mixed_two[3], mixed_two[2], cotangent, pieces[3]
    )
    common = (marked, live, waves, features)
    grad, mix_grads_two = mixer_backward(
        False, grad, *common, mixed_two[1:], norm_two, down_grads
    )
    grad, norm_two, down_grads, glu_grads_one = glu_backward(
        grad, mixed_one[0], mixed_one[3], mixed_one[2], second[1:], pieces[1]
    )
    third = glu_grads_one.shape[4] // 3
    mix_rows = mix_grads_two.shape[4]
    last = (mix_rows // 32) * 16
    grad, sums = backward(
        (glu_grads_two, mix_grads_two, glu_grads_one),
        ((third,) * 3, (mix_rows,), (third,) * 3, (mix_rows - last, last)),
        (grad, mixed_one[1], *common) + tuple(mixed_one[2:]) + (norm_two, down_grads),
        2,
    )
    sums = (sums[3], sums[2], sums[1], sums[0])
    found = finish(sums, shards)
    return output, grad, found[-1].reshape(-1), found[:-1]


def finish_kernel(*refs):
    sums, outs = refs[: 2 * LAYERS], refs[2 * LAYERS :]
    found = dict(zip(GRADS, outs))
    mask = outs[-1]
    rows, block = found[2].shape[2:]
    order = found[10].shape[2]
    features, step = found[6].shape[0], found[6].shape[2]
    third, fourth = 2 * rows, rows + order
    for layer in range(LAYERS):
        mix, glu = sums[2 * layer : 2 * layer + 2]
        pack = jnp.concatenate([mix[index] for index in range(4)], axis=0).astype(F32)
        cut = lambda low, high, k: pack[low:high, k * block : (k + 1) * block]
        table = pack[third : third + 16, block : block + rows]
        smalls = pack[third + 16 : third + 32, 2 * block : 2 * block + step]
        for u in range(2):
            found[0][layer, u : u + 1] = table[u : u + 1]
            found[1][layer, u : u + 1] = table[2 + u : 3 + u]
            found[2][layer, u] = cut(0, rows, u)
            found[3][layer, u] = cut(0, rows, 2 + u)
        for index in range(3):
            found[4][index, layer : layer + 1] = table[4 + index : 5 + index]
        found[5][layer : layer + 1] = table[7:8]
        for index in range(features):
            found[6][index, layer : layer + 1] = smalls[index : index + 1]
        found[7][layer : layer + 1] = smalls[8:9]
        found[8][layer] = pack[third : third + step, 2 * block : 2 * block + order]
        found[9][layer : layer + 1] = smalls[9:10]
        found[10][layer] = cut(rows, fourth, 3).T
        found[12][layer] = cut(rows, third, 0)
        found[13][layer] = cut(rows, third, 1)
        found[16][layer] = jnp.concatenate(
            [cut(fourth, fourth + rows, index) for index in range(4)], axis=0
        ).T
        found[17][layer] = cut(rows, third, 2)
        if layer == 0:
            mask[...] = table[9:10]
        tall, short = found[15].shape[2] // 2, found[14].shape[2] // 2
        for u in range(2):
            for core in range(2):
                quarter = glu[2 * u + core].astype(F32)
                found[15][layer, u, core * tall : (core + 1) * tall] = quarter[:tall]
                found[14][layer, u, core * short : (core + 1) * short] = quarter[tall:]


TURNED = {4: (0, 1), 6: (0, 1), 10: (1, 2), 16: (1, 2)}


def finish(sums, shards):
    outs = []
    for index in GRADS:
        shape = list(shards[index].shape)
        for one, two in [TURNED[index]] if index in TURNED else []:
            shape[one], shape[two] = shape[two], shape[one]
        outs.append((tuple(shape), F32))
    outs.append(((1, shards[5].shape[1]), F32))
    found = call(finish_kernel, "finish", outs, tuple(sums), (), (), [])
    return [
        jnp.swapaxes(array, *TURNED[index]) if index in TURNED else array
        for index, array in zip(GRADS + (-1,), found)
    ]


def is_staged(shards, mesh_shape):
    short, block = shards[2].shape[2:]
    order, outs = shards[10].shape[1:]
    return (
        tuple(mesh_shape) == (8, 4)
        and short == 96
        and block == 192
        and order == 128
        and outs == block
        and shards[14].shape[2:] == (short, 8 * short)
        and shards[15].shape[2:] == (4 * short, 8 * short)
    )


def narrow_total(parts):
    flattened = jnp.concatenate([member.reshape(-1) for member in parts])
    summed = lax.psum(flattened.astype(jnp.bfloat16), "narrow").astype(jnp.float32)
    result = []
    offset = 0
    for member in parts:
        result.append(summed[offset : offset + member.size].reshape(member.shape))
        offset = offset + member.size
    return result


def plain_body(shards, mask_vector, hidden_in, cotangent, live_mask, marked):
    seq_count = live_mask.shape[0]
    mask_full = lax.all_gather(mask_vector, "wide", axis=0, tiled=True)
    weights = [gather_plain(shards, layer_index) for layer_index in range(LAYERS)]
    hidden = jnp.where(
        marked, mask_full.astype(jnp.float32)[None, :], hidden_in.astype(jnp.float32)
    )
    saved_layers = []
    for layer_index in range(LAYERS):
        hidden, saved = forward_layer(hidden, weights[layer_index], live_mask)
        saved_layers.append(saved)
    output = hidden.astype(jnp.bfloat16)
    share = 0.5 * seq_count
    grad_hidden = cotangent.astype(jnp.float32)
    layer_grads = [None] * LAYERS
    mask_grad = None
    for layer_index in reversed(range(LAYERS)):
        grad_hidden, grads = backward_layer(
            grad_hidden, weights[layer_index], saved_layers[layer_index], live_mask, share
        )
        if layer_index > 0:
            layer_grads[layer_index] = scatter_plain(grads, None)
        else:
            mask_term = jnp.sum(jnp.where(marked, grad_hidden, 0.0), axis=0)
            reduced = scatter_plain(grads, mask_term)
            layer_grads[0] = reduced[:-1]
            mask_grad = reduced[-1]
    grad_input = jnp.where(marked, 0.0, grad_hidden)
    final_grads = [
        jnp.stack([layer_grads[position][member_index] for position in range(LAYERS)])
        for member_index in range(17)
    ]
    return output, grad_input, mask_grad, final_grads


def body(
    mesh_shape,
    hidden_in,
    seq_lengths,
    mask_positions,
    mask_vector,
    cotangent,
    norm_gain,
    norm_bias,
    in_right,
    in_left,
    conv_taps,
    skip_bias,
    filter_in,
    filter_in_bias,
    filter_mid,
    filter_mid_bias,
    filter_out,
    decay_rates,
    out_right,
    out_left,
    glu_right,
    glu_left,
    down_right,
    down_left,
):
    row_count = hidden_in.shape[0]
    seq_count = seq_lengths.shape[0]
    length = row_count // seq_count
    places = jnp.arange(length, dtype=jnp.int32)
    live_mask = (places[None, :] < seq_lengths[:, None]).astype(jnp.float32)[:, :, None]
    marked = jnp.any(mask_positions[:, :, None] == places[None, None, :], axis=1).reshape(
        row_count, 1
    )
    shards = (
        norm_gain,
        norm_bias,
        in_right,
        in_left,
        conv_taps,
        skip_bias,
        filter_in,
        filter_in_bias,
        filter_mid,
        filter_mid_bias,
        filter_out,
        decay_rates,
        out_right,
        out_left,
        glu_right,
        glu_left,
        down_right,
        down_left,
    )
    if is_staged(shards, mesh_shape):
        output, grad_input, mask_grad, final_grads = staged_body(
            shards, mask_vector, hidden_in, cotangent, seq_lengths, mask_positions
        )
    else:
        output, grad_input, mask_grad, final_grads = plain_body(
            shards, mask_vector, hidden_in, cotangent, live_mask, marked
        )
    return (output, grad_input, mask_grad) + tuple(final_grads)


def solution(mesh):
    placed = (
        P(("wide", "narrow"), None),
        P(("wide", "narrow")),
        P(("wide", "narrow"), None),
        P("wide"),
        P(("wide", "narrow"), None),
        P(None, None, "wide"),
        P(None, None, "wide"),
        P(None, None, "wide", None),
        P(None, None, "wide", None),
        P(None, None, "wide"),
        P(None, "wide"),
        P(None, None, "wide"),
        P(None, "wide"),
        P(None, "wide", None),
        P(None, "wide"),
        P(None, None, "wide"),
        P(None, "wide"),
        P(None, "wide", None),
        P(None, "wide", None),
        P(None, None, "wide", None),
        P(None, None, "wide", None),
        P(None, "wide", None),
        P(None, "wide", None),
    )
    return jax.shard_map(
        partial(body, (mesh.shape["wide"], mesh.shape["narrow"])),
        mesh=mesh,
        in_specs=placed,
        out_specs=(
            P(("wide", "narrow"), None),
            P(("wide", "narrow"), None),
            P("wide"),
            P(None, None, "wide"),
            P(None, None, "wide"),
            P(None, None, "wide", None),
            P(None, None, "wide", None),
            P(None, None, "wide"),
            P(None, "wide"),
            P(None, None, "wide"),
            P(None, "wide"),
            P(None, "wide", None),
            P(None, "wide"),
            P(None, None, "wide"),
            P(None, "wide", None),
            P(None, "wide", None),
            P(None, None, "wide", None),
            P(None, None, "wide", None),
            P(None, "wide", None),
            P(None, "wide", None),
        ),
        check_vma=False,
    )
```

```python
from functools import partial
import math

import jax
import jax.numpy as jnp
import numpy as np
from jax import lax
from jax.experimental import pallas as pl
from jax.experimental.pallas import tpu as pltpu
from jax.sharding import PartitionSpec as P

BLOCKS = 4
EMB = 5
LAYERS = 2


EPSILON = 1e-05
highest_precision = lax.Precision.HIGHEST


def permute(values):
    array_shape = values.shape
    blocks = array_shape[-2]
    split_view = values.reshape(array_shape[:-1] + (blocks, array_shape[-1] // blocks))
    return jnp.swapaxes(split_view, -3, -2).reshape(array_shape)


def monarch_forward(inputs, right_factor, left_factor):
    row_count = inputs.shape[0]
    right_blocks = right_factor.reshape(BLOCKS, -1, right_factor.shape[-1])
    left_blocks = left_factor.reshape(BLOCKS, -1, left_factor.shape[-1])
    middle = jnp.einsum(
        "rbi,bio->rbo",
        inputs.reshape(row_count, BLOCKS, -1),
        right_blocks,
        preferred_element_type=jnp.float32,
    )
    middle = permute(middle).astype(jnp.bfloat16)
    output = jnp.einsum("rbi,bio->rbo", middle, left_blocks, preferred_element_type=jnp.float32)
    return (middle, output.reshape(row_count, -1))


def monarch_backward(inputs, middle, right_factor, left_factor, grad_output):
    row_count = inputs.shape[0]
    right_blocks = right_factor.reshape(BLOCKS, -1, right_factor.shape[-1])
    left_blocks = left_factor.reshape(BLOCKS, -1, left_factor.shape[-1])
    grad_low = grad_output.astype(jnp.bfloat16).reshape(row_count, BLOCKS, -1)
    grad_left = jnp.einsum("rbi,rbo->bio", middle, grad_low, preferred_element_type=jnp.float32)
    grad_middle = jnp.einsum(
        "rbo,bio->rbi", grad_low, left_blocks, preferred_element_type=jnp.float32
    )
    grad_middle = permute(grad_middle).astype(jnp.bfloat16)
    input_blocks = inputs.reshape(row_count, BLOCKS, -1)
    grad_right = jnp.einsum(
        "rbi,rbo->bio", input_blocks, grad_middle, preferred_element_type=jnp.float32
    )
    grad_inputs = jnp.einsum(
        "rbo,bio->rbi", grad_middle, right_blocks, preferred_element_type=jnp.float32
    )
    return (
        grad_inputs.reshape(row_count, -1),
        grad_right.reshape(right_factor.shape),
        grad_left.reshape(left_factor.shape),
    )


def layer_norm(values, norm_gain, norm_bias):
    average = jnp.mean(values, axis=-1, keepdims=True)
    centred = values - average
    variance = jnp.mean(centred * centred, axis=-1, keepdims=True)
    return centred * lax.rsqrt(variance + EPSILON) * norm_gain + norm_bias


def position_features(length):
    positions = jnp.arange(length, dtype=jnp.float32)
    fraction = positions / length
    features = [fraction]
    for band_index in range(1, (EMB - 1) // 2 + 1):
        features.append(jnp.cos(2.0 * math.pi * band_index * fraction))
        features.append(jnp.sin(2.0 * math.pi * band_index * fraction))
    return jnp.stack(features, axis=1)


def make_filter(
    filter_in, filter_in_bias, filter_mid, filter_mid_bias, filter_out, decay_rates, length
):
    embedding = position_features(length)
    first_hidden = jnp.sin(
        jnp.dot(embedding, filter_in, precision=highest_precision) + filter_in_bias
    )
    second = jnp.sin(
        jnp.dot(first_hidden, filter_mid, precision=highest_precision) + filter_mid_bias
    )
    kernel = jnp.dot(second, filter_out, precision=highest_precision)
    fraction = jnp.arange(length, dtype=jnp.float32)[:, None] / length
    both_rates = jnp.concatenate([decay_rates, decay_rates])
    return kernel * jnp.exp(-fraction * both_rates[None, :])


def short_convolution(signal_rows, conv_taps):
    padded = jnp.pad(signal_rows, ((0, 0), (2, 0), (0, 0)))
    return (
        conv_taps[0] * padded[:, :-2]
        + conv_taps[1] * padded[:, 1:-1]
        + conv_taps[2] * padded[:, 2:]
    )


def spectral_tables(length, span):
    padded_length = 2 * length
    frequency = jnp.arange(length + 1, dtype=jnp.int32)
    places = jnp.arange(span, dtype=jnp.int32)
    phase_index = frequency[:, None] * places[None, :] % padded_length
    angles = phase_index.astype(jnp.float32) * (2.0 * math.pi / padded_length)
    ends = (frequency == 0) | (frequency == length)
    weights = jnp.where(ends, 1.0, 2.0).astype(jnp.float32) / padded_length
    return (jnp.cos(angles), jnp.sin(angles), weights)


def circular_kernel(kernel):
    width = kernel.shape[1] // 2
    forward_part = kernel[:, :width]
    reverse_part = kernel[:, width:]
    first_row = forward_part[:1] + reverse_part[:1]
    spacer = jnp.zeros((1, width), jnp.float32)
    return jnp.concatenate(
        [first_row, forward_part[1:], spacer, jnp.flip(reverse_part[1:], axis=0)], axis=0
    )


def long_convolution(signal_rows, kernel):
    length = signal_rows.shape[1]
    cosine_lookup, sine_lookup, weights = spectral_tables(length, length)
    kernel_cosine, kernel_sine, unused = spectral_tables(length, 2 * length)
    circular = circular_kernel(kernel)
    real_signal = jnp.einsum("ik,hkm->him", cosine_lookup, signal_rows, precision=highest_precision)
    imaginary_signal = -jnp.einsum(
        "ik,hkm->him", sine_lookup, signal_rows, precision=highest_precision
    )
    kernel_real = jnp.dot(kernel_cosine, circular, precision=highest_precision)
    kernel_imaginary = -jnp.dot(kernel_sine, circular, precision=highest_precision)
    real_product = real_signal * kernel_real - imaginary_signal * kernel_imaginary
    imaginary_product = real_signal * kernel_imaginary + imaginary_signal * kernel_real
    inverse_cosine_table = cosine_lookup * weights[:, None]
    inverse_sine_table = sine_lookup * weights[:, None]
    return jnp.einsum(
        "hp,ihj->ipj", inverse_cosine_table, real_product, precision=highest_precision
    ) - jnp.einsum(
        "hp,ihj->ipj", inverse_sine_table, imaginary_product, precision=highest_precision
    )


def mixer_piece(
    value_path,
    gate_path,
    conv_taps,
    skip_bias,
    filter_in,
    filter_in_bias,
    filter_mid,
    filter_mid_bias,
    filter_out,
    decay_rates,
    live_mask,
    share,
):
    length = live_mask.shape[1]
    kernel = make_filter(
        filter_in, filter_in_bias, filter_mid, filter_mid_bias, filter_out, decay_rates, length
    )
    signal_rows = value_path.reshape(live_mask.shape[0], length, -1) * live_mask
    signal_rows = short_convolution(signal_rows, conv_taps) * live_mask
    mixed_signal = long_convolution(signal_rows, kernel) + signal_rows * skip_bias
    return (mixed_signal.reshape(value_path.shape) * gate_path, share * jnp.sum(kernel * kernel))


def glu_piece(upper_branch, gate_branch):
    return jax.nn.gelu(gate_branch, approximate=False) * upper_branch


def small_weights(layer_weights):
    return tuple(
        (layer_weights[position].astype(jnp.float32) for position in (4, 5, 6, 7, 8, 9, 10))
    )


def forward_layer(hidden, layer_weights, live_mask):
    (
        norm_gain,
        norm_bias,
        in_right,
        in_left,
        conv_taps,
        skip_bias,
        filter_in,
        filter_in_bias,
        filter_mid,
        filter_mid_bias,
        filter_out,
        decay_rates,
        out_right,
        out_left,
        glu_right,
        glu_left,
        down_right,
        down_left,
    ) = layer_weights
    gains = norm_gain.astype(jnp.float32)
    biases = norm_bias.astype(jnp.float32)
    small = small_weights(layer_weights)
    normed = layer_norm(hidden, gains[0], biases[0]).astype(jnp.bfloat16)
    middle_value, value_path = monarch_forward(normed, in_right[0], in_left[0])
    middle_gate, gate_path = monarch_forward(normed, in_right[1], in_left[1])
    mixed_signal, unused = mixer_piece(
        value_path,
        gate_path,
        small[0],
        small[1],
        small[2],
        small[3],
        small[4],
        small[5],
        small[6],
        decay_rates.astype(jnp.float32),
        live_mask,
        0.0,
    )
    mixed_signal = mixed_signal.astype(jnp.bfloat16)
    middle_out, branch = monarch_forward(mixed_signal, out_right, out_left)
    middle_hidden = hidden + branch
    normed_two = layer_norm(middle_hidden, gains[1], biases[1]).astype(jnp.bfloat16)
    middle_up, upper_branch = monarch_forward(normed_two, glu_right[0], glu_left[0])
    middle_glu, gate_branch = monarch_forward(normed_two, glu_right[1], glu_left[1])
    glu_hidden = glu_piece(upper_branch, gate_branch).astype(jnp.bfloat16)
    middle_down, branch_two = monarch_forward(glu_hidden, down_right, down_left)
    saved = (
        hidden,
        normed,
        middle_value,
        value_path,
        middle_gate,
        gate_path,
        mixed_signal,
        middle_out,
        middle_hidden,
        normed_two,
        middle_up,
        upper_branch,
        middle_glu,
        gate_branch,
        glu_hidden,
        middle_down,
    )
    return (middle_hidden + branch_two, saved)


def backward_layer(grad_hidden, layer_weights, saved, live_mask, share):
    (
        norm_gain,
        norm_bias,
        in_right,
        in_left,
        conv_taps,
        skip_bias,
        filter_in,
        filter_in_bias,
        filter_mid,
        filter_mid_bias,
        filter_out,
        decay_rates,
        out_right,
        out_left,
        glu_right,
        glu_left,
        down_right,
        down_left,
    ) = layer_weights
    (
        hidden,
        normed,
        middle_value,
        value_path,
        middle_gate,
        gate_path,
        mixed_signal,
        middle_out,
        middle_hidden,
        normed_two,
        middle_up,
        upper_branch,
        middle_glu,
        gate_branch,
        glu_hidden,
        middle_down,
    ) = saved
    gains = norm_gain.astype(jnp.float32)
    biases = norm_bias.astype(jnp.float32)
    small = small_weights(layer_weights)
    grad_glu, grad_down_right, grad_down_left = monarch_backward(
        glu_hidden, middle_down, down_right, down_left, grad_hidden
    )
    unused, glu_pull = jax.vjp(glu_piece, upper_branch, gate_branch)
    grad_upper, grad_gate = glu_pull(grad_glu)
    grad_normed_up, grad_right_up, grad_left_up = monarch_backward(
        normed_two, middle_up, glu_right[0], glu_left[0], grad_upper
    )
    grad_normed_gate, grad_right_gate, grad_left_gate = monarch_backward(
        normed_two, middle_glu, glu_right[1], glu_left[1], grad_gate
    )
    unused, norm_pull = jax.vjp(layer_norm, middle_hidden, gains[1], biases[1])
    grad_middle, grad_gain_two, grad_bias_two = norm_pull(grad_normed_up + grad_normed_gate)
    grad_middle = grad_middle + grad_hidden
    grad_mixed, grad_out_right, grad_out_left = monarch_backward(
        mixed_signal, middle_out, out_right, out_left, grad_middle
    )
    mixer_local = partial(
        mixer_piece, decay_rates=decay_rates.astype(jnp.float32), live_mask=live_mask, share=share
    )
    unused, mixer_pull = jax.vjp(
        mixer_local,
        value_path,
        gate_path,
        small[0],
        small[1],
        small[2],
        small[3],
        small[4],
        small[5],
        small[6],
    )
    mixer_grads = mixer_pull((grad_mixed, jnp.ones((), jnp.float32)))
    grad_normed_value, grad_right_value, grad_left_value = monarch_backward(
        normed, middle_value, in_right[0], in_left[0], mixer_grads[0]
    )
    grad_normed_path, grad_right_path, grad_left_path = monarch_backward(
        normed, middle_gate, in_right[1], in_left[1], mixer_grads[1]
    )
    unused, norm_pull_one = jax.vjp(layer_norm, hidden, gains[0], biases[0])
    grad_before, grad_gain_one, grad_bias_one = norm_pull_one(grad_normed_value + grad_normed_path)
    grads = (
        jnp.stack([grad_gain_one, grad_gain_two]),
        jnp.stack([grad_bias_one, grad_bias_two]),
        jnp.stack([grad_right_value, grad_right_path]),
        jnp.stack([grad_left_value, grad_left_path]),
        mixer_grads[2],
        mixer_grads[3],
        mixer_grads[4],
        mixer_grads[5],
        mixer_grads[6],
        mixer_grads[7],
        mixer_grads[8],
        grad_out_right,
        grad_out_left,
        jnp.stack([grad_right_up, grad_right_gate]),
        jnp.stack([grad_left_up, grad_left_gate]),
        grad_down_right,
        grad_down_left,
    )
    return (grad_before + grad_middle, grads)


F32 = jnp.float32
BF16 = jnp.bfloat16
VMEM_BYTES = 60 * 1024 * 1024


def dot(left, right):
    return jnp.dot(left, right, preferred_element_type=F32)


def dot_rows(left, right):
    return lax.dot_general(left, right, (((0,), (0,)), ((), ())), preferred_element_type=F32)


def dot_columns(left, right):
    return lax.dot_general(left, right, (((1,), (1,)), ((), ())), preferred_element_type=F32)


def exact(left, right, dims=(1, 0)):
    return lax.dot_general(
        left,
        right,
        (((dims[0],), (dims[1],)), ((), ())),
        precision=highest_precision,
        preferred_element_type=F32,
    )


def columns(values, index, width):
    return values[:, index * width : (index + 1) * width]


def shuffled(parts):
    chunk = parts[0].shape[1] // BLOCKS
    return [
        jnp.concatenate([columns(part, index, chunk) for part in parts], axis=1)
        for index in range(BLOCKS)
    ]


def normalised(values):
    average = jnp.mean(values, axis=-1, keepdims=True)
    centred = values - average
    variance = jnp.mean(centred * centred, axis=-1, keepdims=True)
    scale = lax.rsqrt(variance + EPSILON)
    return centred * scale, scale


def norm_backward(grad, hidden, gain):
    unit, scale = normalised(hidden)
    grad_gain = jnp.sum(grad * unit, axis=0, keepdims=True)
    grad_bias = jnp.sum(grad, axis=0, keepdims=True)
    scaled = grad * gain
    mean_one = jnp.mean(scaled, axis=-1, keepdims=True)
    mean_two = jnp.mean(scaled * unit, axis=-1, keepdims=True)
    return scale * (scaled - mean_one - unit * mean_two), grad_gain, grad_bias


def flip(bit, by):
    return 1 - bit if by else bit


def place():
    w = lax.axis_index("wide")
    n = lax.axis_index("narrow")
    return w // 2, w % 2, n // 2, n % 2


def relative(z, distance):
    high, low = z // 2, z % 2
    return 2 * flip(high, distance // 2) + flip(low, distance % 2)


def piece_copies(pieces, sems, targets_of):
    z, x, y, c = place()
    copies = []
    for core in range(2):
        for dx in range(2):
            for dy in range(2):
                for dz in range(4):
                    owner = (relative(z, dz), flip(x, dx), flip(y, dy), flip(c, core))
                    for row, target in targets_of(*owner):
                        view = pieces.at[core, dx, dy, dz, pl.ds(row, target.shape[0])]
                        copies.append(pltpu.make_async_copy(view, target, sems.at[len(copies)]))
    return copies


def grad_copies(result, sems, sources_of):
    z, x, y, c = place()
    copies = []
    for core in range(2):
        for dx in range(2):
            for dy in range(2):
                for dz in range(4):
                    owner = (relative(z, dz), flip(x, dx), flip(y, dy), flip(c, core))
                    for row, source in sources_of(*owner):
                        view = result.at[core, dx, dy, dz, pl.ds(row, source.shape[0])]
                        copies.append(pltpu.make_async_copy(source, view, sems.at[len(copies)]))
    return copies


def start_all(copies):
    for copy in copies:
        copy.start()


def wait_all(copies):
    for copy in copies:
        copy.wait()


def glu_moves(pieces, left, right, sems, out):
    z, x, y, c = place()
    tall, short = left.shape[2] // 4, right.shape[1] // 16
    lefts, rights = [[] for q in range(BLOCKS)], []
    count = 0
    for q in range(BLOCKS):
        for core in range(2):
            for dx in range(2):
                for dy in range(2):
                    u = flip(y, dy)
                    spot = 2 * flip(x, dx) + flip(c, core)
                    tall_row = pl.multiple_of(spot * tall, 16)
                    short_row = pl.multiple_of((4 * q + spot) * short, 16)
                    ends = (
                        (0, left.at[u, q, pl.ds(tall_row, tall)], lefts[q]),
                        (tall, right.at[u, pl.ds(short_row, short)], rights),
                    )
                    for row, whole, group in ends:
                        rows = pl.ds(row, whole.shape[0])
                        piece = pieces.at[core, dx, dy, relative(z, q), rows]
                        source, target = (whole, piece) if out else (piece, whole)
                        group.append(pltpu.make_async_copy(source, target, sems.at[count]))
                        count += 1
    return lefts, rights


def mix_spots(mix):
    def spots(z, x, y, c):
        rows = mix.shape[1] // 4
        return ((0, mix.at[2 * z + x, pl.ds(pl.multiple_of((2 * y + c) * rows, 16), rows)]),)

    return spots


def factor(mix, rows, kind, block):
    width = mix.shape[2] // 4
    low = kind * width
    top = mix[2 * block, rows : rows + width // 2, low : low + width]
    bottom = mix[2 * block + 1, rows : rows + width // 2, low : low + width]
    return jnp.concatenate([top, bottom], axis=0)


def down_factor(mix, first, block):
    width = mix.shape[2] // 4
    half = width // 2
    parts = []
    for shard in (2 * block, 2 * block + 1):
        for index in range(4):
            parts.append(mix[shard, first : first + half, index * width : (index + 1) * width])
    return jnp.concatenate(parts, axis=0)


def monarch_small(inputs, right, left):
    width = inputs.shape[1] // BLOCKS
    parts = [dot(columns(inputs, b, width), right(b)) for b in range(BLOCKS)]
    middle = [part.astype(BF16) for part in shuffled(parts)]
    return middle, [dot(middle[b], left(b)) for b in range(BLOCKS)]


def monarch_small_backward(inputs, middle, grads, right, left):
    width = inputs.shape[1] // BLOCKS
    grad_left = [dot_rows(middle[b], grads[b]) for b in range(BLOCKS)]
    back = shuffled([dot_columns(grads[b], left(b)) for b in range(BLOCKS)])
    back = [part.astype(BF16) for part in back]
    grad_right = [dot_rows(columns(inputs, b, width), back[b]) for b in range(BLOCKS)]
    return [dot_columns(back[b], right(b)) for b in range(BLOCKS)], grad_right, grad_left


def store_factor(mix, rows, kind, block, value):
    width = mix.shape[2] // 4
    half = width // 2
    low = kind * width
    mix[2 * block, rows : rows + half, low : low + width] = value[:half].astype(BF16)
    mix[2 * block + 1, rows : rows + half, low : low + width] = value[half:].astype(BF16)


MIXER_OUTS, GLU_OUTS = 12, 6


def cell(values):
    rise = 0.5 * (1.0 + lax.erf(values * (0.5**0.5)))
    return rise, jnp.exp(-0.5 * values * values) * ((2.0 * math.pi) ** -0.5)


def glu_forward_kernel(hidden, table, mix, *refs):
    pieces, result, normed_out, middle_out, branch_out, glu_out, down_out = refs[:7]
    left, right, parts, sems = refs[7:]
    lefts, rights = glu_moves(pieces, left, right, sems, False)
    start_all(rights)
    for q in range(BLOCKS):
        start_all(lefts[q])
    rows, width = hidden.shape
    block = width // BLOCKS
    unit, unused = normalised(hidden[...])
    normed = (unit * table[1:2] + table[3:4]).astype(BF16)
    normed_out[...] = normed
    wait_all(rights)
    for u in range(2):
        for b in range(BLOCKS):
            part = dot(columns(normed, b, block), right[u, b * block : (b + 1) * block]).astype(BF16)
            for q in range(BLOCKS):
                middle_out[u, q, :, b * block : (b + 1) * block] = columns(part, q, block)
    for q in range(BLOCKS):
        wait_all(lefts[q])
        upper = dot(middle_out[0, q], left[0, q])
        gate = dot(middle_out[1, q], left[1, q])
        branch_out[0, q] = upper.astype(BF16)
        branch_out[1, q] = gate.astype(BF16)
        glu = (gate * cell(gate)[0] * upper).astype(BF16)
        glu_out[q] = glu
        parts[q] = dot(glu, down_factor(mix, 7 * block // 6, q))
    down = [part.astype(BF16) for part in shuffled([parts[q] for q in range(BLOCKS)])]
    for b in range(BLOCKS):
        down_out[b] = down[b]
        span = slice(b * block, (b + 1) * block)
        result[:, span] = hidden[:, span] + dot(down[b], factor(mix, block // 2, 2, b))


def glu_backward_kernel(arriving, grad, hidden, table, mix, normed, middle, branch, glu, down, *refs):
    pieces, result, norm_out, mix_grad, glu_grad = refs[:5]
    left, right, low, back, out_sems = refs[5:]
    lefts, rights = arriving
    left_writes, right_writes = glu_moves(glu_grad, left, right, out_sems, True)
    rows, width = hidden.shape
    block = width // BLOCKS
    incoming = grad[...].astype(F32)
    half = incoming.astype(BF16)
    backs = []
    for b in range(BLOCKS):
        part = columns(half, b, block)
        mix_grad[1, b] = dot_rows(down[b], part).astype(BF16)
        backs.append(dot_columns(part, factor(mix, block // 2, 2, b)))
    backs = shuffled(backs)
    for q in range(BLOCKS):
        low[q] = backs[q].astype(BF16)
    for q in range(BLOCKS):
        wait_all(lefts[q])
        step = low[q]
        product = dot_rows(glu[q], step).astype(BF16)
        for index in range(BLOCKS):
            mix_grad[2 + index, q] = product[index * block : (index + 1) * block]
        grad_glu = dot_columns(step, down_factor(mix, 7 * block // 6, q))
        upper = branch[0, q].astype(F32)
        gate = branch[1, q].astype(F32)
        rise, density = cell(gate)
        terms = (grad_glu * gate * rise, grad_glu * upper * (rise + gate * density))
        for u in range(2):
            term = terms[u].astype(BF16)
            wide = dot_columns(term, left[u, q]).astype(BF16)
            left[u, q] = dot_rows(middle[u, q], term).astype(BF16)
            for b in range(BLOCKS):
                back[u, b, :, q * block : (q + 1) * block] = columns(wide, b, block)
        start_all(left_writes[q])
    wait_all(rights)
    outgoing = []
    for b in range(BLOCKS):
        span = slice(b * block, (b + 1) * block)
        total = None
        for u in range(2):
            term = dot_columns(back[u, b], right[u, span])
            right[u, span] = dot_rows(normed[:, span], back[u, b]).astype(BF16)
            total = term if total is None else total + term
        outgoing.append(total)
    start_all(right_writes)
    through, gain, bias = norm_backward(
        jnp.concatenate(outgoing, axis=1), hidden[...], table[1:2]
    )
    result[...] = incoming + through
    norm_out[0:1] = gain
    norm_out[1:2] = bias
    for q in range(BLOCKS):
        wait_all(left_writes[q])
    wait_all(right_writes)


def shifted(values, by):
    length = values.shape[0]
    rolled = pltpu.roll(values, by % length, 0)
    row = lax.broadcasted_iota(jnp.int32, values.shape, 0)
    keep = row >= by if by > 0 else row < length + by
    return jnp.where(keep, rolled, 0.0)


def two_parts(values):
    high = values.astype(BF16)
    return high, (values - high.astype(F32)).astype(BF16)


def to_spectrum(waves, values):
    high, low = two_parts(values)
    return dot(waves[0], high) + (dot(waves[1], high) + dot(waves[0], low))


def from_spectrum(waves, values):
    high, low = two_parts(values)
    return dot_rows(waves[0], high) + (dot_rows(waves[1], high) + dot_rows(waves[0], low))


def multiplied(spectrum, kernel, back):
    length = kernel.shape[1]
    real, imaginary = spectrum[:length], spectrum[length:]
    sign = -1.0 if back else 1.0
    return jnp.concatenate(
        [
            real * kernel[0] - sign * imaginary * kernel[1],
            sign * real * kernel[1] + imaginary * kernel[2],
        ],
        axis=0,
    )


def mixer_forward_kernel(first_layer, *refs):
    hidden_in, marked, live, waves, features = refs[:5]
    pieces = refs[5]
    outs = refs[6:18]
    (
        result,
        hidden_out,
        mix,
        table,
        spectrum_out,
        kernel_out,
        filter_out,
        normed_out,
        middle_out,
        saved_out,
        mixed_out,
        middle_two_out,
    ) = outs
    sems = refs[18]
    copies = piece_copies(pieces, sems, mix_spots(mix))
    start_all(copies)
    wait_all(copies)
    rows, width = hidden_in.shape
    block = width // BLOCKS
    half = block // 2
    length = waves.shape[2]
    wide = mix.shape[0]
    third = 2 * half
    fourth = third + length - half
    span = half
    for w in range(wide):
        table[:, w * span : (w + 1) * span] = mix[w, third : third + 16, block : block + span].astype(F32)
    order = length
    step = order // wide
    smalls = jnp.concatenate(
        [mix[w, third + 16 : third + 32, 2 * block : 2 * block + step] for w in range(wide)], axis=1
    ).astype(F32)
    middle_filter = jnp.concatenate(
        [mix[w, third : third + 16, 2 * block : 2 * block + order] for w in range(wide)], axis=0
    ).astype(F32)
    last = jnp.concatenate(
        [
            mix[w, half:fourth, 3 * block :]
            for w in range(wide)
        ],
        axis=1,
    ).astype(F32)
    lead = exact(features[...], smalls[:8]) + smalls[8:9]
    one = jnp.sin(lead)
    lead_two = exact(one, middle_filter) + smalls[9:10]
    two = jnp.sin(lead_two)
    filter_out[0] = one
    filter_out[1] = two
    filter_out[2] = jnp.cos(lead)
    filter_out[3] = jnp.cos(lead_two)
    fraction = features[:, 0:1]
    window = jnp.exp(-fraction * table[8:9])
    ahead = exact(two, last[:, :width]) * window
    behind = exact(two, last[:, width:]) * window
    kernel_out[:, :width] = ahead
    kernel_out[:, width:] = behind
    wave = waves[0].astype(F32) + waves[1].astype(F32)
    row = lax.broadcasted_iota(jnp.int32, (length, 1), 0)
    weight = jnp.where(row == 0, 0.5 / length, 1.0 / length)
    sums = exact(wave, ahead + behind)
    differences = exact(wave[length:], ahead - behind)
    real = sums[:length]
    spectrum_out[0] = real * weight
    spectrum_out[1] = jnp.where(row == 0, 0.0, differences) * weight
    spectrum_out[2] = jnp.where(row == 0, sums[length : length + 1], real) * weight

    if first_layer:
        hidden = jnp.where(marked[...] > 0.5, table[9:10], hidden_in[...].astype(F32))
    else:
        hidden = hidden_in[...]
    hidden_out[...] = hidden
    unit, unused = normalised(hidden)
    normed = (unit * table[0:1] + table[2:3]).astype(BF16)
    normed_out[...] = normed
    for u in range(2):
        middle, blocks = monarch_small(
            normed, lambda b: factor(mix, 0, u, b), lambda b: factor(mix, 0, 2 + u, b)
        )
        for b in range(BLOCKS):
            middle_out[u, b] = middle[b]
        path = jnp.concatenate(blocks, axis=1)
        saved_out[u] = (path * live[...] if u == 0 else path).astype(BF16)
        if u == 0:
            value = path * live[...]
    gate = path
    for s in range(rows // length):
        inside = slice(s * length, (s + 1) * length)
        alive = live[inside]
        signal = value[inside]
        signal = alive * (
            table[4:5] * shifted(signal, 2) + table[5:6] * shifted(signal, 1) + table[6:7] * signal
        )
        product = multiplied(to_spectrum(waves, signal), spectrum_out, False)
        mixed = from_spectrum(waves, product) + table[7:8] * signal
        saved_out[2, inside] = mixed.astype(BF16)
        mixed_out[inside] = (mixed * gate[inside]).astype(BF16)
    middle, blocks = monarch_small(
        mixed_out[...], lambda b: factor(mix, half, 0, b), lambda b: factor(mix, half, 1, b)
    )
    for b in range(BLOCKS):
        middle_two_out[b] = middle[b]
    result[...] = hidden + jnp.concatenate(blocks, axis=1)


def mixer_backward_kernel(first_layer, tick, *refs):
    (
        grad,
        hidden_in,
        marked,
        live,
        waves,
        features,
        mix,
        table,
        spectrum,
        kernel_in,
        filters,
        normed,
        middle,
        saved,
        mixed,
        middle_two,
        norm_two,
        down_grads,
    ) = refs[:18]
    result, grad_out = refs[18:20]
    mix_grad, sum_scratch, value_scratch, table_grad, sems = refs[20:]
    rows, width = hidden_in.shape
    block = width // BLOCKS
    half = block // 2
    length = waves.shape[2]
    wide = mix.shape[0]
    third = 2 * half
    fourth = third + length - half
    mix_grad[:, third:fourth] = jnp.zeros((wide, fourth - third, width), BF16)
    incoming = grad[...]
    low = incoming.astype(BF16)
    blocks = [columns(low, b, block) for b in range(BLOCKS)]
    outs, right_grads, left_grads = monarch_small_backward(
        mixed[...],
        [middle_two[b] for b in range(BLOCKS)],
        blocks,
        lambda b: factor(mix, half, 0, b),
        lambda b: factor(mix, half, 1, b),
    )
    for b in range(BLOCKS):
        store_factor(mix_grad, half, 0, b, right_grads[b])
        store_factor(mix_grad, half, 1, b, left_grads[b])
        store_factor(mix_grad, half, 2, b, down_grads[1, b])
        for index in range(4):
            w = 2 * b + index // 2
            for part in range(2):
                position = (index % 2) * 2 + part
                mix_grad[w, fourth : fourth + half, position * block : (position + 1) * block] = (
                    down_grads[2 + index, b, part * half : (part + 1) * half]
                )
    grad_mixed = jnp.concatenate(outs, axis=1)
    gate = saved[1].astype(F32)
    value_scratch[1] = grad_mixed * saved[2].astype(F32)
    value_scratch[0] = grad_mixed * gate
    tick(0)
    table_grad[...] = jnp.zeros_like(table_grad)
    sum_scratch[...] = jnp.zeros_like(sum_scratch)
    for s in range(rows // length):
        inside = slice(s * length, (s + 1) * length)
        alive = live[inside]
        value = saved[0, inside].astype(F32)
        behind_two, behind_one = shifted(value, 2), shifted(value, 1)
        signal = alive * (
            table[4:5] * behind_two + table[5:6] * behind_one + table[6:7] * value
        )
        inner = value_scratch[0, inside]
        table_grad[7:8] += jnp.sum(inner * signal, axis=0, keepdims=True)
        wave_signal = to_spectrum(waves, signal)
        wave_grad = to_spectrum(waves, inner)
        real, imaginary = wave_signal[:length], wave_signal[length:]
        grad_real, grad_imaginary = wave_grad[:length], wave_grad[length:]
        sum_scratch[0] += grad_real * real
        sum_scratch[1] += grad_imaginary * real - grad_real * imaginary
        sum_scratch[2] += grad_imaginary * imaginary
        grad_signal = from_spectrum(waves, multiplied(wave_grad, spectrum, True))
        grad_signal = alive * (grad_signal + table[7:8] * inner)
        table_grad[4:5] += jnp.sum(grad_signal * behind_two, axis=0, keepdims=True)
        table_grad[5:6] += jnp.sum(grad_signal * behind_one, axis=0, keepdims=True)
        table_grad[6:7] += jnp.sum(grad_signal * value, axis=0, keepdims=True)
        value_scratch[0, inside] = alive * (
            table[6:7] * grad_signal
            + table[5:6] * shifted(grad_signal, -1)
            + table[4:5] * shifted(grad_signal, -2)
        )
    tick(1)
    row = lax.broadcasted_iota(jnp.int32, (length, 1), 0)
    weight = jnp.where(row == 0, 0.5 / length, 1.0 / length)
    wave = waves[0].astype(F32) + waves[1].astype(F32)
    real = sum_scratch[0] * weight
    other = sum_scratch[2] * weight
    turning = jnp.where(row == 0, 0.0, sum_scratch[1] * weight)
    total = jnp.where(row == 0, real, real + other)
    last_row = jnp.where(row == 0, other, 0.0)
    sums = exact(wave[:length], total, (0, 0)) + exact(wave[length:], last_row, (0, 0))
    differences = exact(wave[length:], turning, (0, 0))
    fraction = features[:, 0:1]
    window = jnp.exp(-fraction * table[8:9])
    count = float(rows // length)
    grad_ahead = (sums + differences + count * kernel_in[:, :width]) * window
    grad_behind = (sums - differences + count * kernel_in[:, width:]) * window
    one, two = filters[0], filters[1]
    middle_filter = jnp.concatenate(
        [mix[w, third : third + 16, 2 * block : 2 * block + length] for w in range(wide)], axis=0
    ).astype(F32)
    grad_two = None
    for w in range(wide):
        source = grad_ahead if w < wide // 2 else grad_behind
        piece = columns(source, w % (wide // 2), block)
        factor_out = mix[w, half:fourth, 3 * block :].astype(F32)
        term = exact(piece, factor_out, (1, 1))
        grad_two = term if grad_two is None else grad_two + term
        mix_grad[w, half:fourth, 3 * block :] = exact(two, piece, (0, 0)).astype(BF16)
    grad_two = grad_two * filters[3]
    grad_one = exact(grad_two, middle_filter, (1, 1)) * filters[2]
    filter_grad = exact(one, grad_two, (0, 0)).astype(BF16)
    smalls = jnp.concatenate(
        [
            exact(features[...], grad_one, (0, 0)),
            jnp.sum(grad_one, axis=0, keepdims=True),
            jnp.sum(grad_two, axis=0, keepdims=True),
            jnp.zeros((6, length), F32),
        ],
        axis=0,
    )
    step = length // wide
    for w in range(wide):
        mix_grad[w, third : third + 16, 2 * block : 2 * block + length] = filter_grad[
            w * step : (w + 1) * step
        ]
        mix_grad[w, third + 16 : third + 32, 2 * block : 2 * block + step] = columns(
            smalls, w, step
        ).astype(BF16)
    tick(2)
    total_in = None
    for u in range(2):
        low = value_scratch[u].astype(BF16)
        outs, right_grads, left_grads = monarch_small_backward(
            normed[...],
            [middle[u, b] for b in range(BLOCKS)],
            [columns(low, b, block) for b in range(BLOCKS)],
            lambda b: factor(mix, 0, u, b),
            lambda b: factor(mix, 0, 2 + u, b),
        )
        for b in range(BLOCKS):
            store_factor(mix_grad, 0, u, b, right_grads[b])
            store_factor(mix_grad, 0, 2 + u, b, left_grads[b])
        joint = jnp.concatenate(outs, axis=1)
        total_in = joint if total_in is None else total_in + joint
    through, gain, bias = norm_backward(total_in, hidden_in[...], table[0:1])
    outgoing = grad[...] + through
    table_grad[0:1] = gain
    table_grad[1:2] = norm_two[0:1]
    table_grad[2:3] = bias
    table_grad[3:4] = norm_two[1:2]
    if first_layer:
        chosen = marked[...] > 0.5
        table_grad[9:10] = jnp.sum(jnp.where(chosen, outgoing, 0.0), axis=0, keepdims=True)
        outgoing = jnp.where(chosen, 0.0, outgoing)
    result[...] = outgoing
    for w in range(wide):
        mix_grad[w, third : third + 16, block : block + half] = columns(
            table_grad[...], w, half
        ).astype(BF16)
    writes = grad_copies(grad_out, sems, mix_spots(mix_grad))
    start_all(writes)
    wait_all(writes)


COSTS = {"finish": 10, "glu_middle": 50, "glu_backward": 38, "mixer_backward": 24}


def call(kernel, name, outs, operands, anywhere, any_outs, scratch):
    vmem = pl.BlockSpec(memory_space=pltpu.VMEM)
    any_space = pl.BlockSpec(memory_space=pl.ANY)
    return pl.pallas_call(
        kernel,
        out_shape=[jax.ShapeDtypeStruct(shape, dtype) for shape, dtype in outs],
        in_specs=[any_space if index in anywhere else vmem for index in range(len(operands))],
        out_specs=[any_space if index in any_outs else vmem for index in range(len(outs))],
        scratch_shapes=scratch,
        compiler_params=pltpu.CompilerParams(vmem_limit_bytes=VMEM_BYTES),
        cost_estimate=pl.CostEstimate(
            flops=COSTS[name] * 10**9, bytes_accessed=COSTS[name] * 10**6, transcendentals=0
        ),
        name=name,
    )(*operands)


def mixer_outs(rows, width, length, quarter):
    block = width // BLOCKS
    return [
        ((rows, width), F32),
        ((rows, width), F32),
        ((8, 4 * quarter, width), BF16),
        ((16, width), F32),
        ((3, length, width), F32),
        ((length, 2 * width), F32),
        ((4, length, length), F32),
        ((rows, width), BF16),
        ((2, BLOCKS, rows, block), BF16),
        ((3, rows, width), BF16),
        ((rows, width), BF16),
        ((BLOCKS, rows, block), BF16),
    ]


def glu_outs(rows, width):
    return [
        ((rows, width), F32),
        ((rows, width), BF16),
        ((2, BLOCKS, rows, width), BF16),
        ((2, BLOCKS, rows, width), BF16),
        ((BLOCKS, rows, width), BF16),
        ((BLOCKS, rows, width // BLOCKS), BF16),
    ]


def glu_middle_kernel(hidden, table, mix, cotangent, pieces, *refs):
    output, result, norm_out, mix_grad, glu_grad = refs[:5]
    saved, refs = refs[5 : 5 + GLU_OUTS], refs[5 + GLU_OUTS :]
    left, right, parts, low, back, sems, out_sems = refs
    glu_forward_kernel(hidden, table, mix, pieces, *saved, left, right, parts, sems)
    output[...] = saved[0][...].astype(BF16)
    outs = (result, norm_out, mix_grad, glu_grad)
    scratch = (left, right, low, back, out_sems)
    glu_backward_kernel(
        ([[]] * BLOCKS, []), cotangent, hidden, table, mix, *saved[1:], pieces, *outs, *scratch
    )


def glu_middle(hidden, table, mix, cotangent, pieces):
    rows, width = hidden.shape
    block = width // BLOCKS
    outs = [
        ((rows, width), BF16),
        ((rows, width), F32),
        ((8, width), F32),
        ((6, BLOCKS, block, block), BF16),
        (pieces.shape, BF16),
    ]
    return call(
        glu_middle_kernel,
        "glu_middle",
        outs,
        (hidden, table, mix, cotangent, pieces),
        (4,),
        (4,),
        [pltpu.VMEM(shape, dtype) for shape, dtype in glu_outs(rows, width)]
        + [
            pltpu.VMEM((2, BLOCKS, width, width), BF16),
            pltpu.VMEM((2, width, width), BF16),
            pltpu.VMEM((BLOCKS, rows, block), F32),
            pltpu.VMEM((BLOCKS, rows, block), BF16),
            pltpu.VMEM((2, BLOCKS, rows, width), BF16),
            pltpu.SemaphoreType.DMA((64,)),
            pltpu.SemaphoreType.DMA((64,)),
        ],
    )


def glu_backward_lean(tick, arrays, scratch, sems):
    grad, table, mix, hidden, normed, down, norm_out, mix_grad = arrays[:8]
    middle, branch, glu, pieces, glu_grad = arrays[8:]
    middle_in, branch_in, glu_in, left, right, low, total = scratch
    rows, width = hidden.shape
    block = width // BLOCKS
    piece_sems, save_sems, out_sems = sems
    whole = LeftSlots(left)
    lefts, rights = glu_moves(pieces, whole, right, piece_sems, False)
    left_writes, right_writes = glu_moves(glu_grad, whole, right, out_sems, True)

    def fetch(q):
        return save_all(
            [middle.at[:, q], branch.at[:, q], glu.at[q]],
            [middle_in, branch_in, glu_in],
            save_sems,
            3 * q,
        )

    start_all(rights)
    start_all(lefts[0])
    coming = fetch(0)
    half = grad[...].astype(BF16)
    backs = []
    for b in range(BLOCKS):
        part = columns(half, b, block)
        mix_grad[1, b] = dot_rows(down[b], part).astype(BF16)
        backs.append(dot_columns(part, factor(mix, block // 2, 2, b)))
    backs = shuffled(backs)
    for q in range(BLOCKS):
        low[q] = backs[q].astype(BF16)
    total[...] = jnp.zeros_like(total)
    wait_all(rights)
    for q in range(BLOCKS):
        if q >= 1:
            tick(q)
        if q + 1 < BLOCKS:
            if q >= 1:
                wait_all(left_writes[q - 1])
            start_all(lefts[q + 1])
        wait_all(coming)
        wait_all(lefts[q])
        step = low[q]
        product = dot_rows(glu_in[...], step).astype(BF16)
        for index in range(BLOCKS):
            mix_grad[2 + index, q] = product[index * block : (index + 1) * block]
        down_block = down_factor(mix, 7 * block // 6, q)
        size = rows // 3
        for part in range(3):
            span = slice(part * size, (part + 1) * size)
            grad_glu = dot_columns(step[span], down_block)
            upper = branch_in[0, span].astype(F32)
            gate = branch_in[1, span].astype(F32)
            rise, density = cell(gate)
            branch_in[0, span] = (grad_glu * gate * rise).astype(BF16)
            branch_in[1, span] = (grad_glu * upper * (rise + gate * density)).astype(BF16)
        for u in range(2):
            term = branch_in[u]
            wide = dot_columns(term, left[q % 2, u]).astype(BF16)
            left[q % 2, u] = dot_rows(middle_in[u], term).astype(BF16)
            here = slice(q * block, (q + 1) * block)
            for b in range(BLOCKS):
                span = slice(b * block, (b + 1) * block)
                chunk = columns(wide, b, block)
                total[b] += dot_columns(chunk, right[u, span, here])
                right[u, span, here] = dot_rows(normed[:, span], chunk).astype(BF16)
        start_all(left_writes[q])
        if q + 1 < BLOCKS:
            coming = fetch(q + 1)
    start_all(right_writes)
    through, gain, bias = norm_backward(
        jnp.concatenate([total[b] for b in range(BLOCKS)], axis=1), hidden[...], table[1:2]
    )
    grad[...] = grad[...] + through
    norm_out[0:1] = gain
    norm_out[1:2] = bias
    for q in (BLOCKS - 2, BLOCKS - 1):
        wait_all(left_writes[q])
    wait_all(right_writes)


class LeftSlots:
    def __init__(self, slots):
        self.slots = slots
        self.shape = (slots.shape[1], BLOCKS) + slots.shape[2:]

    @property
    def at(self):
        return self

    def __getitem__(self, index):
        u, q, rows = index
        return self.slots.at[q % 2, u, rows]


PEERS = ((1, 0, 0, 0), (2, 0, 0, 0), (3, 0, 0, 0), (0, 1, 0, 0), (0, 0, 1, 0), (0, 0, 0, 1))
ALONG_X, ALONG_Y, ACROSS = PEERS[3], PEERS[4], PEERS[5]


def peer(distance, dx, dy, dc):
    z, x, y, c = place()
    return (2 * relative(z, distance) + flip(x, dx), 2 * flip(y, dy) + flip(c, dc))


def greet():
    barrier = pltpu.get_barrier_semaphore()
    for target in PEERS:
        pl.semaphore_signal(
            barrier, inc=1, device_id=peer(*target), device_id_type=pl.DeviceIdType.MESH
        )
    pl.semaphore_wait(barrier, len(PEERS))


class Mail:
    def __init__(self, sent, received):
        self.sent, self.received, self.copies, self.settled = sent, received, [], []

    def send(self, source, target, to):
        index = len(self.copies)
        copy = pltpu.make_async_remote_copy(
            src_ref=source,
            dst_ref=target,
            send_sem=self.sent.at[index],
            recv_sem=self.received.at[index],
            device_id=peer(*to),
            device_id_type=pl.DeviceIdType.MESH,
        )
        copy.start()
        self.copies.append(copy)
        return copy

    def settle(self, copy):
        copy.wait_send()
        self.settled.append(copy)

    def finish(self):
        for copy in self.copies:
            if not any(copy is other for other in self.settled):
                copy.wait_send()


MIXER_BACK = 18
GATHER_COPIES = 12


def gather_steps(mail, own, pieces, rows):
    view = lambda core, dx, dy, first, count: pieces.at[core, dx, dy, pl.ds(first, count), rows]
    along_z = [
        mail.send(own, pieces.at[0, 0, 0, distance, rows], PEERS[distance - 1])
        for distance in (1, 2, 3)
    ]
    yield
    for copy in along_z:
        copy.wait_recv()
    along_x = mail.send(view(0, 0, 0, 0, 4), view(0, 1, 0, 0, 4), ALONG_X)
    along_y = mail.send(view(0, 0, 0, 0, 4), view(0, 0, 1, 0, 4), ALONG_Y)
    across = [mail.send(view(0, 0, 0, 0, 4), view(1, 0, 0, 0, 4), ACROSS)]
    yield
    along_y.wait_recv()
    low = mail.send(view(0, 0, 1, 0, 2), view(0, 1, 1, 0, 2), ALONG_X)
    across.append(mail.send(view(0, 0, 1, 0, 4), view(1, 0, 1, 0, 4), ACROSS))
    along_x.wait_recv()
    high = mail.send(view(0, 1, 0, 2, 2), view(0, 1, 1, 2, 2), ALONG_Y)
    across.append(mail.send(view(0, 1, 0, 0, 4), view(1, 1, 0, 0, 4), ACROSS))
    yield
    low.wait_recv()
    across.append(mail.send(view(0, 1, 1, 0, 2), view(1, 1, 1, 0, 2), ACROSS))
    high.wait_recv()
    across.append(mail.send(view(0, 1, 1, 2, 2), view(1, 1, 1, 2, 2), ACROSS))
    yield
    for copy in across:
        copy.wait_recv()
    yield


def rounds(starts):
    running = []
    waiting = list(starts)
    while waiting or running:
        if waiting:
            running.append(waiting.pop(0)())
        for chunk in reversed(list(running)):
            try:
                next(chunk)
            except StopIteration:
                running.remove(chunk)
        yield


def pipeline(starts, between):
    for number, unused in enumerate(rounds(starts)):
        if number in between:
            between[number]()


def save_all(sources, targets, sems, first):
    copies = [
        pltpu.make_async_copy(source, target, sems.at[first + index])
        for index, (source, target) in enumerate(zip(sources, targets))
    ]
    start_all(copies)
    return copies


def forward_kernel(counts, *refs):
    groups = len(counts)
    owns, refs = refs[:groups], refs[groups:]
    hidden_in, marked, live, waves, features = refs[:5]
    pieces, refs = refs[5 : 5 + groups], refs[5 + groups :]
    first_outs, refs = refs[:MIXER_OUTS], refs[MIXER_OUTS:]
    glu_outs, refs = refs[:GLU_OUTS], refs[GLU_OUTS:]
    second_outs, refs = refs[:MIXER_OUTS], refs[MIXER_OUTS:]
    mixer, refs = refs[:MIXER_OUTS], refs[MIXER_OUTS:]
    glu, refs = refs[:GLU_OUTS], refs[GLU_OUTS:]
    staged, refs = refs[:groups], refs[groups:]
    left, right, parts, sent, received, local, loads = refs
    mail = Mail(sent, received)
    copies = [
        pltpu.make_async_copy(own, stage, local.at[index])
        for index, (own, stage) in enumerate(zip(owns, staged))
    ]
    start_all(copies)
    greet()
    starts = []
    for index, count in enumerate(counts):
        size = owns[index].shape[0] // count
        for part in range(count):
            rows = pl.ds(part * size, size)
            starts.append(
                partial(gather_steps, mail, owns[index].at[rows], pieces[index], rows)
            )
    wait_all(copies)
    own_copies = save_all(
        staged, [array.at[0, 0, 0, 0] for array in pieces], local, groups
    )
    saves = []

    def store_own():
        wait_all(own_copies)

    def first_mixer():
        mixer_forward_kernel(
            True, hidden_in, marked, live, waves, features, pieces[0], *mixer, loads
        )
        saves.extend(save_all(mixer, first_outs, local, 2 * groups))

    def first_glu():
        glu_forward_kernel(
            mixer[0], mixer[3], mixer[2], pieces[1], *glu, left, right, parts, loads
        )
        saves.extend(save_all(glu, glu_outs, local, 2 * groups + MIXER_OUTS))

    def second_mixer():
        wait_all(saves[:MIXER_OUTS])
        mixer_forward_kernel(
            False, glu[0], marked, live, waves, features, pieces[2], *mixer, loads
        )
        saves.extend(save_all(mixer, second_outs, local, 2 * groups + MIXER_OUTS + GLU_OUTS))

    ready = [sum(counts[: index + 1]) + 3 for index in range(3)]
    pipeline(
        starts, {0: store_own, ready[0]: first_mixer, ready[1]: first_glu, ready[2]: second_mixer}
    )
    wait_all(saves[MIXER_OUTS:])
    mail.finish()


def forward(quarters, counts, hidden, marked, live, waves, features, number):
    rows, width = hidden.shape
    groups = len(counts)
    anywhere = pl.BlockSpec(memory_space=pl.ANY)
    vmem = pl.BlockSpec(memory_space=pltpu.VMEM)
    total = GATHER_COPIES * sum(counts)
    mixer = mixer_outs(rows, width, waves.shape[2], quarters[0].shape[0])
    glu = glu_outs(rows, width)
    outs = [((2, 2, 2, 4) + quarter.shape, BF16) for quarter in quarters] + mixer + glu + mixer
    block = width // BLOCKS
    result = pl.pallas_call(
        partial(forward_kernel, counts),
        out_shape=[jax.ShapeDtypeStruct(shape, dtype) for shape, dtype in outs],
        in_specs=[anywhere] * groups + [vmem] * 5,
        out_specs=[anywhere] * len(outs),
        scratch_shapes=[pltpu.VMEM(shape, dtype) for shape, dtype in mixer + glu]
        + [pltpu.VMEM(quarter.shape, BF16) for quarter in quarters]
        + [
            pltpu.VMEM((2, BLOCKS, width, width), BF16),
            pltpu.VMEM((2, width, width), BF16),
            pltpu.VMEM((BLOCKS, rows, block), F32),
            pltpu.SemaphoreType.DMA((total,)),
            pltpu.SemaphoreType.DMA((total,)),
            pltpu.SemaphoreType.DMA((2 * groups + 2 * MIXER_OUTS + GLU_OUTS,)),
            pltpu.SemaphoreType.DMA((64,)),
        ],
        compiler_params=pltpu.CompilerParams(
            collective_id=number, has_side_effects=True, vmem_limit_bytes=VMEM_BYTES
        ),
        name="forward",
    )(*quarters, hidden, marked, live, waves, features)
    pieces, result = result[:groups], result[groups:]
    return (
        pieces,
        result[:MIXER_OUTS],
        result[MIXER_OUTS : MIXER_OUTS + GLU_OUTS],
        result[MIXER_OUTS + GLU_OUTS :],
    )


SCATTER_COPIES = 11
SLOTS = 3


def scatter_steps(mail, local, number, grads, landing, rows, result, spots, users, buffers):
    slots, other, pairs, low_landing, high_landing, three, four, own, last = buffers
    size = own.shape[0]
    slot = number % SLOTS
    first = slots.at[slot, :, :, :, pl.ds(0, size)]
    other = other.at[:, :, :, pl.ds(0, size)]
    split = 2 + number % 2
    two_x = pairs.at[slot, :, pl.ds(0, split), pl.ds(0, size)]
    two_y = pairs.at[slot, :, pl.ds(split, 4 - split), pl.ds(0, size)]
    landed = landing.at[:, :, :, rows]
    x_core = mail.send(grads.at[1, :, :, :, rows], landed, ACROSS)
    for copy in users.pop(slot, ()):
        mail.settle(copy)
    load = pltpu.make_async_copy(grads.at[0, :, :, :, rows], first, local.at[0])
    load.start()
    yield
    x_core.wait_recv()
    fetch = pltpu.make_async_copy(landed, other, local.at[3])
    fetch.start()
    load.wait()
    fetch.wait()
    for dx in range(2):
        for dy in range(2):
            first[dx, dy] += other[dx, dy]
    low = mail.send(first.at[1, :, pl.ds(0, split)], low_landing, ALONG_X)
    high = mail.send(first.at[:, 1, pl.ds(split, 4 - split)], high_landing, ALONG_Y)
    users[slot] = [low, high]
    yield
    low.wait_recv()
    fetch = pltpu.make_async_copy(low_landing, two_x, local.at[4])
    fetch.start()
    high.wait_recv()
    fetch_too = pltpu.make_async_copy(high_landing, two_y, local.at[5])
    fetch_too.start()
    fetch.wait()
    for dy in (1, 0):
        two_x[dy] += first[0, dy, 0:split]
        if dy == 1:
            low = mail.send(two_x.at[1], three.at[pl.ds(0, split)], ALONG_Y)
    fetch_too.wait()
    for dx in (1, 0):
        two_y[dx] += first[dx, 0, split:4]
        if dx == 1:
            high = mail.send(two_y.at[1], three.at[pl.ds(split, 4 - split)], ALONG_X)
    users[slot] += [low, high]
    yield
    low.wait_recv()
    three[0:split] += two_x[0]
    along_z = [mail.send(three.at[d], four.at[d - 1], PEERS[d - 1]) for d in range(1, split)]
    high.wait_recv()
    three[split:4] += two_y[0]
    along_z += [mail.send(three.at[d], four.at[d - 1], PEERS[d - 1]) for d in range(split, 4)]
    yield
    total = three[0].astype(F32)
    for index, copy in enumerate(along_z):
        copy.wait_recv()
        total = total + four[index].astype(F32)
    own[...] = total.astype(BF16)
    mine, theirs = spots
    across = [mail.send(own, result.at[mine, rows], ACROSS)]
    along_y = mail.send(own, last, ALONG_Y)
    keep = pltpu.make_async_copy(own, result.at[mine, rows], local.at[1])
    keep.start()
    yield
    along_y.wait_recv()
    across.append(mail.send(last, result.at[theirs, rows], ACROSS))
    keep_too = pltpu.make_async_copy(last, result.at[theirs, rows], local.at[2])
    keep_too.start()
    yield
    for copy in across:
        copy.wait_recv()
    keep.wait()
    keep_too.wait()
    yield


def scatter_buffers(size, width):
    return [
        pltpu.VMEM((4, size, width), BF16),
        pltpu.VMEM((3, size, width), BF16),
        pltpu.VMEM((size, width), BF16),
        pltpu.VMEM((size, width), BF16),
    ]


COMMON, MADE = (2, 3, 4, 5), (0, 16, 17)


def backward_kernel(parts, *refs):
    take = lambda count: (refs[:count], refs[count:])
    groups = len(parts)
    chunks = sum(len(part) for part in parts)
    (glu_two,), refs = take(1)
    second, refs = take(MIXER_BACK)
    others = [index for index in range(MIXER_BACK) if index not in COMMON + MADE]
    first, refs = take(len(others))
    glu_fixed, refs = take(3)
    glu_saved, refs = take(4)
    (result, mix_two, glu_one, mix_one), refs = take(4)
    results, refs = take(groups)
    landings, refs = take(groups)
    pair_landings, refs = take(2 * chunks)
    inner, refs = take(MIXER_BACK)
    scratch, refs = take(4)
    fixed, refs = take(3)
    lean, refs = take(7)
    (sent, received, local, loads, outs, slots, other, pairs), refs = take(8)
    buffers = refs
    grads = (glu_two, mix_two, glu_one, mix_one)
    fetched = save_all(second, inner, loads, 0)
    fixed_copies = save_all(glu_fixed, fixed, loads, MIXER_BACK)
    mail = Mail(sent, received)
    unused, unused, y, c = place()
    spots = (2 * y + c, 2 * (1 - y) + c)
    greet()
    users = {}
    starts = []
    for index, sizes in enumerate(parts):
        row = 0
        for size in sizes:
            number = len(starts)
            own = (slots, other, pairs) + tuple(pair_landings[2 * number : 2 * number + 2])
            starts.append(
                partial(
                    scatter_steps,
                    mail,
                    local.at[number],
                    number,
                    grads[index],
                    landings[index],
                    pl.ds(row, size),
                    results[index],
                    spots,
                    users,
                    own + tuple(buffers[4 * number : 4 * number + 4]),
                )
            )
            row += size
    running = rounds(starts)
    done = [0]

    def turn(count):
        for unused in range(count):
            next(running, None)
            done[0] += 1

    turn(2)
    wait_all(fetched)
    mixer_backward_kernel(
        False, lambda part: turn(part == 1), *inner, inner[0], mix_two, *scratch, outs
    )
    fetched = save_all(first, [inner[index] for index in others], loads, 0)
    turn(1)
    wait_all(fetched + fixed_copies)
    hidden, normed, down = fixed
    middle, branch, glu, pieces = glu_saved
    arrays = (inner[0], inner[7], inner[6], hidden, normed, down, inner[16], inner[17])
    glu_backward_lean(
        lambda part: turn(1),
        arrays + (middle, branch, glu, pieces, glu_one),
        lean,
        (loads.at[pl.ds(0, 64)], loads.at[pl.ds(64, 12)], outs),
    )
    assert done[0] <= len(parts[0]) + len(parts[1])
    turn(1)
    mixer_backward_kernel(
        True, lambda part: turn(1), *inner, inner[0], mix_one, *scratch, outs
    )
    assert done[0] <= chunks - len(parts[3])
    saves = save_all([inner[0]], [result], loads, 0)
    for unused in running:
        pass
    wait_all(saves)
    mail.finish()


def backward(glu_two, parts, second, first, glu_saved, number):
    anywhere = pl.BlockSpec(memory_space=pl.ANY)
    chunks = sum(len(part) for part in parts)
    rows, width = second[0].shape
    block = width // BLOCKS
    mix = second[6]
    length = second[4].shape[2]
    mix_shape = (2, 2, 2, 4, mix.shape[1] // 4, width)
    shapes = [glu_two.shape, mix_shape, glu_two.shape, mix_shape]
    sizes = [size for part in parts for size in part]
    largest = max(sizes)
    buffers, pair_landings = [], []
    for index, size in enumerate(sizes):
        buffers += scatter_buffers(size, width)
        split = 2 + index % 2
        pair_landings += [((2, count, size, width), BF16) for count in (split, 4 - split)]
    total = SCATTER_COPIES * chunks
    outs = (
        [((rows, width), F32)]
        + [(shape, BF16) for shape in shapes[1:]]
        + [((4,) + shape[4:], BF16) for shape in shapes]
        + [(shape[1:], BF16) for shape in shapes]
        + pair_landings
    )
    others = [index for index in range(MIXER_BACK) if index not in COMMON + MADE]
    hidden, normed, middle, branch, glu, down, pieces = glu_saved
    operands = (glu_two,) + tuple(second) + tuple(first[index] for index in others)
    operands += (hidden, normed, down, middle, branch, glu, pieces)
    results = pl.pallas_call(
        partial(backward_kernel, parts),
        out_shape=[jax.ShapeDtypeStruct(shape, dtype) for shape, dtype in outs],
        in_specs=[anywhere] * len(operands),
        out_specs=[anywhere] * len(outs),
        scratch_shapes=[pltpu.VMEM(array.shape, array.dtype) for array in second]
        + [
            pltpu.VMEM(mix.shape, BF16),
            pltpu.VMEM((3, length, width), F32),
            pltpu.VMEM((2, rows, width), F32),
            pltpu.VMEM((16, width), F32),
            pltpu.VMEM(hidden.shape, F32),
            pltpu.VMEM(normed.shape, BF16),
            pltpu.VMEM(down.shape, BF16),
            pltpu.VMEM((2, rows, width), BF16),
            pltpu.VMEM((2, rows, width), BF16),
            pltpu.VMEM((rows, width), BF16),
            pltpu.VMEM((2, 2, width, width), BF16),
            pltpu.VMEM((2, width, width), BF16),
            pltpu.VMEM((BLOCKS, rows, block), BF16),
            pltpu.VMEM((BLOCKS, rows, block), F32),
            pltpu.SemaphoreType.DMA((total,)),
            pltpu.SemaphoreType.DMA((total,)),
            pltpu.SemaphoreType.DMA((chunks, 6)),
            pltpu.SemaphoreType.DMA((80,)),
            pltpu.SemaphoreType.DMA((64,)),
            pltpu.VMEM((SLOTS, 2, 2, 4, largest, width), BF16),
            pltpu.VMEM((2, 2, 4, largest, width), BF16),
            pltpu.VMEM((SLOTS, 2, 4, largest, width), BF16),
        ]
        + buffers,
        compiler_params=pltpu.CompilerParams(
            collective_id=number, has_side_effects=True, vmem_limit_bytes=VMEM_BYTES
        ),
        name="backward",
    )(*operands)
    return results[0], results[4 : 4 + len(parts)]


def prepare_kernel(lengths, positions, mask_vector, *refs):
    members, refs = refs[:18], refs[18:]
    quarters, (live, marked, pack) = refs[: 2 * LAYERS], refs[2 * LAYERS :]
    unused, unused, y, c = place()
    rows, block = members[2].shape[2:]
    order = members[10].shape[2]
    step = members[9].shape[1]
    features = members[6].shape[1]
    third, fourth = 2 * rows, rows + order
    size = pack.shape[0] // 4
    length = live.shape[0] // positions.shape[0]
    place_of = lax.broadcasted_iota(jnp.int32, (length, positions.shape[1]), 0)
    for s in range(positions.shape[0]):
        inside = slice(s * length, (s + 1) * length)
        found = jnp.where(place_of == positions[s : s + 1], 1.0, 0.0)
        marked[inside] = jnp.max(found, axis=1, keepdims=True)
        live[inside] = jnp.where(place_of[:, :1] < lengths[s], 1.0, 0.0)
    flat = {index: members[index][...].astype(F32) for index in (5, 7, 9, 11)}
    for layer in range(LAYERS):
        for u in range(2):
            pack[:rows, u * block : (u + 1) * block] = members[2][layer, u]
            pack[:rows, (2 + u) * block : (3 + u) * block] = members[3][layer, u]
        pack[rows:third, :block] = members[12][layer]
        pack[rows:third, block : 2 * block] = members[13][layer]
        pack[rows:third, 2 * block : 3 * block] = members[17][layer]
        pack[third:fourth] = jnp.zeros((fourth - third, pack.shape[1]), BF16)
        pack[rows:fourth, 3 * block :] = members[10][layer].astype(F32).T.astype(BF16)
        top = [members[index][layer].astype(F32) for index in (0, 1, 4)]
        top += [flat[5][layer : layer + 1], flat[11][layer : layer + 1]]
        top += [mask_vector[...].astype(F32), jnp.zeros((6, rows), F32)]
        pack[third : third + 16, block : block + rows] = jnp.concatenate(top, axis=0).astype(BF16)
        pack[third : third + step, 2 * block : 2 * block + order] = members[8][layer]
        low = [members[6][layer].astype(F32), jnp.zeros((8 - features, step), F32)]
        low += [flat[7][layer : layer + 1], flat[9][layer : layer + 1], jnp.zeros((6, step), F32)]
        pack[third + 16 : third + 32, 2 * block : 2 * block + step] = jnp.concatenate(
            low, axis=0
        ).astype(BF16)
        down = members[16][layer].astype(F32).T.astype(BF16)
        for index in range(4):
            pack[fourth:, index * block : (index + 1) * block] = down[
                index * rows : (index + 1) * rows
            ]
        first = pl.multiple_of((2 * y + c) * size, 16)
        quarters[2 * layer][...] = pack[pl.ds(first, size)]
        start = 0
        for index in (15, 14):
            count = members[index].shape[2] // 2
            first = pl.multiple_of(c * count, 16)
            quarters[2 * layer + 1][start : start + count] = members[index][
                layer, y, pl.ds(first, count)
            ]
            start += count


def prepare(lengths, positions, mask_vector, shards, rows):
    members = list(shards)
    for index in (10, 16):
        members[index] = jnp.swapaxes(members[index], 1, 2)
    width = shards[15].shape[3]
    tall, short = shards[15].shape[2] // 2, shards[14].shape[2] // 2
    height = 2 * shards[2].shape[2] + shards[10].shape[1]
    outs = [((height // 4, width), BF16), ((tall + short, width), BF16)] * LAYERS
    outs += [((rows, 1), F32)] * 2
    vmem = pl.BlockSpec(memory_space=pltpu.VMEM)
    result = pl.pallas_call(
        prepare_kernel,
        out_shape=[jax.ShapeDtypeStruct(shape, dtype) for shape, dtype in outs],
        in_specs=[pl.BlockSpec(memory_space=pltpu.SMEM)] + [vmem] * (2 + len(members)),
        out_specs=[vmem] * len(outs),
        scratch_shapes=[pltpu.VMEM((height, width), BF16)],
        compiler_params=pltpu.CompilerParams(vmem_limit_bytes=VMEM_BYTES),
        name="prepare",
    )(lengths, positions, mask_vector[None], *members)
    return result[: 2 * LAYERS], result[2 * LAYERS], result[2 * LAYERS + 1]


GRADS = (0, 1, 2, 3, 4, 5, 6, 7, 8, 9, 10, 12, 13, 14, 15, 16, 17)
SHARD_AXIS = (1, 1, 1, 1, 1, 0, 1, 0, 0, 0, 1, 0, 0, 0, 1, 1, 0, 0)


def gather_plain(shards, layer_index):
    return tuple(
        lax.all_gather(shards[index][layer_index], "wide", axis=SHARD_AXIS[index], tiled=True)
        for index in range(18)
    )


def scatter_plain(grads, mask_term):
    terms = list(grads) + ([] if mask_term is None else [mask_term])
    axes = [SHARD_AXIS[index] for index in GRADS] + [0]
    return narrow_total(
        [
            lax.psum_scatter(term, "wide", scatter_dimension=axis, tiled=True)
            for term, axis in zip(terms, axes)
        ]
    )


def wave_table(length):
    frequency = np.arange(length)[:, None]
    places = np.arange(length)[None, :]
    angles = (frequency * places % (2 * length)) * (math.pi / length)
    turned = -np.sin(angles)
    turned[0] = np.where(np.arange(length) % 2 == 0, 1.0, -1.0)
    table = jnp.asarray(np.concatenate([np.cos(angles), turned]), F32)
    high = table.astype(BF16)
    return jnp.stack([high, (table - high.astype(F32)).astype(BF16)])


def staged_body(shards, mask_vector, hidden_in, cotangent, seq_lengths, mask_positions):
    rows = hidden_in.shape[0]
    length = rows // seq_lengths.shape[0]
    waves = wave_table(length)
    features = jnp.pad(position_features(length), ((0, 0), (0, 8 - EMB)))
    quarters, live, marked = prepare(seq_lengths, mask_positions, mask_vector, shards, rows)
    pieces, mixed_one, second, mixed_two = forward(
        quarters, (1, 3) * LAYERS, hidden_in, marked, live, waves, features, 1
    )
    output, grad, norm_two, down_grads, glu_grads_two = glu_middle(
        mixed_two[0], mixed_two[3], mixed_two[2], cotangent, pieces[3]
    )
    common = (marked, live, waves, features)
    mix_rows = mixed_two[2].shape[1] // 4
    glu_rows = glu_grads_two.shape[4]
    tall = 16 * (glu_rows // 80)
    glu_parts = (tall,) * (glu_rows // tall)
    mix_parts = (tall, mix_rows - tall)
    arrange = lambda made, mixed: (made[0], mixed[1], *common) + tuple(mixed[2:]) + made[1:]
    made = (grad, norm_two, down_grads)
    grad, sums = backward(
        glu_grads_two,
        (glu_parts, mix_parts) * LAYERS,
        arrange(made, mixed_two),
        arrange(made, mixed_one),
        (mixed_one[0],) + tuple(second[1:]) + (pieces[1],),
        2,
    )
    sums = (sums[3], sums[2], sums[1], sums[0])
    found = finish(sums, shards)
    return output, grad, found[-1].reshape(-1), found[:-1]


def finish_kernel(*refs):
    sums, outs = refs[: 2 * LAYERS], refs[2 * LAYERS :]
    found = dict(zip(GRADS, outs))
    mask = outs[-1]
    rows, block = found[2].shape[2:]
    order = found[10].shape[2]
    features, step = found[6].shape[0], found[6].shape[2]
    third, fourth = 2 * rows, rows + order
    for layer in range(LAYERS):
        mix, glu = sums[2 * layer : 2 * layer + 2]
        pack = jnp.concatenate([mix[index] for index in range(4)], axis=0).astype(F32)
        cut = lambda low, high, k: pack[low:high, k * block : (k + 1) * block]
        table = pack[third : third + 16, block : block + rows]
        smalls = pack[third + 16 : third + 32, 2 * block : 2 * block + step]
        for u in range(2):
            found[0][layer, u : u + 1] = table[u : u + 1]
            found[1][layer, u : u + 1] = table[2 + u : 3 + u]
            found[2][layer, u] = cut(0, rows, u)
            found[3][layer, u] = cut(0, rows, 2 + u)
        for index in range(3):
            found[4][index, layer : layer + 1] = table[4 + index : 5 + index]
        found[5][layer : layer + 1] = table[7:8]
        for index in range(features):
            found[6][index, layer : layer + 1] = smalls[index : index + 1]
        found[7][layer : layer + 1] = smalls[8:9]
        found[8][layer] = pack[third : third + step, 2 * block : 2 * block + order]
        found[9][layer : layer + 1] = smalls[9:10]
        found[10][layer] = cut(rows, fourth, 3).T
        found[12][layer] = cut(rows, third, 0)
        found[13][layer] = cut(rows, third, 1)
        found[16][layer] = jnp.concatenate(
            [cut(fourth, fourth + rows, index) for index in range(4)], axis=0
        ).T
        found[17][layer] = cut(rows, third, 2)
        if layer == 0:
            mask[...] = table[9:10]
        tall, short = found[15].shape[2] // 2, found[14].shape[2] // 2
        for u in range(2):
            for core in range(2):
                quarter = glu[2 * u + core].astype(F32)
                found[15][layer, u, core * tall : (core + 1) * tall] = quarter[:tall]
                found[14][layer, u, core * short : (core + 1) * short] = quarter[tall:]


TURNED = {4: (0, 1), 6: (0, 1), 10: (1, 2), 16: (1, 2)}


def finish(sums, shards):
    outs = []
    for index in GRADS:
        shape = list(shards[index].shape)
        for one, two in [TURNED[index]] if index in TURNED else []:
            shape[one], shape[two] = shape[two], shape[one]
        outs.append((tuple(shape), F32))
    outs.append(((1, shards[5].shape[1]), F32))
    found = call(finish_kernel, "finish", outs, tuple(sums), (), (), [])
    return [
        jnp.swapaxes(array, *TURNED[index]) if index in TURNED else array
        for index, array in zip(GRADS + (-1,), found)
    ]


def is_staged(shards, mesh_shape):
    short, block = shards[2].shape[2:]
    order, outs = shards[10].shape[1:]
    return (
        tuple(mesh_shape) == (8, 4)
        and short == 96
        and block == 192
        and order == 128
        and outs == block
        and shards[14].shape[2:] == (short, 8 * short)
        and shards[15].shape[2:] == (4 * short, 8 * short)
    )


def narrow_total(parts):
    flattened = jnp.concatenate([member.reshape(-1) for member in parts])
    summed = lax.psum(flattened.astype(jnp.bfloat16), "narrow").astype(jnp.float32)
    result = []
    offset = 0
    for member in parts:
        result.append(summed[offset : offset + member.size].reshape(member.shape))
        offset = offset + member.size
    return result


def plain_body(shards, mask_vector, hidden_in, cotangent, live_mask, marked):
    seq_count = live_mask.shape[0]
    mask_full = lax.all_gather(mask_vector, "wide", axis=0, tiled=True)
    weights = [gather_plain(shards, layer_index) for layer_index in range(LAYERS)]
    hidden = jnp.where(
        marked, mask_full.astype(jnp.float32)[None, :], hidden_in.astype(jnp.float32)
    )
    saved_layers = []
    for layer_index in range(LAYERS):
        hidden, saved = forward_layer(hidden, weights[layer_index], live_mask)
        saved_layers.append(saved)
    output = hidden.astype(jnp.bfloat16)
    share = 0.5 * seq_count
    grad_hidden = cotangent.astype(jnp.float32)
    layer_grads = [None] * LAYERS
    mask_grad = None
    for layer_index in reversed(range(LAYERS)):
        grad_hidden, grads = backward_layer(
            grad_hidden, weights[layer_index], saved_layers[layer_index], live_mask, share
        )
        if layer_index > 0:
            layer_grads[layer_index] = scatter_plain(grads, None)
        else:
            mask_term = jnp.sum(jnp.where(marked, grad_hidden, 0.0), axis=0)
            reduced = scatter_plain(grads, mask_term)
            layer_grads[0] = reduced[:-1]
            mask_grad = reduced[-1]
    grad_input = jnp.where(marked, 0.0, grad_hidden)
    final_grads = [
        jnp.stack([layer_grads[position][member_index] for position in range(LAYERS)])
        for member_index in range(17)
    ]
    return output, grad_input, mask_grad, final_grads


def body(
    mesh_shape,
    hidden_in,
    seq_lengths,
    mask_positions,
    mask_vector,
    cotangent,
    norm_gain,
    norm_bias,
    in_right,
    in_left,
    conv_taps,
    skip_bias,
    filter_in,
    filter_in_bias,
    filter_mid,
    filter_mid_bias,
    filter_out,
    decay_rates,
    out_right,
    out_left,
    glu_right,
    glu_left,
    down_right,
    down_left,
):
    row_count = hidden_in.shape[0]
    seq_count = seq_lengths.shape[0]
    length = row_count // seq_count
    places = jnp.arange(length, dtype=jnp.int32)
    live_mask = (places[None, :] < seq_lengths[:, None]).astype(jnp.float32)[:, :, None]
    marked = jnp.any(mask_positions[:, :, None] == places[None, None, :], axis=1).reshape(
        row_count, 1
    )
    shards = (
        norm_gain,
        norm_bias,
        in_right,
        in_left,
        conv_taps,
        skip_bias,
        filter_in,
        filter_in_bias,
        filter_mid,
        filter_mid_bias,
        filter_out,
        decay_rates,
        out_right,
        out_left,
        glu_right,
        glu_left,
        down_right,
        down_left,
    )
    if is_staged(shards, mesh_shape):
        output, grad_input, mask_grad, final_grads = staged_body(
            shards, mask_vector, hidden_in, cotangent, seq_lengths, mask_positions
        )
    else:
        output, grad_input, mask_grad, final_grads = plain_body(
            shards, mask_vector, hidden_in, cotangent, live_mask, marked
        )
    return (output, grad_input, mask_grad) + tuple(final_grads)


def solution(mesh):
    placed = (
        P(("wide", "narrow"), None),
        P(("wide", "narrow")),
        P(("wide", "narrow"), None),
        P("wide"),
        P(("wide", "narrow"), None),
        P(None, None, "wide"),
        P(None, None, "wide"),
        P(None, None, "wide", None),
        P(None, None, "wide", None),
        P(None, None, "wide"),
        P(None, "wide"),
        P(None, None, "wide"),
        P(None, "wide"),
        P(None, "wide", None),
        P(None, "wide"),
        P(None, None, "wide"),
        P(None, "wide"),
        P(None, "wide", None),
        P(None, "wide", None),
        P(None, None, "wide", None),
        P(None, None, "wide", None),
        P(None, "wide", None),
        P(None, "wide", None),
    )
    return jax.shard_map(
        partial(body, (mesh.shape["wide"], mesh.shape["narrow"])),
        mesh=mesh,
        in_specs=placed,
        out_specs=(
            P(("wide", "narrow"), None),
            P(("wide", "narrow"), None),
            P("wide"),
            P(None, None, "wide"),
            P(None, None, "wide"),
            P(None, None, "wide", None),
            P(None, None, "wide", None),
            P(None, None, "wide"),
            P(None, "wide"),
            P(None, None, "wide"),
            P(None, "wide"),
            P(None, "wide", None),
            P(None, "wide"),
            P(None, None, "wide"),
            P(None, "wide", None),
            P(None, "wide", None),
            P(None, None, "wide", None),
            P(None, None, "wide", None),
            P(None, "wide", None),
            P(None, "wide", None),
        ),
        check_vma=False,
    )
```

```python
from functools import partial
import math

import jax
import jax.numpy as jnp
import numpy as np
from jax import lax
from jax.experimental import pallas as pl
from jax.experimental.pallas import tpu as pltpu
from jax.sharding import PartitionSpec as P

BLOCKS = 4
EMB = 5
LAYERS = 2


EPSILON = 1e-05
highest_precision = lax.Precision.HIGHEST


def permute(values):
    array_shape = values.shape
    blocks = array_shape[-2]
    split_view = values.reshape(array_shape[:-1] + (blocks, array_shape[-1] // blocks))
    return jnp.swapaxes(split_view, -3, -2).reshape(array_shape)


def monarch_forward(inputs, right_factor, left_factor):
    row_count = inputs.shape[0]
    right_blocks = right_factor.reshape(BLOCKS, -1, right_factor.shape[-1])
    left_blocks = left_factor.reshape(BLOCKS, -1, left_factor.shape[-1])
    middle = jnp.einsum(
        "rbi,bio->rbo",
        inputs.reshape(row_count, BLOCKS, -1),
        right_blocks,
        preferred_element_type=jnp.float32,
    )
    middle = permute(middle).astype(jnp.bfloat16)
    output = jnp.einsum("rbi,bio->rbo", middle, left_blocks, preferred_element_type=jnp.float32)
    return (middle, output.reshape(row_count, -1))


def monarch_backward(inputs, middle, right_factor, left_factor, grad_output):
    row_count = inputs.shape[0]
    right_blocks = right_factor.reshape(BLOCKS, -1, right_factor.shape[-1])
    left_blocks = left_factor.reshape(BLOCKS, -1, left_factor.shape[-1])
    grad_low = grad_output.astype(jnp.bfloat16).reshape(row_count, BLOCKS, -1)
    grad_left = jnp.einsum("rbi,rbo->bio", middle, grad_low, preferred_element_type=jnp.float32)
    grad_middle = jnp.einsum(
        "rbo,bio->rbi", grad_low, left_blocks, preferred_element_type=jnp.float32
    )
    grad_middle = permute(grad_middle).astype(jnp.bfloat16)
    input_blocks = inputs.reshape(row_count, BLOCKS, -1)
    grad_right = jnp.einsum(
        "rbi,rbo->bio", input_blocks, grad_middle, preferred_element_type=jnp.float32
    )
    grad_inputs = jnp.einsum(
        "rbo,bio->rbi", grad_middle, right_blocks, preferred_element_type=jnp.float32
    )
    return (
        grad_inputs.reshape(row_count, -1),
        grad_right.reshape(right_factor.shape),
        grad_left.reshape(left_factor.shape),
    )


def layer_norm(values, norm_gain, norm_bias):
    average = jnp.mean(values, axis=-1, keepdims=True)
    centred = values - average
    variance = jnp.mean(centred * centred, axis=-1, keepdims=True)
    return centred * lax.rsqrt(variance + EPSILON) * norm_gain + norm_bias


def position_features(length):
    positions = jnp.arange(length, dtype=jnp.float32)
    fraction = positions / length
    features = [fraction]
    for band_index in range(1, (EMB - 1) // 2 + 1):
        features.append(jnp.cos(2.0 * math.pi * band_index * fraction))
        features.append(jnp.sin(2.0 * math.pi * band_index * fraction))
    return jnp.stack(features, axis=1)


def make_filter(
    filter_in, filter_in_bias, filter_mid, filter_mid_bias, filter_out, decay_rates, length
):
    embedding = position_features(length)
    first_hidden = jnp.sin(
        jnp.dot(embedding, filter_in, precision=highest_precision) + filter_in_bias
    )
    second = jnp.sin(
        jnp.dot(first_hidden, filter_mid, precision=highest_precision) + filter_mid_bias
    )
    kernel = jnp.dot(second, filter_out, precision=highest_precision)
    fraction = jnp.arange(length, dtype=jnp.float32)[:, None] / length
    both_rates = jnp.concatenate([decay_rates, decay_rates])
    return kernel * jnp.exp(-fraction * both_rates[None, :])


def short_convolution(signal_rows, conv_taps):
    padded = jnp.pad(signal_rows, ((0, 0), (2, 0), (0, 0)))
    return (
        conv_taps[0] * padded[:, :-2]
        + conv_taps[1] * padded[:, 1:-1]
        + conv_taps[2] * padded[:, 2:]
    )


def spectral_tables(length, span):
    padded_length = 2 * length
    frequency = jnp.arange(length + 1, dtype=jnp.int32)
    places = jnp.arange(span, dtype=jnp.int32)
    phase_index = frequency[:, None] * places[None, :] % padded_length
    angles = phase_index.astype(jnp.float32) * (2.0 * math.pi / padded_length)
    ends = (frequency == 0) | (frequency == length)
    weights = jnp.where(ends, 1.0, 2.0).astype(jnp.float32) / padded_length
    return (jnp.cos(angles), jnp.sin(angles), weights)


def circular_kernel(kernel):
    width = kernel.shape[1] // 2
    forward_part = kernel[:, :width]
    reverse_part = kernel[:, width:]
    first_row = forward_part[:1] + reverse_part[:1]
    spacer = jnp.zeros((1, width), jnp.float32)
    return jnp.concatenate(
        [first_row, forward_part[1:], spacer, jnp.flip(reverse_part[1:], axis=0)], axis=0
    )


def long_convolution(signal_rows, kernel):
    length = signal_rows.shape[1]
    cosine_lookup, sine_lookup, weights = spectral_tables(length, length)
    kernel_cosine, kernel_sine, unused = spectral_tables(length, 2 * length)
    circular = circular_kernel(kernel)
    real_signal = jnp.einsum("ik,hkm->him", cosine_lookup, signal_rows, precision=highest_precision)
    imaginary_signal = -jnp.einsum(
        "ik,hkm->him", sine_lookup, signal_rows, precision=highest_precision
    )
    kernel_real = jnp.dot(kernel_cosine, circular, precision=highest_precision)
    kernel_imaginary = -jnp.dot(kernel_sine, circular, precision=highest_precision)
    real_product = real_signal * kernel_real - imaginary_signal * kernel_imaginary
    imaginary_product = real_signal * kernel_imaginary + imaginary_signal * kernel_real
    inverse_cosine_table = cosine_lookup * weights[:, None]
    inverse_sine_table = sine_lookup * weights[:, None]
    return jnp.einsum(
        "hp,ihj->ipj", inverse_cosine_table, real_product, precision=highest_precision
    ) - jnp.einsum(
        "hp,ihj->ipj", inverse_sine_table, imaginary_product, precision=highest_precision
    )


def mixer_piece(
    value_path,
    gate_path,
    conv_taps,
    skip_bias,
    filter_in,
    filter_in_bias,
    filter_mid,
    filter_mid_bias,
    filter_out,
    decay_rates,
    live_mask,
    share,
):
    length = live_mask.shape[1]
    kernel = make_filter(
        filter_in, filter_in_bias, filter_mid, filter_mid_bias, filter_out, decay_rates, length
    )
    signal_rows = value_path.reshape(live_mask.shape[0], length, -1) * live_mask
    signal_rows = short_convolution(signal_rows, conv_taps) * live_mask
    mixed_signal = long_convolution(signal_rows, kernel) + signal_rows * skip_bias
    return (mixed_signal.reshape(value_path.shape) * gate_path, share * jnp.sum(kernel * kernel))


def glu_piece(upper_branch, gate_branch):
    return jax.nn.gelu(gate_branch, approximate=False) * upper_branch


def small_weights(layer_weights):
    return tuple(
        (layer_weights[position].astype(jnp.float32) for position in (4, 5, 6, 7, 8, 9, 10))
    )


def forward_layer(hidden, layer_weights, live_mask):
    (
        norm_gain,
        norm_bias,
        in_right,
        in_left,
        conv_taps,
        skip_bias,
        filter_in,
        filter_in_bias,
        filter_mid,
        filter_mid_bias,
        filter_out,
        decay_rates,
        out_right,
        out_left,
        glu_right,
        glu_left,
        down_right,
        down_left,
    ) = layer_weights
    gains = norm_gain.astype(jnp.float32)
    biases = norm_bias.astype(jnp.float32)
    small = small_weights(layer_weights)
    normed = layer_norm(hidden, gains[0], biases[0]).astype(jnp.bfloat16)
    middle_value, value_path = monarch_forward(normed, in_right[0], in_left[0])
    middle_gate, gate_path = monarch_forward(normed, in_right[1], in_left[1])
    mixed_signal, unused = mixer_piece(
        value_path,
        gate_path,
        small[0],
        small[1],
        small[2],
        small[3],
        small[4],
        small[5],
        small[6],
        decay_rates.astype(jnp.float32),
        live_mask,
        0.0,
    )
    mixed_signal = mixed_signal.astype(jnp.bfloat16)
    middle_out, branch = monarch_forward(mixed_signal, out_right, out_left)
    middle_hidden = hidden + branch
    normed_two = layer_norm(middle_hidden, gains[1], biases[1]).astype(jnp.bfloat16)
    middle_up, upper_branch = monarch_forward(normed_two, glu_right[0], glu_left[0])
    middle_glu, gate_branch = monarch_forward(normed_two, glu_right[1], glu_left[1])
    glu_hidden = glu_piece(upper_branch, gate_branch).astype(jnp.bfloat16)
    middle_down, branch_two = monarch_forward(glu_hidden, down_right, down_left)
    saved = (
        hidden,
        normed,
        middle_value,
        value_path,
        middle_gate,
        gate_path,
        mixed_signal,
        middle_out,
        middle_hidden,
        normed_two,
        middle_up,
        upper_branch,
        middle_glu,
        gate_branch,
        glu_hidden,
        middle_down,
    )
    return (middle_hidden + branch_two, saved)


def backward_layer(grad_hidden, layer_weights, saved, live_mask, share):
    (
        norm_gain,
        norm_bias,
        in_right,
        in_left,
        conv_taps,
        skip_bias,
        filter_in,
        filter_in_bias,
        filter_mid,
        filter_mid_bias,
        filter_out,
        decay_rates,
        out_right,
        out_left,
        glu_right,
        glu_left,
        down_right,
        down_left,
    ) = layer_weights
    (
        hidden,
        normed,
        middle_value,
        value_path,
        middle_gate,
        gate_path,
        mixed_signal,
        middle_out,
        middle_hidden,
        normed_two,
        middle_up,
        upper_branch,
        middle_glu,
        gate_branch,
        glu_hidden,
        middle_down,
    ) = saved
    gains = norm_gain.astype(jnp.float32)
    biases = norm_bias.astype(jnp.float32)
    small = small_weights(layer_weights)
    grad_glu, grad_down_right, grad_down_left = monarch_backward(
        glu_hidden, middle_down, down_right, down_left, grad_hidden
    )
    unused, glu_pull = jax.vjp(glu_piece, upper_branch, gate_branch)
    grad_upper, grad_gate = glu_pull(grad_glu)
    grad_normed_up, grad_right_up, grad_left_up = monarch_backward(
        normed_two, middle_up, glu_right[0], glu_left[0], grad_upper
    )
    grad_normed_gate, grad_right_gate, grad_left_gate = monarch_backward(
        normed_two, middle_glu, glu_right[1], glu_left[1], grad_gate
    )
    unused, norm_pull = jax.vjp(layer_norm, middle_hidden, gains[1], biases[1])
    grad_middle, grad_gain_two, grad_bias_two = norm_pull(grad_normed_up + grad_normed_gate)
    grad_middle = grad_middle + grad_hidden
    grad_mixed, grad_out_right, grad_out_left = monarch_backward(
        mixed_signal, middle_out, out_right, out_left, grad_middle
    )
    mixer_local = partial(
        mixer_piece, decay_rates=decay_rates.astype(jnp.float32), live_mask=live_mask, share=share
    )
    unused, mixer_pull = jax.vjp(
        mixer_local,
        value_path,
        gate_path,
        small[0],
        small[1],
        small[2],
        small[3],
        small[4],
        small[5],
        small[6],
    )
    mixer_grads = mixer_pull((grad_mixed, jnp.ones((), jnp.float32)))
    grad_normed_value, grad_right_value, grad_left_value = monarch_backward(
        normed, middle_value, in_right[0], in_left[0], mixer_grads[0]
    )
    grad_normed_path, grad_right_path, grad_left_path = monarch_backward(
        normed, middle_gate, in_right[1], in_left[1], mixer_grads[1]
    )
    unused, norm_pull_one = jax.vjp(layer_norm, hidden, gains[0], biases[0])
    grad_before, grad_gain_one, grad_bias_one = norm_pull_one(grad_normed_value + grad_normed_path)
    grads = (
        jnp.stack([grad_gain_one, grad_gain_two]),
        jnp.stack([grad_bias_one, grad_bias_two]),
        jnp.stack([grad_right_value, grad_right_path]),
        jnp.stack([grad_left_value, grad_left_path]),
        mixer_grads[2],
        mixer_grads[3],
        mixer_grads[4],
        mixer_grads[5],
        mixer_grads[6],
        mixer_grads[7],
        mixer_grads[8],
        grad_out_right,
        grad_out_left,
        jnp.stack([grad_right_up, grad_right_gate]),
        jnp.stack([grad_left_up, grad_left_gate]),
        grad_down_right,
        grad_down_left,
    )
    return (grad_before + grad_middle, grads)


F32 = jnp.float32
BF16 = jnp.bfloat16
VMEM_BYTES = 60 * 1024 * 1024


def dot(left, right):
    return jnp.dot(left, right, preferred_element_type=F32)


def dot_rows(left, right):
    return lax.dot_general(left, right, (((0,), (0,)), ((), ())), preferred_element_type=F32)


def dot_columns(left, right):
    return lax.dot_general(left, right, (((1,), (1,)), ((), ())), preferred_element_type=F32)


def exact(left, right, dims=(1, 0)):
    return lax.dot_general(
        left,
        right,
        (((dims[0],), (dims[1],)), ((), ())),
        precision=highest_precision,
        preferred_element_type=F32,
    )


def columns(values, index, width):
    return values[:, index * width : (index + 1) * width]


def shuffled(parts):
    chunk = parts[0].shape[1] // BLOCKS
    return [
        jnp.concatenate([columns(part, index, chunk) for part in parts], axis=1)
        for index in range(BLOCKS)
    ]


def normalised(values):
    average = jnp.mean(values, axis=-1, keepdims=True)
    centred = values - average
    variance = jnp.mean(centred * centred, axis=-1, keepdims=True)
    scale = lax.rsqrt(variance + EPSILON)
    return centred * scale, scale


def norm_backward(grad, hidden, gain):
    unit, scale = normalised(hidden)
    grad_gain = jnp.sum(grad * unit, axis=0, keepdims=True)
    grad_bias = jnp.sum(grad, axis=0, keepdims=True)
    scaled = grad * gain
    mean_one = jnp.mean(scaled, axis=-1, keepdims=True)
    mean_two = jnp.mean(scaled * unit, axis=-1, keepdims=True)
    return scale * (scaled - mean_one - unit * mean_two), grad_gain, grad_bias


def flip(bit, by):
    return 1 - bit if by else bit


def place():
    w = lax.axis_index("wide")
    n = lax.axis_index("narrow")
    return w // 2, w % 2, n // 2, n % 2


def relative(z, distance):
    high, low = z // 2, z % 2
    return 2 * flip(high, distance // 2) + flip(low, distance % 2)


def piece_copies(pieces, sems, targets_of):
    z, x, y, c = place()
    copies = []
    for core in range(2):
        for dx in range(2):
            for dy in range(2):
                for dz in range(4):
                    owner = (relative(z, dz), flip(x, dx), flip(y, dy), flip(c, core))
                    for row, target in targets_of(*owner):
                        view = pieces.at[core, dx, dy, dz, pl.ds(row, target.shape[0])]
                        copies.append(pltpu.make_async_copy(view, target, sems.at[len(copies)]))
    return copies


def grad_copies(result, sems, sources_of):
    z, x, y, c = place()
    copies = []
    for core in range(2):
        for dx in range(2):
            for dy in range(2):
                for dz in range(4):
                    owner = (relative(z, dz), flip(x, dx), flip(y, dy), flip(c, core))
                    for row, source in sources_of(*owner):
                        view = result.at[core, dx, dy, dz, pl.ds(row, source.shape[0])]
                        copies.append(pltpu.make_async_copy(source, view, sems.at[len(copies)]))
    return copies


def start_all(copies):
    for copy in copies:
        copy.start()


def wait_all(copies):
    for copy in copies:
        copy.wait()


def glu_moves(pieces, left, right, sems, out):
    z, x, y, c = place()
    tall, short = left.shape[2] // 4, right.shape[1] // 16
    lefts, rights = [[] for q in range(BLOCKS)], []
    count = 0
    for q in range(BLOCKS):
        for core in range(2):
            for dx in range(2):
                for dy in range(2):
                    u = flip(y, dy)
                    spot = 2 * flip(x, dx) + flip(c, core)
                    tall_row = pl.multiple_of(spot * tall, 16)
                    short_row = pl.multiple_of((4 * q + spot) * short, 16)
                    ends = (
                        (0, left.at[u, q, pl.ds(tall_row, tall)], lefts[q]),
                        (tall, right.at[u, pl.ds(short_row, short)], rights),
                    )
                    for row, whole, group in ends:
                        rows = pl.ds(row, whole.shape[0])
                        piece = pieces.at[core, dx, dy, relative(z, q), rows]
                        source, target = (whole, piece) if out else (piece, whole)
                        group.append(pltpu.make_async_copy(source, target, sems.at[count]))
                        count += 1
    return lefts, rights


def mix_spots(mix):
    def spots(z, x, y, c):
        rows = mix.shape[1] // 4
        return ((0, mix.at[2 * z + x, pl.ds(pl.multiple_of((2 * y + c) * rows, 16), rows)]),)

    return spots


def factor(mix, rows, kind, block):
    width = mix.shape[2] // 4
    low = kind * width
    top = mix[2 * block, rows : rows + width // 2, low : low + width]
    bottom = mix[2 * block + 1, rows : rows + width // 2, low : low + width]
    return jnp.concatenate([top, bottom], axis=0)


def down_factor(mix, first, block):
    width = mix.shape[2] // 4
    half = width // 2
    parts = []
    for shard in (2 * block, 2 * block + 1):
        for index in range(4):
            parts.append(mix[shard, first : first + half, index * width : (index + 1) * width])
    return jnp.concatenate(parts, axis=0)


def monarch_small(inputs, right, left):
    width = inputs.shape[1] // BLOCKS
    parts = [dot(columns(inputs, b, width), right(b)) for b in range(BLOCKS)]
    middle = [part.astype(BF16) for part in shuffled(parts)]
    return middle, [dot(middle[b], left(b)) for b in range(BLOCKS)]


def monarch_small_backward(inputs, middle, grads, right, left):
    width = inputs.shape[1] // BLOCKS
    grad_left = [dot_rows(middle[b], grads[b]) for b in range(BLOCKS)]
    back = shuffled([dot_columns(grads[b], left(b)) for b in range(BLOCKS)])
    back = [part.astype(BF16) for part in back]
    grad_right = [dot_rows(columns(inputs, b, width), back[b]) for b in range(BLOCKS)]
    return [dot_columns(back[b], right(b)) for b in range(BLOCKS)], grad_right, grad_left


def store_factor(mix, rows, kind, block, value):
    width = mix.shape[2] // 4
    half = width // 2
    low = kind * width
    mix[2 * block, rows : rows + half, low : low + width] = value[:half].astype(BF16)
    mix[2 * block + 1, rows : rows + half, low : low + width] = value[half:].astype(BF16)


MIXER_OUTS, GLU_OUTS = 12, 6


def cell(values):
    rise = 0.5 * (1.0 + lax.erf(values * (0.5**0.5)))
    return rise, jnp.exp(-0.5 * values * values) * ((2.0 * math.pi) ** -0.5)


def glu_forward_kernel(hidden, table, mix, *refs):
    pieces, result, normed_out, middle_out, branch_out, glu_out, down_out = refs[:7]
    left, right, parts, sems = refs[7:]
    lefts, rights = glu_moves(pieces, left, right, sems, False)
    start_all(rights)
    for q in range(BLOCKS):
        start_all(lefts[q])
    rows, width = hidden.shape
    block = width // BLOCKS
    unit, unused = normalised(hidden[...])
    normed = (unit * table[1:2] + table[3:4]).astype(BF16)
    normed_out[...] = normed
    wait_all(rights)
    for u in range(2):
        for b in range(BLOCKS):
            part = dot(columns(normed, b, block), right[u, b * block : (b + 1) * block]).astype(BF16)
            for q in range(BLOCKS):
                middle_out[u, q, :, b * block : (b + 1) * block] = columns(part, q, block)
    for q in range(BLOCKS):
        wait_all(lefts[q])
        upper = dot(middle_out[0, q], left[0, q])
        gate = dot(middle_out[1, q], left[1, q])
        branch_out[0, q] = upper.astype(BF16)
        branch_out[1, q] = gate.astype(BF16)
        glu = (gate * cell(gate)[0] * upper).astype(BF16)
        glu_out[q] = glu
        parts[q] = dot(glu, down_factor(mix, 7 * block // 6, q))
    down = [part.astype(BF16) for part in shuffled([parts[q] for q in range(BLOCKS)])]
    for b in range(BLOCKS):
        down_out[b] = down[b]
        span = slice(b * block, (b + 1) * block)
        result[:, span] = hidden[:, span] + dot(down[b], factor(mix, block // 2, 2, b))


def glu_backward_kernel(arriving, grad, hidden, table, mix, normed, middle, branch, glu, down, *refs):
    pieces, result, norm_out, mix_grad, glu_grad = refs[:5]
    left, right, low, back, out_sems = refs[5:]
    lefts, rights = arriving
    left_writes, right_writes = glu_moves(glu_grad, left, right, out_sems, True)
    rows, width = hidden.shape
    block = width // BLOCKS
    incoming = grad[...].astype(F32)
    half = incoming.astype(BF16)
    backs = []
    for b in range(BLOCKS):
        part = columns(half, b, block)
        mix_grad[1, b] = dot_rows(down[b], part).astype(BF16)
        backs.append(dot_columns(part, factor(mix, block // 2, 2, b)))
    backs = shuffled(backs)
    for q in range(BLOCKS):
        low[q] = backs[q].astype(BF16)
    for q in range(BLOCKS):
        wait_all(lefts[q])
        step = low[q]
        product = dot_rows(glu[q], step).astype(BF16)
        for index in range(BLOCKS):
            mix_grad[2 + index, q] = product[index * block : (index + 1) * block]
        grad_glu = dot_columns(step, down_factor(mix, 7 * block // 6, q))
        upper = branch[0, q].astype(F32)
        gate = branch[1, q].astype(F32)
        rise, density = cell(gate)
        terms = (grad_glu * gate * rise, grad_glu * upper * (rise + gate * density))
        for u in range(2):
            term = terms[u].astype(BF16)
            wide = dot_columns(term, left[u, q]).astype(BF16)
            left[u, q] = dot_rows(middle[u, q], term).astype(BF16)
            for b in range(BLOCKS):
                back[u, b, :, q * block : (q + 1) * block] = columns(wide, b, block)
        start_all(left_writes[q])
    wait_all(rights)
    outgoing = []
    for b in range(BLOCKS):
        span = slice(b * block, (b + 1) * block)
        total = None
        for u in range(2):
            term = dot_columns(back[u, b], right[u, span])
            right[u, span] = dot_rows(normed[:, span], back[u, b]).astype(BF16)
            total = term if total is None else total + term
        outgoing.append(total)
    start_all(right_writes)
    through, gain, bias = norm_backward(
        jnp.concatenate(outgoing, axis=1), hidden[...], table[1:2]
    )
    result[...] = incoming + through
    norm_out[0:1] = gain
    norm_out[1:2] = bias
    for q in range(BLOCKS):
        wait_all(left_writes[q])
    wait_all(right_writes)


def shifted(values, by):
    length = values.shape[0]
    rolled = pltpu.roll(values, by % length, 0)
    row = lax.broadcasted_iota(jnp.int32, values.shape, 0)
    keep = row >= by if by > 0 else row < length + by
    return jnp.where(keep, rolled, 0.0)


def two_parts(values):
    high = values.astype(BF16)
    return high, (values - high.astype(F32)).astype(BF16)


def to_spectrum(waves, values):
    high, low = two_parts(values)
    return dot(waves[0], high) + (dot(waves[1], high) + dot(waves[0], low))


def from_spectrum(waves, values):
    high, low = two_parts(values)
    return dot_rows(waves[0], high) + (dot_rows(waves[1], high) + dot_rows(waves[0], low))


def multiplied(spectrum, kernel, back):
    length = kernel.shape[1]
    real, imaginary = spectrum[:length], spectrum[length:]
    sign = -1.0 if back else 1.0
    return jnp.concatenate(
        [
            real * kernel[0] - sign * imaginary * kernel[1],
            sign * real * kernel[1] + imaginary * kernel[2],
        ],
        axis=0,
    )


def mixer_forward_kernel(first_layer, *refs):
    hidden_in, marked, live, waves, features = refs[:5]
    pieces = refs[5]
    outs = refs[6:18]
    (
        result,
        hidden_out,
        mix,
        table,
        spectrum_out,
        kernel_out,
        filter_out,
        normed_out,
        middle_out,
        saved_out,
        mixed_out,
        middle_two_out,
    ) = outs
    sems = refs[18]
    copies = piece_copies(pieces, sems, mix_spots(mix))
    start_all(copies)
    wait_all(copies)
    rows, width = hidden_in.shape
    block = width // BLOCKS
    half = block // 2
    length = waves.shape[2]
    wide = mix.shape[0]
    third = 2 * half
    fourth = third + length - half
    span = half
    for w in range(wide):
        table[:, w * span : (w + 1) * span] = mix[w, third : third + 16, block : block + span].astype(F32)
    order = length
    step = order // wide
    smalls = jnp.concatenate(
        [mix[w, third + 16 : third + 32, 2 * block : 2 * block + step] for w in range(wide)], axis=1
    ).astype(F32)
    middle_filter = jnp.concatenate(
        [mix[w, third : third + 16, 2 * block : 2 * block + order] for w in range(wide)], axis=0
    ).astype(F32)
    last = jnp.concatenate(
        [
            mix[w, half:fourth, 3 * block :]
            for w in range(wide)
        ],
        axis=1,
    ).astype(F32)
    lead = exact(features[...], smalls[:8]) + smalls[8:9]
    one = jnp.sin(lead)
    lead_two = exact(one, middle_filter) + smalls[9:10]
    two = jnp.sin(lead_two)
    filter_out[0] = one
    filter_out[1] = two
    filter_out[2] = jnp.cos(lead)
    filter_out[3] = jnp.cos(lead_two)
    fraction = features[:, 0:1]
    window = jnp.exp(-fraction * table[8:9])
    ahead = exact(two, last[:, :width]) * window
    behind = exact(two, last[:, width:]) * window
    kernel_out[:, :width] = ahead
    kernel_out[:, width:] = behind
    wave = waves[0].astype(F32) + waves[1].astype(F32)
    row = lax.broadcasted_iota(jnp.int32, (length, 1), 0)
    weight = jnp.where(row == 0, 0.5 / length, 1.0 / length)
    sums = exact(wave, ahead + behind)
    differences = exact(wave[length:], ahead - behind)
    real = sums[:length]
    spectrum_out[0] = real * weight
    spectrum_out[1] = jnp.where(row == 0, 0.0, differences) * weight
    spectrum_out[2] = jnp.where(row == 0, sums[length : length + 1], real) * weight

    if first_layer:
        hidden = jnp.where(marked[...] > 0.5, table[9:10], hidden_in[...].astype(F32))
    else:
        hidden = hidden_in[...]
    hidden_out[...] = hidden
    unit, unused = normalised(hidden)
    normed = (unit * table[0:1] + table[2:3]).astype(BF16)
    normed_out[...] = normed
    for u in range(2):
        middle, blocks = monarch_small(
            normed, lambda b: factor(mix, 0, u, b), lambda b: factor(mix, 0, 2 + u, b)
        )
        for b in range(BLOCKS):
            middle_out[u, b] = middle[b]
        path = jnp.concatenate(blocks, axis=1)
        saved_out[u] = (path * live[...] if u == 0 else path).astype(BF16)
        if u == 0:
            value = path * live[...]
    gate = path
    for s in range(rows // length):
        inside = slice(s * length, (s + 1) * length)
        alive = live[inside]
        signal = value[inside]
        signal = alive * (
            table[4:5] * shifted(signal, 2) + table[5:6] * shifted(signal, 1) + table[6:7] * signal
        )
        product = multiplied(to_spectrum(waves, signal), spectrum_out, False)
        mixed = from_spectrum(waves, product) + table[7:8] * signal
        saved_out[2, inside] = mixed.astype(BF16)
        mixed_out[inside] = (mixed * gate[inside]).astype(BF16)
    middle, blocks = monarch_small(
        mixed_out[...], lambda b: factor(mix, half, 0, b), lambda b: factor(mix, half, 1, b)
    )
    for b in range(BLOCKS):
        middle_two_out[b] = middle[b]
    result[...] = hidden + jnp.concatenate(blocks, axis=1)


def mixer_backward_kernel(first_layer, tick, *refs):
    (
        grad,
        hidden_in,
        marked,
        live,
        waves,
        features,
        mix,
        table,
        spectrum,
        kernel_in,
        filters,
        normed,
        middle,
        saved,
        mixed,
        middle_two,
        norm_two,
        down_grads,
    ) = refs[:18]
    result, grad_out = refs[18:20]
    mix_grad, sum_scratch, value_scratch, table_grad, sems = refs[20:]
    rows, width = hidden_in.shape
    block = width // BLOCKS
    half = block // 2
    length = waves.shape[2]
    wide = mix.shape[0]
    third = 2 * half
    fourth = third + length - half
    mix_grad[:, third:fourth] = jnp.zeros((wide, fourth - third, width), BF16)
    incoming = grad[...]
    low = incoming.astype(BF16)
    blocks = [columns(low, b, block) for b in range(BLOCKS)]
    outs, right_grads, left_grads = monarch_small_backward(
        mixed[...],
        [middle_two[b] for b in range(BLOCKS)],
        blocks,
        lambda b: factor(mix, half, 0, b),
        lambda b: factor(mix, half, 1, b),
    )
    for b in range(BLOCKS):
        store_factor(mix_grad, half, 0, b, right_grads[b])
        store_factor(mix_grad, half, 1, b, left_grads[b])
        store_factor(mix_grad, half, 2, b, down_grads[1, b])
        for index in range(4):
            w = 2 * b + index // 2
            for part in range(2):
                position = (index % 2) * 2 + part
                mix_grad[w, fourth : fourth + half, position * block : (position + 1) * block] = (
                    down_grads[2 + index, b, part * half : (part + 1) * half]
                )
    grad_mixed = jnp.concatenate(outs, axis=1)
    gate = saved[1].astype(F32)
    value_scratch[1] = grad_mixed * saved[2].astype(F32)
    value_scratch[0] = grad_mixed * gate
    tick(0)
    table_grad[...] = jnp.zeros_like(table_grad)
    sum_scratch[...] = jnp.zeros_like(sum_scratch)
    for s in range(rows // length):
        inside = slice(s * length, (s + 1) * length)
        alive = live[inside]
        value = saved[0, inside].astype(F32)
        behind_two, behind_one = shifted(value, 2), shifted(value, 1)
        signal = alive * (
            table[4:5] * behind_two + table[5:6] * behind_one + table[6:7] * value
        )
        inner = value_scratch[0, inside]
        table_grad[7:8] += jnp.sum(inner * signal, axis=0, keepdims=True)
        wave_signal = to_spectrum(waves, signal)
        wave_grad = to_spectrum(waves, inner)
        real, imaginary = wave_signal[:length], wave_signal[length:]
        grad_real, grad_imaginary = wave_grad[:length], wave_grad[length:]
        sum_scratch[0] += grad_real * real
        sum_scratch[1] += grad_imaginary * real - grad_real * imaginary
        sum_scratch[2] += grad_imaginary * imaginary
        grad_signal = from_spectrum(waves, multiplied(wave_grad, spectrum, True))
        grad_signal = alive * (grad_signal + table[7:8] * inner)
        table_grad[4:5] += jnp.sum(grad_signal * behind_two, axis=0, keepdims=True)
        table_grad[5:6] += jnp.sum(grad_signal * behind_one, axis=0, keepdims=True)
        table_grad[6:7] += jnp.sum(grad_signal * value, axis=0, keepdims=True)
        value_scratch[0, inside] = alive * (
            table[6:7] * grad_signal
            + table[5:6] * shifted(grad_signal, -1)
            + table[4:5] * shifted(grad_signal, -2)
        )
    tick(1)
    row = lax.broadcasted_iota(jnp.int32, (length, 1), 0)
    weight = jnp.where(row == 0, 0.5 / length, 1.0 / length)
    wave = waves[0].astype(F32) + waves[1].astype(F32)
    real = sum_scratch[0] * weight
    other = sum_scratch[2] * weight
    turning = jnp.where(row == 0, 0.0, sum_scratch[1] * weight)
    total = jnp.where(row == 0, real, real + other)
    last_row = jnp.where(row == 0, other, 0.0)
    sums = exact(wave[:length], total, (0, 0)) + exact(wave[length:], last_row, (0, 0))
    differences = exact(wave[length:], turning, (0, 0))
    fraction = features[:, 0:1]
    window = jnp.exp(-fraction * table[8:9])
    count = float(rows // length)
    grad_ahead = (sums + differences + count * kernel_in[:, :width]) * window
    grad_behind = (sums - differences + count * kernel_in[:, width:]) * window
    one, two = filters[0], filters[1]
    middle_filter = jnp.concatenate(
        [mix[w, third : third + 16, 2 * block : 2 * block + length] for w in range(wide)], axis=0
    ).astype(F32)
    grad_two = None
    for w in range(wide):
        source = grad_ahead if w < wide // 2 else grad_behind
        piece = columns(source, w % (wide // 2), block)
        factor_out = mix[w, half:fourth, 3 * block :].astype(F32)
        term = exact(piece, factor_out, (1, 1))
        grad_two = term if grad_two is None else grad_two + term
        mix_grad[w, half:fourth, 3 * block :] = exact(two, piece, (0, 0)).astype(BF16)
    grad_two = grad_two * filters[3]
    grad_one = exact(grad_two, middle_filter, (1, 1)) * filters[2]
    filter_grad = exact(one, grad_two, (0, 0)).astype(BF16)
    smalls = jnp.concatenate(
        [
            exact(features[...], grad_one, (0, 0)),
            jnp.sum(grad_one, axis=0, keepdims=True),
            jnp.sum(grad_two, axis=0, keepdims=True),
            jnp.zeros((6, length), F32),
        ],
        axis=0,
    )
    step = length // wide
    for w in range(wide):
        mix_grad[w, third : third + 16, 2 * block : 2 * block + length] = filter_grad[
            w * step : (w + 1) * step
        ]
        mix_grad[w, third + 16 : third + 32, 2 * block : 2 * block + step] = columns(
            smalls, w, step
        ).astype(BF16)
    tick(2)
    total_in = None
    for u in range(2):
        low = value_scratch[u].astype(BF16)
        outs, right_grads, left_grads = monarch_small_backward(
            normed[...],
            [middle[u, b] for b in range(BLOCKS)],
            [columns(low, b, block) for b in range(BLOCKS)],
            lambda b: factor(mix, 0, u, b),
            lambda b: factor(mix, 0, 2 + u, b),
        )
        for b in range(BLOCKS):
            store_factor(mix_grad, 0, u, b, right_grads[b])
            store_factor(mix_grad, 0, 2 + u, b, left_grads[b])
        joint = jnp.concatenate(outs, axis=1)
        total_in = joint if total_in is None else total_in + joint
    through, gain, bias = norm_backward(total_in, hidden_in[...], table[0:1])
    outgoing = grad[...] + through
    table_grad[0:1] = gain
    table_grad[1:2] = norm_two[0:1]
    table_grad[2:3] = bias
    table_grad[3:4] = norm_two[1:2]
    if first_layer:
        chosen = marked[...] > 0.5
        table_grad[9:10] = jnp.sum(jnp.where(chosen, outgoing, 0.0), axis=0, keepdims=True)
        outgoing = jnp.where(chosen, 0.0, outgoing)
    result[...] = outgoing
    for w in range(wide):
        mix_grad[w, third : third + 16, block : block + half] = columns(
            table_grad[...], w, half
        ).astype(BF16)
    writes = grad_copies(grad_out, sems, mix_spots(mix_grad))
    start_all(writes)
    wait_all(writes)


COSTS = {"finish": 10, "glu_middle": 50, "glu_backward": 38, "mixer_backward": 24}


def call(kernel, name, outs, operands, anywhere, any_outs, scratch):
    vmem = pl.BlockSpec(memory_space=pltpu.VMEM)
    any_space = pl.BlockSpec(memory_space=pl.ANY)
    return pl.pallas_call(
        kernel,
        out_shape=[jax.ShapeDtypeStruct(shape, dtype) for shape, dtype in outs],
        in_specs=[any_space if index in anywhere else vmem for index in range(len(operands))],
        out_specs=[any_space if index in any_outs else vmem for index in range(len(outs))],
        scratch_shapes=scratch,
        compiler_params=pltpu.CompilerParams(vmem_limit_bytes=VMEM_BYTES),
        cost_estimate=pl.CostEstimate(
            flops=COSTS[name] * 10**9, bytes_accessed=COSTS[name] * 10**6, transcendentals=0
        ),
        name=name,
    )(*operands)


def mixer_outs(rows, width, length, quarter):
    block = width // BLOCKS
    return [
        ((rows, width), F32),
        ((rows, width), F32),
        ((8, 4 * quarter, width), BF16),
        ((16, width), F32),
        ((3, length, width), F32),
        ((length, 2 * width), F32),
        ((4, length, length), F32),
        ((rows, width), BF16),
        ((2, BLOCKS, rows, block), BF16),
        ((3, rows, width), BF16),
        ((rows, width), BF16),
        ((BLOCKS, rows, block), BF16),
    ]


def glu_outs(rows, width):
    return [
        ((rows, width), F32),
        ((rows, width), BF16),
        ((2, BLOCKS, rows, width), BF16),
        ((2, BLOCKS, rows, width), BF16),
        ((BLOCKS, rows, width), BF16),
        ((BLOCKS, rows, width // BLOCKS), BF16),
    ]


def glu_middle_kernel(hidden, table, mix, cotangent, pieces, *refs):
    output, result, norm_out, mix_grad, glu_grad = refs[:5]
    saved, refs = refs[5 : 5 + GLU_OUTS], refs[5 + GLU_OUTS :]
    left, right, parts, low, back, sems, out_sems = refs
    glu_forward_kernel(hidden, table, mix, pieces, *saved, left, right, parts, sems)
    output[...] = saved[0][...].astype(BF16)
    outs = (result, norm_out, mix_grad, glu_grad)
    scratch = (left, right, low, back, out_sems)
    glu_backward_kernel(
        ([[]] * BLOCKS, []), cotangent, hidden, table, mix, *saved[1:], pieces, *outs, *scratch
    )


def glu_middle(hidden, table, mix, cotangent, pieces):
    rows, width = hidden.shape
    block = width // BLOCKS
    outs = [
        ((rows, width), BF16),
        ((rows, width), F32),
        ((8, width), F32),
        ((6, BLOCKS, block, block), BF16),
        (pieces.shape, BF16),
    ]
    return call(
        glu_middle_kernel,
        "glu_middle",
        outs,
        (hidden, table, mix, cotangent, pieces),
        (4,),
        (4,),
        [pltpu.VMEM(shape, dtype) for shape, dtype in glu_outs(rows, width)]
        + [
            pltpu.VMEM((2, BLOCKS, width, width), BF16),
            pltpu.VMEM((2, width, width), BF16),
            pltpu.VMEM((BLOCKS, rows, block), F32),
            pltpu.VMEM((BLOCKS, rows, block), BF16),
            pltpu.VMEM((2, BLOCKS, rows, width), BF16),
            pltpu.SemaphoreType.DMA((64,)),
            pltpu.SemaphoreType.DMA((64,)),
        ],
    )


def glu_backward_lean(tick, arrays, scratch, sems):
    grad, table, mix, hidden, normed, down, norm_out, mix_grad = arrays[:8]
    middle, branch, glu, pieces, glu_grad = arrays[8:]
    middle_in, branch_in, glu_in, left, right, low, total = scratch
    rows, width = hidden.shape
    block = width // BLOCKS
    piece_sems, save_sems, out_sems = sems
    whole = LeftSlots(left)
    lefts, rights = glu_moves(pieces, whole, right, piece_sems, False)
    left_writes, right_writes = glu_moves(glu_grad, whole, right, out_sems, True)

    def fetch(q):
        return save_all(
            [middle.at[:, q], branch.at[:, q], glu.at[q]],
            [middle_in, branch_in, glu_in],
            save_sems,
            3 * q,
        )

    start_all(rights)
    start_all(lefts[0])
    coming = fetch(0)
    half = grad[...].astype(BF16)
    backs = []
    for b in range(BLOCKS):
        part = columns(half, b, block)
        mix_grad[1, b] = dot_rows(down[b], part).astype(BF16)
        backs.append(dot_columns(part, factor(mix, block // 2, 2, b)))
    backs = shuffled(backs)
    for q in range(BLOCKS):
        low[q] = backs[q].astype(BF16)
    total[...] = jnp.zeros_like(total)
    wait_all(rights)
    for q in range(BLOCKS):
        if q >= 1:
            tick(q)
        if q + 1 < BLOCKS:
            if q >= 1:
                wait_all(left_writes[q - 1])
            start_all(lefts[q + 1])
        wait_all(coming)
        wait_all(lefts[q])
        step = low[q]
        product = dot_rows(glu_in[...], step).astype(BF16)
        for index in range(BLOCKS):
            mix_grad[2 + index, q] = product[index * block : (index + 1) * block]
        down_block = down_factor(mix, 7 * block // 6, q)
        size = rows // 3
        for part in range(3):
            span = slice(part * size, (part + 1) * size)
            grad_glu = dot_columns(step[span], down_block)
            upper = branch_in[0, span].astype(F32)
            gate = branch_in[1, span].astype(F32)
            rise, density = cell(gate)
            branch_in[0, span] = (grad_glu * gate * rise).astype(BF16)
            branch_in[1, span] = (grad_glu * upper * (rise + gate * density)).astype(BF16)
        for u in range(2):
            term = branch_in[u]
            wide = dot_columns(term, left[q % 2, u]).astype(BF16)
            left[q % 2, u] = dot_rows(middle_in[u], term).astype(BF16)
            here = slice(q * block, (q + 1) * block)
            for b in range(BLOCKS):
                span = slice(b * block, (b + 1) * block)
                chunk = columns(wide, b, block)
                total[b] += dot_columns(chunk, right[u, span, here])
                right[u, span, here] = dot_rows(normed[:, span], chunk).astype(BF16)
        start_all(left_writes[q])
        if q + 1 < BLOCKS:
            coming = fetch(q + 1)
    start_all(right_writes)
    through, gain, bias = norm_backward(
        jnp.concatenate([total[b] for b in range(BLOCKS)], axis=1), hidden[...], table[1:2]
    )
    grad[...] = grad[...] + through
    norm_out[0:1] = gain
    norm_out[1:2] = bias
    for q in (BLOCKS - 2, BLOCKS - 1):
        wait_all(left_writes[q])
    wait_all(right_writes)


class LeftSlots:
    def __init__(self, slots):
        self.slots = slots
        self.shape = (slots.shape[1], BLOCKS) + slots.shape[2:]

    @property
    def at(self):
        return self

    def __getitem__(self, index):
        u, q, rows = index
        return self.slots.at[q % 2, u, rows]


PEERS = ((1, 0, 0, 0), (2, 0, 0, 0), (3, 0, 0, 0), (0, 1, 0, 0), (0, 0, 1, 0), (0, 0, 0, 1))
ALONG_X, ALONG_Y, ACROSS = PEERS[3], PEERS[4], PEERS[5]


def peer(distance, dx, dy, dc):
    z, x, y, c = place()
    return (2 * relative(z, distance) + flip(x, dx), 2 * flip(y, dy) + flip(c, dc))


def greet():
    barrier = pltpu.get_barrier_semaphore()
    for target in PEERS:
        pl.semaphore_signal(
            barrier, inc=1, device_id=peer(*target), device_id_type=pl.DeviceIdType.MESH
        )
    pl.semaphore_wait(barrier, len(PEERS))


class Mail:
    def __init__(self, sent, received):
        self.sent, self.received, self.copies, self.settled = sent, received, [], []

    def send(self, source, target, to):
        index = len(self.copies)
        copy = pltpu.make_async_remote_copy(
            src_ref=source,
            dst_ref=target,
            send_sem=self.sent.at[index],
            recv_sem=self.received.at[index],
            device_id=peer(*to),
            device_id_type=pl.DeviceIdType.MESH,
        )
        copy.start()
        self.copies.append(copy)
        return copy

    def settle(self, copy):
        copy.wait_send()
        self.settled.append(copy)

    def finish(self):
        for copy in self.copies:
            if not any(copy is other for other in self.settled):
                copy.wait_send()


MIXER_BACK = 18
GATHER_COPIES = 12


def gather_steps(mail, own, pieces, rows):
    view = lambda core, dx, dy, first, count: pieces.at[core, dx, dy, pl.ds(first, count), rows]
    along_z = [
        mail.send(own, pieces.at[0, 0, 0, distance, rows], PEERS[distance - 1])
        for distance in (1, 2, 3)
    ]
    yield
    for copy in along_z:
        copy.wait_recv()
    along_x = mail.send(view(0, 0, 0, 0, 4), view(0, 1, 0, 0, 4), ALONG_X)
    along_y = mail.send(view(0, 0, 0, 0, 4), view(0, 0, 1, 0, 4), ALONG_Y)
    across = [mail.send(view(0, 0, 0, 0, 4), view(1, 0, 0, 0, 4), ACROSS)]
    yield
    along_y.wait_recv()
    low = mail.send(view(0, 0, 1, 0, 2), view(0, 1, 1, 0, 2), ALONG_X)
    across.append(mail.send(view(0, 0, 1, 0, 4), view(1, 0, 1, 0, 4), ACROSS))
    along_x.wait_recv()
    high = mail.send(view(0, 1, 0, 2, 2), view(0, 1, 1, 2, 2), ALONG_Y)
    across.append(mail.send(view(0, 1, 0, 0, 4), view(1, 1, 0, 0, 4), ACROSS))
    yield
    low.wait_recv()
    across.append(mail.send(view(0, 1, 1, 0, 2), view(1, 1, 1, 0, 2), ACROSS))
    high.wait_recv()
    across.append(mail.send(view(0, 1, 1, 2, 2), view(1, 1, 1, 2, 2), ACROSS))
    yield
    for copy in across:
        copy.wait_recv()
    yield


def rounds(starts):
    running = []
    waiting = list(starts)
    while waiting or running:
        if waiting:
            running.append(waiting.pop(0)())
        for chunk in reversed(list(running)):
            try:
                next(chunk)
            except StopIteration:
                running.remove(chunk)
        yield


def pipeline(starts, between):
    for number, unused in enumerate(rounds(starts)):
        if number in between:
            between[number]()


def save_all(sources, targets, sems, first):
    copies = [
        pltpu.make_async_copy(source, target, sems.at[first + index])
        for index, (source, target) in enumerate(zip(sources, targets))
    ]
    start_all(copies)
    return copies


def forward_kernel(counts, *refs):
    groups = len(counts)
    owns, refs = refs[:groups], refs[groups:]
    hidden_in, marked, live, waves, features = refs[:5]
    pieces, refs = refs[5 : 5 + groups], refs[5 + groups :]
    first_outs, refs = refs[:MIXER_OUTS], refs[MIXER_OUTS:]
    glu_outs, refs = refs[:GLU_OUTS], refs[GLU_OUTS:]
    second_outs, refs = refs[:MIXER_OUTS], refs[MIXER_OUTS:]
    mixer, refs = refs[:MIXER_OUTS], refs[MIXER_OUTS:]
    glu, refs = refs[:GLU_OUTS], refs[GLU_OUTS:]
    staged, refs = refs[:groups], refs[groups:]
    left, right, parts, sent, received, local, loads = refs
    mail = Mail(sent, received)
    copies = [
        pltpu.make_async_copy(own, stage, local.at[index])
        for index, (own, stage) in enumerate(zip(owns, staged))
    ]
    start_all(copies)
    greet()
    starts = []
    for index, count in enumerate(counts):
        size = owns[index].shape[0] // count
        for part in range(count):
            rows = pl.ds(part * size, size)
            starts.append(
                partial(gather_steps, mail, owns[index].at[rows], pieces[index], rows)
            )
    wait_all(copies)
    own_copies = save_all(
        staged, [array.at[0, 0, 0, 0] for array in pieces], local, groups
    )
    saves = []

    def store_own():
        wait_all(own_copies)

    def first_mixer():
        mixer_forward_kernel(
            True, hidden_in, marked, live, waves, features, pieces[0], *mixer, loads
        )
        saves.extend(save_all(mixer, first_outs, local, 2 * groups))

    def first_glu():
        glu_forward_kernel(
            mixer[0], mixer[3], mixer[2], pieces[1], *glu, left, right, parts, loads
        )
        saves.extend(save_all(glu, glu_outs, local, 2 * groups + MIXER_OUTS))

    def second_mixer():
        wait_all(saves[:MIXER_OUTS])
        mixer_forward_kernel(
            False, glu[0], marked, live, waves, features, pieces[2], *mixer, loads
        )
        saves.extend(save_all(mixer, second_outs, local, 2 * groups + MIXER_OUTS + GLU_OUTS))

    ready = [sum(counts[: index + 1]) + 3 for index in range(3)]
    pipeline(
        starts, {0: store_own, ready[0]: first_mixer, ready[1]: first_glu, ready[2]: second_mixer}
    )
    wait_all(saves[MIXER_OUTS:])
    mail.finish()


def forward(quarters, counts, hidden, marked, live, waves, features, number):
    rows, width = hidden.shape
    groups = len(counts)
    anywhere = pl.BlockSpec(memory_space=pl.ANY)
    vmem = pl.BlockSpec(memory_space=pltpu.VMEM)
    total = GATHER_COPIES * sum(counts)
    mixer = mixer_outs(rows, width, waves.shape[2], quarters[0].shape[0])
    glu = glu_outs(rows, width)
    outs = [((2, 2, 2, 4) + quarter.shape, BF16) for quarter in quarters] + mixer + glu + mixer
    block = width // BLOCKS
    result = pl.pallas_call(
        partial(forward_kernel, counts),
        out_shape=[jax.ShapeDtypeStruct(shape, dtype) for shape, dtype in outs],
        in_specs=[anywhere] * groups + [vmem] * 5,
        out_specs=[anywhere] * len(outs),
        scratch_shapes=[pltpu.VMEM(shape, dtype) for shape, dtype in mixer + glu]
        + [pltpu.VMEM(quarter.shape, BF16) for quarter in quarters]
        + [
            pltpu.VMEM((2, BLOCKS, width, width), BF16),
            pltpu.VMEM((2, width, width), BF16),
            pltpu.VMEM((BLOCKS, rows, block), F32),
            pltpu.SemaphoreType.DMA((total,)),
            pltpu.SemaphoreType.DMA((total,)),
            pltpu.SemaphoreType.DMA((2 * groups + 2 * MIXER_OUTS + GLU_OUTS,)),
            pltpu.SemaphoreType.DMA((64,)),
        ],
        compiler_params=pltpu.CompilerParams(
            collective_id=number, has_side_effects=True, vmem_limit_bytes=VMEM_BYTES
        ),
        name="forward",
    )(*quarters, hidden, marked, live, waves, features)
    pieces, result = result[:groups], result[groups:]
    return (
        pieces,
        result[:MIXER_OUTS],
        result[MIXER_OUTS : MIXER_OUTS + GLU_OUTS],
        result[MIXER_OUTS + GLU_OUTS :],
    )


SCATTER_COPIES = 11
SLOTS = 3


def scatter_steps(mail, local, number, grads, landing, rows, result, spots, users, buffers):
    slots, other, pairs, low_landing, high_landing, three, four, own, last = buffers
    size = own.shape[0]
    slot = number % SLOTS
    first = slots.at[slot, :, :, :, pl.ds(0, size)]
    other = other.at[:, :, :, pl.ds(0, size)]
    split = 2 + number % 2
    two_x = pairs.at[slot, :, pl.ds(0, split), pl.ds(0, size)]
    two_y = pairs.at[slot, :, pl.ds(split, 4 - split), pl.ds(0, size)]
    landed = landing.at[:, :, :, rows]
    x_core = mail.send(grads.at[1, :, :, :, rows], landed, ACROSS)
    for copy in users.pop(slot, ()):
        mail.settle(copy)
    load = pltpu.make_async_copy(grads.at[0, :, :, :, rows], first, local.at[0])
    load.start()
    yield
    x_core.wait_recv()
    fetch = pltpu.make_async_copy(landed, other, local.at[3])
    fetch.start()
    load.wait()
    fetch.wait()
    for dx in range(2):
        for dy in range(2):
            first[dx, dy] += other[dx, dy]
    low = mail.send(first.at[1, :, pl.ds(0, split)], low_landing, ALONG_X)
    high = mail.send(first.at[:, 1, pl.ds(split, 4 - split)], high_landing, ALONG_Y)
    users[slot] = [low, high]
    yield
    low.wait_recv()
    fetch = pltpu.make_async_copy(low_landing, two_x, local.at[4])
    fetch.start()
    high.wait_recv()
    fetch_too = pltpu.make_async_copy(high_landing, two_y, local.at[5])
    fetch_too.start()
    fetch.wait()
    for dy in (1, 0):
        two_x[dy] += first[0, dy, 0:split]
        if dy == 1:
            low = mail.send(two_x.at[1], three.at[pl.ds(0, split)], ALONG_Y)
    fetch_too.wait()
    for dx in (1, 0):
        two_y[dx] += first[dx, 0, split:4]
        if dx == 1:
            high = mail.send(two_y.at[1], three.at[pl.ds(split, 4 - split)], ALONG_X)
    users[slot] += [low, high]
    yield
    low.wait_recv()
    three[0:split] += two_x[0]
    along_z = [mail.send(three.at[d], four.at[d - 1], PEERS[d - 1]) for d in range(1, split)]
    high.wait_recv()
    three[split:4] += two_y[0]
    along_z += [mail.send(three.at[d], four.at[d - 1], PEERS[d - 1]) for d in range(split, 4)]
    yield
    total = three[0].astype(F32)
    for index, copy in enumerate(along_z):
        copy.wait_recv()
        total = total + four[index].astype(F32)
    own[...] = total.astype(BF16)
    mine, theirs = spots
    across = [mail.send(own, result.at[mine, rows], ACROSS)]
    along_y = mail.send(own, last, ALONG_Y)
    keep = pltpu.make_async_copy(own, result.at[mine, rows], local.at[1])
    keep.start()
    yield
    along_y.wait_recv()
    across.append(mail.send(last, result.at[theirs, rows], ACROSS))
    keep_too = pltpu.make_async_copy(last, result.at[theirs, rows], local.at[2])
    keep_too.start()
    yield
    for copy in across:
        copy.wait_recv()
    keep.wait()
    keep_too.wait()
    yield


def scatter_buffers(size, width):
    return [
        pltpu.VMEM((4, size, width), BF16),
        pltpu.VMEM((3, size, width), BF16),
        pltpu.VMEM((size, width), BF16),
        pltpu.VMEM((size, width), BF16),
    ]


COMMON, MADE = (2, 3, 4, 5), (0, 16, 17)


def backward_kernel(parts, *refs):
    take = lambda count: (refs[:count], refs[count:])
    groups = len(parts)
    chunks = sum(len(part) for part in parts)
    (glu_two,), refs = take(1)
    second, refs = take(MIXER_BACK)
    others = [index for index in range(MIXER_BACK) if index not in COMMON + MADE]
    first, refs = take(len(others))
    glu_fixed, refs = take(3)
    glu_saved, refs = take(4)
    (result, mix_two, glu_one, mix_one), refs = take(4)
    results, refs = take(groups)
    landings, refs = take(groups)
    pair_landings, refs = take(2 * chunks)
    inner, refs = take(MIXER_BACK)
    scratch, refs = take(4)
    fixed, refs = take(3)
    lean, refs = take(7)
    (sent, received, local, loads, outs, slots, other, pairs), refs = take(8)
    buffers = refs
    grads = (glu_two, mix_two, glu_one, mix_one)
    fetched = save_all(second, inner, loads, 0)
    fixed_copies = save_all(glu_fixed, fixed, loads, MIXER_BACK)
    mail = Mail(sent, received)
    unused, unused, y, c = place()
    spots = (2 * y + c, 2 * (1 - y) + c)
    greet()
    users = {}
    starts = []
    for index, sizes in enumerate(parts):
        row = 0
        for size in sizes:
            number = len(starts)
            own = (slots, other, pairs) + tuple(pair_landings[2 * number : 2 * number + 2])
            starts.append(
                partial(
                    scatter_steps,
                    mail,
                    local.at[number],
                    number,
                    grads[index],
                    landings[index],
                    pl.ds(row, size),
                    results[index],
                    spots,
                    users,
                    own + tuple(buffers[4 * number : 4 * number + 4]),
                )
            )
            row += size
    running = rounds(starts)
    done = [0]

    def turn(count):
        for unused in range(count):
            next(running, None)
            done[0] += 1

    turn(2)
    wait_all(fetched)
    mixer_backward_kernel(
        False, lambda part: turn(part == 1), *inner, inner[0], mix_two, *scratch, outs
    )
    fetched = save_all(first, [inner[index] for index in others], loads, 0)
    turn(1)
    wait_all(fetched + fixed_copies)
    hidden, normed, down = fixed
    middle, branch, glu, pieces = glu_saved
    arrays = (inner[0], inner[7], inner[6], hidden, normed, down, inner[16], inner[17])
    glu_backward_lean(
        lambda part: turn(1),
        arrays + (middle, branch, glu, pieces, glu_one),
        lean,
        (loads.at[pl.ds(0, 64)], loads.at[pl.ds(64, 12)], outs),
    )
    assert done[0] <= len(parts[0]) + len(parts[1])
    turn(1)
    mixer_backward_kernel(
        True, lambda part: turn(1), *inner, inner[0], mix_one, *scratch, outs
    )
    assert done[0] <= chunks - len(parts[3])
    saves = save_all([inner[0]], [result], loads, 0)
    for unused in running:
        pass
    wait_all(saves)
    mail.finish()


def backward(glu_two, parts, second, first, glu_saved, number):
    anywhere = pl.BlockSpec(memory_space=pl.ANY)
    chunks = sum(len(part) for part in parts)
    rows, width = second[0].shape
    block = width // BLOCKS
    mix = second[6]
    length = second[4].shape[2]
    mix_shape = (2, 2, 2, 4, mix.shape[1] // 4, width)
    shapes = [glu_two.shape, mix_shape, glu_two.shape, mix_shape]
    sizes = [size for part in parts for size in part]
    largest = max(sizes)
    buffers, pair_landings = [], []
    for index, size in enumerate(sizes):
        buffers += scatter_buffers(size, width)
        split = 2 + index % 2
        pair_landings += [((2, count, size, width), BF16) for count in (split, 4 - split)]
    total = SCATTER_COPIES * chunks
    outs = (
        [((rows, width), F32)]
        + [(shape, BF16) for shape in shapes[1:]]
        + [((4,) + shape[4:], BF16) for shape in shapes]
        + [(shape[1:], BF16) for shape in shapes]
        + pair_landings
    )
    others = [index for index in range(MIXER_BACK) if index not in COMMON + MADE]
    hidden, normed, middle, branch, glu, down, pieces = glu_saved
    operands = (glu_two,) + tuple(second) + tuple(first[index] for index in others)
    operands += (hidden, normed, down, middle, branch, glu, pieces)
    results = pl.pallas_call(
        partial(backward_kernel, parts),
        out_shape=[jax.ShapeDtypeStruct(shape, dtype) for shape, dtype in outs],
        in_specs=[anywhere] * len(operands),
        out_specs=[anywhere] * len(outs),
        scratch_shapes=[pltpu.VMEM(array.shape, array.dtype) for array in second]
        + [
            pltpu.VMEM(mix.shape, BF16),
            pltpu.VMEM((3, length, width), F32),
            pltpu.VMEM((2, rows, width), F32),
            pltpu.VMEM((16, width), F32),
            pltpu.VMEM(hidden.shape, F32),
            pltpu.VMEM(normed.shape, BF16),
            pltpu.VMEM(down.shape, BF16),
            pltpu.VMEM((2, rows, width), BF16),
            pltpu.VMEM((2, rows, width), BF16),
            pltpu.VMEM((rows, width), BF16),
            pltpu.VMEM((2, 2, width, width), BF16),
            pltpu.VMEM((2, width, width), BF16),
            pltpu.VMEM((BLOCKS, rows, block), BF16),
            pltpu.VMEM((BLOCKS, rows, block), F32),
            pltpu.SemaphoreType.DMA((total,)),
            pltpu.SemaphoreType.DMA((total,)),
            pltpu.SemaphoreType.DMA((chunks, 6)),
            pltpu.SemaphoreType.DMA((80,)),
            pltpu.SemaphoreType.DMA((64,)),
            pltpu.VMEM((SLOTS, 2, 2, 4, largest, width), BF16),
            pltpu.VMEM((2, 2, 4, largest, width), BF16),
            pltpu.VMEM((SLOTS, 2, 4, largest, width), BF16),
        ]
        + buffers,
        compiler_params=pltpu.CompilerParams(
            collective_id=number, has_side_effects=True, vmem_limit_bytes=VMEM_BYTES
        ),
        name="backward",
    )(*operands)
    return results[0], results[4 : 4 + len(parts)]


def prepare_kernel(lengths, positions, mask_vector, *refs):
    members, refs = refs[:18], refs[18:]
    quarters, (live, marked, pack) = refs[: 2 * LAYERS], refs[2 * LAYERS :]
    unused, unused, y, c = place()
    rows, block = members[2].shape[2:]
    order = members[10].shape[2]
    step = members[9].shape[1]
    features = members[6].shape[0]
    third, fourth = 2 * rows, rows + order
    size = pack.shape[0] // 4
    length = live.shape[0] // positions.shape[0]
    place_of = lax.broadcasted_iota(jnp.int32, (length, positions.shape[1]), 0)
    for s in range(positions.shape[0]):
        inside = slice(s * length, (s + 1) * length)
        found = jnp.where(place_of == positions[s : s + 1], 1.0, 0.0)
        marked[inside] = jnp.max(found, axis=1, keepdims=True)
        live[inside] = jnp.where(place_of[:, :1] < lengths[s], 1.0, 0.0)
    flat = {index: members[index][...].astype(F32) for index in (4, 5, 6, 7, 9, 11)}
    for layer in range(LAYERS):
        for u in range(2):
            pack[:rows, u * block : (u + 1) * block] = members[2][layer, u]
            pack[:rows, (2 + u) * block : (3 + u) * block] = members[3][layer, u]
        pack[rows:third, :block] = members[12][layer]
        pack[rows:third, block : 2 * block] = members[13][layer]
        pack[rows:third, 2 * block : 3 * block] = members[17][layer]
        pack[third:fourth] = jnp.zeros((fourth - third, pack.shape[1]), BF16)
        pack[rows:fourth, 3 * block :] = members[10][layer].astype(F32).T.astype(BF16)
        top = [members[index][layer].astype(F32) for index in (0, 1)]
        top += [flat[4][index, layer : layer + 1] for index in range(flat[4].shape[0])]
        top += [flat[5][layer : layer + 1], flat[11][layer : layer + 1]]
        top += [mask_vector[...].astype(F32), jnp.zeros((6, rows), F32)]
        pack[third : third + 16, block : block + rows] = jnp.concatenate(top, axis=0).astype(BF16)
        pack[third : third + step, 2 * block : 2 * block + order] = members[8][layer]
        low = [flat[6][index, layer : layer + 1] for index in range(features)]
        low += [jnp.zeros((8 - features, step), F32)]
        low += [flat[7][layer : layer + 1], flat[9][layer : layer + 1], jnp.zeros((6, step), F32)]
        pack[third + 16 : third + 32, 2 * block : 2 * block + step] = jnp.concatenate(
            low, axis=0
        ).astype(BF16)
        down = members[16][layer].astype(F32).T.astype(BF16)
        for index in range(4):
            pack[fourth:, index * block : (index + 1) * block] = down[
                index * rows : (index + 1) * rows
            ]
        first = pl.multiple_of((2 * y + c) * size, 16)
        quarters[2 * layer][...] = pack[pl.ds(first, size)]
        start = 0
        for index in (15, 14):
            count = members[index].shape[2] // 2
            first = pl.multiple_of(c * count, 16)
            quarters[2 * layer + 1][start : start + count] = members[index][
                layer, y, pl.ds(first, count)
            ]
            start += count


def prepare(lengths, positions, mask_vector, shards, rows):
    members = list(shards)
    for index, axes in TURNED.items():
        members[index] = jnp.swapaxes(members[index], *axes)
    width = shards[15].shape[3]
    tall, short = shards[15].shape[2] // 2, shards[14].shape[2] // 2
    height = 2 * shards[2].shape[2] + shards[10].shape[1]
    outs = [((height // 4, width), BF16), ((tall + short, width), BF16)] * LAYERS
    outs += [((rows, 1), F32)] * 2
    vmem = pl.BlockSpec(memory_space=pltpu.VMEM)
    result = pl.pallas_call(
        prepare_kernel,
        out_shape=[jax.ShapeDtypeStruct(shape, dtype) for shape, dtype in outs],
        in_specs=[pl.BlockSpec(memory_space=pltpu.SMEM)] + [vmem] * (2 + len(members)),
        out_specs=[vmem] * len(outs),
        scratch_shapes=[pltpu.VMEM((height, width), BF16)],
        compiler_params=pltpu.CompilerParams(vmem_limit_bytes=VMEM_BYTES),
        name="prepare",
    )(lengths, positions, mask_vector[None], *members)
    return result[: 2 * LAYERS], result[2 * LAYERS], result[2 * LAYERS + 1]


GRADS = (0, 1, 2, 3, 4, 5, 6, 7, 8, 9, 10, 12, 13, 14, 15, 16, 17)
SHARD_AXIS = (1, 1, 1, 1, 1, 0, 1, 0, 0, 0, 1, 0, 0, 0, 1, 1, 0, 0)


def gather_plain(shards, layer_index):
    return tuple(
        lax.all_gather(shards[index][layer_index], "wide", axis=SHARD_AXIS[index], tiled=True)
        for index in range(18)
    )


def scatter_plain(grads, mask_term):
    terms = list(grads) + ([] if mask_term is None else [mask_term])
    axes = [SHARD_AXIS[index] for index in GRADS] + [0]
    return narrow_total(
        [
            lax.psum_scatter(term, "wide", scatter_dimension=axis, tiled=True)
            for term, axis in zip(terms, axes)
        ]
    )


def wave_table(length):
    frequency = np.arange(length)[:, None]
    places = np.arange(length)[None, :]
    angles = (frequency * places % (2 * length)) * (math.pi / length)
    turned = -np.sin(angles)
    turned[0] = np.where(np.arange(length) % 2 == 0, 1.0, -1.0)
    table = jnp.asarray(np.concatenate([np.cos(angles), turned]), F32)
    high = table.astype(BF16)
    return jnp.stack([high, (table - high.astype(F32)).astype(BF16)])


def feature_table(length):
    fraction = np.arange(length) / length
    table = np.zeros((length, 8))
    table[:, 0] = fraction
    for band in range(1, (EMB - 1) // 2 + 1):
        table[:, 2 * band - 1] = np.cos(2.0 * math.pi * band * fraction)
        table[:, 2 * band] = np.sin(2.0 * math.pi * band * fraction)
    return jnp.asarray(table, F32)


def staged_body(shards, mask_vector, hidden_in, cotangent, seq_lengths, mask_positions):
    rows = hidden_in.shape[0]
    length = rows // seq_lengths.shape[0]
    waves = wave_table(length)
    features = feature_table(length)
    quarters, live, marked = prepare(seq_lengths, mask_positions, mask_vector, shards, rows)
    pieces, mixed_one, second, mixed_two = forward(
        quarters, (1, 3) * LAYERS, hidden_in, marked, live, waves, features, 1
    )
    output, grad, norm_two, down_grads, glu_grads_two = glu_middle(
        mixed_two[0], mixed_two[3], mixed_two[2], cotangent, pieces[3]
    )
    common = (marked, live, waves, features)
    mix_rows = mixed_two[2].shape[1] // 4
    glu_rows = glu_grads_two.shape[4]
    tall = 16 * (glu_rows // 80)
    glu_parts = (tall,) * (glu_rows // tall)
    mix_parts = (tall, mix_rows - tall)
    arrange = lambda made, mixed: (made[0], mixed[1], *common) + tuple(mixed[2:]) + made[1:]
    made = (grad, norm_two, down_grads)
    grad, sums = backward(
        glu_grads_two,
        (glu_parts, mix_parts) * LAYERS,
        arrange(made, mixed_two),
        arrange(made, mixed_one),
        (mixed_one[0],) + tuple(second[1:]) + (pieces[1],),
        2,
    )
    sums = (sums[3], sums[2], sums[1], sums[0])
    found = finish(sums, shards)
    return output, grad, found[-1].reshape(-1), found[:-1]


def finish_kernel(*refs):
    sums, outs = refs[: 2 * LAYERS], refs[2 * LAYERS :]
    found = dict(zip(GRADS, outs))
    mask = outs[-1]
    rows, block = found[2].shape[2:]
    order = found[10].shape[2]
    features, step = found[6].shape[0], found[6].shape[2]
    third, fourth = 2 * rows, rows + order
    for layer in range(LAYERS):
        mix, glu = sums[2 * layer : 2 * layer + 2]
        pack = jnp.concatenate([mix[index] for index in range(4)], axis=0).astype(F32)
        cut = lambda low, high, k: pack[low:high, k * block : (k + 1) * block]
        table = pack[third : third + 16, block : block + rows]
        smalls = pack[third + 16 : third + 32, 2 * block : 2 * block + step]
        for u in range(2):
            found[0][layer, u : u + 1] = table[u : u + 1]
            found[1][layer, u : u + 1] = table[2 + u : 3 + u]
            found[2][layer, u] = cut(0, rows, u)
            found[3][layer, u] = cut(0, rows, 2 + u)
        for index in range(3):
            found[4][index, layer : layer + 1] = table[4 + index : 5 + index]
        found[5][layer : layer + 1] = table[7:8]
        for index in range(features):
            found[6][index, layer : layer + 1] = smalls[index : index + 1]
        found[7][layer : layer + 1] = smalls[8:9]
        found[8][layer] = pack[third : third + step, 2 * block : 2 * block + order]
        found[9][layer : layer + 1] = smalls[9:10]
        found[10][layer] = cut(rows, fourth, 3).T
        found[12][layer] = cut(rows, third, 0)
        found[13][layer] = cut(rows, third, 1)
        found[16][layer] = jnp.concatenate(
            [cut(fourth, fourth + rows, index) for index in range(4)], axis=0
        ).T
        found[17][layer] = cut(rows, third, 2)
        if layer == 0:
            mask[...] = table[9:10]
        tall, short = found[15].shape[2] // 2, found[14].shape[2] // 2
        for u in range(2):
            for core in range(2):
                quarter = glu[2 * u + core].astype(F32)
                found[15][layer, u, core * tall : (core + 1) * tall] = quarter[:tall]
                found[14][layer, u, core * short : (core + 1) * short] = quarter[tall:]


TURNED = {4: (0, 1), 6: (0, 1), 10: (1, 2), 16: (1, 2)}


def finish(sums, shards):
    outs = []
    for index in GRADS:
        shape = list(shards[index].shape)
        for one, two in [TURNED[index]] if index in TURNED else []:
            shape[one], shape[two] = shape[two], shape[one]
        outs.append((tuple(shape), F32))
    outs.append(((1, shards[5].shape[1]), F32))
    found = call(finish_kernel, "finish", outs, tuple(sums), (), (), [])
    return [
        jnp.swapaxes(array, *TURNED[index]) if index in TURNED else array
        for index, array in zip(GRADS + (-1,), found)
    ]


def is_staged(shards, mesh_shape):
    short, block = shards[2].shape[2:]
    order, outs = shards[10].shape[1:]
    return (
        tuple(mesh_shape) == (8, 4)
        and short == 96
        and block == 192
        and order == 128
        and outs == block
        and shards[14].shape[2:] == (short, 8 * short)
        and shards[15].shape[2:] == (4 * short, 8 * short)
    )


def narrow_total(parts):
    flattened = jnp.concatenate([member.reshape(-1) for member in parts])
    summed = lax.psum(flattened.astype(jnp.bfloat16), "narrow").astype(jnp.float32)
    result = []
    offset = 0
    for member in parts:
        result.append(summed[offset : offset + member.size].reshape(member.shape))
        offset = offset + member.size
    return result


def plain_body(shards, mask_vector, hidden_in, cotangent, live_mask, marked):
    seq_count = live_mask.shape[0]
    mask_full = lax.all_gather(mask_vector, "wide", axis=0, tiled=True)
    weights = [gather_plain(shards, layer_index) for layer_index in range(LAYERS)]
    hidden = jnp.where(
        marked, mask_full.astype(jnp.float32)[None, :], hidden_in.astype(jnp.float32)
    )
    saved_layers = []
    for layer_index in range(LAYERS):
        hidden, saved = forward_layer(hidden, weights[layer_index], live_mask)
        saved_layers.append(saved)
    output = hidden.astype(jnp.bfloat16)
    share = 0.5 * seq_count
    grad_hidden = cotangent.astype(jnp.float32)
    layer_grads = [None] * LAYERS
    mask_grad = None
    for layer_index in reversed(range(LAYERS)):
        grad_hidden, grads = backward_layer(
            grad_hidden, weights[layer_index], saved_layers[layer_index], live_mask, share
        )
        if layer_index > 0:
            layer_grads[layer_index] = scatter_plain(grads, None)
        else:
            mask_term = jnp.sum(jnp.where(marked, grad_hidden, 0.0), axis=0)
            reduced = scatter_plain(grads, mask_term)
            layer_grads[0] = reduced[:-1]
            mask_grad = reduced[-1]
    grad_input = jnp.where(marked, 0.0, grad_hidden)
    final_grads = [
        jnp.stack([layer_grads[position][member_index] for position in range(LAYERS)])
        for member_index in range(17)
    ]
    return output, grad_input, mask_grad, final_grads


def body(
    mesh_shape,
    hidden_in,
    seq_lengths,
    mask_positions,
    mask_vector,
    cotangent,
    norm_gain,
    norm_bias,
    in_right,
    in_left,
    conv_taps,
    skip_bias,
    filter_in,
    filter_in_bias,
    filter_mid,
    filter_mid_bias,
    filter_out,
    decay_rates,
    out_right,
    out_left,
    glu_right,
    glu_left,
    down_right,
    down_left,
):
    row_count = hidden_in.shape[0]
    seq_count = seq_lengths.shape[0]
    length = row_count // seq_count
    places = jnp.arange(length, dtype=jnp.int32)
    live_mask = (places[None, :] < seq_lengths[:, None]).astype(jnp.float32)[:, :, None]
    marked = jnp.any(mask_positions[:, :, None] == places[None, None, :], axis=1).reshape(
        row_count, 1
    )
    shards = (
        norm_gain,
        norm_bias,
        in_right,
        in_left,
        conv_taps,
        skip_bias,
        filter_in,
        filter_in_bias,
        filter_mid,
        filter_mid_bias,
        filter_out,
        decay_rates,
        out_right,
        out_left,
        glu_right,
        glu_left,
        down_right,
        down_left,
    )
    if is_staged(shards, mesh_shape):
        output, grad_input, mask_grad, final_grads = staged_body(
            shards, mask_vector, hidden_in, cotangent, seq_lengths, mask_positions
        )
    else:
        output, grad_input, mask_grad, final_grads = plain_body(
            shards, mask_vector, hidden_in, cotangent, live_mask, marked
        )
    return (output, grad_input, mask_grad) + tuple(final_grads)


def solution(mesh):
    placed = (
        P(("wide", "narrow"), None),
        P(("wide", "narrow")),
        P(("wide", "narrow"), None),
        P("wide"),
        P(("wide", "narrow"), None),
        P(None, None, "wide"),
        P(None, None, "wide"),
        P(None, None, "wide", None),
        P(None, None, "wide", None),
        P(None, None, "wide"),
        P(None, "wide"),
        P(None, None, "wide"),
        P(None, "wide"),
        P(None, "wide", None),
        P(None, "wide"),
        P(None, None, "wide"),
        P(None, "wide"),
        P(None, "wide", None),
        P(None, "wide", None),
        P(None, None, "wide", None),
        P(None, None, "wide", None),
        P(None, "wide", None),
        P(None, "wide", None),
    )
    return jax.shard_map(
        partial(body, (mesh.shape["wide"], mesh.shape["narrow"])),
        mesh=mesh,
        in_specs=placed,
        out_specs=(
            P(("wide", "narrow"), None),
            P(("wide", "narrow"), None),
            P("wide"),
            P(None, None, "wide"),
            P(None, None, "wide"),
            P(None, None, "wide", None),
            P(None, None, "wide", None),
            P(None, None, "wide"),
            P(None, "wide"),
            P(None, None, "wide"),
            P(None, "wide"),
            P(None, "wide", None),
            P(None, "wide"),
            P(None, None, "wide"),
            P(None, "wide", None),
            P(None, "wide", None),
            P(None, None, "wide", None),
            P(None, None, "wide", None),
            P(None, "wide", None),
            P(None, "wide", None),
        ),
        check_vma=False,
    )
```
